32 devices in a mesh: ctx: 4 (over z), fsdp: 8 (over y, x, core).
Axes of the slice: x: 2, y: 2, z: 4, core: 2. Of those that a mesh axis runs over, the one named last changes fastest.
Arguments:
- inputs: bfloat16 [8, 1024, 2048], P('fsdp', 'ctx'), may hold values from -6 to 6
- block_ids: int32 [8, 1024], P('fsdp'), may hold values from 0 to 3, never falling along the last dimension, each value on 1 to 512 neighbouring positions
- expert_ids: int32 [8, 1024, 8], P('fsdp', 'ctx'), may hold values from 0 to 31, all different within a row
- drop_order: int32 [8, 4, 256], P('fsdp', 'ctx'), may hold values from 0 to 255, each once within a row
- attn_gain: bfloat16 [2048], P('fsdp'), may hold values from 0.5 to 1.5
- w_query: bfloat16 [2048, 4096], P('fsdp'), may hold values from -0.125 to 0.125
- key_projection_weight: bfloat16 [2048, 512], P('fsdp'), may hold values from -0.125 to 0.125
- value_projection_weight: bfloat16 [2048, 512], P('fsdp'), may hold values from -0.125 to 0.125
- q_gain: bfloat16 [128], P('fsdp'), may hold values from 0.099609375 to 1.8984375
- key_norm_gain: bfloat16 [128], P('fsdp'), may hold values from 0.099609375 to 1.8984375
- w_out: bfloat16 [4096, 2048], P('fsdp'), may hold values from -0.75 to 0.75
- ffn_gain: bfloat16 [2048], P('fsdp'), may hold values from 0.5 to 1.5
- w_router: bfloat16 [2048, 32], P('fsdp'), may hold values from -0.06591797 to 0.06591797
- expert_gate: bfloat16 [32, 2048, 768], P(('ctx', 'fsdp')), may hold values from -0.125 to 0.125
- expert_up: bfloat16 [32, 2048, 768], P(('ctx', 'fsdp')), may hold values from -0.125 to 0.125
- expert_down: bfloat16 [32, 768, 2048], P(('ctx', 'fsdp')), may hold values from -0.875 to 0.875
- cotangent: bfloat16 [8, 1024, 2048], P('fsdp', 'ctx'), may hold values from -6 to 6
Outputs:
- output: bfloat16 [8, 1024, 2048], P('fsdp', 'ctx')
- input_grad: bfloat16 [8, 1024, 2048], P('fsdp', 'ctx')
- attn_gain_grad: float32 [2048], P('fsdp')
- w_query_grad: float32 [2048, 4096], P('fsdp')
- w_key_grad: float32 [2048, 512], P('fsdp')
- w_value_grad: float32 [2048, 512], P('fsdp')
- q_gain_grad: float32 [128], P('fsdp')
- k_gain_grad: float32 [128], P('fsdp')
- w_out_grad: float32 [4096, 2048], P('fsdp')
- ffn_gain_grad: float32 [2048], P('fsdp')
- w_router_grad: float32 [2048, 32], P('fsdp')
- expert_gate_grad: float32 [32, 2048, 768], P(('ctx', 'fsdp'))
- expert_up_grad: float32 [32, 2048, 768], P(('ctx', 'fsdp'))
- expert_down_grad: float32 [32, 768, 2048], P(('ctx', 'fsdp'))
The draws below stay inside these ranges and needn't reach their ends.
Inputs may be any that keep to these rules, and one draw needn't show every extreme that they name: `block_ids`: block numbers never fall along a sequence; a block holds 1 to 512 positions. `expert_ids`: each token names 8 different experts. `drop_order`: for each device's group of 256 tokens the ranks are a permutation.
All inputs are finite; a program needn't handle non-finite values.
Results may differ from the reference program's by a relative error of at most 0.025.
Values may be sent and summed in bfloat16 or wider, within the bound.
A program may use at most 320 MiB of HBM per device.

```python
import math
import jax
import jax.numpy as jnp
import numpy as np
from jax import lax

MODEL_WIDTH = 2048
QUERY_HEADS = 32
KEY_VALUE_HEADS = 4
HEAD_SIZE = 128
FF = 768
TOP = 8
SEQ_LEN = 1024
BLOCK = 256
SEQ_DEV = 1
SPAN = 256
TOK_DEV = 256
SEQS = 8
EXPERTS = 32
CAP = 80
BLOCKS = 4
N_CTX = 4
N_FSDP = 8


def steps_of(own_key, dims, pieces, least, largest):
    def one(dim, shards_of):
        draws = jax.random.uniform(jax.random.fold_in(jax.random.fold_in(own_key, 6), dim), (shards_of,), jnp.float32, least / len(pieces), largest / len(pieces))
        return jnp.repeat(jnp.exp(draws), dims[dim] // shards_of).reshape((-1,) + (1,) * (len(dims) - dim - 1))

    gain = one(*pieces[0])
    for cut in pieces[1:]:
        gain = gain * one(*cut)
    return gain


def different_ones(rng, rows, number_of, top, lift):
    ranking = jax.random.permutation(jax.random.fold_in(rng, 1), number_of)
    boost = ranking
    for power in range(3):
        boost = boost * boost // number_of
    boost = boost * lift // number_of
    tickets = jax.random.randint(jax.random.fold_in(rng, 2), (rows, number_of), 0, 4096) + boost
    fixed_rows = jax.random.permutation(jax.random.fold_in(rng, 3), rows)[jnp.arange(number_of) % rows]
    tickets = jnp.where(jnp.arange(rows)[:, None] == fixed_rows[None, :], 1 << 14, tickets)
    priority = tickets * number_of + jnp.arange(number_of)
    return lax.top_k(priority.astype(jnp.int32), top)[1].astype(jnp.int32)


def length_profile(number_of, total, limit, skew):
    weights = [(1 << 20) // math.isqrt(standing ** skew) + 1 for standing in range(2, number_of + 1)]
    spare, given = total - limit - (number_of - 1), [1] * (number_of - 1)
    while spare > 0:
        candidates = [i for i in range(number_of - 1) if given[i] < limit]
        whole, left = sum([weights[i] for i in candidates]), spare
        for i in candidates:
            extra = min(limit - given[i], max(1, left * weights[i] // whole), spare)
            given[i] = given[i] + extra
            spare = spare - extra
    return np.array([limit] + given)


def ragged_sizes(stream_key, count, total, most, slope):
    if count == 2:
        one = jax.random.randint(stream_key, (), max(1, total - most), min(most, total - 1) + 1)
        return jnp.stack([one, total - one])
    sizes = jnp.asarray(length_profile(count, total, most, slope), jnp.int32)
    pairs = (count - 1) // 2
    donor, sink = sizes[1:1 + 2 * pairs:2], sizes[2:2 + 2 * pairs:2]
    slack = jnp.minimum(donor - 1, most - sink)
    passed = jax.random.randint(jax.random.fold_in(stream_key, 1), (pairs,), 0, 1 << 20) % (slack + 1)
    sizes = sizes.at[1:1 + 2 * pairs:2].set(donor - passed).at[2:2 + 2 * pairs:2].set(sink + passed)
    return sizes[jax.random.permutation(jax.random.fold_in(stream_key, 2), count)]


def centred(key, extent, scale, reach, cuts=(), held_as=jnp.bfloat16):
    values = scale * jax.random.normal(key, extent, jnp.float32)
    if cuts:
        values = values * steps_of(key, extent, cuts, -0.22, 0.18)
    return jnp.clip(values, -reach, reach).astype(held_as)


def setup_inputs(seed: int = 0) -> dict:
    keys = jax.random.split(jax.random.key(seed), 18)
    return {
        "inputs": centred(keys[0], (SEQS, SEQ_LEN, MODEL_WIDTH), 1.0, 6.0, ((0, 8), (1, 4))),
        "block_ids": jax.vmap(lambda own: jnp.searchsorted(jnp.cumsum(ragged_sizes(own, BLOCKS, SEQ_LEN, 2 * BLOCK, 2)), jnp.arange(SEQ_LEN), side="right"))(jax.random.split(keys[1], SEQS)).reshape((SEQS, SEQ_LEN)).astype(jnp.int32),
        "expert_ids": different_ones(keys[2], SEQS * SEQ_LEN, EXPERTS, TOP, 2048).reshape((SEQS, SEQ_LEN, TOP)),
        "drop_order": jax.vmap(lambda own: jax.random.permutation(own, TOK_DEV))(jax.random.split(keys[3], N_FSDP * N_CTX)).reshape((N_FSDP, N_CTX, TOK_DEV)).astype(jnp.int32),
        "attn_gain": jnp.clip(1.0 + 0.1 * jax.random.normal(keys[4], (MODEL_WIDTH,), jnp.float32), 0.5, 1.5).astype(jnp.bfloat16),
        "w_query": centred(keys[5], (MODEL_WIDTH, QUERY_HEADS * HEAD_SIZE), MODEL_WIDTH ** -0.5, 0.125, ((0, 8),)),
        "key_projection_weight": centred(keys[6], (MODEL_WIDTH, KEY_VALUE_HEADS * HEAD_SIZE), MODEL_WIDTH ** -0.5, 0.125, ((0, 8),)),
        "value_projection_weight": centred(keys[7], (MODEL_WIDTH, KEY_VALUE_HEADS * HEAD_SIZE), MODEL_WIDTH ** -0.5, 0.125, ((0, 8),)),
        "q_gain": jnp.clip(1.0 + 0.18 * jax.random.normal(keys[8], (HEAD_SIZE,), jnp.float32), 0.099609375, 1.8984375).astype(jnp.bfloat16),
        "key_norm_gain": jnp.clip(1.0 + 0.18 * jax.random.normal(keys[9], (HEAD_SIZE,), jnp.float32), 0.099609375, 1.8984375).astype(jnp.bfloat16),
        "w_out": centred(keys[10], (QUERY_HEADS * HEAD_SIZE, MODEL_WIDTH), (QUERY_HEADS * HEAD_SIZE // 64) ** -0.5, 0.75, ((0, 8),)),
        "ffn_gain": jnp.clip(1.0 + 0.1 * jax.random.normal(keys[11], (MODEL_WIDTH,), jnp.float32), 0.5, 1.5).astype(jnp.bfloat16),
        "w_router": centred(keys[12], (MODEL_WIDTH, EXPERTS), (0.5 / MODEL_WIDTH ** 0.5), 0.06591797, ((0, 8),)),
        "expert_gate": centred(keys[13], (EXPERTS, MODEL_WIDTH, FF), MODEL_WIDTH ** -0.5, 0.125, ((0, 32),)),
        "expert_up": centred(keys[14], (EXPERTS, MODEL_WIDTH, FF), MODEL_WIDTH ** -0.5, 0.125, ((0, 32),)),
        "expert_down": centred(keys[15], (EXPERTS, FF, MODEL_WIDTH), (FF // 16) ** -0.5, 0.875, ((0, 32),)),
        "cotangent": centred(keys[16], (SEQS, SEQ_LEN, MODEL_WIDTH), 1.0, 6.0, ((0, 8), (1, 4))),
    }


EPSILON = 1e-06
ROPE_BASE = 1000000.0
PRECISE = lax.Precision.HIGHEST
MASKED = -1000000000.0

@jax.custom_vjp
def reduced_precision(v):
    return lax.optimization_barrier(v.astype(jnp.bfloat16)).astype(jnp.float32)

@jax.custom_vjp
def low_back(v):
    return v

def low_keep(v):
    return (reduced_precision(v), None)

def low_pass(kept, grad):
    return (grad,)

def back_keep(v):
    return (v, None)

def back_low(kept, grad):
    return (reduced_precision(grad),)
reduced_precision.defvjp(low_keep, low_pass)
low_back.defvjp(back_keep, back_low)

def normalized_rows(values, gain_scale_apply):
    return values * lax.rsqrt(lax.optimization_barrier(jnp.mean(values * values, axis=-1, keepdims=True)) + EPSILON) * gain_scale_apply

def apply_rotation(values, token_positions):
    half_dim = values.shape[-1] // 2
    exponent = jnp.arange(half_dim, dtype=jnp.float32) * (2.0 / values.shape[-1])
    angles = token_positions.astype(jnp.float32)[:, None] * (ROPE_BASE ** (-exponent))[None, :]
    cosine = jnp.cos(angles)[:, None, :]
    sine_part = jnp.sin(angles)[:, None, :]
    first_half = values[..., :half_dim]
    second = values[..., half_dim:]
    return jnp.concatenate([first_half * cosine - second * sine_part, second * cosine + first_half * sine_part], axis=-1)

def to_groups(tensor):
    shaped = tensor.reshape((N_FSDP, SEQ_DEV, N_CTX, SPAN) + tensor.shape[2:])
    return jnp.swapaxes(shaped, 1, 2).reshape((N_FSDP * N_CTX, TOK_DEV) + tensor.shape[2:])

def from_groups(tensor):
    shaped = tensor.reshape((N_FSDP, N_CTX, SEQ_DEV, SPAN) + tensor.shape[2:])
    return jnp.swapaxes(shaped, 1, 2).reshape((SEQS, SEQ_LEN) + tensor.shape[2:])

def slot_table(expert_ids, drop_order):
    routed = to_groups(expert_ids)
    group_total = N_FSDP * N_CTX
    ranks = drop_order.reshape(group_total, TOK_DEV).astype(jnp.int32)
    group_rows = jnp.arange(group_total, dtype=jnp.int32)[:, None]
    token_rows = jnp.broadcast_to(jnp.arange(TOK_DEV, dtype=jnp.int32)[None, :], (group_total, TOK_DEV))
    by_rank = jnp.zeros((group_total, TOK_DEV), jnp.int32).at[group_rows, ranks].set(token_rows)
    chosen = (routed[..., None] == jnp.arange(EXPERTS, dtype=jnp.int32)).astype(jnp.int32)
    member = lax.optimization_barrier(jnp.sum(chosen, axis=2))
    in_order = jnp.take_along_axis(member, by_rank[:, :, None], axis=1)
    running = jnp.cumsum(in_order, axis=1) - in_order
    position = jnp.take_along_axis(running, ranks[:, :, None], axis=1)
    placed = lax.optimization_barrier(jnp.sum(chosen * position[:, :, None, :], axis=-1))
    return jnp.where(placed < CAP, routed * CAP + placed, EXPERTS * CAP).astype(jnp.int32)

def attend_sequence(hidden, block_row, w_query, key_projection_weight, value_projection_weight, q_gain, key_norm_gain):
    sequence_length = hidden.shape[0]
    token_positions = jnp.arange(sequence_length, dtype=jnp.int32)
    q_raw = low_back(jnp.dot(hidden, w_query, precision=PRECISE))
    key_unrotated = low_back(jnp.dot(hidden, key_projection_weight, precision=PRECISE))
    value_unprojected = low_back(jnp.dot(hidden, value_projection_weight, precision=PRECISE))
    query_matrix = reduced_precision(apply_rotation(normalized_rows(q_raw.reshape(sequence_length, QUERY_HEADS, HEAD_SIZE), q_gain), token_positions))
    key_rotated = reduced_precision(apply_rotation(normalized_rows(key_unrotated.reshape(sequence_length, KEY_VALUE_HEADS, HEAD_SIZE), key_norm_gain), token_positions))
    value_rows_reduced = reduced_precision(value_unprojected).reshape(sequence_length, KEY_VALUE_HEADS, HEAD_SIZE)
    visible = block_row[None, :] <= block_row[:, None]
    grouped_rows = query_matrix.reshape(sequence_length, KEY_VALUE_HEADS, QUERY_HEADS // KEY_VALUE_HEADS, HEAD_SIZE).transpose(1, 2, 0, 3)

    def one_head(operands):
        q_head, k_head, v_head = operands
        scores = jnp.einsum('gqd,kd->gqk', q_head, k_head, precision=PRECISE) * HEAD_SIZE ** (-0.5)
        scores = low_back(jnp.where(visible[None], scores, MASKED))
        weights = jax.nn.softmax(scores, axis=-1)
        return jnp.einsum('gqk,kd->gqd', reduced_precision(weights), v_head, precision=PRECISE)
    mixed = lax.map(jax.checkpoint(one_head), (grouped_rows, key_rotated.transpose(1, 0, 2), value_rows_reduced.transpose(1, 0, 2)))
    mixed = mixed.transpose(2, 0, 1, 3).reshape(sequence_length, QUERY_HEADS * HEAD_SIZE)
    return reduced_precision(low_back(mixed))

def expert_group(operands, expert_gate, expert_up, expert_down):
    rows_in, gate_mix, slot_ids = operands
    total_slots = EXPERTS * CAP
    flat_slots = slot_ids.reshape(-1)
    token_ids = jnp.repeat(jnp.arange(TOK_DEV, dtype=jnp.int32), TOP)
    owner_row = jnp.zeros(total_slots, jnp.int32).at[flat_slots].set(token_ids, mode='drop')
    filled = jnp.zeros(total_slots, jnp.float32).at[flat_slots].set(1.0, mode='drop')
    received_rows = low_back(rows_in[owner_row] * filled[:, None]).reshape(EXPERTS, CAP, MODEL_WIDTH)
    gate_act = low_back(jnp.einsum('ecd,edf->ecf', received_rows, expert_gate, precision=PRECISE))
    up_act = low_back(jnp.einsum('ecd,edf->ecf', received_rows, expert_up, precision=PRECISE))
    inner_act = reduced_precision(jax.nn.silu(gate_act) * up_act)
    result = reduced_precision(low_back(jnp.einsum('ecf,efd->ecd', inner_act, expert_down, precision=PRECISE)))
    result = result.reshape(total_slots, MODEL_WIDTH)
    kept_mask = slot_ids < total_slots
    picked = result[jnp.minimum(slot_ids, total_slots - 1)]
    return jnp.einsum('tk,tkd->td', jnp.where(kept_mask, gate_mix, 0.0), picked, precision=PRECISE)

def forward(inputs, attn_gain, w_query, key_projection_weight, value_projection_weight, q_gain, key_norm_gain, w_out, ffn_gain, w_router, expert_gate, expert_up, expert_down, block_ids, expert_ids, slot_ids):
    hidden = reduced_precision(normalized_rows(inputs, attn_gain))

    def one_sequence(operands):
        return attend_sequence(operands[0], operands[1], w_query, key_projection_weight, value_projection_weight, q_gain, key_norm_gain)
    mixed = lax.map(jax.checkpoint(one_sequence), (hidden, block_ids))
    attn_out = low_back(jnp.dot(mixed.reshape(-1, QUERY_HEADS * HEAD_SIZE), w_out, precision=PRECISE)).reshape(SEQS, SEQ_LEN, MODEL_WIDTH)
    resid = inputs + attn_out
    normed = reduced_precision(normalized_rows(resid, ffn_gain))
    logits = low_back(jnp.dot(normed.reshape(-1, MODEL_WIDTH), w_router, precision=PRECISE))
    gate_mix = jax.nn.softmax(jnp.take_along_axis(logits, expert_ids.reshape(-1, TOP), axis=1), axis=-1)

    def one_group(operands):
        return expert_group(operands, expert_gate, expert_up, expert_down)
    moe_out = lax.map(jax.checkpoint(one_group), (to_groups(normed), to_groups(gate_mix.reshape(SEQS, SEQ_LEN, TOP)), slot_ids))
    return resid + from_groups(moe_out)

def reference(inputs, block_ids, expert_ids, drop_order, attn_gain, w_query, key_projection_weight, value_projection_weight, q_gain, key_norm_gain, w_out, ffn_gain, w_router, expert_gate, expert_up, expert_down, cotangent):
    slot_ids = slot_table(expert_ids, drop_order)
    floats = tuple((tensor.astype(jnp.float32) for tensor in (inputs, attn_gain, w_query, key_projection_weight, value_projection_weight, q_gain, key_norm_gain, w_out, ffn_gain, w_router, expert_gate, expert_up, expert_down)))

    def whole(*params):
        return forward(*params, block_ids, expert_ids, slot_ids)
    output, pullback = jax.vjp(whole, *floats)
    grads = pullback(cotangent.astype(jnp.float32))
    return (output.astype(jnp.bfloat16), grads[0].astype(jnp.bfloat16), grads[1], grads[2], grads[3], grads[4], grads[5], grads[6], grads[7], grads[8], grads[9], grads[10], grads[11], grads[12])
```

```python
import functools

import jax
import jax.numpy as jnp
from jax import lax
from jax.experimental import pallas as pl
from jax.experimental.pallas import tpu as pltpu
from jax.sharding import PartitionSpec as P

QUERY_HEADS = 32
KEY_VALUE_HEADS = 4
HEAD_SIZE = 128
TOP = 8

EPSILON = 1e-06
ROPE_BASE = 1000000.0
MASKED = -1000000000.0
SCALE = HEAD_SIZE ** (-0.5)
HALF = HEAD_SIZE // 2
BF = jnp.bfloat16
F32 = jnp.float32


def nt(a, b):
    return lax.dot_general(a, b, (((1,), (1,)), ((), ())), preferred_element_type=F32)


def nn(a, b):
    return lax.dot_general(a, b, (((1,), (0,)), ((), ())), preferred_element_type=F32)


def tn(a, b):
    return lax.dot_general(a, b, (((0,), (0,)), ((), ())), preferred_element_type=F32)


def inverse_rms(values):
    return lax.rsqrt(jnp.mean(values * values, axis=-1, keepdims=True) + EPSILON)


def norm_rope(raw, gain, cosine, sine):
    z = raw * inverse_rms(raw) * gain
    return z * cosine + pltpu.roll(z, HALF, 1) * sine


def norm_rope_back(raw, gain, cosine, sine, grad):
    dz = grad * cosine - pltpu.roll(grad, HALF, 1) * sine
    r = inverse_rms(raw)
    n = dz * gain
    d_raw = r * n - raw * (r * r * r) * jnp.mean(n * raw, axis=-1, keepdims=True)
    return d_raw, jnp.sum(dz * raw * r, axis=0, keepdims=True)


def attention_forward(
    q_ref, k_ref, v_ref, cos_ref, sin_ref, gains_ref, own_ref, key_ref, mixed_ref, total_ref, keys, values_t
):
    cosine, sine = cos_ref[...], sin_ref[...]

    @pl.when(pl.program_id(0) == 0)
    def _():
        keys[...] = norm_rope(k_ref[...], gains_ref[1:2, :], cosine, sine).astype(BF)
        values_t[...] = v_ref[...].T.astype(BF)

    queries = norm_rope(q_ref[...], gains_ref[0:1, :], cosine, sine).astype(BF)
    length = queries.shape[0]
    chunk = 256
    for start in range(0, length, chunk):
        scores = nt(keys[...], queries[start : start + chunk]) * SCALE
        seen = key_ref[...] <= own_ref[0:1, start : start + chunk]
        scores = jnp.where(seen, scores, MASKED)
        top = jnp.max(scores, axis=0, keepdims=True)
        weights = jnp.exp(scores - top)
        total = jnp.sum(weights, axis=0, keepdims=True)
        out = nn(values_t[...], weights.astype(BF)) / total
        mixed_ref[start : start + chunk, :] = out.T.astype(BF)
        total_ref[0, :, start : start + chunk] = jnp.broadcast_to(top + jnp.log(total), (8, chunk))


def attention_backward(
    heads,
    q_ref,
    k_ref,
    v_ref,
    grad_ref,
    total_ref,
    cos_ref,
    sin_ref,
    gains_ref,
    own_ref,
    key_ref,
    dq_ref,
    dkv_ref,
    dgain_ref,
    keys,
    keys_t,
    values,
    dk,
    dv,
):
    cosine, sine = cos_ref[...], sin_ref[...]
    head = pl.program_id(0)

    @pl.when(head == 0)
    def _():
        rotated = norm_rope(k_ref[...], gains_ref[1:2, :], cosine, sine)
        keys[...] = rotated.astype(BF)
        keys_t[...] = rotated.T.astype(BF)
        values[...] = v_ref[...].astype(BF)
        dk[...] = jnp.zeros_like(dk)
        dv[...] = jnp.zeros_like(dv)
        dgain_ref[...] = jnp.zeros_like(dgain_ref)

    queries = norm_rope(q_ref[...], gains_ref[0:1, :], cosine, sine).astype(BF)
    length = queries.shape[0]
    chunk = 256
    for start in range(0, length, chunk):
        rows = slice(start, start + chunk)
        q_part = queries[rows]
        grad = grad_ref[rows, :]
        scores = nt(keys[...], q_part) * SCALE
        seen = key_ref[...] <= own_ref[0:1, rows]
        scores = jnp.where(seen, scores, MASKED)
        weights = jnp.exp(scores - total_ref[0, 0:1, rows])
        d_weights = nt(values[...], grad)
        row_dot = jnp.sum(weights * d_weights, axis=0, keepdims=True)
        d_scores = (weights * (d_weights - row_dot)).astype(BF)
        dv[...] += nn(weights.astype(BF), grad)
        dk[...] += nn(d_scores, q_part)
        d_queries = nn(keys_t[...], d_scores).T * SCALE
        d_raw, d_gain = norm_rope_back(
            q_ref[rows, :], gains_ref[0:1, :], cos_ref[rows, :], sin_ref[rows, :], d_queries
        )
        dq_ref[rows, :] = d_raw.astype(BF)
        dgain_ref[0:1, :] += d_gain

    @pl.when(head == heads - 1)
    def _():
        d_raw, d_gain = norm_rope_back(
            k_ref[...], gains_ref[1:2, :], cosine, sine, dk[...] * SCALE
        )
        dkv_ref[:, :HEAD_SIZE] = d_raw.astype(BF)
        dkv_ref[:, HEAD_SIZE:] = dv[...].astype(BF)
        dgain_ref[1:2, :] = d_gain


def attention_specs(heads, length):
    whole = lambda shape: pl.BlockSpec(shape, lambda h: (0,) * len(shape))
    column = lambda at: pl.BlockSpec((length, HEAD_SIZE), lambda h: (0, at))
    head_column = pl.BlockSpec((length, HEAD_SIZE), lambda h: (0, h))
    totals = pl.BlockSpec((1, 8, length), lambda h: (h, 0, 0))
    shared = [
        whole((length, HEAD_SIZE)),
        whole((length, HEAD_SIZE)),
        whole((8, HEAD_SIZE)),
        whole((8, length)),
        whole((length, 1)),
    ]
    return whole, column, head_column, totals, shared


def run_attention(qkv, heads, cosine, sine, gains, own, key_blocks):
    length = qkv.shape[0]
    whole, column, head_column, totals, shared = attention_specs(heads, length)
    return pl.pallas_call(
        attention_forward,
        grid=(heads,),
        in_specs=[head_column, column(heads), column(heads + 1)] + shared,
        out_specs=[head_column, totals],
        out_shape=[
            jax.ShapeDtypeStruct((length, heads * HEAD_SIZE), BF),
            jax.ShapeDtypeStruct((heads, 8, length), F32),
        ],
        scratch_shapes=[
            pltpu.VMEM((length, HEAD_SIZE), BF),
            pltpu.VMEM((HEAD_SIZE, length), BF),
        ],
        compiler_params=pltpu.CompilerParams(vmem_limit_bytes=48 * 2**20),
        cost_estimate=pl.CostEstimate(
            flops=4 * heads * length * length * HEAD_SIZE,
            bytes_accessed=8 * heads * length * HEAD_SIZE,
            transcendentals=heads * length * length,
        ),
    )(qkv, qkv, qkv, cosine, sine, gains, own, key_blocks)


def run_attention_back(qkv, grad, totals_in, heads, cosine, sine, gains, own, key_blocks):
    length = qkv.shape[0]
    whole, column, head_column, totals, shared = attention_specs(heads, length)
    return pl.pallas_call(
        functools.partial(attention_backward, heads),
        grid=(heads,),
        in_specs=[head_column, column(heads), column(heads + 1), head_column, totals] + shared,
        out_specs=[head_column, whole((length, 2 * HEAD_SIZE)), whole((8, HEAD_SIZE))],
        out_shape=[
            jax.ShapeDtypeStruct((length, heads * HEAD_SIZE), BF),
            jax.ShapeDtypeStruct((length, 2 * HEAD_SIZE), BF),
            jax.ShapeDtypeStruct((8, HEAD_SIZE), F32),
        ],
        scratch_shapes=[
            pltpu.VMEM((length, HEAD_SIZE), BF),
            pltpu.VMEM((HEAD_SIZE, length), BF),
            pltpu.VMEM((length, HEAD_SIZE), BF),
            pltpu.VMEM((length, HEAD_SIZE), F32),
            pltpu.VMEM((length, HEAD_SIZE), F32),
        ],
        compiler_params=pltpu.CompilerParams(vmem_limit_bytes=48 * 2**20),
        cost_estimate=pl.CostEstimate(
            flops=10 * heads * length * length * HEAD_SIZE,
            bytes_accessed=10 * heads * length * HEAD_SIZE,
            transcendentals=heads * length * length,
        ),
    )(qkv, qkv, qkv, grad, totals_in, cosine, sine, gains, own, key_blocks)


def push(source, target, sends, recvs, device):
    copy = pltpu.make_async_remote_copy(
        src_ref=source,
        dst_ref=target,
        send_sem=sends,
        recv_sem=recvs,
        device_id=device,
        device_id_type=pl.DeviceIdType.MESH,
    )
    return copy


def greet(devices):
    barrier = pltpu.get_barrier_semaphore()
    for device in devices:
        pl.semaphore_signal(barrier, 1, device_id=device, device_id_type=pl.DeviceIdType.MESH)
    pl.semaphore_wait(barrier, len(devices))


def line_gather(n_ctx, ctx, fsdp, own_ref, all_ref, up, down, arrived):
    def hop(block, step, sems, to):
        def start(source):
            push(source, all_ref.at[block], sems.at[step], arrived.at[block], (to, fsdp)).start()

        if step == 0:
            start(own_ref)
        else:
            push(
                all_ref.at[block], all_ref.at[block], sems.at[step], arrived.at[block], (to, fsdp)
            ).wait_recv()
            start(all_ref.at[block])

    for step in range(n_ctx - 1):

        @pl.when((ctx - step >= 0) & (ctx < n_ctx - 1))
        def _():
            hop(ctx - step, step, up, ctx + 1)

        @pl.when((ctx + step < n_ctx) & (ctx > 0))
        def _():
            hop(ctx + step, step, down, ctx - 1)

    def finish(block):
        push(own_ref, all_ref.at[block], up.at[0], arrived.at[block], (ctx, fsdp)).wait_recv()

    for other in range(1, n_ctx):

        @pl.when(ctx == n_ctx - 1)
        def _():
            finish(n_ctx - 1 - other)

        @pl.when(ctx == 0)
        def _():
            finish(other)

    for step in range(n_ctx - 1):

        @pl.when((ctx - step >= 0) & (ctx < n_ctx - 1))
        def _():
            push(own_ref, all_ref.at[0], up.at[step], arrived.at[0], (ctx, fsdp)).wait_send()

        @pl.when((ctx + step < n_ctx) & (ctx > 0))
        def _():
            push(own_ref, all_ref.at[0], down.at[step], arrived.at[0], (ctx, fsdp)).wait_send()


def first_gather(
    n_ctx,
    n_fsdp,
    x_ref,
    table_ref,
    packed_ref,
    x_all,
    table_all,
    packed_all,
    local,
    up,
    down,
    arrived,
    table_send,
    table_arrived,
    packed_send,
    passed_send,
    packed_arrived,
):
    ctx, fsdp = lax.axis_index("ctx"), lax.axis_index("fsdp")
    sibling = lax.rem(fsdp + 1, 2) + (fsdp // 2) * 2
    chips = n_fsdp // 2

    def same_core(offset):
        return lax.rem(fsdp + 2 * offset, n_fsdp)

    def along(offset):
        return lax.rem(ctx + offset, n_ctx)

    greet(
        [(along(i), fsdp) for i in range(1, n_ctx)]
        + [(ctx, same_core(i)) for i in range(1, chips)]
        + [(ctx, sibling)]
    )
    kept = [
        pltpu.make_async_copy(x_ref, x_all.at[ctx], local.at[0]),
        pltpu.make_async_copy(table_ref, table_all.at[ctx], local.at[1]),
        pltpu.make_async_copy(packed_ref, packed_all.at[fsdp], local.at[2]),
    ]
    for copy in kept:
        copy.start()

    def packed_copy(source, owner, sems, to):
        return push(source, packed_all.at[owner], sems, packed_arrived.at[owner], (ctx, to))

    for i in range(1, chips):
        packed_copy(packed_ref, fsdp, packed_send.at[i], same_core(i)).start()
    packed_copy(packed_ref, fsdp, packed_send.at[0], sibling).start()
    for i in range(1, n_ctx):
        push(
            table_ref, table_all.at[ctx], table_send.at[i], table_arrived.at[ctx], (along(i), fsdp)
        ).start()
    line_gather(n_ctx, ctx, fsdp, x_ref, x_all, up, down, arrived)
    for i in range(1, chips):
        owner = same_core(chips - i)
        packed_copy(packed_ref, owner, packed_send.at[i], sibling).wait_recv()
        packed_copy(packed_all.at[owner], owner, passed_send.at[i], sibling).start()
    for i in range(chips):
        owner = lax.rem(sibling + 2 * i, n_fsdp)
        packed_copy(packed_ref, owner, packed_send.at[0], sibling).wait_recv()
    for i in range(1, n_ctx):
        owner = along(i)
        push(
            table_ref, table_all.at[owner], table_send.at[i], table_arrived.at[owner], (owner, fsdp)
        ).wait()
    for i in range(chips):
        packed_copy(packed_ref, fsdp, packed_send.at[i], sibling).wait_send()
    for i in range(1, chips):
        packed_copy(packed_ref, fsdp, passed_send.at[i], sibling).wait_send()
    for copy in kept:
        copy.wait()


def run_first_gather(n_ctx, n_fsdp, x, table, packed):
    anywhere = pl.BlockSpec(memory_space=pl.ANY)
    dma = pltpu.SemaphoreType.DMA
    return pl.pallas_call(
        functools.partial(first_gather, n_ctx, n_fsdp),
        in_specs=[anywhere] * 3,
        out_specs=[anywhere] * 3,
        out_shape=[
            jax.ShapeDtypeStruct((n_ctx,) + x.shape, x.dtype),
            jax.ShapeDtypeStruct((n_ctx,) + table.shape, table.dtype),
            jax.ShapeDtypeStruct((n_fsdp,) + packed.shape, packed.dtype),
        ],
        scratch_shapes=[
            dma((3,)),
            dma((n_ctx,)),
            dma((n_ctx,)),
            dma((n_ctx,)),
            dma((n_ctx,)),
            dma((n_ctx,)),
            dma((n_fsdp // 2,)),
            dma((n_fsdp // 2,)),
            dma((n_fsdp,)),
        ],
        compiler_params=pltpu.CompilerParams(collective_id=1, has_side_effects=True),
        cost_estimate=pl.CostEstimate(
            flops=0, bytes_accessed=200 * 2**20, transcendentals=0
        ),
    )(x, table, packed)


def on_device(
    inputs,
    block_ids,
    expert_ids,
    drop_order,
    attn_gain,
    w_query,
    key_projection_weight,
    value_projection_weight,
    q_gain,
    key_norm_gain,
    w_out,
    ffn_gain,
    w_router,
    expert_gate,
    expert_up,
    expert_down,
    cotangent,
):
    n_ctx, n_fsdp = lax.axis_size("ctx"), lax.axis_size("fsdp")
    ctx = lax.axis_index("ctx")
    span, width = inputs.shape[1], inputs.shape[2]
    length = block_ids.shape[1]
    experts = n_ctx * n_fsdp
    capacity = 5 * span * TOP // (4 * experts)
    slots = experts * capacity
    heads = QUERY_HEADS // n_ctx
    share = n_ctx // KEY_VALUE_HEADS
    own_rows = w_query.shape[0]
    q_width = heads * HEAD_SIZE
    qkv_width = q_width + 2 * HEAD_SIZE
    extra_width = -(-(experts + 4) // 128) * 128

    def gather_ctx(array):
        return lax.all_gather(array, "ctx", axis=0, tiled=True)

    def scatter_ctx(array):
        return lax.psum_scatter(array.astype(BF), "ctx", scatter_dimension=0, tiled=True)

    def scatter_fsdp(array):
        parts = route(array.astype(BF).reshape((n_fsdp, -1) + array.shape[1:]))
        return jnp.sum(parts.astype(F32), axis=0).astype(BF)

    def route(rows):
        return lax.all_to_all(rows, "fsdp", split_axis=0, concat_axis=0, tiled=True)

    def columns(weight, index, count):
        return lax.dynamic_slice_in_dim(weight, index * count, count, axis=1)

    def as_column(vector):
        return jnp.pad(vector, (0, own_rows - vector.shape[0]))[:, None]

    packed = jnp.concatenate(
        [
            columns(w_query, ctx, q_width),
            columns(key_projection_weight, ctx // share, HEAD_SIZE),
            columns(value_projection_weight, ctx // share, HEAD_SIZE),
            w_router,
            as_column(attn_gain),
            as_column(ffn_gain),
            as_column(q_gain),
            as_column(key_norm_gain),
            jnp.zeros((own_rows, extra_width - experts - 4), BF),
        ],
        axis=1,
    )
    table = jnp.concatenate(
        [expert_ids[0].T, drop_order[0], jnp.zeros((7, span), jnp.int32)], axis=0
    )
    inputs_all, tables, packed_all = run_first_gather(n_ctx, n_fsdp, inputs[0], table, packed)
    inputs_all = inputs_all.reshape(length, width)
    packed_all = packed_all.reshape(width, qkv_width + extra_width)
    w_qkv = packed_all[:, :qkv_width]
    extra = packed_all[:, qkv_width:].T
    router_t = extra[:experts]
    gain_attn = extra[experts : experts + 1].astype(F32)
    gain_ffn = extra[experts + 1 : experts + 2].astype(F32)

    def head_gain(at):
        return extra[at].reshape(n_fsdp, own_rows)[:, : HEAD_SIZE // n_fsdp].reshape(1, HEAD_SIZE)

    gains = jnp.concatenate(
        [head_gain(experts + 2), head_gain(experts + 3), jnp.zeros((6, HEAD_SIZE), BF)], axis=0
    ).astype(F32)

    named = tables[:, :TOP, :]
    ranks = tables[:, TOP, :]
    here = ctx * n_fsdp + jnp.arange(n_fsdp, dtype=jnp.int32)
    member = jnp.any(named[:, :, None, :] == here[None, None, :, None], axis=1)
    before = (ranks[:, :, None] < ranks[:, None, :]).astype(BF)
    place = jnp.einsum(
        "gjs,gst->gjt", member.astype(BF), before, preferred_element_type=F32
    ).astype(jnp.int32)
    place = jnp.where(member, place, capacity)
    select = (
        place[:, :, None, :] == jnp.arange(capacity, dtype=jnp.int32)[None, None, :, None]
    ).astype(BF)
    chosen = jnp.any(
        named[:, :, :, None] == jnp.arange(experts, dtype=jnp.int32), axis=1
    ).reshape(length, experts)

    def dispatch(rows):
        picked = jnp.einsum(
            "gjkt,gtd->jgkd", select, rows.reshape(n_ctx, span, width), preferred_element_type=F32
        ).astype(BF)
        return route(picked).reshape(slots, width)

    def combine(rows):
        back = route(rows.reshape(n_fsdp, n_ctx, capacity, width))
        return jnp.einsum("gjkt,jgkd->gtd", select, back, preferred_element_type=F32).reshape(
            length, width
        )

    fsdp = lax.axis_index("fsdp")
    chips = n_fsdp // 2
    half = jnp.where(fsdp // 2 == ctx, w_out, jnp.zeros_like(w_out))
    for offset in range(1, chips):
        pairs = [
            (c * n_fsdp + 2 * c + core, c * n_fsdp + 2 * (c ^ offset) + core)
            for c in range(n_ctx)
            for core in range(2)
        ]
        half = half + lax.ppermute(w_out, ("ctx", "fsdp"), pairs)
    other = lax.ppermute(half, "fsdp", [(f, f ^ 1) for f in range(n_fsdp)])
    first = fsdp % 2 == 0
    out_here = jnp.concatenate(
        [jnp.where(first, half, other), jnp.where(first, other, half)], axis=0
    )

    x_all = inputs_all.astype(F32)
    r_all = inverse_rms(x_all)
    hidden = (x_all * r_all * gain_attn).astype(BF)
    qkv = nn(hidden, w_qkv)
    exponent = jnp.arange(HALF, dtype=F32) * (2.0 / HEAD_SIZE)
    angles = jnp.arange(length, dtype=F32)[:, None] * (ROPE_BASE ** (-exponent))[None, :]
    cosine = jnp.tile(jnp.cos(angles), (1, 2))
    sine = jnp.concatenate([-jnp.sin(angles), jnp.sin(angles)], axis=1)
    own_blocks = jnp.broadcast_to(block_ids, (8, length))
    key_blocks = block_ids.reshape(length, 1)
    mixed, totals = run_attention(qkv, heads, cosine, sine, gains, own_blocks, key_blocks)
    grad_own, qkv = lax.optimization_barrier((cotangent[0], qkv))
    grad_all = gather_ctx(grad_own)
    grad_rows = dispatch(grad_all)

    mixed, grad_all = lax.optimization_barrier((mixed, grad_all))
    attn_out = scatter_ctx(nn(mixed, out_here))

    x = inputs[0].astype(F32)
    resid = x + attn_out.astype(F32)
    r_ffn = inverse_rms(resid)
    normed = gather_ctx((resid * r_ffn * gain_ffn).astype(BF))
    normed, grad_rows = lax.optimization_barrier((normed, grad_rows))
    grad_inner = nt(grad_rows, expert_down[0])
    logits = nt(normed, router_t)
    gates = jax.nn.softmax(jnp.where(chosen, logits, -jnp.inf), axis=-1)
    gates_here = lax.dynamic_slice_in_dim(gates, ctx * n_fsdp, n_fsdp, axis=1)
    gates_here = gates_here.reshape(n_ctx, span, n_fsdp).transpose(0, 2, 1)
    slot_gates = jnp.sum(select.astype(F32) * gates_here[:, :, None, :], axis=-1)
    slot_gates = route(slot_gates.transpose(1, 0, 2)).reshape(slots, 1)
    rows = dispatch(normed)

    piece = QUERY_HEADS * HEAD_SIZE // experts
    groups = n_fsdp // n_ctx
    dealt = mixed.reshape(length, groups, n_ctx, piece).transpose(2, 0, 1, 3)
    dealt = lax.all_to_all(
        dealt.reshape(n_ctx, length, groups * piece), "ctx", split_axis=0, concat_axis=0, tiled=True
    )
    rows, dealt = lax.optimization_barrier((rows, dealt))

    g = nn(rows, expert_gate[0])
    u = nn(rows, expert_up[0])
    s = jax.nn.sigmoid(g)
    inner = g * s * u
    inner_low = inner.astype(BF)
    slot_dgates = jnp.sum(inner * grad_inner, axis=-1).reshape(n_fsdp, n_ctx, capacity)
    d_inner = grad_inner * slot_gates
    dg = (d_inner * u * s * (1.0 + g * (1.0 - s))).astype(BF)
    du = (d_inner * g * s).astype(BF)
    d_rows = (nt(dg, expert_gate[0]) + nt(du, expert_up[0])).astype(BF)
    y = (nn(inner_low, expert_down[0]) * slot_gates).astype(BF)
    gate_grad = tn(rows, dg)
    up_grad = tn(rows, du)
    down_grad = tn((inner * slot_gates).astype(BF), grad_rows)

    d_gates = jnp.einsum(
        "gjkt,jgk->gjt", select.astype(F32), route(slot_dgates), precision=lax.Precision.HIGHEST
    )
    weighted = (d_gates * gates_here).transpose(0, 2, 1).reshape(length, n_fsdp)
    d_logits = lax.dynamic_update_slice_in_dim(
        jnp.zeros((length, experts), F32), weighted, ctx * n_fsdp, axis=1
    ) - gates * jnp.sum(weighted, axis=1, keepdims=True)
    d_logits = d_logits.astype(BF)
    d_normed = scatter_ctx(combine(d_rows) + nn(d_logits, router_t)).astype(F32)
    router_grad = tn(normed, d_logits)

    grad = cotangent[0].astype(F32)
    n = d_normed * gain_ffn
    d_resid = grad + r_ffn * n - resid * r_ffn**3 * jnp.mean(n * resid, axis=-1, keepdims=True)
    ffn_gain_grad = jnp.sum(d_normed * resid * r_ffn, axis=0)
    d_attn = gather_ctx(d_resid.astype(BF))
    y_all = combine(y).astype(BF)
    d_attn, y_all = lax.optimization_barrier((d_attn, y_all))
    d_mixed = nt(d_attn, out_here).astype(BF)

    moe = scatter_ctx(y_all).astype(F32)
    output = (resid + moe).astype(BF)[None]

    out_grad = jnp.einsum("ntk,td->nkd", dealt, d_attn, preferred_element_type=F32).astype(BF)
    out_grad = scatter_fsdp(out_grad.reshape(n_fsdp * piece, width))
    out_grad = gather_ctx(out_grad).astype(F32)

    dq, dkv, dgains = run_attention_back(
        qkv, d_mixed, totals, heads, cosine, sine, gains, own_blocks, key_blocks
    )
    dq, moe = lax.optimization_barrier((dq, moe))
    d_qkv = jnp.concatenate([dq, dkv], axis=1)
    d_hidden = nt(d_qkv, w_qkv)
    attn_gain_grad = jnp.sum(d_hidden * x_all * r_all, axis=0)
    d_hidden = scatter_ctx(d_hidden).astype(F32)
    r_attn = inverse_rms(x)
    n = d_hidden * gain_attn
    input_grad = d_resid + r_attn * n - x * r_attn**3 * jnp.mean(n * x, axis=-1, keepdims=True)
    input_grad = input_grad.astype(BF)[None]

    def spread(vector):
        parts = vector.reshape(n_fsdp, HEAD_SIZE // n_fsdp)
        return jnp.pad(parts, ((0, 0), (0, own_rows - parts.shape[1]))).reshape(width)

    small = jnp.stack(
        [attn_gain_grad, ffn_gain_grad, spread(dgains[0]), spread(dgains[1])], axis=1
    )
    extra_grad = jnp.concatenate(
        [
            router_grad.astype(BF),
            small.astype(BF),
            jnp.zeros((width, extra_width - experts - 4), BF),
        ],
        axis=1,
    )
    shared_grad = jnp.concatenate(
        [scatter_fsdp(tn(hidden, d_qkv)), scatter_fsdp(extra_grad)], axis=1
    )
    shared_grad = lax.all_gather(shared_grad, "ctx", axis=0, tiled=False)
    query_grad = (
        shared_grad[:, :, :q_width].transpose(1, 0, 2).reshape(own_rows, n_ctx * q_width).astype(F32)
    )

    def kv_grad(at):
        parts = shared_grad[:, :, at : at + HEAD_SIZE].astype(F32)
        parts = parts.reshape(KEY_VALUE_HEADS, share, own_rows, HEAD_SIZE).sum(axis=1)
        return parts.transpose(1, 0, 2).reshape(own_rows, KEY_VALUE_HEADS * HEAD_SIZE)

    key_grad, value_grad = kv_grad(q_width), kv_grad(q_width + HEAD_SIZE)
    rest = shared_grad[:, :, qkv_width:].astype(F32).sum(axis=0)
    head_rows = HEAD_SIZE // n_fsdp
    return (
        output,
        input_grad,
        rest[:, experts],
        query_grad,
        key_grad,
        value_grad,
        rest[:head_rows, experts + 2],
        rest[:head_rows, experts + 3],
        out_grad,
        rest[:, experts + 1],
        rest[:, :experts],
        gate_grad[None],
        up_grad[None],
        down_grad[None],
    )


def solution(mesh):
    rows, tokens = P("fsdp", None), P("fsdp", "ctx", None)
    vector, expert = P("fsdp"), P(("ctx", "fsdp"), None, None)
    in_specs = (
        tokens,
        rows,
        tokens,
        tokens,
        vector,
        rows,
        rows,
        rows,
        vector,
        vector,
        rows,
        vector,
        rows,
        expert,
        expert,
        expert,
        tokens,
    )
    out_specs = (
        tokens,
        tokens,
        vector,
        rows,
        rows,
        rows,
        vector,
        vector,
        rows,
        vector,
        rows,
        expert,
        expert,
        expert,
    )
    return jax.shard_map(
        on_device, mesh=mesh, in_specs=in_specs, out_specs=out_specs, check_vma=False
    )
```

```python
import functools

import jax
import jax.numpy as jnp
from jax import lax
from jax.experimental import pallas as pl
from jax.experimental.pallas import tpu as pltpu
from jax.sharding import PartitionSpec as P

QUERY_HEADS = 32
KEY_VALUE_HEADS = 4
HEAD_SIZE = 128
TOP = 8

EPSILON = 1e-06
ROPE_BASE = 1000000.0
MASKED = -1000000000.0
SCALE = HEAD_SIZE ** (-0.5)
HALF = HEAD_SIZE // 2
BF = jnp.bfloat16
F32 = jnp.float32


def nt(a, b):
    return lax.dot_general(a, b, (((1,), (1,)), ((), ())), preferred_element_type=F32)


def nn(a, b):
    return lax.dot_general(a, b, (((1,), (0,)), ((), ())), preferred_element_type=F32)


def tn(a, b):
    return lax.dot_general(a, b, (((0,), (0,)), ((), ())), preferred_element_type=F32)


def inverse_rms(values):
    return lax.rsqrt(jnp.mean(values * values, axis=-1, keepdims=True) + EPSILON)


def norm_rope(raw, gain, cosine, sine):
    z = raw * inverse_rms(raw) * gain
    return z * cosine + pltpu.roll(z, HALF, 1) * sine


def norm_rope_back(raw, gain, cosine, sine, grad):
    dz = grad * cosine - pltpu.roll(grad, HALF, 1) * sine
    r = inverse_rms(raw)
    n = dz * gain
    d_raw = r * n - raw * (r * r * r) * jnp.mean(n * raw, axis=-1, keepdims=True)
    return d_raw, jnp.sum(dz * raw * r, axis=0, keepdims=True)


def attention_forward(
    q_ref, k_ref, v_ref, cos_ref, sin_ref, gains_ref, own_ref, key_ref, mixed_ref, total_ref, dealt_ref, keys, values_t
):
    cosine, sine = cos_ref[...], sin_ref[...]

    @pl.when(pl.program_id(0) == 0)
    def _():
        keys[...] = norm_rope(k_ref[...], gains_ref[1:2, :], cosine, sine).astype(BF)
        values_t[...] = v_ref[...].T.astype(BF)

    queries = norm_rope(q_ref[...], gains_ref[0:1, :], cosine, sine).astype(BF)
    length = queries.shape[0]
    chunk = 256
    for start in range(0, length, chunk):
        scores = nt(keys[...], queries[start : start + chunk]) * SCALE
        seen = key_ref[...] <= own_ref[0:1, start : start + chunk]
        scores = jnp.where(seen, scores, MASKED)
        top = jnp.max(scores, axis=0, keepdims=True)
        weights = jnp.exp(scores - top)
        total = jnp.sum(weights, axis=0, keepdims=True)
        out = nn(values_t[...], weights.astype(BF)) / total
        mixed_ref[start : start + chunk, :] = out.T.astype(BF)
        dealt_ref[0, start : start + chunk, :] = out.T.astype(BF)
        total_ref[0, :, start : start + chunk] = jnp.broadcast_to(top + jnp.log(total), (8, chunk))


def attention_backward(
    heads,
    q_ref,
    k_ref,
    v_ref,
    grad_ref,
    total_ref,
    cos_ref,
    sin_ref,
    gains_ref,
    own_ref,
    key_ref,
    dq_ref,
    dkv_ref,
    dgain_ref,
    keys,
    keys_t,
    values,
    dk,
    dv,
):
    cosine, sine = cos_ref[...], sin_ref[...]
    head = pl.program_id(0)

    @pl.when(head == 0)
    def _():
        rotated = norm_rope(k_ref[...], gains_ref[1:2, :], cosine, sine)
        keys[...] = rotated.astype(BF)
        keys_t[...] = rotated.T.astype(BF)
        values[...] = v_ref[...].astype(BF)
        dk[...] = jnp.zeros_like(dk)
        dv[...] = jnp.zeros_like(dv)
        dgain_ref[...] = jnp.zeros_like(dgain_ref)

    queries = norm_rope(q_ref[...], gains_ref[0:1, :], cosine, sine).astype(BF)
    length = queries.shape[0]
    chunk = 256
    for start in range(0, length, chunk):
        rows = slice(start, start + chunk)
        q_part = queries[rows]
        grad = grad_ref[rows, :]
        scores = nt(keys[...], q_part) * SCALE
        seen = key_ref[...] <= own_ref[0:1, rows]
        scores = jnp.where(seen, scores, MASKED)
        weights = jnp.exp(scores - total_ref[0, 0:1, rows])
        d_weights = nt(values[...], grad)
        row_dot = jnp.sum(weights * d_weights, axis=0, keepdims=True)
        d_scores = (weights * (d_weights - row_dot)).astype(BF)
        dv[...] += nn(weights.astype(BF), grad)
        dk[...] += nn(d_scores, q_part)
        d_queries = nn(keys_t[...], d_scores).T * SCALE
        d_raw, d_gain = norm_rope_back(
            q_ref[rows, :], gains_ref[0:1, :], cos_ref[rows, :], sin_ref[rows, :], d_queries
        )
        dq_ref[rows, :] = d_raw.astype(BF)
        dgain_ref[0:1, :] += d_gain

    @pl.when(head == heads - 1)
    def _():
        d_raw, d_gain = norm_rope_back(
            k_ref[...], gains_ref[1:2, :], cosine, sine, dk[...] * SCALE
        )
        dkv_ref[:, :HEAD_SIZE] = d_raw.astype(BF)
        dkv_ref[:, HEAD_SIZE:] = dv[...].astype(BF)
        dgain_ref[1:2, :] = d_gain


def attention_specs(heads, length):
    whole = lambda shape: pl.BlockSpec(shape, lambda h: (0,) * len(shape))
    column = lambda at: pl.BlockSpec((length, HEAD_SIZE), lambda h: (0, at))
    head_column = pl.BlockSpec((length, HEAD_SIZE), lambda h: (0, h))
    totals = pl.BlockSpec((1, 8, length), lambda h: (h, 0, 0))
    shared = [
        whole((length, HEAD_SIZE)),
        whole((length, HEAD_SIZE)),
        whole((8, HEAD_SIZE)),
        whole((8, length)),
        whole((length, 1)),
    ]
    return whole, column, head_column, totals, shared


def run_attention(qkv, heads, n_ctx, cosine, sine, gains, own, key_blocks):
    length = qkv.shape[0]
    whole, column, head_column, totals, shared = attention_specs(heads, length)
    deals = min(n_ctx, heads)
    return pl.pallas_call(
        attention_forward,
        grid=(heads,),
        in_specs=[head_column, column(heads), column(heads + 1)] + shared,
        out_specs=[
            head_column,
            totals,
            pl.BlockSpec((1, length, HEAD_SIZE), lambda h: (h % deals, 0, h // deals)),
        ],
        out_shape=[
            jax.ShapeDtypeStruct((length, heads * HEAD_SIZE), BF),
            jax.ShapeDtypeStruct((heads, 8, length), F32),
            jax.ShapeDtypeStruct((deals, length, heads // deals * HEAD_SIZE), BF),
        ],
        scratch_shapes=[
            pltpu.VMEM((length, HEAD_SIZE), BF),
            pltpu.VMEM((HEAD_SIZE, length), BF),
        ],
        compiler_params=pltpu.CompilerParams(vmem_limit_bytes=48 * 2**20),
        cost_estimate=pl.CostEstimate(
            flops=4 * heads * length * length * HEAD_SIZE,
            bytes_accessed=8 * heads * length * HEAD_SIZE,
            transcendentals=heads * length * length,
        ),
    )(qkv, qkv, qkv, cosine, sine, gains, own, key_blocks)


def run_attention_back(qkv, grad, totals_in, heads, cosine, sine, gains, own, key_blocks):
    length = qkv.shape[0]
    whole, column, head_column, totals, shared = attention_specs(heads, length)
    return pl.pallas_call(
        functools.partial(attention_backward, heads),
        grid=(heads,),
        in_specs=[head_column, column(heads), column(heads + 1), head_column, totals] + shared,
        out_specs=[head_column, whole((length, 2 * HEAD_SIZE)), whole((8, HEAD_SIZE))],
        out_shape=[
            jax.ShapeDtypeStruct((length, heads * HEAD_SIZE), BF),
            jax.ShapeDtypeStruct((length, 2 * HEAD_SIZE), BF),
            jax.ShapeDtypeStruct((8, HEAD_SIZE), F32),
        ],
        scratch_shapes=[
            pltpu.VMEM((length, HEAD_SIZE), BF),
            pltpu.VMEM((HEAD_SIZE, length), BF),
            pltpu.VMEM((length, HEAD_SIZE), BF),
            pltpu.VMEM((length, HEAD_SIZE), F32),
            pltpu.VMEM((length, HEAD_SIZE), F32),
        ],
        compiler_params=pltpu.CompilerParams(vmem_limit_bytes=48 * 2**20),
        cost_estimate=pl.CostEstimate(
            flops=10 * heads * length * length * HEAD_SIZE,
            bytes_accessed=10 * heads * length * HEAD_SIZE,
            transcendentals=heads * length * length,
        ),
    )(qkv, qkv, qkv, grad, totals_in, cosine, sine, gains, own, key_blocks)


def push(source, target, sends, recvs, device):
    copy = pltpu.make_async_remote_copy(
        src_ref=source,
        dst_ref=target,
        send_sem=sends,
        recv_sem=recvs,
        device_id=device,
        device_id_type=pl.DeviceIdType.MESH,
    )
    return copy


def greet(devices):
    barrier = pltpu.get_barrier_semaphore()
    for device in devices:
        pl.semaphore_signal(barrier, 1, device_id=device, device_id_type=pl.DeviceIdType.MESH)
    pl.semaphore_wait(barrier, len(devices))


class LineGather:
    def __init__(self, n_ctx, ctx, fsdp, own_ref, all_ref, up, down, arrived):
        self.n_ctx, self.ctx, self.fsdp = n_ctx, ctx, fsdp
        self.own_ref, self.all_ref = own_ref, all_ref
        self.up, self.down, self.arrived = up, down, arrived

    def copy(self, source, block, sems, step, to):
        return push(
            source, self.all_ref.at[block], sems.at[step], self.arrived.at[block], (to, self.fsdp)
        )

    def going_up(self, step):
        return (self.ctx - step >= 0) & (self.ctx < self.n_ctx - 1)

    def going_down(self, step):
        return (self.ctx + step < self.n_ctx) & (self.ctx > 0)

    def hop(self, block, step, sems, to):
        if step == 0:
            self.copy(self.own_ref, block, sems, step, to).start()
        else:
            self.copy(self.own_ref, block, sems, step, to).wait_recv()
            self.copy(self.all_ref.at[block], block, sems, step, to).start()

    def step(self, step):
        @pl.when(self.going_up(step))
        def _():
            self.hop(self.ctx - step, step, self.up, self.ctx + 1)

        @pl.when(self.going_down(step))
        def _():
            self.hop(self.ctx + step, step, self.down, self.ctx - 1)

    def finish(self):
        for other in range(1, self.n_ctx):

            @pl.when(self.ctx == self.n_ctx - 1)
            def _():
                self.copy(self.own_ref, self.n_ctx - 1 - other, self.up, 0, self.ctx).wait_recv()

            @pl.when(self.ctx == 0)
            def _():
                self.copy(self.own_ref, other, self.up, 0, self.ctx).wait_recv()

        for step in range(self.n_ctx - 1):

            @pl.when(self.going_up(step))
            def _():
                self.copy(self.own_ref, 0, self.up, step, self.ctx).wait_send()

            @pl.when(self.going_down(step))
            def _():
                self.copy(self.own_ref, 0, self.down, step, self.ctx).wait_send()


def first_gather(
    n_ctx,
    n_fsdp,
    x_ref,
    table_ref,
    packed_ref,
    x_all,
    table_all,
    packed_all,
    local,
    up,
    down,
    arrived,
    table_send,
    table_arrived,
    packed_send,
    passed_send,
    packed_arrived,
):
    ctx, fsdp = lax.axis_index("ctx"), lax.axis_index("fsdp")
    sibling = lax.rem(fsdp + 1, 2) + (fsdp // 2) * 2
    chips = n_fsdp // 2

    def same_core(offset):
        return lax.rem(fsdp + 2 * offset, n_fsdp)

    def along(offset):
        return lax.rem(ctx + offset, n_ctx)

    greet(
        [(along(i), fsdp) for i in range(1, n_ctx)]
        + [(ctx, same_core(i)) for i in range(1, chips)]
        + [(ctx, sibling)]
    )
    kept = [
        pltpu.make_async_copy(x_ref, x_all.at[ctx], local.at[0]),
        pltpu.make_async_copy(table_ref, table_all.at[ctx], local.at[1]),
        pltpu.make_async_copy(packed_ref, packed_all.at[fsdp], local.at[2]),
    ]
    for copy in kept:
        copy.start()

    def packed_copy(source, owner, sems, to):
        return push(source, packed_all.at[owner], sems, packed_arrived.at[owner], (ctx, to))

    for i in range(1, chips):
        packed_copy(packed_ref, fsdp, packed_send.at[i], same_core(i)).start()
    packed_copy(packed_ref, fsdp, packed_send.at[0], sibling).start()
    for i in range(1, n_ctx):
        push(
            table_ref, table_all.at[ctx], table_send.at[i], table_arrived.at[ctx], (along(i), fsdp)
        ).start()
    line = LineGather(n_ctx, ctx, fsdp, x_ref, x_all, up, down, arrived)
    for step in range(n_ctx - 1):
        line.step(step)
    for i in range(1, chips):
        owner = same_core(chips - i)
        packed_copy(packed_ref, owner, packed_send.at[i], sibling).wait_recv()
        packed_copy(packed_all.at[owner], owner, passed_send.at[i], sibling).start()
    for i in range(chips):
        owner = lax.rem(sibling + 2 * i, n_fsdp)
        packed_copy(packed_ref, owner, packed_send.at[0], sibling).wait_recv()
    for i in range(1, n_ctx):
        owner = along(i)
        push(
            table_ref, table_all.at[owner], table_send.at[i], table_arrived.at[owner], (owner, fsdp)
        ).wait()
    line.finish()
    for i in range(chips):
        packed_copy(packed_ref, fsdp, packed_send.at[i], sibling).wait_send()
    for i in range(1, chips):
        packed_copy(packed_ref, fsdp, passed_send.at[i], sibling).wait_send()
    for copy in kept:
        copy.wait()


def run_first_gather(n_ctx, n_fsdp, x, table, packed):
    anywhere = pl.BlockSpec(memory_space=pl.ANY)
    dma = pltpu.SemaphoreType.DMA
    return pl.pallas_call(
        functools.partial(first_gather, n_ctx, n_fsdp),
        in_specs=[anywhere] * 3,
        out_specs=[anywhere] * 3,
        out_shape=[
            jax.ShapeDtypeStruct((n_ctx,) + x.shape, x.dtype),
            jax.ShapeDtypeStruct((n_ctx,) + table.shape, table.dtype),
            jax.ShapeDtypeStruct((n_fsdp,) + packed.shape, packed.dtype),
        ],
        scratch_shapes=[
            dma((3,)),
            dma((n_ctx,)),
            dma((n_ctx,)),
            dma((n_ctx,)),
            dma((n_ctx,)),
            dma((n_ctx,)),
            dma((n_fsdp // 2,)),
            dma((n_fsdp // 2,)),
            dma((n_fsdp,)),
        ],
        compiler_params=pltpu.CompilerParams(collective_id=1, has_side_effects=True),
        cost_estimate=pl.CostEstimate(
            flops=0, bytes_accessed=200 * 2**20, transcendentals=0
        ),
    )(x, table, packed)


TILE = 512
AUX = 128


def expert_exchange(
    n_ctx,
    n_fsdp,
    x_ref,
    sel_ref,
    selt_ref,
    gate_ref,
    up_ref,
    down_ref,
    grad_ref,
    dealt_ref,
    rows_ref,
    back_ref,
    part_ref,
    inner_ref,
    dg_ref,
    du_ref,
    y_ref,
    dealt_all,
    w_gate,
    w_up,
    w_down,
    held,
    staged,
    rows_in,
    grad_in,
    inner_out,
    dg_out,
    du_out,
    y_out,
    back_in,
    w_sems,
    local,
    held_send,
    held_arrived,
    rows_send,
    rows_arrived,
    back_send,
    back_arrived,
    part_send,
    part_arrived,
    dealt_send,
    dealt_arrived,
    out_sems,
):
    ctx, fsdp = lax.axis_index("ctx"), lax.axis_index("fsdp")
    experts = n_ctx * n_fsdp
    expert = ctx * n_fsdp + fsdp
    width, hidden = w_gate.shape
    wide = held.shape[2]
    capacity = staged.shape[2]
    half = n_fsdp // 2
    tiles = [(at, min(TILE, wide - at)) for at in range(0, wide, TILE)]

    def along(offset):
        return lax.rem(ctx + offset, n_ctx)

    def around(offset):
        return lax.rem(fsdp + offset, n_fsdp)

    greet(
        [(along(i), fsdp) for i in range(1, n_ctx)] + [(ctx, around(i)) for i in range(1, n_fsdp)]
    )
    weights = [
        pltpu.make_async_copy(gate_ref, w_gate, w_sems.at[0]),
        pltpu.make_async_copy(up_ref, w_up, w_sems.at[1]),
        pltpu.make_async_copy(down_ref, w_down, w_sems.at[2]),
    ]
    own = pltpu.make_async_copy(x_ref, held.at[ctx], local.at[0])
    own.start()
    for copy in weights:
        copy.start()

    def held_copy(step):
        to = lax.rem(ctx + n_ctx - step, n_ctx)
        return push(x_ref, held.at[ctx], held_send.at[step], held_arrived.at[ctx], (to, fsdp))

    def rows_copy(step, group, offset):
        to = around(offset)
        return push(
            staged.at[step, to],
            rows_ref.at[fsdp, group],
            rows_send.at[step, offset],
            rows_arrived.at[group, fsdp],
            (ctx, to),
        )

    def rows_kept(step, group):
        return pltpu.make_async_copy(
            staged.at[step, fsdp], rows_ref.at[fsdp, group], rows_arrived.at[group, fsdp]
        )

    def back_copy(step, group, offset):
        to = around(offset)
        return push(
            staged.at[step, to],
            back_ref.at[group, fsdp],
            back_send.at[step, offset],
            back_arrived.at[group, fsdp],
            (ctx, to),
        )

    def back_kept(step, group):
        return pltpu.make_async_copy(
            staged.at[step, fsdp], back_ref.at[group, fsdp], back_arrived.at[group, fsdp]
        )

    def outputs(group):
        return [
            pltpu.make_async_copy(inner_out, inner_ref.at[:, group], out_sems.at[0]),
            pltpu.make_async_copy(dg_out, dg_ref.at[:, group], out_sems.at[1]),
            pltpu.make_async_copy(du_out, du_ref.at[:, group], out_sems.at[2]),
            pltpu.make_async_copy(y_out, y_ref.at[:, group], out_sems.at[3]),
        ]

    def dispatch(step):
        group = along(step)

        @pl.when(step == 0)
        def _():
            own.wait()

        @pl.when(step > 0)
        def _():
            push(
                x_ref, held.at[group], held_send.at[step], held_arrived.at[group], (group, fsdp)
            ).wait_recv()

        @pl.when(step + 1 < n_ctx)
        def _():
            held_copy(step + 1).start()

        for at, size in tiles:
            picked = nn(sel_ref[group], held[group, :, at : at + size])
            staged[step, :, :, at : at + size] = picked.astype(BF).reshape(n_fsdp, capacity, size)
        rows_kept(step, group).start()
        for offset in range(1, n_fsdp):
            rows_copy(step, group, offset).start()

    def compute(step):
        group = along(step)
        rows_kept(step, group).wait()
        for offset in range(1, n_fsdp):
            source = around(offset)
            push(
                staged.at[step, source],
                rows_ref.at[source, group],
                rows_send.at[step, offset],
                rows_arrived.at[group, source],
                (ctx, source),
            ).wait_recv()
        load_rows = pltpu.make_async_copy(rows_ref.at[:, group], rows_in, local.at[1])
        load_inner = pltpu.make_async_copy(grad_ref.at[:, group], grad_in, local.at[2])
        load_rows.start()
        load_inner.start()

        @pl.when(step == 0)
        def _():
            for copy in weights:
                copy.wait()

        @pl.when(step > 0)
        def _():
            for copy in outputs(group):
                copy.wait()

        for offset in range(1, n_fsdp):
            rows_copy(step, group, offset).wait_send()
        load_rows.wait()
        load_inner.wait()
        count = half * capacity
        lane = lax.broadcasted_iota(jnp.int32, (count, AUX), 1)
        high, low = lane == expert, lane == experts + expert

        @pl.loop(0, 2)
        def _(part):
            sources = pl.ds(part * half, half)
            rows = rows_in[sources, :, :width].reshape(count, width)
            aux = rows_in[sources, :, width:].reshape(count, AUX).astype(F32)
            gate = jnp.sum(jnp.where(high | low, aux, 0.0), axis=1, keepdims=True)
            g = nn(rows, w_gate[...])
            u = nn(rows, w_up[...])
            s = jax.nn.sigmoid(g)
            inner = g * s * u
            d_inner = nt(grad_in[sources].reshape(count, width), w_down[...])
            d_gate = jnp.sum(inner * d_inner, axis=1, keepdims=True)
            d_inner = d_inner * gate
            dg = (d_inner * u * s * (1.0 + g * (1.0 - s))).astype(BF)
            du = (d_inner * g * s).astype(BF)
            inner_out[sources] = (inner * gate).astype(BF).reshape(half, capacity, hidden)
            dg_out[sources] = dg.reshape(half, capacity, hidden)
            du_out[sources] = du.reshape(half, capacity, hidden)
            rest = d_gate - d_gate.astype(BF).astype(F32)
            staged[step, sources, :, width:] = (
                jnp.where(high, d_gate, jnp.where(low, rest, 0.0))
                .astype(BF)
                .reshape(half, capacity, AUX)
            )
            for at in range(0, width, TILE):
                grad = nt(dg, w_gate[at : at + TILE, :]) + nt(du, w_up[at : at + TILE, :])
                staged[step, sources, :, at : at + TILE] = grad.astype(BF).reshape(
                    half, capacity, TILE
                )
            low_inner = inner.astype(BF)
            for at in range(0, width, TILE):
                y = nn(low_inner, w_down[:, at : at + TILE]) * gate
                y_out[sources, :, at : at + TILE] = y.astype(BF).reshape(half, capacity, TILE)

        back_kept(step, group).start()
        for offset in range(1, n_fsdp):
            back_copy(step, group, offset).start()
        for copy in outputs(group):
            copy.start()

    def combine(step):
        group = along(step)
        back_kept(step, group).wait()
        for offset in range(1, n_fsdp):
            source = around(offset)
            push(
                staged.at[step, source],
                back_ref.at[group, source],
                back_send.at[step, offset],
                back_arrived.at[group, source],
                (ctx, source),
            ).wait_recv()
        load = pltpu.make_async_copy(back_ref.at[group], back_in, local.at[1])
        load.start()
        load.wait()
        for at, size in tiles:
            back = back_in[:, :, at : at + size].reshape(n_fsdp * capacity, size)
            held[group, :, at : at + size] = nn(selt_ref[group], back).astype(BF)

        @pl.when(step == 0)
        def _():
            pltpu.make_async_copy(
                held.at[group], part_ref.at[ctx], part_arrived.at[ctx]
            ).start()

        @pl.when(step > 0)
        def _():
            push(
                held.at[group],
                part_ref.at[ctx],
                part_send.at[step],
                part_arrived.at[ctx],
                (group, fsdp),
            ).start()

    def dealt_copy(offset):
        to = along(offset)
        return push(
            dealt_ref.at[to],
            dealt_all.at[ctx],
            dealt_send.at[offset],
            dealt_arrived.at[ctx],
            (to, fsdp),
        )

    dealt_kept = pltpu.make_async_copy(
        dealt_ref.at[ctx], dealt_all.at[ctx], dealt_arrived.at[ctx]
    )

    @pl.loop(0, n_ctx + 3)
    def _(tick):
        @pl.when(tick < n_ctx)
        def _():
            dispatch(tick)

        @pl.when(tick == n_ctx - 1)
        def _():
            dealt_kept.start()
            for offset in range(1, n_ctx):
                dealt_copy(offset).start()

        @pl.when((tick >= 1) & (tick <= n_ctx))
        def _():
            compute(tick - 1)

        @pl.when(tick >= 3)
        def _():
            combine(tick - 3)

    pltpu.make_async_copy(held.at[ctx], part_ref.at[ctx], part_arrived.at[ctx]).wait()
    for step in range(1, n_ctx):
        other = along(step)
        copy = push(
            held.at[other], part_ref.at[other], part_send.at[step], part_arrived.at[other], (other, fsdp)
        )
        copy.wait()
        held_copy(step).wait_send()
    dealt_kept.wait()
    for offset in range(1, n_ctx):
        other = along(offset)
        push(
            dealt_ref.at[other],
            dealt_all.at[other],
            dealt_send.at[offset],
            dealt_arrived.at[other],
            (other, fsdp),
        ).wait()
    for step in range(n_ctx):
        for offset in range(1, n_fsdp):
            back_copy(step, along(step), offset).wait_send()
    for copy in outputs(along(n_ctx - 1)):
        copy.wait()


def run_expert_exchange(n_ctx, n_fsdp, x, select, select_t, gate, up, down, grads, dealt):
    anywhere, inside = pl.BlockSpec(memory_space=pl.ANY), pl.BlockSpec(memory_space=pltpu.VMEM)
    span, wide = x.shape
    width, hidden = gate.shape
    capacity = grads.shape[2]
    slots = (n_fsdp, n_ctx, capacity)
    one = (n_fsdp, capacity)
    dma, vmem, shape = pltpu.SemaphoreType.DMA, pltpu.VMEM, jax.ShapeDtypeStruct
    return pl.pallas_call(
        functools.partial(expert_exchange, n_ctx, n_fsdp),
        in_specs=[anywhere, inside, inside] + [anywhere] * 5,
        out_specs=[anywhere] * 8,
        out_shape=[
            shape(slots + (wide,), BF),
            shape((n_ctx, n_fsdp, capacity, wide), BF),
            shape((n_ctx, span, wide), BF),
            shape(slots + (hidden,), BF),
            shape(slots + (hidden,), BF),
            shape(slots + (hidden,), BF),
            shape(slots + (width,), BF),
            shape(dealt.shape, BF),
        ],
        scratch_shapes=[
            vmem((width, hidden), BF),
            vmem((width, hidden), BF),
            vmem((hidden, width), BF),
            vmem((n_ctx, span, wide), BF),
            vmem((n_ctx,) + one + (wide,), BF),
            vmem(one + (wide,), BF),
            vmem(one + (width,), BF),
            vmem(one + (hidden,), BF),
            vmem(one + (hidden,), BF),
            vmem(one + (hidden,), BF),
            vmem(one + (width,), BF),
            vmem(one + (wide,), BF),
            dma((3,)),
            dma((3,)),
            dma((n_ctx,)),
            dma((n_ctx,)),
            dma((n_ctx, n_fsdp)),
            dma((n_ctx, n_fsdp)),
            dma((n_ctx, n_fsdp)),
            dma((n_ctx, n_fsdp)),
            dma((n_ctx,)),
            dma((n_ctx,)),
            dma((n_ctx,)),
            dma((n_ctx,)),
            dma((4,)),
        ],
        compiler_params=pltpu.CompilerParams(
            collective_id=2, has_side_effects=True, vmem_limit_bytes=60 * 2**20
        ),
        cost_estimate=pl.CostEstimate(
            flops=12 * n_fsdp * n_ctx * capacity * width * hidden,
            bytes_accessed=600 * 2**20,
            transcendentals=0,
        ),
    )(x, select, select_t, gate, up, down, grads, dealt)


def last_reduce(n_ctx, n_fsdp, chunks, dh_ref, *refs):
    ctx, fsdp = lax.axis_index("ctx"), lax.axis_index("fsdp")
    count = (len(refs) - 9) // 11
    ins, refs = refs[:count], refs[count:]
    total_ref, refs = refs[0], refs[1:]
    alls, refs = refs[:count], refs[count:]
    held, low, high, local, up_send, low_arrived, down_send, refs = refs[:7] + (refs[7:],)
    high_arrived, refs = refs[0], refs[1:]
    items = [refs[9 * i : 9 * i + 9] for i in range(count)]
    chips, chip, core = n_fsdp // 2, fsdp // 2, lax.rem(fsdp, 2)
    sibling = chip * 2 + 1 - core

    def along(offset):
        return lax.rem(ctx + offset, n_ctx)

    def other_chip(offset):
        return lax.rem(chip + offset, chips)

    greet(
        [(along(i), fsdp) for i in range(1, n_ctx)]
        + [(ctx, other_chip(i) * 2 + core) for i in range(1, chips)]
        + [(ctx, sibling)]
    )
    load = pltpu.make_async_copy(dh_ref, held, local.at[0])
    load.start()
    crossing, loads, lines = [], [], []
    for at, (in_ref, all_ref, item) in enumerate(zip(ins, alls, items)):
        mine, beside, landed, own, cross, sends, arrived, line_sems, line_arrived = item
        crossing.append(
            push(in_ref.at[:, 1 - core], beside, cross.at[0], cross.at[1], (ctx, sibling))
        )
        crossing[-1].start()
        loads.append(pltpu.make_async_copy(in_ref.at[:, core], mine, local.at[1 + at]))
        loads[-1].start()
        lines.append(
            LineGather(
                n_ctx, ctx, fsdp, own, all_ref, line_sems.at[0], line_sems.at[1], line_arrived
            )
        )
    load.wait()
    size = held.shape[1] // chunks

    def travel(landing, block, chunk, sends, arrived, to):
        rows = pl.ds(chunk * size, size)
        return push(
            held.at[block, rows],
            landing.at[block, rows],
            sends.at[block, chunk],
            arrived.at[block, chunk],
            (to, fsdp),
        )

    def up(block, chunk, to):
        return travel(low, block, chunk, up_send, low_arrived, to)

    def down(block, chunk, to):
        return travel(high, block, chunk, down_send, high_arrived, to)

    def scatter(chunk):
        rows = slice(chunk * size, (chunk + 1) * size)

        def add(block, landing):
            held[block, rows, :] = (
                held[block, rows, :].astype(F32) + landing[block, rows, :].astype(F32)
            ).astype(BF)

        for step in range(n_ctx - 1):
            above, below = n_ctx - 1 - step, step

            @pl.when(ctx < above)
            def _():
                @pl.when(ctx > 0)
                def _():
                    up(above, chunk, ctx).wait_recv()
                    add(above, low)

                up(above, chunk, ctx + 1).start()

            @pl.when(ctx > below)
            def _():
                @pl.when(ctx < n_ctx - 1)
                def _():
                    down(below, chunk, ctx).wait_recv()
                    add(below, high)

                down(below, chunk, ctx - 1).start()

    def settle(chunk):
        rows = slice(chunk * size, (chunk + 1) * size)
        total_ref[rows, :] = held[ctx, rows, :].astype(F32)

        @pl.when(ctx > 0)
        def _():
            up(ctx, chunk, ctx).wait_recv()
            total_ref[rows, :] += low[ctx, rows, :].astype(F32)

        @pl.when(ctx < n_ctx - 1)
        def _():
            down(ctx, chunk, ctx).wait_recv()
            total_ref[rows, :] += high[ctx, rows, :].astype(F32)

    def chip_copy(item, offset):
        mine, beside, landed, own, cross, sends, arrived, line_sems, line_arrived = item
        to = other_chip(offset)
        return push(
            mine.at[to], landed.at[chip], sends.at[offset], arrived.at[chip], (ctx, to * 2 + core)
        )

    scatter(0)
    scatter(1)
    for crossed, loaded, item in zip(crossing, loads, items):
        mine, beside = item[:2]
        loaded.wait()
        crossed.wait_recv()
        for offset in range(1, chips + 1):
            to = other_chip(offset)
            mine[to] = (mine[to].astype(F32) + beside[to].astype(F32)).astype(BF)
            if offset < chips:
                chip_copy(item, offset).start()
    for chunk in range(2, chunks):
        scatter(chunk)
    keeps = []
    for at, (item, line, all_ref) in enumerate(zip(items, lines, alls)):
        mine, beside, landed, own, cross, sends, arrived, line_sems, line_arrived = item
        total = mine[chip].astype(F32)
        for offset in range(1, chips):
            source = other_chip(offset)
            push(
                mine.at[source], landed.at[source], sends.at[offset], arrived.at[source], (ctx, sibling)
            ).wait_recv()
            total = total + landed[source].astype(F32)
        own[...] = total.astype(BF)
        line.step(0)
        keeps.append(pltpu.make_async_copy(own, all_ref.at[ctx], local.at[1 + at]))
        keeps[-1].start()
    for step in range(1, n_ctx - 1):
        for line in lines:
            line.step(step)
    for chunk in range(chunks):
        settle(chunk)
    for crossed, keep, line, item in zip(crossing, keeps, lines, items):
        crossed.wait_send()
        keep.wait()
        line.finish()
        for offset in range(1, chips):
            chip_copy(item, offset).wait_send()
    for chunk in range(chunks):
        for step in range(n_ctx - 1):
            above, below = n_ctx - 1 - step, step

            @pl.when(ctx < above)
            def _():
                up(above, chunk, ctx).wait_send()

            @pl.when(ctx > below)
            def _():
                down(below, chunk, ctx).wait_send()


def run_last_reduce(n_ctx, n_fsdp, d_hidden, grads):
    anywhere = pl.BlockSpec(memory_space=pl.ANY)
    dma, vmem, shape = pltpu.SemaphoreType.DMA, pltpu.VMEM, jax.ShapeDtypeStruct
    chunks, chips = 4, n_fsdp // 2
    _, span, width = d_hidden.shape
    grads = [grad.reshape((chips, 2, -1) + grad.shape[-1:]) for grad in grads]
    blocks = [grad.shape[2:] for grad in grads]
    scratch = [
        vmem(d_hidden.shape, BF),
        vmem(d_hidden.shape, BF),
        vmem(d_hidden.shape, BF),
        dma((1 + len(grads),)),
        dma((n_ctx, chunks)),
        dma((n_ctx, chunks)),
        dma((n_ctx, chunks)),
        dma((n_ctx, chunks)),
    ]
    for block in blocks:
        scratch += [
            vmem((chips,) + block, BF),
            vmem((chips,) + block, BF),
            vmem((chips,) + block, BF),
            vmem(block, BF),
            dma((2,)),
            dma((chips,)),
            dma((chips,)),
            dma((2, n_ctx)),
            dma((n_ctx,)),
        ]
    return pl.pallas_call(
        functools.partial(last_reduce, n_ctx, n_fsdp, chunks),
        in_specs=[anywhere] * (1 + len(grads)),
        out_specs=[pl.BlockSpec(memory_space=pltpu.VMEM)] + [anywhere] * len(grads),
        out_shape=[shape((span, width), F32)] + [shape((n_ctx,) + block, BF) for block in blocks],
        scratch_shapes=scratch,
        compiler_params=pltpu.CompilerParams(
            collective_id=3, has_side_effects=True, vmem_limit_bytes=60 * 2**20
        ),
        cost_estimate=pl.CostEstimate(flops=0, bytes_accessed=300 * 2**20, transcendentals=0),
    )(d_hidden, *grads)


def widen_columns(in_ref, out_ref):
    out_ref[...] = in_ref[0].astype(F32)


def run_widen_columns(blocks, columns):
    n, rows, _ = blocks.shape
    return pl.pallas_call(
        widen_columns,
        grid=(n,),
        in_specs=[pl.BlockSpec((1, rows, columns), lambda i: (i, 0, 0))],
        out_specs=pl.BlockSpec((rows, columns), lambda i: (0, i)),
        out_shape=jax.ShapeDtypeStruct((rows, n * columns), F32),
    )(blocks)


def pick_rows(select_ref, rows_ref, out_ref):
    shape = out_ref.shape
    for at in range(0, shape[3], TILE):
        picked = nn(select_ref[0], rows_ref[0, :, at : at + TILE])
        out_ref[:, 0, :, at : at + TILE] = picked.astype(BF).reshape(shape[0], shape[2], TILE)


def run_pick_rows(select, rows, n_fsdp):
    n_ctx, count, span = select.shape
    capacity, width = count // n_fsdp, rows.shape[2]
    return pl.pallas_call(
        pick_rows,
        grid=(n_ctx,),
        in_specs=[
            pl.BlockSpec((1, count, span), lambda g: (g, 0, 0)),
            pl.BlockSpec((1, span, width), lambda g: (g, 0, 0)),
        ],
        out_specs=pl.BlockSpec((n_fsdp, 1, capacity, width), lambda g: (0, g, 0, 0)),
        out_shape=jax.ShapeDtypeStruct((n_fsdp, n_ctx, capacity, width), BF),
    )(select, rows)


def on_device(
    inputs,
    block_ids,
    expert_ids,
    drop_order,
    attn_gain,
    w_query,
    key_projection_weight,
    value_projection_weight,
    q_gain,
    key_norm_gain,
    w_out,
    ffn_gain,
    w_router,
    expert_gate,
    expert_up,
    expert_down,
    cotangent,
):
    n_ctx, n_fsdp = lax.axis_size("ctx"), lax.axis_size("fsdp")
    ctx = lax.axis_index("ctx")
    span, width = inputs.shape[1], inputs.shape[2]
    length = block_ids.shape[1]
    experts = n_ctx * n_fsdp
    capacity = 5 * span * TOP // (4 * experts)
    slots = experts * capacity
    heads = QUERY_HEADS // n_ctx
    share = n_ctx // KEY_VALUE_HEADS
    own_rows = w_query.shape[0]
    q_width = heads * HEAD_SIZE
    qkv_width = q_width + 2 * HEAD_SIZE
    extra_width = -(-(experts + 4) // 128) * 128

    def gather_ctx(array):
        return lax.all_gather(array, "ctx", axis=0, tiled=True)

    def scatter_ctx(array):
        return lax.psum_scatter(array.astype(BF), "ctx", scatter_dimension=0, tiled=True)

    def route(rows):
        return lax.all_to_all(rows, "fsdp", split_axis=0, concat_axis=0, tiled=True)

    def columns(weight, index, count):
        return lax.dynamic_slice_in_dim(weight, index * count, count, axis=1)

    def as_column(vector):
        return jnp.pad(vector, (0, own_rows - vector.shape[0]))[:, None]

    packed = jnp.concatenate(
        [
            columns(w_query, ctx, q_width),
            columns(key_projection_weight, ctx // share, HEAD_SIZE),
            columns(value_projection_weight, ctx // share, HEAD_SIZE),
            w_router,
            as_column(attn_gain),
            as_column(ffn_gain),
            as_column(q_gain),
            as_column(key_norm_gain),
            jnp.zeros((own_rows, extra_width - experts - 4), BF),
        ],
        axis=1,
    )
    table = jnp.concatenate(
        [expert_ids[0].T, drop_order[0], jnp.zeros((7, span), jnp.int32)], axis=0
    )
    grad_all = gather_ctx(cotangent[0])
    inputs_all, tables, packed_all = run_first_gather(n_ctx, n_fsdp, inputs[0], table, packed)
    w_out, grad_all = lax.optimization_barrier((w_out, grad_all))
    out_all = lax.all_gather(w_out, "fsdp", axis=0, tiled=True)
    out_here = lax.dynamic_slice_in_dim(out_all, ctx * q_width, q_width, axis=0)
    inputs_all = inputs_all.reshape(length, width)
    packed_all = packed_all.reshape(width, qkv_width + extra_width)
    w_qkv = packed_all[:, :qkv_width]
    extra = packed_all[:, qkv_width:].T
    router_t = extra[:experts]
    gain_attn = extra[experts : experts + 1].astype(F32)
    gain_ffn = extra[experts + 1 : experts + 2].astype(F32)

    def head_gain(at):
        return extra[at].reshape(n_fsdp, own_rows)[:, : HEAD_SIZE // n_fsdp].reshape(1, HEAD_SIZE)

    gains = jnp.concatenate(
        [head_gain(experts + 2), head_gain(experts + 3), jnp.zeros((6, HEAD_SIZE), BF)], axis=0
    ).astype(F32)

    named = tables[:, :TOP, :]
    ranks = tables[:, TOP, :]
    here = ctx * n_fsdp + jnp.arange(n_fsdp, dtype=jnp.int32)
    member = jnp.any(named[:, :, None, :] == here[None, None, :, None], axis=1)
    before = (ranks[:, :, None] < ranks[:, None, :]).astype(BF)
    place = jnp.einsum(
        "gjs,gst->gjt", member.astype(BF), before, preferred_element_type=F32
    ).astype(jnp.int32)
    place = jnp.where(member, place, capacity)
    select = (
        place[:, :, None, :] == jnp.arange(capacity, dtype=jnp.int32)[None, None, :, None]
    ).astype(BF)

    fused = capacity % 16 == 0 and 2 * experts <= AUX
    select_rows = select.reshape(n_ctx, n_fsdp * capacity, span)

    def dispatch(rows):
        if fused:
            return route(
                run_pick_rows(select_rows, rows.reshape(n_ctx, span, width), n_fsdp)
            ).reshape(slots, width)
        picked = jnp.einsum(
            "gjkt,gtd->jgkd", select, rows.reshape(n_ctx, span, width), preferred_element_type=F32
        ).astype(BF)
        return route(picked).reshape(slots, width)

    def combine(rows):
        back = route(rows.reshape(n_fsdp, n_ctx, capacity, width))
        return jnp.einsum("gjkt,jgkd->gtd", select, back, preferred_element_type=F32).reshape(
            length, width
        )

    x_all = inputs_all.astype(F32)
    r_all = inverse_rms(x_all)
    hidden = (x_all * r_all * gain_attn).astype(BF)
    qkv = nn(hidden, w_qkv)
    exponent = jnp.arange(HALF, dtype=F32) * (2.0 / HEAD_SIZE)
    angles = jnp.arange(length, dtype=F32)[:, None] * (ROPE_BASE ** (-exponent))[None, :]
    cosine = jnp.tile(jnp.cos(angles), (1, 2))
    sine = jnp.concatenate([-jnp.sin(angles), jnp.sin(angles)], axis=1)
    own_blocks = jnp.broadcast_to(block_ids, (8, length))
    key_blocks = block_ids.reshape(length, 1)
    mixed, totals, dealt = run_attention(
        qkv, heads, n_ctx, cosine, sine, gains, own_blocks, key_blocks
    )
    piece = QUERY_HEADS * HEAD_SIZE // experts
    groups = n_fsdp // n_ctx
    if piece != HEAD_SIZE:
        dealt = mixed.reshape(length, groups, n_ctx, piece).transpose(2, 0, 1, 3)
        dealt = dealt.reshape(n_ctx, length, groups * piece)
    grad_rows = dispatch(grad_all)
    attn_out = scatter_ctx(nn(mixed, out_here))

    x = inputs[0].astype(F32)
    resid = x + attn_out.astype(F32)
    r_ffn = inverse_rms(resid)
    normed = (resid * r_ffn * gain_ffn).astype(BF)
    if fused:
        chosen = jnp.any(
            expert_ids[0][:, :, None] == jnp.arange(experts, dtype=jnp.int32), axis=1
        )
        logits = nt(normed, router_t)
        gates = jax.nn.softmax(jnp.where(chosen, logits, -jnp.inf), axis=-1)
        high = lax.reduce_precision(gates, 8, 7)
        payload = jnp.concatenate(
            [
                normed,
                high.astype(BF),
                (gates - high).astype(BF),
                jnp.zeros((span, AUX - 2 * experts), BF),
            ],
            axis=1,
        )
        rows, _, parts, inner_low, dg, du, y, dealt = run_expert_exchange(
            n_ctx,
            n_fsdp,
            payload,
            select_rows,
            select_rows.swapaxes(1, 2),
            expert_gate[0],
            expert_up[0],
            expert_down[0],
            grad_rows.reshape(n_fsdp, n_ctx, capacity, width),
            dealt,
        )
        rows = rows.reshape(slots, width + AUX)[:, :width]
        inner_low, dg, du = (array.reshape(slots, -1) for array in (inner_low, dg, du))
        y = y.reshape(slots, width)
        parts = jnp.sum(parts.astype(F32), axis=0)
        d_gates = parts[:, width : width + experts] + parts[:, width + experts : width + 2 * experts]
        d_logits = gates * (d_gates - jnp.sum(gates * d_gates, axis=-1, keepdims=True))
        d_logits = d_logits.astype(BF)
        d_normed = parts[:, :width] + nn(d_logits, router_t)
    else:
        dealt = lax.all_to_all(dealt, "ctx", split_axis=0, concat_axis=0, tiled=True)
        chosen = jnp.any(
            named[:, :, :, None] == jnp.arange(experts, dtype=jnp.int32), axis=1
        ).reshape(length, experts)
        normed = gather_ctx(normed)
        normed, grad_rows = lax.optimization_barrier((normed, grad_rows))
        grad_inner = nt(grad_rows, expert_down[0])
        logits = nt(normed, router_t)
        gates = jax.nn.softmax(jnp.where(chosen, logits, -jnp.inf), axis=-1)
        gates_here = lax.dynamic_slice_in_dim(gates, ctx * n_fsdp, n_fsdp, axis=1)
        gates_here = gates_here.reshape(n_ctx, span, n_fsdp).transpose(0, 2, 1)
        slot_gates = jnp.sum(select.astype(F32) * gates_here[:, :, None, :], axis=-1)
        slot_gates = route(slot_gates.transpose(1, 0, 2)).reshape(slots, 1)
        rows = dispatch(normed)
        g = nn(rows, expert_gate[0])
        u = nn(rows, expert_up[0])
        s = jax.nn.sigmoid(g)
        inner = g * s * u
        slot_dgates = jnp.sum(inner * grad_inner, axis=-1).reshape(n_fsdp, n_ctx, capacity)
        d_inner = grad_inner * slot_gates
        dg = (d_inner * u * s * (1.0 + g * (1.0 - s))).astype(BF)
        du = (d_inner * g * s).astype(BF)
        d_rows = (nt(dg, expert_gate[0]) + nt(du, expert_up[0])).astype(BF)
        y = (nn(inner.astype(BF), expert_down[0]) * slot_gates).astype(BF)
        inner_low = (inner * slot_gates).astype(BF)
        d_gates = jnp.einsum(
            "gjkt,jgk->gjt", select.astype(F32), route(slot_dgates), precision=lax.Precision.HIGHEST
        )
        weighted = (d_gates * gates_here).transpose(0, 2, 1).reshape(length, n_fsdp)
        d_logits = lax.dynamic_update_slice_in_dim(
            jnp.zeros((length, experts), F32), weighted, ctx * n_fsdp, axis=1
        ) - gates * jnp.sum(weighted, axis=1, keepdims=True)
        d_logits = d_logits.astype(BF)
        d_normed = scatter_ctx(combine(d_rows) + nn(d_logits, router_t)).astype(F32)

    gate_grad = tn(rows, dg)
    up_grad = tn(rows, du)
    down_grad = tn(inner_low, grad_rows)
    router_grad = tn(normed, d_logits)

    grad = cotangent[0].astype(F32)
    n = d_normed * gain_ffn
    d_resid = grad + r_ffn * n - resid * r_ffn**3 * jnp.mean(n * resid, axis=-1, keepdims=True)
    ffn_gain_grad = jnp.sum(d_normed * resid * r_ffn, axis=0)
    d_attn = gather_ctx(d_resid.astype(BF))
    y_all = combine(y).astype(BF)
    d_attn, y_all = lax.optimization_barrier((d_attn, y_all))
    d_mixed = nt(d_attn, out_here).astype(BF)

    moe = scatter_ctx(y_all).astype(F32)
    output = (resid + moe).astype(BF)[None]

    out_grad = jnp.einsum("ntk,td->nkd", dealt, d_attn, preferred_element_type=F32).astype(BF)

    dq, dkv, dgains = run_attention_back(
        qkv, d_mixed, totals, heads, cosine, sine, gains, own_blocks, key_blocks
    )
    dq, moe = lax.optimization_barrier((dq, moe))
    d_qkv = jnp.concatenate([dq, dkv], axis=1)
    d_hidden = nt(d_qkv, w_qkv)
    attn_gain_grad = jnp.sum(d_hidden * x_all * r_all, axis=0)

    def spread(vector):
        parts = vector.reshape(n_fsdp, HEAD_SIZE // n_fsdp)
        return jnp.pad(parts, ((0, 0), (0, own_rows - parts.shape[1]))).reshape(width)

    small = jnp.stack(
        [attn_gain_grad, ffn_gain_grad, spread(dgains[0]), spread(dgains[1])], axis=1
    )
    extra_grad = jnp.concatenate(
        [
            router_grad.astype(BF),
            small.astype(BF),
            jnp.zeros((width, extra_width - experts - 4), BF),
        ],
        axis=1,
    )
    d_hidden, shared_grad, rest, out_grad = run_last_reduce(
        n_ctx,
        n_fsdp,
        d_hidden.astype(BF).reshape(n_ctx, span, width),
        [tn(hidden, d_qkv).astype(BF), extra_grad, out_grad.reshape(n_fsdp * piece, width)],
    )
    out_grad = out_grad.reshape(n_ctx * piece, width).astype(F32)
    rest = rest.astype(F32).sum(axis=0)
    r_attn = inverse_rms(x)
    n = d_hidden * gain_attn
    input_grad = d_resid + r_attn * n - x * r_attn**3 * jnp.mean(n * x, axis=-1, keepdims=True)
    input_grad = input_grad.astype(BF)[None]

    query_grad = run_widen_columns(shared_grad, q_width)

    def kv_grad(at):
        parts = shared_grad[:, :, at : at + HEAD_SIZE].astype(F32)
        parts = parts.reshape(KEY_VALUE_HEADS, share, own_rows, HEAD_SIZE).sum(axis=1)
        return parts.transpose(1, 0, 2).reshape(own_rows, KEY_VALUE_HEADS * HEAD_SIZE)

    key_grad, value_grad = kv_grad(q_width), kv_grad(q_width + HEAD_SIZE)
    head_rows = HEAD_SIZE // n_fsdp
    return (
        output,
        input_grad,
        rest[:, experts],
        query_grad,
        key_grad,
        value_grad,
        rest[:head_rows, experts + 2],
        rest[:head_rows, experts + 3],
        out_grad,
        rest[:, experts + 1],
        rest[:, :experts],
        gate_grad[None],
        up_grad[None],
        down_grad[None],
    )


def solution(mesh):
    rows, tokens = P("fsdp", None), P("fsdp", "ctx", None)
    vector, expert = P("fsdp"), P(("ctx", "fsdp"), None, None)
    in_specs = (
        tokens,
        rows,
        tokens,
        tokens,
        vector,
        rows,
        rows,
        rows,
        vector,
        vector,
        rows,
        vector,
        rows,
        expert,
        expert,
        expert,
        tokens,
    )
    out_specs = (
        tokens,
        tokens,
        vector,
        rows,
        rows,
        rows,
        vector,
        vector,
        rows,
        vector,
        rows,
        expert,
        expert,
        expert,
    )
    return jax.shard_map(
        on_device, mesh=mesh, in_specs=in_specs, out_specs=out_specs, check_vma=False
    )
```

```python
import functools

import jax
import jax.numpy as jnp
from jax import lax
from jax.experimental import pallas as pl
from jax.experimental.pallas import tpu as pltpu
from jax.sharding import PartitionSpec as P

QUERY_HEADS = 32
KEY_VALUE_HEADS = 4
HEAD_SIZE = 128
TOP = 8

EPSILON = 1e-06
ROPE_BASE = 1000000.0
MASKED = -1000000000.0
SCALE = HEAD_SIZE ** (-0.5)
HALF = HEAD_SIZE // 2
BF = jnp.bfloat16
F32 = jnp.float32


def nt(a, b):
    return lax.dot_general(a, b, (((1,), (1,)), ((), ())), preferred_element_type=F32)


def nn(a, b):
    return lax.dot_general(a, b, (((1,), (0,)), ((), ())), preferred_element_type=F32)


def tn(a, b):
    return lax.dot_general(a, b, (((0,), (0,)), ((), ())), preferred_element_type=F32)


def inverse_rms(values):
    return lax.rsqrt(jnp.mean(values * values, axis=-1, keepdims=True) + EPSILON)


def norm_rope(raw, gain, cosine, sine):
    z = raw * inverse_rms(raw) * gain
    return z * cosine + pltpu.roll(z, HALF, 1) * sine


def norm_rope_back(raw, gain, cosine, sine, grad):
    dz = grad * cosine - pltpu.roll(grad, HALF, 1) * sine
    r = inverse_rms(raw)
    n = dz * gain
    d_raw = r * n - raw * (r * r * r) * jnp.mean(n * raw, axis=-1, keepdims=True)
    return d_raw, jnp.sum(dz * raw * r, axis=0, keepdims=True)


def prepare_keys(k_ref, v_ref, cos_ref, sin_ref, gains_ref, keys, values_t):
    rotated = norm_rope(k_ref[...], gains_ref[1:2, :], cos_ref[...], sin_ref[...])
    keys[...] = rotated.astype(BF)
    values_t[...] = v_ref[...].T.astype(BF)


def attend_head(
    q_ref, cos_ref, sin_ref, gains_ref, own_ref, key_ref, total_ref, dealt_ref, keys, values_t, store
):
    queries = norm_rope(q_ref[...], gains_ref[0:1, :], cos_ref[...], sin_ref[...]).astype(BF)
    length = queries.shape[0]
    chunk = 256
    for start in range(0, length, chunk):
        scores = nt(keys[...], queries[start : start + chunk]) * SCALE
        seen = key_ref[...] <= own_ref[0:1, start : start + chunk]
        scores = jnp.where(seen, scores, MASKED)
        top = jnp.max(scores, axis=0, keepdims=True)
        weights = jnp.exp(scores - top)
        total = jnp.sum(weights, axis=0, keepdims=True)
        out = (nn(values_t[...], weights.astype(BF)) / total).T.astype(BF)
        store(start, chunk, out)
        dealt_ref[0, start : start + chunk, :] = out
        total_ref[0, :, start : start + chunk] = jnp.broadcast_to(top + jnp.log(total), (8, chunk))


def attention_forward(
    q_ref,
    k_ref,
    v_ref,
    cos_ref,
    sin_ref,
    gains_ref,
    own_ref,
    key_ref,
    mixed_ref,
    total_ref,
    dealt_ref,
    keys,
    values_t,
):
    @pl.when(pl.program_id(0) == 0)
    def _():
        prepare_keys(k_ref, v_ref, cos_ref, sin_ref, gains_ref, keys, values_t)

    def store(start, count, out):
        mixed_ref[start : start + count, :] = out

    attend_head(
        q_ref, cos_ref, sin_ref, gains_ref, own_ref, key_ref, total_ref, dealt_ref, keys, values_t, store
    )


def attention_backward(
    heads,
    q_ref,
    k_ref,
    v_ref,
    grad_ref,
    total_ref,
    cos_ref,
    sin_ref,
    gains_ref,
    own_ref,
    key_ref,
    dq_ref,
    dkv_ref,
    dgain_ref,
    keys,
    keys_t,
    values,
    dk,
    dv,
):
    cosine, sine = cos_ref[...], sin_ref[...]
    head = pl.program_id(0)

    @pl.when(head == 0)
    def _():
        rotated = norm_rope(k_ref[...], gains_ref[1:2, :], cosine, sine)
        keys[...] = rotated.astype(BF)
        keys_t[...] = rotated.T.astype(BF)
        values[...] = v_ref[...].astype(BF)
        dk[...] = jnp.zeros_like(dk)
        dv[...] = jnp.zeros_like(dv)
        dgain_ref[...] = jnp.zeros_like(dgain_ref)

    queries = norm_rope(q_ref[...], gains_ref[0:1, :], cosine, sine).astype(BF)
    length = queries.shape[0]
    chunk = 256
    for start in range(0, length, chunk):
        rows = slice(start, start + chunk)
        q_part = queries[rows]
        grad = grad_ref[rows, :]
        scores = nt(keys[...], q_part) * SCALE
        seen = key_ref[...] <= own_ref[0:1, rows]
        scores = jnp.where(seen, scores, MASKED)
        weights = jnp.exp(scores - total_ref[0, 0:1, rows])
        d_weights = nt(values[...], grad)
        row_dot = jnp.sum(weights * d_weights, axis=0, keepdims=True)
        d_scores = (weights * (d_weights - row_dot)).astype(BF)
        dv[...] += nn(weights.astype(BF), grad)
        dk[...] += nn(d_scores, q_part)
        d_queries = nn(keys_t[...], d_scores).T * SCALE
        d_raw, d_gain = norm_rope_back(
            q_ref[rows, :], gains_ref[0:1, :], cos_ref[rows, :], sin_ref[rows, :], d_queries
        )
        dq_ref[rows, :] = d_raw.astype(BF)
        dgain_ref[0:1, :] += d_gain

    @pl.when(head == heads - 1)
    def _():
        d_raw, d_gain = norm_rope_back(
            k_ref[...], gains_ref[1:2, :], cosine, sine, dk[...] * SCALE
        )
        dkv_ref[:, :HEAD_SIZE] = d_raw.astype(BF)
        dkv_ref[:, HEAD_SIZE:] = dv[...].astype(BF)
        dgain_ref[1:2, :] = d_gain


def attention_specs(heads, length):
    whole = lambda shape: pl.BlockSpec(shape, lambda h: (0,) * len(shape))
    column = lambda at: pl.BlockSpec((length, HEAD_SIZE), lambda h: (0, at))
    head_column = pl.BlockSpec((length, HEAD_SIZE), lambda h: (0, h))
    totals = pl.BlockSpec((1, 8, length), lambda h: (h, 0, 0))
    shared = [
        whole((length, HEAD_SIZE)),
        whole((length, HEAD_SIZE)),
        whole((8, HEAD_SIZE)),
        whole((8, length)),
        whole((length, 1)),
    ]
    return whole, column, head_column, totals, shared


def run_attention(qkv, heads, n_ctx, cosine, sine, gains, own, key_blocks):
    length = qkv.shape[0]
    whole, column, head_column, totals, shared = attention_specs(heads, length)
    deals = min(n_ctx, heads)
    return pl.pallas_call(
        attention_forward,
        grid=(heads,),
        in_specs=[head_column, column(heads), column(heads + 1)] + shared,
        out_specs=[
            head_column,
            totals,
            pl.BlockSpec((1, length, HEAD_SIZE), lambda h: (h % deals, 0, h // deals)),
        ],
        out_shape=[
            jax.ShapeDtypeStruct((length, heads * HEAD_SIZE), BF),
            jax.ShapeDtypeStruct((heads, 8, length), F32),
            jax.ShapeDtypeStruct((deals, length, heads // deals * HEAD_SIZE), BF),
        ],
        scratch_shapes=[
            pltpu.VMEM((length, HEAD_SIZE), BF),
            pltpu.VMEM((HEAD_SIZE, length), BF),
        ],
        compiler_params=pltpu.CompilerParams(vmem_limit_bytes=48 * 2**20),
        cost_estimate=pl.CostEstimate(
            flops=4 * heads * length * length * HEAD_SIZE,
            bytes_accessed=8 * heads * length * HEAD_SIZE,
            transcendentals=heads * length * length,
        ),
    )(qkv, qkv, qkv, cosine, sine, gains, own, key_blocks)


def run_attention_back(qkv, grad, totals_in, heads, cosine, sine, gains, own, key_blocks):
    length = qkv.shape[0]
    whole, column, head_column, totals, shared = attention_specs(heads, length)
    return pl.pallas_call(
        functools.partial(attention_backward, heads),
        grid=(heads,),
        in_specs=[head_column, column(heads), column(heads + 1), head_column, totals] + shared,
        out_specs=[head_column, whole((length, 2 * HEAD_SIZE)), whole((8, HEAD_SIZE))],
        out_shape=[
            jax.ShapeDtypeStruct((length, heads * HEAD_SIZE), BF),
            jax.ShapeDtypeStruct((length, 2 * HEAD_SIZE), BF),
            jax.ShapeDtypeStruct((8, HEAD_SIZE), F32),
        ],
        scratch_shapes=[
            pltpu.VMEM((length, HEAD_SIZE), BF),
            pltpu.VMEM((HEAD_SIZE, length), BF),
            pltpu.VMEM((length, HEAD_SIZE), BF),
            pltpu.VMEM((length, HEAD_SIZE), F32),
            pltpu.VMEM((length, HEAD_SIZE), F32),
        ],
        compiler_params=pltpu.CompilerParams(vmem_limit_bytes=48 * 2**20),
        cost_estimate=pl.CostEstimate(
            flops=10 * heads * length * length * HEAD_SIZE,
            bytes_accessed=10 * heads * length * HEAD_SIZE,
            transcendentals=heads * length * length,
        ),
    )(qkv, qkv, qkv, grad, totals_in, cosine, sine, gains, own, key_blocks)


def push(source, target, sends, recvs, device):
    copy = pltpu.make_async_remote_copy(
        src_ref=source,
        dst_ref=target,
        send_sem=sends,
        recv_sem=recvs,
        device_id=device,
        device_id_type=pl.DeviceIdType.MESH,
    )
    return copy


def greet(devices):
    barrier = pltpu.get_barrier_semaphore()
    for device in devices:
        pl.semaphore_signal(barrier, 1, device_id=device, device_id_type=pl.DeviceIdType.MESH)
    pl.semaphore_wait(barrier, len(devices))


class LineGather:
    def __init__(self, n_ctx, ctx, fsdp, own_ref, all_ref, up, down, arrived):
        self.n_ctx, self.ctx, self.fsdp = n_ctx, ctx, fsdp
        self.own_ref, self.all_ref = own_ref, all_ref
        self.up, self.down, self.arrived = up, down, arrived

    def copy(self, source, block, sems, step, to):
        return push(
            source, self.all_ref.at[block], sems.at[step], self.arrived.at[block], (to, self.fsdp)
        )

    def going_up(self, step):
        return (self.ctx - step >= 0) & (self.ctx < self.n_ctx - 1)

    def going_down(self, step):
        return (self.ctx + step < self.n_ctx) & (self.ctx > 0)

    def step(self, step):
        def hop(block, sems, to, more):
            if step > 0:
                self.copy(self.own_ref, block, sems, 0, to).wait_recv()

            @pl.when(more)
            def _():
                source = self.all_ref.at[block] if step > 0 else self.own_ref
                self.copy(source, block, sems, step, to).start()

        @pl.when(self.ctx - step >= 0)
        def _():
            hop(self.ctx - step, self.up, self.ctx + 1, self.ctx < self.n_ctx - 1)

        @pl.when(self.ctx + step < self.n_ctx)
        def _():
            hop(self.ctx + step, self.down, self.ctx - 1, self.ctx > 0)

    def finish(self):
        for step in range(self.n_ctx - 1):

            @pl.when(self.going_up(step))
            def _():
                self.copy(self.own_ref, 0, self.up, step, self.ctx).wait_send()

            @pl.when(self.going_down(step))
            def _():
                self.copy(self.own_ref, 0, self.down, step, self.ctx).wait_send()


class LineScatter:
    def __init__(self, n_ctx, ctx, fsdp, chunks, held, low, high, up, down, low_in, high_in):
        self.n_ctx, self.ctx, self.fsdp, self.chunks = n_ctx, ctx, fsdp, chunks
        self.held, self.low, self.high = held, low, high
        self.sems = {"up": (low, up, low_in), "down": (high, down, high_in)}
        self.size = held.shape[1] // chunks

    def copy(self, way, block, chunk, to):
        landing, sends, arrived = self.sems[way]
        rows = pl.ds(chunk * self.size, self.size)
        return push(
            self.held.at[block, rows],
            landing.at[block, rows],
            sends.at[block, chunk],
            arrived.at[block, chunk],
            (to, self.fsdp),
        )

    def scatter(self, chunk):
        rows = slice(chunk * self.size, (chunk + 1) * self.size)
        ctx, held = self.ctx, self.held

        def pass_on(way, block, to, first):
            @pl.when(jnp.logical_not(first))
            def _():
                self.copy(way, block, chunk, ctx).wait_recv()
                held[block, rows, :] = (
                    held[block, rows, :].astype(F32)
                    + self.sems[way][0][block, rows, :].astype(F32)
                ).astype(BF)

            self.copy(way, block, chunk, to).start()

        for step in range(self.n_ctx - 1):

            @pl.when(ctx < self.n_ctx - 1 - step)
            def _():
                pass_on("up", self.n_ctx - 1 - step, ctx + 1, ctx == 0)

            @pl.when(ctx > step)
            def _():
                pass_on("down", step, ctx - 1, ctx == self.n_ctx - 1)

    def settle(self, chunk, total_ref):
        rows = slice(chunk * self.size, (chunk + 1) * self.size)
        total_ref[rows, :] = self.held[self.ctx, rows, :].astype(F32)

        @pl.when(self.ctx > 0)
        def _():
            self.copy("up", self.ctx, chunk, self.ctx).wait_recv()
            total_ref[rows, :] += self.low[self.ctx, rows, :].astype(F32)

        @pl.when(self.ctx < self.n_ctx - 1)
        def _():
            self.copy("down", self.ctx, chunk, self.ctx).wait_recv()
            total_ref[rows, :] += self.high[self.ctx, rows, :].astype(F32)

    def finish(self):
        for chunk in range(self.chunks):
            for step in range(self.n_ctx - 1):

                @pl.when(self.ctx < self.n_ctx - 1 - step)
                def _():
                    self.copy("up", self.n_ctx - 1 - step, chunk, self.ctx).wait_send()

                @pl.when(self.ctx > step)
                def _():
                    self.copy("down", step, chunk, self.ctx).wait_send()


def first_gather(
    n_ctx,
    n_fsdp,
    x_ref,
    table_ref,
    packed_ref,
    x_all,
    table_all,
    packed_all,
    local,
    up,
    down,
    arrived,
    table_send,
    table_arrived,
    packed_send,
    passed_send,
    packed_arrived,
):
    ctx, fsdp = lax.axis_index("ctx"), lax.axis_index("fsdp")
    sibling = lax.rem(fsdp + 1, 2) + (fsdp // 2) * 2
    chips = n_fsdp // 2

    def same_core(offset):
        return lax.rem(fsdp + 2 * offset, n_fsdp)

    def along(offset):
        return lax.rem(ctx + offset, n_ctx)

    greet(
        [(along(i), fsdp) for i in range(1, n_ctx)]
        + [(ctx, same_core(i)) for i in range(1, chips)]
        + [(ctx, sibling)]
    )
    kept = [
        pltpu.make_async_copy(x_ref, x_all.at[ctx], local.at[0]),
        pltpu.make_async_copy(table_ref, table_all.at[ctx], local.at[1]),
        pltpu.make_async_copy(packed_ref, packed_all.at[fsdp], local.at[2]),
    ]
    for copy in kept:
        copy.start()

    def packed_copy(source, owner, sems, to):
        return push(source, packed_all.at[owner], sems, packed_arrived.at[owner], (ctx, to))

    for i in range(1, chips):
        packed_copy(packed_ref, fsdp, packed_send.at[i], same_core(i)).start()
    packed_copy(packed_ref, fsdp, packed_send.at[0], sibling).start()
    for i in range(1, n_ctx):
        push(
            table_ref, table_all.at[ctx], table_send.at[i], table_arrived.at[ctx], (along(i), fsdp)
        ).start()
    line = LineGather(n_ctx, ctx, fsdp, x_ref, x_all, up, down, arrived)
    for step in range(n_ctx):
        line.step(step)
    for i in range(1, chips):
        owner = same_core(chips - i)
        packed_copy(packed_ref, owner, packed_send.at[i], sibling).wait_recv()
        packed_copy(packed_all.at[owner], owner, passed_send.at[i], sibling).start()
    for i in range(chips):
        owner = lax.rem(sibling + 2 * i, n_fsdp)
        packed_copy(packed_ref, owner, packed_send.at[0], sibling).wait_recv()
    for i in range(1, n_ctx):
        owner = along(i)
        push(
            table_ref, table_all.at[owner], table_send.at[i], table_arrived.at[owner], (owner, fsdp)
        ).wait()
    line.finish()
    for i in range(chips):
        packed_copy(packed_ref, fsdp, packed_send.at[i], sibling).wait_send()
    for i in range(1, chips):
        packed_copy(packed_ref, fsdp, passed_send.at[i], sibling).wait_send()
    for copy in kept:
        copy.wait()


def run_first_gather(n_ctx, n_fsdp, x, table, packed):
    anywhere = pl.BlockSpec(memory_space=pl.ANY)
    dma = pltpu.SemaphoreType.DMA
    return pl.pallas_call(
        functools.partial(first_gather, n_ctx, n_fsdp),
        in_specs=[anywhere] * 3,
        out_specs=[anywhere] * 3,
        out_shape=[
            jax.ShapeDtypeStruct((n_ctx,) + x.shape, x.dtype),
            jax.ShapeDtypeStruct((n_ctx,) + table.shape, table.dtype),
            jax.ShapeDtypeStruct((n_fsdp,) + packed.shape, packed.dtype),
        ],
        scratch_shapes=[
            dma((3,)),
            dma((n_ctx,)),
            dma((n_ctx,)),
            dma((n_ctx,)),
            dma((n_ctx,)),
            dma((n_ctx,)),
            dma((n_fsdp // 2,)),
            dma((n_fsdp // 2,)),
            dma((n_fsdp,)),
        ],
        compiler_params=pltpu.CompilerParams(collective_id=1, has_side_effects=True),
        cost_estimate=pl.CostEstimate(
            flops=0, bytes_accessed=200 * 2**20, transcendentals=0
        ),
    )(x, table, packed)


TILE = 512
AUX = 128


def expert_exchange(
    n_ctx,
    n_fsdp,
    x_ref,
    sel_ref,
    selt_ref,
    gate_ref,
    up_ref,
    down_ref,
    grad_ref,
    dealt_ref,
    rows_ref,
    back_ref,
    part_ref,
    inner_ref,
    dg_ref,
    du_ref,
    y_ref,
    dealt_all,
    w_gate,
    w_up,
    w_down,
    held,
    staged,
    rows_in,
    grad_in,
    inner_out,
    dg_out,
    du_out,
    y_out,
    back_in,
    w_sems,
    local,
    held_send,
    held_arrived,
    rows_send,
    rows_arrived,
    back_send,
    back_arrived,
    part_send,
    part_arrived,
    dealt_send,
    dealt_arrived,
    out_sems,
):
    ctx, fsdp = lax.axis_index("ctx"), lax.axis_index("fsdp")
    experts = n_ctx * n_fsdp
    expert = ctx * n_fsdp + fsdp
    width, hidden = w_gate.shape
    wide = held.shape[2]
    capacity = staged.shape[2]
    half = n_fsdp // 2
    tiles = [(at, min(TILE, wide - at)) for at in range(0, wide, TILE)]

    def along(offset):
        return lax.rem(ctx + offset, n_ctx)

    def around(offset):
        return lax.rem(fsdp + offset, n_fsdp)

    greet(
        [(along(i), fsdp) for i in range(1, n_ctx)] + [(ctx, around(i)) for i in range(1, n_fsdp)]
    )
    weights = [
        pltpu.make_async_copy(gate_ref, w_gate, w_sems.at[0]),
        pltpu.make_async_copy(up_ref, w_up, w_sems.at[1]),
        pltpu.make_async_copy(down_ref, w_down, w_sems.at[2]),
    ]
    own = pltpu.make_async_copy(x_ref, held.at[ctx], local.at[0])
    own.start()
    for copy in weights:
        copy.start()

    def held_copy(step):
        to = lax.rem(ctx + n_ctx - step, n_ctx)
        return push(x_ref, held.at[ctx], held_send.at[step], held_arrived.at[ctx], (to, fsdp))

    def rows_copy(step, group, offset):
        to = around(offset)
        return push(
            staged.at[step, to],
            rows_ref.at[fsdp, group],
            rows_send.at[step, offset],
            rows_arrived.at[group, fsdp],
            (ctx, to),
        )

    def rows_kept(step, group):
        return pltpu.make_async_copy(
            staged.at[step, fsdp], rows_ref.at[fsdp, group], rows_arrived.at[group, fsdp]
        )

    def back_copy(step, group, offset):
        to = around(offset)
        return push(
            staged.at[step, to],
            back_ref.at[group, fsdp],
            back_send.at[step, offset],
            back_arrived.at[group, fsdp],
            (ctx, to),
        )

    def back_kept(step, group):
        return pltpu.make_async_copy(
            staged.at[step, fsdp], back_ref.at[group, fsdp], back_arrived.at[group, fsdp]
        )

    def outputs(group):
        return [
            pltpu.make_async_copy(inner_out, inner_ref.at[:, group], out_sems.at[0]),
            pltpu.make_async_copy(dg_out, dg_ref.at[:, group], out_sems.at[1]),
            pltpu.make_async_copy(du_out, du_ref.at[:, group], out_sems.at[2]),
            pltpu.make_async_copy(y_out, y_ref.at[:, group], out_sems.at[3]),
        ]

    def dispatch(step):
        group = along(step)

        @pl.when(step == 0)
        def _():
            own.wait()

        @pl.when(step > 0)
        def _():
            push(
                x_ref, held.at[group], held_send.at[step], held_arrived.at[group], (group, fsdp)
            ).wait_recv()

        @pl.when(step + 1 < n_ctx)
        def _():
            held_copy(step + 1).start()

        for at, size in tiles:
            picked = nn(sel_ref[group], held[group, :, at : at + size])
            staged[step, :, :, at : at + size] = picked.astype(BF).reshape(n_fsdp, capacity, size)
        rows_kept(step, group).start()
        for offset in range(1, n_fsdp):
            rows_copy(step, group, offset).start()

    def compute(step):
        group = along(step)
        rows_kept(step, group).wait()
        for offset in range(1, n_fsdp):
            source = around(offset)
            push(
                staged.at[step, source],
                rows_ref.at[source, group],
                rows_send.at[step, offset],
                rows_arrived.at[group, source],
                (ctx, source),
            ).wait_recv()
        load_rows = pltpu.make_async_copy(rows_ref.at[:, group], rows_in, local.at[1])
        load_inner = pltpu.make_async_copy(grad_ref.at[:, group], grad_in, local.at[2])
        load_rows.start()
        load_inner.start()

        @pl.when(step == 0)
        def _():
            for copy in weights:
                copy.wait()

        @pl.when(step > 0)
        def _():
            for copy in outputs(group):
                copy.wait()

        for offset in range(1, n_fsdp):
            rows_copy(step, group, offset).wait_send()
        load_rows.wait()
        load_inner.wait()
        count = half * capacity
        lane = lax.broadcasted_iota(jnp.int32, (count, AUX), 1)
        high, low = lane == expert, lane == experts + expert

        @pl.loop(0, 2)
        def _(part):
            sources = pl.ds(part * half, half)
            rows = rows_in[sources, :, :width].reshape(count, width)
            aux = rows_in[sources, :, width:].reshape(count, AUX).astype(F32)
            gate = jnp.sum(jnp.where(high | low, aux, 0.0), axis=1, keepdims=True)
            g = nn(rows, w_gate[...])
            u = nn(rows, w_up[...])
            s = jax.nn.sigmoid(g)
            inner = g * s * u
            d_inner = nt(grad_in[sources].reshape(count, width), w_down[...])
            d_gate = jnp.sum(inner * d_inner, axis=1, keepdims=True)
            d_inner = d_inner * gate
            dg = (d_inner * u * s * (1.0 + g * (1.0 - s))).astype(BF)
            du = (d_inner * g * s).astype(BF)
            inner_out[sources] = (inner * gate).astype(BF).reshape(half, capacity, hidden)
            dg_out[sources] = dg.reshape(half, capacity, hidden)
            du_out[sources] = du.reshape(half, capacity, hidden)
            rest = d_gate - d_gate.astype(BF).astype(F32)
            staged[step, sources, :, width:] = (
                jnp.where(high, d_gate, jnp.where(low, rest, 0.0))
                .astype(BF)
                .reshape(half, capacity, AUX)
            )
            for at in range(0, width, TILE):
                grad = nt(dg, w_gate[at : at + TILE, :]) + nt(du, w_up[at : at + TILE, :])
                staged[step, sources, :, at : at + TILE] = grad.astype(BF).reshape(
                    half, capacity, TILE
                )
            low_inner = inner.astype(BF)
            for at in range(0, width, TILE):
                y = nn(low_inner, w_down[:, at : at + TILE]) * gate
                y_out[sources, :, at : at + TILE] = y.astype(BF).reshape(half, capacity, TILE)

        back_kept(step, group).start()
        for offset in range(1, n_fsdp):
            back_copy(step, group, offset).start()
        for copy in outputs(group):
            copy.start()

    def combine(step):
        group = along(step)
        back_kept(step, group).wait()
        for offset in range(1, n_fsdp):
            source = around(offset)
            push(
                staged.at[step, source],
                back_ref.at[group, source],
                back_send.at[step, offset],
                back_arrived.at[group, source],
                (ctx, source),
            ).wait_recv()
        load = pltpu.make_async_copy(back_ref.at[group], back_in, local.at[1])
        load.start()
        load.wait()
        for at, size in tiles:
            back = back_in[:, :, at : at + size].reshape(n_fsdp * capacity, size)
            held[group, :, at : at + size] = nn(selt_ref[group], back).astype(BF)

        @pl.when(step == 0)
        def _():
            pltpu.make_async_copy(
                held.at[group], part_ref.at[ctx], part_arrived.at[ctx]
            ).start()

        @pl.when(step > 0)
        def _():
            push(
                held.at[group],
                part_ref.at[ctx],
                part_send.at[step],
                part_arrived.at[ctx],
                (group, fsdp),
            ).start()

    def dealt_copy(offset):
        to = along(offset)
        return push(
            dealt_ref.at[to],
            dealt_all.at[ctx],
            dealt_send.at[offset],
            dealt_arrived.at[ctx],
            (to, fsdp),
        )

    dealt_kept = pltpu.make_async_copy(
        dealt_ref.at[ctx], dealt_all.at[ctx], dealt_arrived.at[ctx]
    )

    @pl.loop(0, n_ctx + 3)
    def _(tick):
        @pl.when(tick < n_ctx)
        def _():
            dispatch(tick)

        @pl.when(tick == n_ctx - 1)
        def _():
            dealt_kept.start()
            for offset in range(1, n_ctx):
                dealt_copy(offset).start()

        @pl.when((tick >= 1) & (tick <= n_ctx))
        def _():
            compute(tick - 1)

        @pl.when(tick >= 3)
        def _():
            combine(tick - 3)

    pltpu.make_async_copy(held.at[ctx], part_ref.at[ctx], part_arrived.at[ctx]).wait()
    for step in range(1, n_ctx):
        other = along(step)
        copy = push(
            held.at[other], part_ref.at[other], part_send.at[step], part_arrived.at[other], (other, fsdp)
        )
        copy.wait()
        held_copy(step).wait_send()
    dealt_kept.wait()
    for offset in range(1, n_ctx):
        other = along(offset)
        push(
            dealt_ref.at[other],
            dealt_all.at[other],
            dealt_send.at[offset],
            dealt_arrived.at[other],
            (other, fsdp),
        ).wait()
    for step in range(n_ctx):
        for offset in range(1, n_fsdp):
            back_copy(step, along(step), offset).wait_send()
    for copy in outputs(along(n_ctx - 1)):
        copy.wait()


def run_expert_exchange(n_ctx, n_fsdp, x, select, select_t, gate, up, down, grads, dealt):
    anywhere, inside = pl.BlockSpec(memory_space=pl.ANY), pl.BlockSpec(memory_space=pltpu.VMEM)
    span, wide = x.shape
    width, hidden = gate.shape
    capacity = grads.shape[2]
    slots = (n_fsdp, n_ctx, capacity)
    one = (n_fsdp, capacity)
    dma, vmem, shape = pltpu.SemaphoreType.DMA, pltpu.VMEM, jax.ShapeDtypeStruct
    return pl.pallas_call(
        functools.partial(expert_exchange, n_ctx, n_fsdp),
        in_specs=[anywhere, inside, inside] + [anywhere] * 5,
        out_specs=[anywhere] * 8,
        out_shape=[
            shape(slots + (wide,), BF),
            shape((n_ctx, n_fsdp, capacity, wide), BF),
            shape((n_ctx, span, wide), BF),
            shape(slots + (hidden,), BF),
            shape(slots + (hidden,), BF),
            shape(slots + (hidden,), BF),
            shape(slots + (width,), BF),
            shape(dealt.shape, BF),
        ],
        scratch_shapes=[
            vmem((width, hidden), BF),
            vmem((width, hidden), BF),
            vmem((hidden, width), BF),
            vmem((n_ctx, span, wide), BF),
            vmem((n_ctx,) + one + (wide,), BF),
            vmem(one + (wide,), BF),
            vmem(one + (width,), BF),
            vmem(one + (hidden,), BF),
            vmem(one + (hidden,), BF),
            vmem(one + (hidden,), BF),
            vmem(one + (width,), BF),
            vmem(one + (wide,), BF),
            dma((3,)),
            dma((3,)),
            dma((n_ctx,)),
            dma((n_ctx,)),
            dma((n_ctx, n_fsdp)),
            dma((n_ctx, n_fsdp)),
            dma((n_ctx, n_fsdp)),
            dma((n_ctx, n_fsdp)),
            dma((n_ctx,)),
            dma((n_ctx,)),
            dma((n_ctx,)),
            dma((n_ctx,)),
            dma((4,)),
        ],
        compiler_params=pltpu.CompilerParams(
            collective_id=2, has_side_effects=True, vmem_limit_bytes=60 * 2**20
        ),
        cost_estimate=pl.CostEstimate(
            flops=12 * n_fsdp * n_ctx * capacity * width * hidden,
            bytes_accessed=600 * 2**20,
            transcendentals=0,
        ),
    )(x, select, select_t, gate, up, down, grads, dealt)


def last_reduce(n_ctx, n_fsdp, *refs):
    ctx, fsdp = lax.axis_index("ctx"), lax.axis_index("fsdp")
    count = (len(refs) - 1) // 11
    ins, alls, local, refs = refs[:count], refs[count : 2 * count], refs[2 * count], refs[2 * count + 1 :]
    items = [refs[9 * i : 9 * i + 9] for i in range(count)]
    chips, chip, core = n_fsdp // 2, fsdp // 2, lax.rem(fsdp, 2)
    sibling = chip * 2 + 1 - core

    def along(offset):
        return lax.rem(ctx + offset, n_ctx)

    def other_chip(offset):
        return lax.rem(chip + offset, chips)

    greet(
        [(along(i), fsdp) for i in range(1, n_ctx)]
        + [(ctx, other_chip(i) * 2 + core) for i in range(1, chips)]
        + [(ctx, sibling)]
    )
    crossing, loads, lines = [], [], []
    for at, (in_ref, all_ref, item) in enumerate(zip(ins, alls, items)):
        mine, beside, landed, own, cross, sends, arrived, line_sems, line_arrived = item
        crossing.append(
            push(in_ref.at[:, 1 - core], beside, cross.at[0], cross.at[1], (ctx, sibling))
        )
        crossing[-1].start()
        loads.append(pltpu.make_async_copy(in_ref.at[:, core], mine, local.at[at]))
        loads[-1].start()
        lines.append(
            LineGather(
                n_ctx, ctx, fsdp, own, all_ref, line_sems.at[0], line_sems.at[1], line_arrived
            )
        )

    def chip_copy(item, offset):
        mine, beside, landed, own, cross, sends, arrived, line_sems, line_arrived = item
        to = other_chip(offset)
        return push(
            mine.at[to], landed.at[chip], sends.at[offset], arrived.at[chip], (ctx, to * 2 + core)
        )

    for crossed, loaded, item in zip(crossing, loads, items):
        mine, beside = item[:2]
        loaded.wait()
        crossed.wait_recv()
        for offset in range(1, chips + 1):
            to = other_chip(offset)
            mine[to] = (mine[to].astype(F32) + beside[to].astype(F32)).astype(BF)
            if offset < chips:
                chip_copy(item, offset).start()
    keeps = []
    for at, (item, line, all_ref) in enumerate(zip(items, lines, alls)):
        mine, beside, landed, own, cross, sends, arrived, line_sems, line_arrived = item
        total = mine[chip].astype(F32)
        for offset in range(1, chips):
            source = other_chip(offset)
            push(
                mine.at[source], landed.at[source], sends.at[offset], arrived.at[source], (ctx, sibling)
            ).wait_recv()
            total = total + landed[source].astype(F32)
        own[...] = total.astype(BF)
        line.step(0)
        keeps.append(pltpu.make_async_copy(own, all_ref.at[ctx], local.at[at]))
        keeps[-1].start()
    for step in range(1, n_ctx):
        for line in lines:
            line.step(step)
    for crossed, keep, line, item in zip(crossing, keeps, lines, items):
        crossed.wait_send()
        keep.wait()
        line.finish()
        for offset in range(1, chips):
            chip_copy(item, offset).wait_send()


def run_last_reduce(n_ctx, n_fsdp, grads):
    anywhere = pl.BlockSpec(memory_space=pl.ANY)
    dma, vmem, shape = pltpu.SemaphoreType.DMA, pltpu.VMEM, jax.ShapeDtypeStruct
    chips = n_fsdp // 2
    grads = [grad.reshape((chips, 2, -1) + grad.shape[-1:]) for grad in grads]
    blocks = [grad.shape[2:] for grad in grads]
    scratch = [dma((len(grads),))]
    for block in blocks:
        scratch += [
            vmem((chips,) + block, BF),
            vmem((chips,) + block, BF),
            vmem((chips,) + block, BF),
            vmem(block, BF),
            dma((2,)),
            dma((chips,)),
            dma((chips,)),
            dma((2, n_ctx)),
            dma((n_ctx,)),
        ]
    return pl.pallas_call(
        functools.partial(last_reduce, n_ctx, n_fsdp),
        in_specs=[anywhere] * len(grads),
        out_specs=[anywhere] * len(grads),
        out_shape=[shape((n_ctx,) + block, BF) for block in blocks],
        scratch_shapes=scratch,
        compiler_params=pltpu.CompilerParams(
            collective_id=3, has_side_effects=True, vmem_limit_bytes=60 * 2**20
        ),
        cost_estimate=pl.CostEstimate(flops=0, bytes_accessed=400 * 2**20, transcendentals=0),
    )(*grads)


def widen_columns(in_ref, out_ref):
    out_ref[...] = in_ref[0].astype(F32)


def run_widen_columns(blocks, columns):
    n, rows, _ = blocks.shape
    return pl.pallas_call(
        widen_columns,
        grid=(n,),
        in_specs=[pl.BlockSpec((1, rows, columns), lambda i: (i, 0, 0))],
        out_specs=pl.BlockSpec((rows, columns), lambda i: (0, i)),
        out_shape=jax.ShapeDtypeStruct((rows, n * columns), F32),
    )(blocks)


def attention_exchange(
    n_ctx,
    n_fsdp,
    heads,
    q_ref,
    k_ref,
    v_ref,
    cos_ref,
    sin_ref,
    gains_ref,
    own_ref,
    key_ref,
    sel_ref,
    grad_ref,
    out_ref,
    total_ref,
    dealt_ref,
    attn_ref,
    rows_ref,
    keys,
    values_t,
    mixed,
    w_out,
    held,
    low,
    high,
    grads,
    staged,
    local,
    grad_up,
    grad_down,
    grad_arrived,
    rows_send,
    rows_arrived,
    up_send,
    down_send,
    low_arrived,
    high_arrived,
):
    head = pl.program_id(0)
    ctx, fsdp = lax.axis_index("ctx"), lax.axis_index("fsdp")
    _, span, width = held.shape
    capacity = staged.shape[2]
    q_width = heads * HEAD_SIZE

    def along(offset):
        return lax.rem(ctx + offset, n_ctx)

    def around(offset):
        return lax.rem(fsdp + offset, n_fsdp)

    line = LineGather(n_ctx, ctx, fsdp, grad_ref, grads, grad_up, grad_down, grad_arrived)
    sums = LineScatter(
        n_ctx, ctx, fsdp, 4, held, low, high, up_send, down_send, low_arrived, high_arrived
    )
    own = pltpu.make_async_copy(grad_ref, grads.at[ctx], local.at[0])
    weights = pltpu.make_async_copy(
        out_ref.at[pl.ds(ctx * q_width, q_width)], w_out, local.at[1]
    )

    def rows_copy(group, offset):
        to = around(offset)
        return push(
            staged.at[group, to],
            rows_ref.at[fsdp, group],
            rows_send.at[group, offset],
            rows_arrived.at[group, fsdp],
            (ctx, to),
        )

    def rows_kept(group):
        return pltpu.make_async_copy(
            staged.at[group, fsdp], rows_ref.at[fsdp, group], rows_arrived.at[group, fsdp]
        )

    def pick(group):
        for at in range(0, width, TILE):
            picked = nn(sel_ref[group], grads[group, :, at : at + TILE])
            staged[group, :, :, at : at + TILE] = picked.astype(BF).reshape(n_fsdp, capacity, TILE)
        rows_kept(group).start()
        for offset in range(1, n_fsdp):
            rows_copy(group, offset).start()

    def pick_from(distance):
        @pl.when(ctx - distance >= 0)
        def _():
            pick(ctx - distance)

        @pl.when(ctx + distance < n_ctx)
        def _():
            pick(ctx + distance)

    @pl.when(head == 0)
    def _():
        own.start()
        weights.start()
        greet(
            [(along(i), fsdp) for i in range(1, n_ctx)]
            + [(ctx, around(i)) for i in range(1, n_fsdp)]
        )
        line.step(0)
        own.wait()
        pick(ctx)
        prepare_keys(k_ref, v_ref, cos_ref, sin_ref, gains_ref, keys, values_t)

    @pl.when(head < heads)
    def _():
        def store(start, count, out):
            columns = pl.ds(pl.multiple_of(head * HEAD_SIZE, HEAD_SIZE), HEAD_SIZE)
            mixed[start : start + count, columns] = out

        attend_head(
            q_ref,
            cos_ref,
            sin_ref,
            gains_ref,
            own_ref,
            key_ref,
            total_ref,
            dealt_ref,
            keys,
            values_t,
            store,
        )

    @pl.when(head == heads - 2)
    def _():
        line.step(1)
        pick_from(1)

    @pl.when(head == heads)
    def _():
        weights.wait()
        for block in range(n_ctx):
            for at in range(0, width, TILE):
                held[block, :, at : at + TILE] = nn(
                    mixed[block * span : (block + 1) * span, :], w_out[:, at : at + TILE]
                ).astype(BF)
        line.step(2)
        sums.scatter(0)
        pick_from(2)
        sums.scatter(1)
        for step in range(3, n_ctx):
            line.step(step)
            pick_from(step)
        sums.scatter(2)
        sums.scatter(3)
        for chunk in range(4):
            sums.settle(chunk, attn_ref)
        sums.finish()
        line.finish()
        for group in range(n_ctx):
            rows_kept(group).wait()
            for offset in range(1, n_fsdp):
                source = around(offset)
                push(
                    staged.at[group, source],
                    rows_ref.at[source, group],
                    rows_send.at[group, offset],
                    rows_arrived.at[group, source],
                    (ctx, source),
                ).wait()


def run_attention_exchange(
    qkv, heads, n_ctx, n_fsdp, cosine, sine, gains, own, key_blocks, select, grad, w_out
):
    length = qkv.shape[0]
    span, width = grad.shape
    capacity = select.shape[1] // n_fsdp
    anywhere = pl.BlockSpec(memory_space=pl.ANY)
    dma, vmem, shape = pltpu.SemaphoreType.DMA, pltpu.VMEM, jax.ShapeDtypeStruct
    last = heads - 1
    whole, column, _, _, shared = attention_specs(heads, length)
    clip = lambda h: jnp.minimum(h, last)
    return pl.pallas_call(
        functools.partial(attention_exchange, n_ctx, n_fsdp, heads),
        grid=(heads + 1,),
        in_specs=[
            pl.BlockSpec((length, HEAD_SIZE), lambda h: (0, clip(h))),
            column(heads),
            column(heads + 1),
        ]
        + shared
        + [whole(select.shape), anywhere, anywhere],
        out_specs=[
            pl.BlockSpec((1, 8, length), lambda h: (clip(h), 0, 0)),
            pl.BlockSpec(
                (1, length, HEAD_SIZE),
                lambda h: (lax.rem(clip(h), n_ctx), 0, lax.div(clip(h), n_ctx)),
            ),
            whole((span, width)),
            anywhere,
        ],
        out_shape=[
            shape((heads, 8, length), F32),
            shape((n_ctx, length, heads // n_ctx * HEAD_SIZE), BF),
            shape((span, width), F32),
            shape((n_fsdp, n_ctx, capacity, width), BF),
        ],
        scratch_shapes=[
            vmem((length, HEAD_SIZE), BF),
            vmem((HEAD_SIZE, length), BF),
            vmem((length, heads * HEAD_SIZE), BF),
            vmem((heads * HEAD_SIZE, width), BF),
            vmem((n_ctx, span, width), BF),
            vmem((n_ctx, span, width), BF),
            vmem((n_ctx, span, width), BF),
            vmem((n_ctx, span, width), BF),
            vmem((n_ctx, n_fsdp, capacity, width), BF),
            dma((2,)),
            dma((n_ctx,)),
            dma((n_ctx,)),
            dma((n_ctx,)),
            dma((n_ctx, n_fsdp)),
            dma((n_ctx, n_fsdp)),
            dma((n_ctx, 4)),
            dma((n_ctx, 4)),
            dma((n_ctx, 4)),
            dma((n_ctx, 4)),
        ],
        compiler_params=pltpu.CompilerParams(
            collective_id=4, has_side_effects=True, vmem_limit_bytes=60 * 2**20
        ),
        cost_estimate=pl.CostEstimate(
            flops=4 * heads * length * length * HEAD_SIZE,
            bytes_accessed=400 * 2**20,
            transcendentals=heads * length * length,
        ),
    )(qkv, qkv, qkv, cosine, sine, gains, own, key_blocks, select, grad, w_out)


def on_device(
    inputs,
    block_ids,
    expert_ids,
    drop_order,
    attn_gain,
    w_query,
    key_projection_weight,
    value_projection_weight,
    q_gain,
    key_norm_gain,
    w_out,
    ffn_gain,
    w_router,
    expert_gate,
    expert_up,
    expert_down,
    cotangent,
):
    n_ctx, n_fsdp = lax.axis_size("ctx"), lax.axis_size("fsdp")
    ctx = lax.axis_index("ctx")
    span, width = inputs.shape[1], inputs.shape[2]
    length = block_ids.shape[1]
    experts = n_ctx * n_fsdp
    capacity = 5 * span * TOP // (4 * experts)
    slots = experts * capacity
    heads = QUERY_HEADS // n_ctx
    share = n_ctx // KEY_VALUE_HEADS
    own_rows = w_query.shape[0]
    q_width = heads * HEAD_SIZE
    qkv_width = q_width + 2 * HEAD_SIZE
    extra_width = -(-(experts + 4) // 128) * 128

    def gather_ctx(array):
        return lax.all_gather(array, "ctx", axis=0, tiled=True)

    def scatter_ctx(array):
        return lax.psum_scatter(array.astype(BF), "ctx", scatter_dimension=0, tiled=True)

    def route(rows):
        return lax.all_to_all(rows, "fsdp", split_axis=0, concat_axis=0, tiled=True)

    def columns(weight, index, count):
        return lax.dynamic_slice_in_dim(weight, index * count, count, axis=1)

    def as_column(vector):
        return jnp.pad(vector, (0, own_rows - vector.shape[0]))[:, None]

    packed = jnp.concatenate(
        [
            columns(w_query, ctx, q_width),
            columns(key_projection_weight, ctx // share, HEAD_SIZE),
            columns(value_projection_weight, ctx // share, HEAD_SIZE),
            w_router,
            as_column(attn_gain),
            as_column(ffn_gain),
            as_column(q_gain),
            as_column(key_norm_gain),
            jnp.zeros((own_rows, extra_width - experts - 4), BF),
        ],
        axis=1,
    )
    table = jnp.concatenate(
        [expert_ids[0].T, drop_order[0], jnp.zeros((7, span), jnp.int32)], axis=0
    )
    inputs_all, tables, packed_all = run_first_gather(n_ctx, n_fsdp, inputs[0], table, packed)
    out_all = lax.all_gather(w_out, "fsdp", axis=0, tiled=True)
    out_here = lax.dynamic_slice_in_dim(out_all, ctx * q_width, q_width, axis=0)
    inputs_all = inputs_all.reshape(length, width)
    packed_all = packed_all.reshape(width, qkv_width + extra_width)
    w_qkv = packed_all[:, :qkv_width]
    extra = packed_all[:, qkv_width:].T
    router_t = extra[:experts]
    gain_attn = extra[experts : experts + 1].astype(F32)
    gain_ffn = extra[experts + 1 : experts + 2].astype(F32)

    def head_gain(at):
        return extra[at].reshape(n_fsdp, own_rows)[:, : HEAD_SIZE // n_fsdp].reshape(1, HEAD_SIZE)

    gains = jnp.concatenate(
        [head_gain(experts + 2), head_gain(experts + 3), jnp.zeros((6, HEAD_SIZE), BF)], axis=0
    ).astype(F32)

    named = tables[:, :TOP, :]
    ranks = tables[:, TOP, :]
    here = ctx * n_fsdp + jnp.arange(n_fsdp, dtype=jnp.int32)
    member = jnp.any(named[:, :, None, :] == here[None, None, :, None], axis=1)
    before = (ranks[:, :, None] < ranks[:, None, :]).astype(BF)
    place = jnp.einsum(
        "gjs,gst->gjt", member.astype(BF), before, preferred_element_type=F32
    ).astype(jnp.int32)
    place = jnp.where(member, place, capacity)
    select = (
        place[:, :, None, :] == jnp.arange(capacity, dtype=jnp.int32)[None, None, :, None]
    ).astype(BF)

    fused = capacity % 16 == 0 and 2 * experts <= AUX and experts == QUERY_HEADS
    select_rows = select.reshape(n_ctx, n_fsdp * capacity, span)

    def dispatch(rows):
        picked = jnp.einsum(
            "gjkt,gtd->jgkd", select, rows.reshape(n_ctx, span, width), preferred_element_type=F32
        ).astype(BF)
        return route(picked).reshape(slots, width)

    def combine(rows):
        back = route(rows.reshape(n_fsdp, n_ctx, capacity, width))
        return jnp.einsum("gjkt,jgkd->gtd", select, back, preferred_element_type=F32).reshape(
            length, width
        )

    x_all = inputs_all.astype(F32)
    r_all = inverse_rms(x_all)
    hidden = (x_all * r_all * gain_attn).astype(BF)
    qkv = nn(hidden, w_qkv)
    exponent = jnp.arange(HALF, dtype=F32) * (2.0 / HEAD_SIZE)
    angles = jnp.arange(length, dtype=F32)[:, None] * (ROPE_BASE ** (-exponent))[None, :]
    cosine = jnp.tile(jnp.cos(angles), (1, 2))
    sine = jnp.concatenate([-jnp.sin(angles), jnp.sin(angles)], axis=1)
    own_blocks = jnp.broadcast_to(block_ids, (8, length))
    key_blocks = block_ids.reshape(length, 1)
    piece = QUERY_HEADS * HEAD_SIZE // experts
    groups = n_fsdp // n_ctx
    if fused:
        totals, dealt, attn_out, grad_rows = run_attention_exchange(
            qkv,
            heads,
            n_ctx,
            n_fsdp,
            cosine,
            sine,
            gains,
            own_blocks,
            key_blocks,
            select_rows,
            cotangent[0],
            out_all,
        )
        grad_rows = grad_rows.reshape(slots, width)
    else:
        mixed, totals, _ = run_attention(
            qkv, heads, n_ctx, cosine, sine, gains, own_blocks, key_blocks
        )
        attn_out = scatter_ctx(nn(mixed, out_here))
        grad_rows = dispatch(gather_ctx(cotangent[0]))
        dealt = mixed.reshape(length, groups, n_ctx, piece).transpose(2, 0, 1, 3)
        dealt = dealt.reshape(n_ctx, length, groups * piece)

    x = inputs[0].astype(F32)
    resid = x + attn_out.astype(F32)
    r_ffn = inverse_rms(resid)
    normed = (resid * r_ffn * gain_ffn).astype(BF)
    if fused:
        chosen = jnp.any(
            expert_ids[0][:, :, None] == jnp.arange(experts, dtype=jnp.int32), axis=1
        )
        logits = nt(normed, router_t)
        gates = jax.nn.softmax(jnp.where(chosen, logits, -jnp.inf), axis=-1)
        high = lax.reduce_precision(gates, 8, 7)
        payload = jnp.concatenate(
            [
                normed,
                high.astype(BF),
                (gates - high).astype(BF),
                jnp.zeros((span, AUX - 2 * experts), BF),
            ],
            axis=1,
        )
        rows, _, parts, inner_low, dg, du, y, dealt = run_expert_exchange(
            n_ctx,
            n_fsdp,
            payload,
            select_rows,
            select_rows.swapaxes(1, 2),
            expert_gate[0],
            expert_up[0],
            expert_down[0],
            grad_rows.reshape(n_fsdp, n_ctx, capacity, width),
            dealt,
        )
        rows = rows.reshape(slots, width + AUX)[:, :width]
        inner_low, dg, du = (array.reshape(slots, -1) for array in (inner_low, dg, du))
        y = y.reshape(slots, width)
        parts = jnp.sum(parts.astype(F32), axis=0)
        d_gates = parts[:, width : width + experts] + parts[:, width + experts : width + 2 * experts]
        d_logits = gates * (d_gates - jnp.sum(gates * d_gates, axis=-1, keepdims=True))
        d_logits = d_logits.astype(BF)
        d_normed = parts[:, :width] + nn(d_logits, router_t)
    else:
        dealt = lax.all_to_all(dealt, "ctx", split_axis=0, concat_axis=0, tiled=True)
        chosen = jnp.any(
            named[:, :, :, None] == jnp.arange(experts, dtype=jnp.int32), axis=1
        ).reshape(length, experts)
        normed = gather_ctx(normed)
        normed, grad_rows = lax.optimization_barrier((normed, grad_rows))
        grad_inner = nt(grad_rows, expert_down[0])
        logits = nt(normed, router_t)
        gates = jax.nn.softmax(jnp.where(chosen, logits, -jnp.inf), axis=-1)
        gates_here = lax.dynamic_slice_in_dim(gates, ctx * n_fsdp, n_fsdp, axis=1)
        gates_here = gates_here.reshape(n_ctx, span, n_fsdp).transpose(0, 2, 1)
        slot_gates = jnp.sum(select.astype(F32) * gates_here[:, :, None, :], axis=-1)
        slot_gates = route(slot_gates.transpose(1, 0, 2)).reshape(slots, 1)
        rows = dispatch(normed)
        g = nn(rows, expert_gate[0])
        u = nn(rows, expert_up[0])
        s = jax.nn.sigmoid(g)
        inner = g * s * u
        slot_dgates = jnp.sum(inner * grad_inner, axis=-1).reshape(n_fsdp, n_ctx, capacity)
        d_inner = grad_inner * slot_gates
        dg = (d_inner * u * s * (1.0 + g * (1.0 - s))).astype(BF)
        du = (d_inner * g * s).astype(BF)
        d_rows = (nt(dg, expert_gate[0]) + nt(du, expert_up[0])).astype(BF)
        y = (nn(inner.astype(BF), expert_down[0]) * slot_gates).astype(BF)
        inner_low = (inner * slot_gates).astype(BF)
        d_gates = jnp.einsum(
            "gjkt,jgk->gjt", select.astype(F32), route(slot_dgates), precision=lax.Precision.HIGHEST
        )
        weighted = (d_gates * gates_here).transpose(0, 2, 1).reshape(length, n_fsdp)
        d_logits = lax.dynamic_update_slice_in_dim(
            jnp.zeros((length, experts), F32), weighted, ctx * n_fsdp, axis=1
        ) - gates * jnp.sum(weighted, axis=1, keepdims=True)
        d_logits = d_logits.astype(BF)
        d_normed = scatter_ctx(combine(d_rows) + nn(d_logits, router_t)).astype(F32)

    gate_grad = tn(rows, dg)
    up_grad = tn(rows, du)
    down_grad = tn(inner_low, grad_rows)
    router_grad = tn(normed, d_logits)

    grad = cotangent[0].astype(F32)
    n = d_normed * gain_ffn
    d_resid = grad + r_ffn * n - resid * r_ffn**3 * jnp.mean(n * resid, axis=-1, keepdims=True)
    ffn_gain_grad = jnp.sum(d_normed * resid * r_ffn, axis=0)
    d_attn = gather_ctx(d_resid.astype(BF))
    y_all = combine(y).astype(BF)
    d_attn, gate_grad, up_grad, down_grad = lax.optimization_barrier(
        (d_attn, gate_grad, up_grad, down_grad)
    )
    d_mixed = nt(d_attn, out_here).astype(BF)

    moe = scatter_ctx(y_all).astype(F32)
    out_grad = jnp.einsum("ntk,td->nkd", dealt, d_attn, preferred_element_type=F32).astype(BF)

    dq, dkv, dgains = run_attention_back(
        qkv, d_mixed, totals, heads, cosine, sine, gains, own_blocks, key_blocks
    )
    d_qkv = jnp.concatenate([dq, dkv], axis=1)
    d_hidden = nt(d_qkv, w_qkv)
    attn_gain_grad = jnp.sum(d_hidden * x_all * r_all, axis=0)

    def spread(vector):
        parts = vector.reshape(n_fsdp, HEAD_SIZE // n_fsdp)
        return jnp.pad(parts, ((0, 0), (0, own_rows - parts.shape[1]))).reshape(width)

    small = jnp.stack(
        [attn_gain_grad, ffn_gain_grad, spread(dgains[0]), spread(dgains[1])], axis=1
    )
    extra_grad = jnp.concatenate(
        [
            router_grad.astype(BF),
            small.astype(BF),
            jnp.zeros((width, extra_width - experts - 4), BF),
        ],
        axis=1,
    )
    d_hidden, moe = lax.optimization_barrier((d_hidden.astype(BF), moe))
    d_hidden = scatter_ctx(d_hidden).astype(F32)
    shared_grad, rest, out_grad = run_last_reduce(
        n_ctx,
        n_fsdp,
        [tn(hidden, d_qkv).astype(BF), extra_grad, out_grad.reshape(n_fsdp * piece, width)],
    )
    out_grad = out_grad.reshape(n_ctx * piece, width).astype(F32)
    rest = rest.astype(F32).sum(axis=0)
    output = (resid + moe).astype(BF)[None]
    r_attn = inverse_rms(x)
    n = d_hidden * gain_attn
    input_grad = d_resid + r_attn * n - x * r_attn**3 * jnp.mean(n * x, axis=-1, keepdims=True)
    input_grad = input_grad.astype(BF)[None]

    query_grad = run_widen_columns(shared_grad, q_width)

    def kv_grad(at):
        parts = shared_grad[:, :, at : at + HEAD_SIZE].astype(F32)
        parts = parts.reshape(KEY_VALUE_HEADS, share, own_rows, HEAD_SIZE).sum(axis=1)
        return parts.transpose(1, 0, 2).reshape(own_rows, KEY_VALUE_HEADS * HEAD_SIZE)

    key_grad, value_grad = kv_grad(q_width), kv_grad(q_width + HEAD_SIZE)
    head_rows = HEAD_SIZE // n_fsdp
    return (
        output,
        input_grad,
        rest[:, experts],
        query_grad,
        key_grad,
        value_grad,
        rest[:head_rows, experts + 2],
        rest[:head_rows, experts + 3],
        out_grad,
        rest[:, experts + 1],
        rest[:, :experts],
        gate_grad[None],
        up_grad[None],
        down_grad[None],
    )


def solution(mesh):
    rows, tokens = P("fsdp", None), P("fsdp", "ctx", None)
    vector, expert = P("fsdp"), P(("ctx", "fsdp"), None, None)
    in_specs = (
        tokens,
        rows,
        tokens,
        tokens,
        vector,
        rows,
        rows,
        rows,
        vector,
        vector,
        rows,
        vector,
        rows,
        expert,
        expert,
        expert,
        tokens,
    )
    out_specs = (
        tokens,
        tokens,
        vector,
        rows,
        rows,
        rows,
        vector,
        vector,
        rows,
        vector,
        rows,
        expert,
        expert,
        expert,
    )
    return jax.shard_map(
        on_device, mesh=mesh, in_specs=in_specs, out_specs=out_specs, check_vma=False
    )
```

```python
import functools

import jax
import jax.numpy as jnp
import numpy as np
from jax import lax
from jax.experimental import pallas as pl
from jax.experimental.pallas import tpu as pltpu
from jax.sharding import PartitionSpec as P

QUERY_HEADS = 32
KEY_VALUE_HEADS = 4
HEAD_SIZE = 128
TOP = 8

EPSILON = 1e-06
ROPE_BASE = 1000000.0
MASKED = -1000000000.0
SCALE = HEAD_SIZE ** (-0.5)
HALF = HEAD_SIZE // 2
BF = jnp.bfloat16
F32 = jnp.float32


def nt(a, b):
    return lax.dot_general(a, b, (((1,), (1,)), ((), ())), preferred_element_type=F32)


def nn(a, b):
    return lax.dot_general(a, b, (((1,), (0,)), ((), ())), preferred_element_type=F32)


def tn(a, b):
    return lax.dot_general(a, b, (((0,), (0,)), ((), ())), preferred_element_type=F32)


def inverse_rms(values):
    return lax.rsqrt(jnp.mean(values * values, axis=-1, keepdims=True) + EPSILON)


def norm_rope(raw, gain, cosine, sine):
    z = raw * inverse_rms(raw) * gain
    return z * cosine + pltpu.roll(z, HALF, 1) * sine


def norm_rope_back(raw, gain, cosine, sine, grad):
    dz = grad * cosine - pltpu.roll(grad, HALF, 1) * sine
    r = inverse_rms(raw)
    n = dz * gain
    d_raw = r * n - raw * (r * r * r) * jnp.mean(n * raw, axis=-1, keepdims=True)
    return d_raw, jnp.sum(dz * raw * r, axis=0, keepdims=True)


def prepare_keys(k_ref, v_ref, cos_ref, sin_ref, gains_ref, keys, values_t):
    rotated = norm_rope(k_ref[...], gains_ref[1:2, :], cos_ref[...], sin_ref[...])
    keys[...] = rotated.astype(BF)
    values_t[...] = v_ref[...].T.astype(BF)


def attend_head(
    q_ref, cos_ref, sin_ref, gains_ref, own_ref, key_ref, total_ref, dealt_ref, keys, values_t, store
):
    queries = norm_rope(q_ref[...], gains_ref[0:1, :], cos_ref[...], sin_ref[...]).astype(BF)
    length = queries.shape[0]
    chunk = 256
    for start in range(0, length, chunk):
        scores = nt(keys[...], queries[start : start + chunk]) * SCALE
        seen = key_ref[...] <= own_ref[0:1, start : start + chunk]
        scores = jnp.where(seen, scores, MASKED)
        top = jnp.max(scores, axis=0, keepdims=True)
        weights = jnp.exp(scores - top)
        total = jnp.sum(weights, axis=0, keepdims=True)
        out = (nn(values_t[...], weights.astype(BF)) / total).T.astype(BF)
        store(start, chunk, out)
        dealt_ref[0, start : start + chunk, :] = out
        total_ref[0, :, start : start + chunk] = jnp.broadcast_to(top + jnp.log(total), (8, chunk))


def attention_forward(
    q_ref,
    k_ref,
    v_ref,
    cos_ref,
    sin_ref,
    gains_ref,
    own_ref,
    key_ref,
    mixed_ref,
    total_ref,
    dealt_ref,
    keys,
    values_t,
):
    @pl.when(pl.program_id(0) == 0)
    def _():
        prepare_keys(k_ref, v_ref, cos_ref, sin_ref, gains_ref, keys, values_t)

    def store(start, count, out):
        mixed_ref[start : start + count, :] = out

    attend_head(
        q_ref, cos_ref, sin_ref, gains_ref, own_ref, key_ref, total_ref, dealt_ref, keys, values_t, store
    )


def attention_backward(
    heads,
    q_ref,
    k_ref,
    v_ref,
    grad_ref,
    total_ref,
    cos_ref,
    sin_ref,
    gains_ref,
    own_ref,
    key_ref,
    dq_ref,
    dkv_ref,
    dgain_ref,
    keys,
    keys_t,
    values,
    dk,
    dv,
):
    cosine, sine = cos_ref[...], sin_ref[...]
    head = pl.program_id(0)

    @pl.when(head == 0)
    def _():
        rotated = norm_rope(k_ref[...], gains_ref[1:2, :], cosine, sine)
        keys[...] = rotated.astype(BF)
        keys_t[...] = rotated.T.astype(BF)
        values[...] = v_ref[...].astype(BF)
        dk[...] = jnp.zeros_like(dk)
        dv[...] = jnp.zeros_like(dv)
        dgain_ref[...] = jnp.zeros_like(dgain_ref)

    queries = norm_rope(q_ref[...], gains_ref[0:1, :], cosine, sine).astype(BF)
    length = queries.shape[0]
    chunk = 256
    for start in range(0, length, chunk):
        rows = slice(start, start + chunk)
        q_part = queries[rows]
        grad = grad_ref[rows, :]
        scores = nt(keys[...], q_part) * SCALE
        seen = key_ref[...] <= own_ref[0:1, rows]
        scores = jnp.where(seen, scores, MASKED)
        weights = jnp.exp(scores - total_ref[0, 0:1, rows])
        d_weights = nt(values[...], grad)
        row_dot = jnp.sum(weights * d_weights, axis=0, keepdims=True)
        d_scores = (weights * (d_weights - row_dot)).astype(BF)
        dv[...] += nn(weights.astype(BF), grad)
        dk[...] += nn(d_scores, q_part)
        d_queries = nn(keys_t[...], d_scores).T * SCALE
        d_raw, d_gain = norm_rope_back(
            q_ref[rows, :], gains_ref[0:1, :], cos_ref[rows, :], sin_ref[rows, :], d_queries
        )
        dq_ref[rows, :] = d_raw.astype(BF)
        dgain_ref[0:1, :] += d_gain

    @pl.when(head == heads - 1)
    def _():
        d_raw, d_gain = norm_rope_back(
            k_ref[...], gains_ref[1:2, :], cosine, sine, dk[...] * SCALE
        )
        dkv_ref[:, :HEAD_SIZE] = d_raw.astype(BF)
        dkv_ref[:, HEAD_SIZE:] = dv[...].astype(BF)
        dgain_ref[1:2, :] = d_gain


def attention_specs(heads, length):
    whole = lambda shape: pl.BlockSpec(shape, lambda h: (0,) * len(shape))
    column = lambda at: pl.BlockSpec((length, HEAD_SIZE), lambda h: (0, at))
    head_column = pl.BlockSpec((length, HEAD_SIZE), lambda h: (0, h))
    totals = pl.BlockSpec((1, 8, length), lambda h: (h, 0, 0))
    shared = [
        whole((length, HEAD_SIZE)),
        whole((length, HEAD_SIZE)),
        whole((8, HEAD_SIZE)),
        whole((8, length)),
        whole((length, 1)),
    ]
    return whole, column, head_column, totals, shared


def run_attention(qkv, heads, n_ctx, cosine, sine, gains, own, key_blocks):
    length = qkv.shape[0]
    whole, column, head_column, totals, shared = attention_specs(heads, length)
    deals = min(n_ctx, heads)
    return pl.pallas_call(
        attention_forward,
        grid=(heads,),
        in_specs=[head_column, column(heads), column(heads + 1)] + shared,
        out_specs=[
            head_column,
            totals,
            pl.BlockSpec((1, length, HEAD_SIZE), lambda h: (h % deals, 0, h // deals)),
        ],
        out_shape=[
            jax.ShapeDtypeStruct((length, heads * HEAD_SIZE), BF),
            jax.ShapeDtypeStruct((heads, 8, length), F32),
            jax.ShapeDtypeStruct((deals, length, heads // deals * HEAD_SIZE), BF),
        ],
        scratch_shapes=[
            pltpu.VMEM((length, HEAD_SIZE), BF),
            pltpu.VMEM((HEAD_SIZE, length), BF),
        ],
        compiler_params=pltpu.CompilerParams(vmem_limit_bytes=48 * 2**20),
        cost_estimate=pl.CostEstimate(
            flops=4 * heads * length * length * HEAD_SIZE,
            bytes_accessed=8 * heads * length * HEAD_SIZE,
            transcendentals=heads * length * length,
        ),
    )(qkv, qkv, qkv, cosine, sine, gains, own, key_blocks)


def run_attention_back(qkv, grad, totals_in, heads, cosine, sine, gains, own, key_blocks):
    length = qkv.shape[0]
    whole, column, head_column, totals, shared = attention_specs(heads, length)
    return pl.pallas_call(
        functools.partial(attention_backward, heads),
        grid=(heads,),
        in_specs=[head_column, column(heads), column(heads + 1), head_column, totals] + shared,
        out_specs=[head_column, whole((length, 2 * HEAD_SIZE)), whole((8, HEAD_SIZE))],
        out_shape=[
            jax.ShapeDtypeStruct((length, heads * HEAD_SIZE), BF),
            jax.ShapeDtypeStruct((length, 2 * HEAD_SIZE), BF),
            jax.ShapeDtypeStruct((8, HEAD_SIZE), F32),
        ],
        scratch_shapes=[
            pltpu.VMEM((length, HEAD_SIZE), BF),
            pltpu.VMEM((HEAD_SIZE, length), BF),
            pltpu.VMEM((length, HEAD_SIZE), BF),
            pltpu.VMEM((length, HEAD_SIZE), F32),
            pltpu.VMEM((length, HEAD_SIZE), F32),
        ],
        compiler_params=pltpu.CompilerParams(vmem_limit_bytes=48 * 2**20),
        cost_estimate=pl.CostEstimate(
            flops=10 * heads * length * length * HEAD_SIZE,
            bytes_accessed=10 * heads * length * HEAD_SIZE,
            transcendentals=heads * length * length,
        ),
    )(qkv, qkv, qkv, grad, totals_in, cosine, sine, gains, own, key_blocks)


def push(source, target, sends, recvs, device):
    copy = pltpu.make_async_remote_copy(
        src_ref=source,
        dst_ref=target,
        send_sem=sends,
        recv_sem=recvs,
        device_id=device,
        device_id_type=pl.DeviceIdType.MESH,
    )
    return copy


def greet(devices):
    barrier = pltpu.get_barrier_semaphore()
    for device in devices:
        pl.semaphore_signal(barrier, 1, device_id=device, device_id_type=pl.DeviceIdType.MESH)
    pl.semaphore_wait(barrier, len(devices))


class LineGather:
    def __init__(self, n_ctx, ctx, fsdp, own_ref, all_ref, up, down, arrived):
        self.n_ctx, self.ctx, self.fsdp = n_ctx, ctx, fsdp
        self.own_ref, self.all_ref = own_ref, all_ref
        self.up, self.down, self.arrived = up, down, arrived

    def copy(self, source, block, sems, step, to):
        return push(
            source, self.all_ref.at[block], sems.at[step], self.arrived.at[block], (to, self.fsdp)
        )

    def going_up(self, step):
        return (self.ctx - step >= 0) & (self.ctx < self.n_ctx - 1)

    def going_down(self, step):
        return (self.ctx + step < self.n_ctx) & (self.ctx > 0)

    def step(self, step):
        def hop(block, sems, to, more):
            if step > 0:
                self.copy(self.own_ref, block, sems, 0, to).wait_recv()

            @pl.when(more)
            def _():
                source = self.all_ref.at[block] if step > 0 else self.own_ref
                self.copy(source, block, sems, step, to).start()

        @pl.when(self.ctx - step >= 0)
        def _():
            hop(self.ctx - step, self.up, self.ctx + 1, self.ctx < self.n_ctx - 1)

        @pl.when(self.ctx + step < self.n_ctx)
        def _():
            hop(self.ctx + step, self.down, self.ctx - 1, self.ctx > 0)

    def finish(self):
        for step in range(self.n_ctx - 1):

            @pl.when(self.going_up(step))
            def _():
                self.copy(self.own_ref, 0, self.up, step, self.ctx).wait_send()

            @pl.when(self.going_down(step))
            def _():
                self.copy(self.own_ref, 0, self.down, step, self.ctx).wait_send()


class LineScatter:
    def __init__(self, n_ctx, ctx, fsdp, chunks, held, low, high, up, down, low_in, high_in):
        self.n_ctx, self.ctx, self.fsdp, self.chunks = n_ctx, ctx, fsdp, chunks
        self.held, self.low, self.high = held, low, high
        self.sems = {"up": (low, up, low_in), "down": (high, down, high_in)}
        self.size = held.shape[1] // chunks

    def copy(self, way, block, chunk, to):
        landing, sends, arrived = self.sems[way]
        rows = pl.ds(chunk * self.size, self.size)
        return push(
            self.held.at[block, rows],
            landing.at[block, rows],
            sends.at[block, chunk],
            arrived.at[block, chunk],
            (to, self.fsdp),
        )

    def scatter(self, chunk):
        rows = slice(chunk * self.size, (chunk + 1) * self.size)
        ctx, held = self.ctx, self.held

        def pass_on(way, block, to, first):
            @pl.when(jnp.logical_not(first))
            def _():
                self.copy(way, block, chunk, ctx).wait_recv()
                held[block, rows, :] = (
                    held[block, rows, :].astype(F32)
                    + self.sems[way][0][block, rows, :].astype(F32)
                ).astype(BF)

            self.copy(way, block, chunk, to).start()

        for step in range(self.n_ctx - 1):

            @pl.when(ctx < self.n_ctx - 1 - step)
            def _():
                pass_on("up", self.n_ctx - 1 - step, ctx + 1, ctx == 0)

            @pl.when(ctx > step)
            def _():
                pass_on("down", step, ctx - 1, ctx == self.n_ctx - 1)

    def settle(self, chunk, total_ref):
        rows = slice(chunk * self.size, (chunk + 1) * self.size)
        total_ref[rows, :] = self.held[self.ctx, rows, :].astype(F32)

        @pl.when(self.ctx > 0)
        def _():
            self.copy("up", self.ctx, chunk, self.ctx).wait_recv()
            total_ref[rows, :] += self.low[self.ctx, rows, :].astype(F32)

        @pl.when(self.ctx < self.n_ctx - 1)
        def _():
            self.copy("down", self.ctx, chunk, self.ctx).wait_recv()
            total_ref[rows, :] += self.high[self.ctx, rows, :].astype(F32)

    def finish(self):
        for chunk in range(self.chunks):
            for step in range(self.n_ctx - 1):

                @pl.when(self.ctx < self.n_ctx - 1 - step)
                def _():
                    self.copy("up", self.n_ctx - 1 - step, chunk, self.ctx).wait_send()

                @pl.when(self.ctx > step)
                def _():
                    self.copy("down", step, chunk, self.ctx).wait_send()


def first_gather(
    n_ctx,
    n_fsdp,
    x_ref,
    table_ref,
    packed_ref,
    x_all,
    table_all,
    packed_all,
    local,
    up,
    down,
    arrived,
    table_send,
    table_arrived,
    packed_send,
    passed_send,
    packed_arrived,
):
    ctx, fsdp = lax.axis_index("ctx"), lax.axis_index("fsdp")
    sibling = lax.rem(fsdp + 1, 2) + (fsdp // 2) * 2
    chips = n_fsdp // 2

    def same_core(offset):
        return lax.rem(fsdp + 2 * offset, n_fsdp)

    def along(offset):
        return lax.rem(ctx + offset, n_ctx)

    greet(
        [(along(i), fsdp) for i in range(1, n_ctx)]
        + [(ctx, same_core(i)) for i in range(1, chips)]
        + [(ctx, sibling)]
    )
    kept = [
        pltpu.make_async_copy(x_ref, x_all.at[ctx], local.at[0]),
        pltpu.make_async_copy(table_ref, table_all.at[ctx], local.at[1]),
        pltpu.make_async_copy(packed_ref, packed_all.at[fsdp], local.at[2]),
    ]
    for copy in kept:
        copy.start()

    def packed_copy(source, owner, sems, to):
        return push(source, packed_all.at[owner], sems, packed_arrived.at[owner], (ctx, to))

    for i in range(1, chips):
        packed_copy(packed_ref, fsdp, packed_send.at[i], same_core(i)).start()
    packed_copy(packed_ref, fsdp, packed_send.at[0], sibling).start()
    for i in range(1, n_ctx):
        push(
            table_ref, table_all.at[ctx], table_send.at[i], table_arrived.at[ctx], (along(i), fsdp)
        ).start()
    line = LineGather(n_ctx, ctx, fsdp, x_ref, x_all, up, down, arrived)
    for step in range(n_ctx):
        line.step(step)
    for i in range(1, chips):
        owner = same_core(chips - i)
        packed_copy(packed_ref, owner, packed_send.at[i], sibling).wait_recv()
        packed_copy(packed_all.at[owner], owner, passed_send.at[i], sibling).start()
    for i in range(chips):
        owner = lax.rem(sibling + 2 * i, n_fsdp)
        packed_copy(packed_ref, owner, packed_send.at[0], sibling).wait_recv()
    for i in range(1, n_ctx):
        owner = along(i)
        push(
            table_ref, table_all.at[owner], table_send.at[i], table_arrived.at[owner], (owner, fsdp)
        ).wait()
    line.finish()
    for i in range(chips):
        packed_copy(packed_ref, fsdp, packed_send.at[i], sibling).wait_send()
    for i in range(1, chips):
        packed_copy(packed_ref, fsdp, passed_send.at[i], sibling).wait_send()
    for copy in kept:
        copy.wait()


def run_first_gather(n_ctx, n_fsdp, x, table, packed):
    anywhere = pl.BlockSpec(memory_space=pl.ANY)
    dma = pltpu.SemaphoreType.DMA
    return pl.pallas_call(
        functools.partial(first_gather, n_ctx, n_fsdp),
        in_specs=[anywhere] * 3,
        out_specs=[anywhere] * 3,
        out_shape=[
            jax.ShapeDtypeStruct((n_ctx,) + x.shape, x.dtype),
            jax.ShapeDtypeStruct((n_ctx,) + table.shape, table.dtype),
            jax.ShapeDtypeStruct((n_fsdp,) + packed.shape, packed.dtype),
        ],
        scratch_shapes=[
            dma((3,)),
            dma((n_ctx,)),
            dma((n_ctx,)),
            dma((n_ctx,)),
            dma((n_ctx,)),
            dma((n_ctx,)),
            dma((n_fsdp // 2,)),
            dma((n_fsdp // 2,)),
            dma((n_fsdp,)),
        ],
        compiler_params=pltpu.CompilerParams(collective_id=1, has_side_effects=True),
        cost_estimate=pl.CostEstimate(
            flops=0, bytes_accessed=200 * 2**20, transcendentals=0
        ),
    )(x, table, packed)


TILE = 512
AUX = 128


def expert_exchange(
    n_ctx,
    n_fsdp,
    x_ref,
    sel_ref,
    selt_ref,
    gate_ref,
    up_ref,
    down_ref,
    grad_ref,
    dealt_ref,
    rows_ref,
    back_ref,
    part_ref,
    inner_ref,
    dg_ref,
    du_ref,
    y_ref,
    dealt_all,
    w_gate,
    w_up,
    w_down,
    held,
    staged,
    rows_in,
    grad_in,
    inner_out,
    dg_out,
    du_out,
    y_out,
    back_in,
    w_sems,
    local,
    held_send,
    held_arrived,
    rows_send,
    rows_arrived,
    back_send,
    back_arrived,
    part_send,
    part_arrived,
    dealt_send,
    dealt_arrived,
    out_sems,
):
    ctx, fsdp = lax.axis_index("ctx"), lax.axis_index("fsdp")
    experts = n_ctx * n_fsdp
    expert = ctx * n_fsdp + fsdp
    width, hidden = w_gate.shape
    wide = held.shape[2]
    capacity = staged.shape[2]
    half = n_fsdp // 2
    tiles = [(at, min(TILE, wide - at)) for at in range(0, wide, TILE)]

    def along(offset):
        return lax.rem(ctx + offset, n_ctx)

    def around(offset):
        return lax.rem(fsdp + offset, n_fsdp)

    greet(
        [(along(i), fsdp) for i in range(1, n_ctx)] + [(ctx, around(i)) for i in range(1, n_fsdp)]
    )
    weights = [
        pltpu.make_async_copy(gate_ref, w_gate, w_sems.at[0]),
        pltpu.make_async_copy(up_ref, w_up, w_sems.at[1]),
        pltpu.make_async_copy(down_ref, w_down, w_sems.at[2]),
    ]
    own = pltpu.make_async_copy(x_ref, held.at[ctx], local.at[0])
    own.start()
    for copy in weights:
        copy.start()

    def held_copy(step):
        to = lax.rem(ctx + n_ctx - step, n_ctx)
        return push(x_ref, held.at[ctx], held_send.at[step], held_arrived.at[ctx], (to, fsdp))

    def rows_copy(step, group, offset):
        to = around(offset)
        return push(
            staged.at[step, to],
            rows_ref.at[fsdp, group],
            rows_send.at[step, offset],
            rows_arrived.at[group, fsdp],
            (ctx, to),
        )

    def rows_kept(step, group):
        return pltpu.make_async_copy(
            staged.at[step, fsdp], rows_ref.at[fsdp, group], rows_arrived.at[group, fsdp]
        )

    def back_copy(step, group, offset):
        to = around(offset)
        return push(
            staged.at[step, to],
            back_ref.at[group, fsdp],
            back_send.at[step, offset],
            back_arrived.at[group, fsdp],
            (ctx, to),
        )

    def back_kept(step, group):
        return pltpu.make_async_copy(
            staged.at[step, fsdp], back_ref.at[group, fsdp], back_arrived.at[group, fsdp]
        )

    def outputs(group):
        return [
            pltpu.make_async_copy(inner_out, inner_ref.at[:, group], out_sems.at[0]),
            pltpu.make_async_copy(dg_out, dg_ref.at[:, group], out_sems.at[1]),
            pltpu.make_async_copy(du_out, du_ref.at[:, group], out_sems.at[2]),
            pltpu.make_async_copy(y_out, y_ref.at[:, group], out_sems.at[3]),
        ]

    def dispatch(step):
        group = along(step)

        @pl.when(step == 0)
        def _():
            own.wait()

        @pl.when(step > 0)
        def _():
            push(
                x_ref, held.at[group], held_send.at[step], held_arrived.at[group], (group, fsdp)
            ).wait_recv()

        @pl.when(step + 1 < n_ctx)
        def _():
            held_copy(step + 1).start()

        for at, size in tiles:
            picked = nn(sel_ref[group], held[group, :, at : at + size])
            staged[step, :, :, at : at + size] = picked.astype(BF).reshape(n_fsdp, capacity, size)
        rows_kept(step, group).start()
        for offset in range(1, n_fsdp):
            rows_copy(step, group, offset).start()

    def compute(step):
        group = along(step)
        rows_kept(step, group).wait()
        for offset in range(1, n_fsdp):
            source = around(offset)
            push(
                staged.at[step, source],
                rows_ref.at[source, group],
                rows_send.at[step, offset],
                rows_arrived.at[group, source],
                (ctx, source),
            ).wait_recv()
        load_rows = pltpu.make_async_copy(rows_ref.at[:, group], rows_in, local.at[1])
        load_inner = pltpu.make_async_copy(grad_ref.at[:, group], grad_in, local.at[2])
        load_rows.start()
        load_inner.start()

        @pl.when(step == 0)
        def _():
            for copy in weights:
                copy.wait()

        @pl.when(step > 0)
        def _():
            for copy in outputs(group):
                copy.wait()

        for offset in range(1, n_fsdp):
            rows_copy(step, group, offset).wait_send()
        load_rows.wait()
        load_inner.wait()
        count = half * capacity
        lane = lax.broadcasted_iota(jnp.int32, (count, AUX), 1)
        high, low = lane == expert, lane == experts + expert

        @pl.loop(0, 2)
        def _(part):
            sources = pl.ds(part * half, half)
            rows = rows_in[sources, :, :width].reshape(count, width)
            aux = rows_in[sources, :, width:].reshape(count, AUX).astype(F32)
            gate = jnp.sum(jnp.where(high | low, aux, 0.0), axis=1, keepdims=True)
            g = nn(rows, w_gate[...])
            u = nn(rows, w_up[...])
            s = jax.nn.sigmoid(g)
            inner = g * s * u
            d_inner = nt(grad_in[sources].reshape(count, width), w_down[...])
            d_gate = jnp.sum(inner * d_inner, axis=1, keepdims=True)
            d_inner = d_inner * gate
            dg = (d_inner * u * s * (1.0 + g * (1.0 - s))).astype(BF)
            du = (d_inner * g * s).astype(BF)
            inner_out[sources] = (inner * gate).astype(BF).reshape(half, capacity, hidden)
            dg_out[sources] = dg.reshape(half, capacity, hidden)
            du_out[sources] = du.reshape(half, capacity, hidden)
            rest = d_gate - d_gate.astype(BF).astype(F32)
            staged[step, sources, :, width:] = (
                jnp.where(high, d_gate, jnp.where(low, rest, 0.0))
                .astype(BF)
                .reshape(half, capacity, AUX)
            )
            for at in range(0, width, TILE):
                grad = nt(dg, w_gate[at : at + TILE, :]) + nt(du, w_up[at : at + TILE, :])
                staged[step, sources, :, at : at + TILE] = grad.astype(BF).reshape(
                    half, capacity, TILE
                )
            low_inner = inner.astype(BF)
            for at in range(0, width, TILE):
                y = nn(low_inner, w_down[:, at : at + TILE]) * gate
                y_out[sources, :, at : at + TILE] = y.astype(BF).reshape(half, capacity, TILE)

        def send_back(step, group):
            back_kept(step, group).start()
            for offset in range(1, n_fsdp):
                back_copy(step, group, offset).start()

        @pl.when(step > 0)
        def _():
            send_back(step, group)

        @pl.when(step == n_ctx - 1)
        def _():
            send_back(0, ctx)

        for copy in outputs(group):
            copy.start()

    def combine(step):
        group = along(step)
        back_kept(step, group).wait()
        for offset in range(1, n_fsdp):
            source = around(offset)
            push(
                staged.at[step, source],
                back_ref.at[group, source],
                back_send.at[step, offset],
                back_arrived.at[group, source],
                (ctx, source),
            ).wait_recv()
        load = pltpu.make_async_copy(back_ref.at[group], back_in, local.at[1])
        load.start()
        load.wait()
        for at, size in tiles:
            back = back_in[:, :, at : at + size].reshape(n_fsdp * capacity, size)
            held[group, :, at : at + size] = nn(selt_ref[group], back).astype(BF)

        @pl.when(step == 0)
        def _():
            pltpu.make_async_copy(
                held.at[group], part_ref.at[ctx], part_arrived.at[ctx]
            ).start()

        @pl.when(step > 0)
        def _():
            push(
                held.at[group],
                part_ref.at[ctx],
                part_send.at[step],
                part_arrived.at[ctx],
                (group, fsdp),
            ).start()

    def dealt_copy(offset):
        to = along(offset)
        return push(
            dealt_ref.at[to],
            dealt_all.at[ctx],
            dealt_send.at[offset],
            dealt_arrived.at[ctx],
            (to, fsdp),
        )

    dealt_kept = pltpu.make_async_copy(
        dealt_ref.at[ctx], dealt_all.at[ctx], dealt_arrived.at[ctx]
    )

    @pl.loop(0, n_ctx + 3)
    def _(tick):
        @pl.when(tick < n_ctx)
        def _():
            dispatch(tick)

        @pl.when(tick == n_ctx - 1)
        def _():
            dealt_kept.start()
            for offset in range(1, n_ctx):
                dealt_copy(offset).start()

        @pl.when((tick >= 1) & (tick <= n_ctx))
        def _():
            compute(tick - 1)

        @pl.when(tick >= 3)
        def _():
            combine(lax.rem(tick - 2, n_ctx))

    pltpu.make_async_copy(held.at[ctx], part_ref.at[ctx], part_arrived.at[ctx]).wait()
    for step in range(1, n_ctx):
        other = along(step)
        copy = push(
            held.at[other], part_ref.at[other], part_send.at[step], part_arrived.at[other], (other, fsdp)
        )
        copy.wait()
        held_copy(step).wait_send()
    dealt_kept.wait()
    for offset in range(1, n_ctx):
        other = along(offset)
        push(
            dealt_ref.at[other],
            dealt_all.at[other],
            dealt_send.at[offset],
            dealt_arrived.at[other],
            (other, fsdp),
        ).wait()
    for step in range(n_ctx):
        for offset in range(1, n_fsdp):
            back_copy(step, along(step), offset).wait_send()
    for copy in outputs(along(n_ctx - 1)):
        copy.wait()


def run_expert_exchange(n_ctx, n_fsdp, x, select, select_t, gate, up, down, grads, dealt):
    anywhere, inside = pl.BlockSpec(memory_space=pl.ANY), pl.BlockSpec(memory_space=pltpu.VMEM)
    span, wide = x.shape
    width, hidden = gate.shape
    capacity = grads.shape[2]
    slots = (n_fsdp, n_ctx, capacity)
    one = (n_fsdp, capacity)
    dma, vmem, shape = pltpu.SemaphoreType.DMA, pltpu.VMEM, jax.ShapeDtypeStruct
    return pl.pallas_call(
        functools.partial(expert_exchange, n_ctx, n_fsdp),
        in_specs=[anywhere, inside, inside] + [anywhere] * 5,
        out_specs=[anywhere] * 8,
        out_shape=[
            shape(slots + (wide,), BF),
            shape((n_ctx, n_fsdp, capacity, wide), BF),
            shape((n_ctx, span, wide), BF),
            shape(slots + (hidden,), BF),
            shape(slots + (hidden,), BF),
            shape(slots + (hidden,), BF),
            shape(slots + (width,), BF),
            shape(dealt.shape, BF),
        ],
        scratch_shapes=[
            vmem((width, hidden), BF),
            vmem((width, hidden), BF),
            vmem((hidden, width), BF),
            vmem((n_ctx, span, wide), BF),
            vmem((n_ctx,) + one + (wide,), BF),
            vmem(one + (wide,), BF),
            vmem(one + (width,), BF),
            vmem(one + (hidden,), BF),
            vmem(one + (hidden,), BF),
            vmem(one + (hidden,), BF),
            vmem(one + (width,), BF),
            vmem(one + (wide,), BF),
            dma((3,)),
            dma((3,)),
            dma((n_ctx,)),
            dma((n_ctx,)),
            dma((n_ctx, n_fsdp)),
            dma((n_ctx, n_fsdp)),
            dma((n_ctx, n_fsdp)),
            dma((n_ctx, n_fsdp)),
            dma((n_ctx,)),
            dma((n_ctx,)),
            dma((n_ctx,)),
            dma((n_ctx,)),
            dma((4,)),
        ],
        compiler_params=pltpu.CompilerParams(
            collective_id=2, has_side_effects=True, vmem_limit_bytes=60 * 2**20
        ),
        cost_estimate=pl.CostEstimate(
            flops=12 * n_fsdp * n_ctx * capacity * width * hidden,
            bytes_accessed=600 * 2**20,
            transcendentals=0,
        ),
    )(x, select, select_t, gate, up, down, grads, dealt)


def last_reduce(n_ctx, n_fsdp, *refs):
    ctx, fsdp = lax.axis_index("ctx"), lax.axis_index("fsdp")
    count = (len(refs) - 1) // 11
    ins, alls, local, refs = refs[:count], refs[count : 2 * count], refs[2 * count], refs[2 * count + 1 :]
    items = [refs[9 * i : 9 * i + 9] for i in range(count)]
    chips, chip, core = n_fsdp // 2, fsdp // 2, lax.rem(fsdp, 2)
    sibling = chip * 2 + 1 - core

    def along(offset):
        return lax.rem(ctx + offset, n_ctx)

    def other_chip(offset):
        return lax.rem(chip + offset, chips)

    greet(
        [(along(i), fsdp) for i in range(1, n_ctx)]
        + [(ctx, other_chip(i) * 2 + core) for i in range(1, chips)]
        + [(ctx, sibling)]
    )
    crossing, loads, lines = [], [], []
    for at, (in_ref, all_ref, item) in enumerate(zip(ins, alls, items)):
        mine, beside, landed, own, cross, sends, arrived, line_sems, line_arrived = item
        crossing.append(
            push(in_ref.at[:, 1 - core], beside, cross.at[0], cross.at[1], (ctx, sibling))
        )
        crossing[-1].start()
        loads.append(pltpu.make_async_copy(in_ref.at[:, core], mine, local.at[at]))
        loads[-1].start()
        lines.append(
            LineGather(
                n_ctx, ctx, fsdp, own, all_ref, line_sems.at[0], line_sems.at[1], line_arrived
            )
        )

    def chip_copy(item, offset):
        mine, beside, landed, own, cross, sends, arrived, line_sems, line_arrived = item
        to = other_chip(offset)
        return push(
            mine.at[to], landed.at[chip], sends.at[offset], arrived.at[chip], (ctx, to * 2 + core)
        )

    for crossed, loaded, item in zip(crossing, loads, items):
        mine, beside = item[:2]
        loaded.wait()
        crossed.wait_recv()
        for offset in range(1, chips + 1):
            to = other_chip(offset)
            mine[to] = (mine[to].astype(F32) + beside[to].astype(F32)).astype(BF)
            if offset < chips:
                chip_copy(item, offset).start()
    keeps = []
    for at, (item, line, all_ref) in enumerate(zip(items, lines, alls)):
        mine, beside, landed, own, cross, sends, arrived, line_sems, line_arrived = item
        total = mine[chip].astype(F32)
        for offset in range(1, chips):
            source = other_chip(offset)
            push(
                mine.at[source], landed.at[source], sends.at[offset], arrived.at[source], (ctx, sibling)
            ).wait_recv()
            total = total + landed[source].astype(F32)
        own[...] = total.astype(BF)
        line.step(0)
        keeps.append(pltpu.make_async_copy(own, all_ref.at[ctx], local.at[at]))
        keeps[-1].start()
    for step in range(1, n_ctx):
        for line in lines:
            line.step(step)
    for crossed, keep, line, item in zip(crossing, keeps, lines, items):
        crossed.wait_send()
        keep.wait()
        line.finish()
        for offset in range(1, chips):
            chip_copy(item, offset).wait_send()


def run_last_reduce(n_ctx, n_fsdp, grads):
    anywhere = pl.BlockSpec(memory_space=pl.ANY)
    dma, vmem, shape = pltpu.SemaphoreType.DMA, pltpu.VMEM, jax.ShapeDtypeStruct
    chips = n_fsdp // 2
    grads = [grad.reshape((chips, 2, -1) + grad.shape[-1:]) for grad in grads]
    blocks = [grad.shape[2:] for grad in grads]
    scratch = [dma((len(grads),))]
    for block in blocks:
        scratch += [
            vmem((chips,) + block, BF),
            vmem((chips,) + block, BF),
            vmem((chips,) + block, BF),
            vmem(block, BF),
            dma((2,)),
            dma((chips,)),
            dma((chips,)),
            dma((2, n_ctx)),
            dma((n_ctx,)),
        ]
    return pl.pallas_call(
        functools.partial(last_reduce, n_ctx, n_fsdp),
        in_specs=[anywhere] * len(grads),
        out_specs=[anywhere] * len(grads),
        out_shape=[shape((n_ctx,) + block, BF) for block in blocks],
        scratch_shapes=scratch,
        compiler_params=pltpu.CompilerParams(
            collective_id=3, has_side_effects=True, vmem_limit_bytes=60 * 2**20
        ),
        cost_estimate=pl.CostEstimate(flops=0, bytes_accessed=400 * 2**20, transcendentals=0),
    )(*grads)


def widen_columns(in_ref, out_ref):
    out_ref[...] = in_ref[0].astype(F32)


def run_widen_columns(blocks, columns):
    n, rows, _ = blocks.shape
    return pl.pallas_call(
        widen_columns,
        grid=(n,),
        in_specs=[pl.BlockSpec((1, rows, columns), lambda i: (i, 0, 0))],
        out_specs=pl.BlockSpec((rows, columns), lambda i: (0, i)),
        out_shape=jax.ShapeDtypeStruct((rows, n * columns), F32),
    )(blocks)


def attention_exchange(
    n_ctx,
    n_fsdp,
    heads,
    q_ref,
    k_ref,
    v_ref,
    cos_ref,
    sin_ref,
    gains_ref,
    own_ref,
    key_ref,
    sel_ref,
    grad_ref,
    out_ref,
    total_ref,
    dealt_ref,
    attn_ref,
    rows_ref,
    keys,
    values_t,
    mixed,
    w_out,
    held,
    low,
    high,
    grads,
    staged,
    local,
    grad_up,
    grad_down,
    grad_arrived,
    rows_send,
    rows_arrived,
    up_send,
    down_send,
    low_arrived,
    high_arrived,
):
    head = pl.program_id(0)
    ctx, fsdp = lax.axis_index("ctx"), lax.axis_index("fsdp")
    _, span, width = held.shape
    capacity = staged.shape[2]
    q_width = heads * HEAD_SIZE

    def along(offset):
        return lax.rem(ctx + offset, n_ctx)

    def around(offset):
        return lax.rem(fsdp + offset, n_fsdp)

    line = LineGather(n_ctx, ctx, fsdp, grad_ref, grads, grad_up, grad_down, grad_arrived)
    sums = LineScatter(
        n_ctx, ctx, fsdp, 4, held, low, high, up_send, down_send, low_arrived, high_arrived
    )
    own = pltpu.make_async_copy(grad_ref, grads.at[ctx], local.at[0])
    weights = pltpu.make_async_copy(
        out_ref.at[pl.ds(ctx * q_width, q_width)], w_out, local.at[1]
    )

    def rows_copy(group, offset):
        to = around(offset)
        return push(
            staged.at[group, to],
            rows_ref.at[fsdp, group],
            rows_send.at[group, offset],
            rows_arrived.at[group, fsdp],
            (ctx, to),
        )

    def rows_kept(group):
        return pltpu.make_async_copy(
            staged.at[group, fsdp], rows_ref.at[fsdp, group], rows_arrived.at[group, fsdp]
        )

    def pick(group):
        for at in range(0, width, TILE):
            picked = nn(sel_ref[group], grads[group, :, at : at + TILE])
            staged[group, :, :, at : at + TILE] = picked.astype(BF).reshape(n_fsdp, capacity, TILE)
        rows_kept(group).start()
        for offset in range(1, n_fsdp):
            rows_copy(group, offset).start()

    def pick_from(distance):
        @pl.when(ctx - distance >= 0)
        def _():
            pick(ctx - distance)

        @pl.when(ctx + distance < n_ctx)
        def _():
            pick(ctx + distance)

    @pl.when(head == 0)
    def _():
        own.start()
        weights.start()
        greet(
            [(along(i), fsdp) for i in range(1, n_ctx)]
            + [(ctx, around(i)) for i in range(1, n_fsdp)]
        )
        line.step(0)
        own.wait()
        pick(ctx)
        prepare_keys(k_ref, v_ref, cos_ref, sin_ref, gains_ref, keys, values_t)

    @pl.when(head < heads)
    def _():
        def store(start, count, out):
            columns = pl.ds(pl.multiple_of(head * HEAD_SIZE, HEAD_SIZE), HEAD_SIZE)
            mixed[start : start + count, columns] = out

        attend_head(
            q_ref,
            cos_ref,
            sin_ref,
            gains_ref,
            own_ref,
            key_ref,
            total_ref,
            dealt_ref,
            keys,
            values_t,
            store,
        )

    @pl.when(head == heads - 2)
    def _():
        line.step(1)
        pick_from(1)

    @pl.when(head == heads)
    def _():
        weights.wait()
        for block in range(n_ctx):
            for at in range(0, width, TILE):
                held[block, :, at : at + TILE] = nn(
                    mixed[block * span : (block + 1) * span, :], w_out[:, at : at + TILE]
                ).astype(BF)
        line.step(2)
        sums.scatter(0)
        pick_from(2)
        sums.scatter(1)
        for step in range(3, n_ctx):
            line.step(step)
            pick_from(step)
        sums.scatter(2)
        sums.scatter(3)
        for chunk in range(4):
            sums.settle(chunk, attn_ref)
        sums.finish()
        line.finish()
        for group in range(n_ctx):
            rows_kept(group).wait()
            for offset in range(1, n_fsdp):
                source = around(offset)
                push(
                    staged.at[group, source],
                    rows_ref.at[source, group],
                    rows_send.at[group, offset],
                    rows_arrived.at[group, source],
                    (ctx, source),
                ).wait()


def run_attention_exchange(
    qkv, heads, n_ctx, n_fsdp, cosine, sine, gains, own, key_blocks, select, grad, w_out
):
    length = qkv.shape[0]
    span, width = grad.shape
    capacity = select.shape[1] // n_fsdp
    anywhere = pl.BlockSpec(memory_space=pl.ANY)
    dma, vmem, shape = pltpu.SemaphoreType.DMA, pltpu.VMEM, jax.ShapeDtypeStruct
    last = heads - 1
    whole, column, _, _, shared = attention_specs(heads, length)
    clip = lambda h: jnp.minimum(h, last)
    return pl.pallas_call(
        functools.partial(attention_exchange, n_ctx, n_fsdp, heads),
        grid=(heads + 1,),
        in_specs=[
            pl.BlockSpec((length, HEAD_SIZE), lambda h: (0, clip(h))),
            column(heads),
            column(heads + 1),
        ]
        + shared
        + [whole(select.shape), anywhere, anywhere],
        out_specs=[
            pl.BlockSpec((1, 8, length), lambda h: (clip(h), 0, 0)),
            pl.BlockSpec(
                (1, length, HEAD_SIZE),
                lambda h: (lax.rem(clip(h), n_ctx), 0, lax.div(clip(h), n_ctx)),
            ),
            whole((span, width)),
            anywhere,
        ],
        out_shape=[
            shape((heads, 8, length), F32),
            shape((n_ctx, length, heads // n_ctx * HEAD_SIZE), BF),
            shape((span, width), F32),
            shape((n_fsdp, n_ctx, capacity, width), BF),
        ],
        scratch_shapes=[
            vmem((length, HEAD_SIZE), BF),
            vmem((HEAD_SIZE, length), BF),
            vmem((length, heads * HEAD_SIZE), BF),
            vmem((heads * HEAD_SIZE, width), BF),
            vmem((n_ctx, span, width), BF),
            vmem((n_ctx, span, width), BF),
            vmem((n_ctx, span, width), BF),
            vmem((n_ctx, span, width), BF),
            vmem((n_ctx, n_fsdp, capacity, width), BF),
            dma((2,)),
            dma((n_ctx,)),
            dma((n_ctx,)),
            dma((n_ctx,)),
            dma((n_ctx, n_fsdp)),
            dma((n_ctx, n_fsdp)),
            dma((n_ctx, 4)),
            dma((n_ctx, 4)),
            dma((n_ctx, 4)),
            dma((n_ctx, 4)),
        ],
        compiler_params=pltpu.CompilerParams(
            collective_id=4, has_side_effects=True, vmem_limit_bytes=60 * 2**20
        ),
        cost_estimate=pl.CostEstimate(
            flops=4 * heads * length * length * HEAD_SIZE,
            bytes_accessed=400 * 2**20,
            transcendentals=heads * length * length,
        ),
    )(qkv, qkv, qkv, cosine, sine, gains, own, key_blocks, select, grad, w_out)


def on_device(
    inputs,
    block_ids,
    expert_ids,
    drop_order,
    attn_gain,
    w_query,
    key_projection_weight,
    value_projection_weight,
    q_gain,
    key_norm_gain,
    w_out,
    ffn_gain,
    w_router,
    expert_gate,
    expert_up,
    expert_down,
    cotangent,
):
    n_ctx, n_fsdp = lax.axis_size("ctx"), lax.axis_size("fsdp")
    ctx = lax.axis_index("ctx")
    span, width = inputs.shape[1], inputs.shape[2]
    length = block_ids.shape[1]
    experts = n_ctx * n_fsdp
    capacity = 5 * span * TOP // (4 * experts)
    slots = experts * capacity
    heads = QUERY_HEADS // n_ctx
    share = n_ctx // KEY_VALUE_HEADS
    own_rows = w_query.shape[0]
    q_width = heads * HEAD_SIZE
    qkv_width = q_width + 2 * HEAD_SIZE
    extra_width = -(-(experts + 4) // 128) * 128

    def gather_ctx(array):
        return lax.all_gather(array, "ctx", axis=0, tiled=True)

    def scatter_ctx(array):
        return lax.psum_scatter(array.astype(BF), "ctx", scatter_dimension=0, tiled=True)

    def route(rows):
        return lax.all_to_all(rows, "fsdp", split_axis=0, concat_axis=0, tiled=True)

    def columns(weight, index, count):
        return lax.dynamic_slice_in_dim(weight, index * count, count, axis=1)

    def as_column(vector):
        return jnp.pad(vector, (0, own_rows - vector.shape[0]))[:, None]

    packed = jnp.concatenate(
        [
            columns(w_query, ctx, q_width),
            columns(key_projection_weight, ctx // share, HEAD_SIZE),
            columns(value_projection_weight, ctx // share, HEAD_SIZE),
            w_router,
            as_column(attn_gain),
            as_column(ffn_gain),
            as_column(q_gain),
            as_column(key_norm_gain),
            jnp.zeros((own_rows, extra_width - experts - 4), BF),
        ],
        axis=1,
    )
    table = jnp.concatenate(
        [expert_ids[0].T, drop_order[0], jnp.zeros((7, span), jnp.int32)], axis=0
    )
    inputs_all, tables, packed_all = run_first_gather(n_ctx, n_fsdp, inputs[0], table, packed)
    out_all = lax.all_gather(w_out, "fsdp", axis=0, tiled=True)
    out_here = lax.dynamic_slice_in_dim(out_all, ctx * q_width, q_width, axis=0)
    inputs_all = inputs_all.reshape(length, width)
    packed_all = packed_all.reshape(width, qkv_width + extra_width)
    w_qkv = packed_all[:, :qkv_width]
    extra = packed_all[:, qkv_width:].T
    router_t = extra[:experts]
    gain_attn = extra[experts : experts + 1].astype(F32)
    gain_ffn = extra[experts + 1 : experts + 2].astype(F32)

    def head_gain(at):
        return extra[at].reshape(n_fsdp, own_rows)[:, : HEAD_SIZE // n_fsdp].reshape(1, HEAD_SIZE)

    gains = jnp.concatenate(
        [head_gain(experts + 2), head_gain(experts + 3), jnp.zeros((6, HEAD_SIZE), BF)], axis=0
    ).astype(F32)

    named = tables[:, :TOP, :]
    ranks = tables[:, TOP, :]
    here = ctx * n_fsdp + jnp.arange(n_fsdp, dtype=jnp.int32)
    member = jnp.any(named[:, :, None, :] == here[None, None, :, None], axis=1)
    before = (ranks[:, :, None] < ranks[:, None, :]).astype(BF)
    place = jnp.einsum(
        "gjs,gst->gjt", member.astype(BF), before, preferred_element_type=F32
    ).astype(jnp.int32)
    place = jnp.where(member, place, capacity)
    select = (
        place[:, :, None, :] == jnp.arange(capacity, dtype=jnp.int32)[None, None, :, None]
    ).astype(BF)

    fused = capacity % 16 == 0 and 2 * experts <= AUX and experts == QUERY_HEADS
    select_rows = select.reshape(n_ctx, n_fsdp * capacity, span)

    def dispatch(rows):
        picked = jnp.einsum(
            "gjkt,gtd->jgkd", select, rows.reshape(n_ctx, span, width), preferred_element_type=F32
        ).astype(BF)
        return route(picked).reshape(slots, width)

    def combine(rows):
        return gather_slots(route(rows.reshape(n_fsdp, n_ctx, capacity, width)))

    def gather_slots(back):
        return jnp.einsum("gjkt,jgkd->gtd", select, back, preferred_element_type=F32).reshape(
            length, width
        )

    x_all = inputs_all.astype(F32)
    r_all = inverse_rms(x_all)
    hidden = (x_all * r_all * gain_attn).astype(BF)
    qkv = nn(hidden, w_qkv)
    exponent = np.arange(HALF, dtype=np.float32) * np.float32(2.0 / HEAD_SIZE)
    angles = np.arange(length, dtype=np.float32)[:, None] * (
        np.float32(ROPE_BASE) ** (-exponent)
    )
    cosine = jnp.asarray(np.tile(np.cos(angles), (1, 2)))
    sine = jnp.asarray(np.concatenate([-np.sin(angles), np.sin(angles)], axis=1))
    own_blocks = jnp.broadcast_to(block_ids, (8, length))
    key_blocks = block_ids.reshape(length, 1)
    piece = QUERY_HEADS * HEAD_SIZE // experts
    groups = n_fsdp // n_ctx
    if fused:
        totals, dealt, attn_out, grad_rows = run_attention_exchange(
            qkv,
            heads,
            n_ctx,
            n_fsdp,
            cosine,
            sine,
            gains,
            own_blocks,
            key_blocks,
            select_rows,
            cotangent[0],
            out_all,
        )
        grad_rows = grad_rows.reshape(slots, width)
    else:
        mixed, totals, _ = run_attention(
            qkv, heads, n_ctx, cosine, sine, gains, own_blocks, key_blocks
        )
        attn_out = scatter_ctx(nn(mixed, out_here))
        grad_rows = dispatch(gather_ctx(cotangent[0]))
        dealt = mixed.reshape(length, groups, n_ctx, piece).transpose(2, 0, 1, 3)
        dealt = dealt.reshape(n_ctx, length, groups * piece)

    x = inputs[0].astype(F32)
    resid = x + attn_out.astype(F32)
    r_ffn = inverse_rms(resid)
    normed = (resid * r_ffn * gain_ffn).astype(BF)
    if fused:
        chosen = jnp.any(
            expert_ids[0][:, :, None] == jnp.arange(experts, dtype=jnp.int32), axis=1
        )
        logits = nt(normed, router_t)
        gates = jax.nn.softmax(jnp.where(chosen, logits, -jnp.inf), axis=-1)
        high = lax.reduce_precision(gates, 8, 7)
        payload = jnp.concatenate(
            [
                normed,
                high.astype(BF),
                (gates - high).astype(BF),
                jnp.zeros((span, AUX - 2 * experts), BF),
            ],
            axis=1,
        )
        rows, _, parts, inner_low, dg, du, y, dealt = run_expert_exchange(
            n_ctx,
            n_fsdp,
            payload,
            select_rows,
            select_rows.swapaxes(1, 2),
            expert_gate[0],
            expert_up[0],
            expert_down[0],
            grad_rows.reshape(n_fsdp, n_ctx, capacity, width),
            dealt,
        )
        rows = rows.reshape(slots, width + AUX)[:, :width]
        inner_low, dg, du = (array.reshape(slots, -1) for array in (inner_low, dg, du))
        y = y.reshape(slots, width)
        parts = jnp.sum(parts.astype(F32), axis=0)
        d_gates = parts[:, width : width + experts] + parts[:, width + experts : width + 2 * experts]
        d_logits = gates * (d_gates - jnp.sum(gates * d_gates, axis=-1, keepdims=True))
        d_logits = d_logits.astype(BF)
        d_normed = parts[:, :width] + nn(d_logits, router_t)
    else:
        dealt = lax.all_to_all(dealt, "ctx", split_axis=0, concat_axis=0, tiled=True)
        chosen = jnp.any(
            named[:, :, :, None] == jnp.arange(experts, dtype=jnp.int32), axis=1
        ).reshape(length, experts)
        normed = gather_ctx(normed)
        normed, grad_rows = lax.optimization_barrier((normed, grad_rows))
        grad_inner = nt(grad_rows, expert_down[0])
        logits = nt(normed, router_t)
        gates = jax.nn.softmax(jnp.where(chosen, logits, -jnp.inf), axis=-1)
        gates_here = lax.dynamic_slice_in_dim(gates, ctx * n_fsdp, n_fsdp, axis=1)
        gates_here = gates_here.reshape(n_ctx, span, n_fsdp).transpose(0, 2, 1)
        slot_gates = jnp.sum(select.astype(F32) * gates_here[:, :, None, :], axis=-1)
        slot_gates = route(slot_gates.transpose(1, 0, 2)).reshape(slots, 1)
        rows = dispatch(normed)
        g = nn(rows, expert_gate[0])
        u = nn(rows, expert_up[0])
        s = jax.nn.sigmoid(g)
        inner = g * s * u
        slot_dgates = jnp.sum(inner * grad_inner, axis=-1).reshape(n_fsdp, n_ctx, capacity)
        d_inner = grad_inner * slot_gates
        dg = (d_inner * u * s * (1.0 + g * (1.0 - s))).astype(BF)
        du = (d_inner * g * s).astype(BF)
        d_rows = (nt(dg, expert_gate[0]) + nt(du, expert_up[0])).astype(BF)
        y = (nn(inner.astype(BF), expert_down[0]) * slot_gates).astype(BF)
        inner_low = (inner * slot_gates).astype(BF)
        d_gates = jnp.einsum(
            "gjkt,jgk->gjt", select.astype(F32), route(slot_dgates), precision=lax.Precision.HIGHEST
        )
        weighted = (d_gates * gates_here).transpose(0, 2, 1).reshape(length, n_fsdp)
        d_logits = lax.dynamic_update_slice_in_dim(
            jnp.zeros((length, experts), F32), weighted, ctx * n_fsdp, axis=1
        ) - gates * jnp.sum(weighted, axis=1, keepdims=True)
        d_logits = d_logits.astype(BF)
        d_normed = scatter_ctx(combine(d_rows) + nn(d_logits, router_t)).astype(F32)

    gate_grad = tn(rows, dg)
    up_grad = tn(rows, du)
    down_grad = tn(inner_low, grad_rows)
    router_grad = tn(normed, d_logits)

    grad = cotangent[0].astype(F32)
    n = d_normed * gain_ffn
    d_resid = grad + r_ffn * n - resid * r_ffn**3 * jnp.mean(n * resid, axis=-1, keepdims=True)
    ffn_gain_grad = jnp.sum(d_normed * resid * r_ffn, axis=0)
    d_attn = gather_ctx(d_resid.astype(BF))
    y_back = route(y.reshape(n_fsdp, n_ctx, capacity, width))
    y_back, gate_grad, up_grad, down_grad = lax.optimization_barrier(
        (y_back, gate_grad, up_grad, down_grad)
    )
    y_all = gather_slots(y_back).astype(BF)
    d_attn, y_all = lax.optimization_barrier((d_attn, y_all))

    d_mixed = nt(d_attn, out_here).astype(BF)
    moe = scatter_ctx(y_all).astype(F32)
    out_grad = jnp.einsum("ntk,td->nkd", dealt, d_attn, preferred_element_type=F32).astype(BF)

    dq, dkv, dgains = run_attention_back(
        qkv, d_mixed, totals, heads, cosine, sine, gains, own_blocks, key_blocks
    )
    d_qkv = jnp.concatenate([dq, dkv], axis=1)
    d_hidden = nt(d_qkv, w_qkv)
    attn_gain_grad = jnp.sum(d_hidden * x_all * r_all, axis=0)

    def spread(vector):
        parts = vector.reshape(n_fsdp, HEAD_SIZE // n_fsdp)
        return jnp.pad(parts, ((0, 0), (0, own_rows - parts.shape[1]))).reshape(width)

    small = jnp.stack(
        [attn_gain_grad, ffn_gain_grad, spread(dgains[0]), spread(dgains[1])], axis=1
    )
    extra_grad = jnp.concatenate(
        [
            router_grad.astype(BF),
            small.astype(BF),
            jnp.zeros((width, extra_width - experts - 4), BF),
        ],
        axis=1,
    )
    shared_grad = tn(hidden, d_qkv).astype(BF)
    d_hidden, moe, shared_grad, out_grad = lax.optimization_barrier(
        (d_hidden.astype(BF), moe, shared_grad, out_grad)
    )
    d_hidden = scatter_ctx(d_hidden).astype(F32)
    shared_grad, rest, out_grad = run_last_reduce(
        n_ctx, n_fsdp, [shared_grad, extra_grad, out_grad.reshape(n_fsdp * piece, width)]
    )
    out_grad = out_grad.reshape(n_ctx * piece, width).astype(F32)
    rest = rest.astype(F32).sum(axis=0)
    output = (resid + moe).astype(BF)[None]
    r_attn = inverse_rms(x)
    n = d_hidden * gain_attn
    input_grad = d_resid + r_attn * n - x * r_attn**3 * jnp.mean(n * x, axis=-1, keepdims=True)
    input_grad = input_grad.astype(BF)[None]

    query_grad = run_widen_columns(shared_grad, q_width)

    def kv_grad(at):
        parts = shared_grad[:, :, at : at + HEAD_SIZE].astype(F32)
        parts = parts.reshape(KEY_VALUE_HEADS, share, own_rows, HEAD_SIZE).sum(axis=1)
        return parts.transpose(1, 0, 2).reshape(own_rows, KEY_VALUE_HEADS * HEAD_SIZE)

    key_grad, value_grad = kv_grad(q_width), kv_grad(q_width + HEAD_SIZE)
    head_rows = HEAD_SIZE // n_fsdp
    return (
        output,
        input_grad,
        rest[:, experts],
        query_grad,
        key_grad,
        value_grad,
        rest[:head_rows, experts + 2],
        rest[:head_rows, experts + 3],
        out_grad,
        rest[:, experts + 1],
        rest[:, :experts],
        gate_grad[None],
        up_grad[None],
        down_grad[None],
    )


def solution(mesh):
    rows, tokens = P("fsdp", None), P("fsdp", "ctx", None)
    vector, expert = P("fsdp"), P(("ctx", "fsdp"), None, None)
    in_specs = (
        tokens,
        rows,
        tokens,
        tokens,
        vector,
        rows,
        rows,
        rows,
        vector,
        vector,
        rows,
        vector,
        rows,
        expert,
        expert,
        expert,
        tokens,
    )
    out_specs = (
        tokens,
        tokens,
        vector,
        rows,
        rows,
        rows,
        vector,
        vector,
        rows,
        vector,
        rows,
        expert,
        expert,
        expert,
    )
    return jax.shard_map(
        on_device, mesh=mesh, in_specs=in_specs, out_specs=out_specs, check_vma=False
    )
```

```python
import functools

import jax
import jax.numpy as jnp
import numpy as np
from jax import lax
from jax.experimental import pallas as pl
from jax.experimental.pallas import tpu as pltpu
from jax.sharding import PartitionSpec as P

QUERY_HEADS = 32
KEY_VALUE_HEADS = 4
HEAD_SIZE = 128
TOP = 8

EPSILON = 1e-06
ROPE_BASE = 1000000.0
MASKED = -1000000000.0
SCALE = HEAD_SIZE ** (-0.5)
HALF = HEAD_SIZE // 2
BF = jnp.bfloat16
F32 = jnp.float32


def nt(a, b):
    return lax.dot_general(a, b, (((1,), (1,)), ((), ())), preferred_element_type=F32)


def nn(a, b):
    return lax.dot_general(a, b, (((1,), (0,)), ((), ())), preferred_element_type=F32)


def tn(a, b):
    return lax.dot_general(a, b, (((0,), (0,)), ((), ())), preferred_element_type=F32)


def inverse_rms(values):
    return lax.rsqrt(jnp.mean(values * values, axis=-1, keepdims=True) + EPSILON)


def norm_rope(raw, gain, cosine, sine):
    z = raw * inverse_rms(raw) * gain
    return z * cosine + pltpu.roll(z, HALF, 1) * sine


def norm_rope_back(raw, gain, cosine, sine, grad):
    dz = grad * cosine - pltpu.roll(grad, HALF, 1) * sine
    r = inverse_rms(raw)
    n = dz * gain
    d_raw = r * n - raw * (r * r * r) * jnp.mean(n * raw, axis=-1, keepdims=True)
    return d_raw, jnp.sum(dz * raw * r, axis=0, keepdims=True)


def prepare_keys(k_ref, v_ref, cos_ref, sin_ref, gains_ref, keys, values_t):
    rotated = norm_rope(k_ref[...], gains_ref[1:2, :], cos_ref[...], sin_ref[...])
    keys[...] = rotated.astype(BF)
    values_t[...] = v_ref[...].T.astype(BF)


def attend_head(
    q_ref, cos_ref, sin_ref, gains_ref, own_ref, key_ref, total_ref, dealt_ref, keys, values_t, store
):
    queries = norm_rope(q_ref[...], gains_ref[0:1, :], cos_ref[...], sin_ref[...]).astype(BF)
    length = queries.shape[0]
    chunk = 256
    for start in range(0, length, chunk):
        scores = nt(keys[...], queries[start : start + chunk]) * SCALE
        seen = key_ref[...] <= own_ref[0:1, start : start + chunk]
        scores = jnp.where(seen, scores, MASKED)
        top = jnp.max(scores, axis=0, keepdims=True)
        weights = jnp.exp(scores - top)
        total = jnp.sum(weights, axis=0, keepdims=True)
        out = (nn(values_t[...], weights.astype(BF)) / total).T.astype(BF)
        store(start, chunk, out)
        dealt_ref[0, start : start + chunk, :] = out
        total_ref[0, :, start : start + chunk] = jnp.broadcast_to(top + jnp.log(total), (8, chunk))


def attention_forward(
    q_ref,
    k_ref,
    v_ref,
    cos_ref,
    sin_ref,
    gains_ref,
    own_ref,
    key_ref,
    mixed_ref,
    total_ref,
    dealt_ref,
    keys,
    values_t,
):
    @pl.when(pl.program_id(0) == 0)
    def _():
        prepare_keys(k_ref, v_ref, cos_ref, sin_ref, gains_ref, keys, values_t)

    def store(start, count, out):
        mixed_ref[start : start + count, :] = out

    attend_head(
        q_ref, cos_ref, sin_ref, gains_ref, own_ref, key_ref, total_ref, dealt_ref, keys, values_t, store
    )


def attention_backward(
    heads,
    q_ref,
    k_ref,
    v_ref,
    grad_ref,
    total_ref,
    cos_ref,
    sin_ref,
    gains_ref,
    own_ref,
    key_ref,
    dq_ref,
    dkv_ref,
    dgain_ref,
    keys,
    keys_t,
    values,
    dk,
    dv,
):
    cosine, sine = cos_ref[...], sin_ref[...]
    head = pl.program_id(0)

    @pl.when(head == 0)
    def _():
        rotated = norm_rope(k_ref[...], gains_ref[1:2, :], cosine, sine)
        keys[...] = rotated.astype(BF)
        keys_t[...] = rotated.T.astype(BF)
        values[...] = v_ref[...].astype(BF)
        dk[...] = jnp.zeros_like(dk)
        dv[...] = jnp.zeros_like(dv)
        dgain_ref[...] = jnp.zeros_like(dgain_ref)

    queries = norm_rope(q_ref[...], gains_ref[0:1, :], cosine, sine).astype(BF)
    length = queries.shape[0]
    chunk = 256
    for start in range(0, length, chunk):
        rows = slice(start, start + chunk)
        q_part = queries[rows]
        grad = grad_ref[rows, :]
        scores = nt(keys[...], q_part) * SCALE
        seen = key_ref[...] <= own_ref[0:1, rows]
        scores = jnp.where(seen, scores, MASKED)
        weights = jnp.exp(scores - total_ref[0, 0:1, rows])
        d_weights = nt(values[...], grad)
        row_dot = jnp.sum(weights * d_weights, axis=0, keepdims=True)
        d_scores = (weights * (d_weights - row_dot)).astype(BF)
        dv[...] += nn(weights.astype(BF), grad)
        dk[...] += nn(d_scores, q_part)
        d_queries = nn(keys_t[...], d_scores).T * SCALE
        d_raw, d_gain = norm_rope_back(
            q_ref[rows, :], gains_ref[0:1, :], cos_ref[rows, :], sin_ref[rows, :], d_queries
        )
        dq_ref[rows, :] = d_raw.astype(BF)
        dgain_ref[0:1, :] += d_gain

    @pl.when(head == heads - 1)
    def _():
        d_raw, d_gain = norm_rope_back(
            k_ref[...], gains_ref[1:2, :], cosine, sine, dk[...] * SCALE
        )
        dkv_ref[:, :HEAD_SIZE] = d_raw.astype(BF)
        dkv_ref[:, HEAD_SIZE:] = dv[...].astype(BF)
        dgain_ref[1:2, :] = d_gain


def attention_specs(heads, length):
    whole = lambda shape: pl.BlockSpec(shape, lambda h: (0,) * len(shape))
    column = lambda at: pl.BlockSpec((length, HEAD_SIZE), lambda h: (0, at))
    head_column = pl.BlockSpec((length, HEAD_SIZE), lambda h: (0, h))
    totals = pl.BlockSpec((1, 8, length), lambda h: (h, 0, 0))
    shared = [
        whole((length, HEAD_SIZE)),
        whole((length, HEAD_SIZE)),
        whole((8, HEAD_SIZE)),
        whole((8, length)),
        whole((length, 1)),
    ]
    return whole, column, head_column, totals, shared


def run_attention(qkv, heads, n_ctx, cosine, sine, gains, own, key_blocks):
    length = qkv.shape[0]
    whole, column, head_column, totals, shared = attention_specs(heads, length)
    deals = min(n_ctx, heads)
    return pl.pallas_call(
        attention_forward,
        grid=(heads,),
        in_specs=[head_column, column(heads), column(heads + 1)] + shared,
        out_specs=[
            head_column,
            totals,
            pl.BlockSpec((1, length, HEAD_SIZE), lambda h: (h % deals, 0, h // deals)),
        ],
        out_shape=[
            jax.ShapeDtypeStruct((length, heads * HEAD_SIZE), BF),
            jax.ShapeDtypeStruct((heads, 8, length), F32),
            jax.ShapeDtypeStruct((deals, length, heads // deals * HEAD_SIZE), BF),
        ],
        scratch_shapes=[
            pltpu.VMEM((length, HEAD_SIZE), BF),
            pltpu.VMEM((HEAD_SIZE, length), BF),
        ],
        compiler_params=pltpu.CompilerParams(vmem_limit_bytes=48 * 2**20),
        cost_estimate=pl.CostEstimate(
            flops=4 * heads * length * length * HEAD_SIZE,
            bytes_accessed=8 * heads * length * HEAD_SIZE,
            transcendentals=heads * length * length,
        ),
    )(qkv, qkv, qkv, cosine, sine, gains, own, key_blocks)


def run_attention_back(qkv, grad, totals_in, heads, cosine, sine, gains, own, key_blocks):
    length = qkv.shape[0]
    whole, column, head_column, totals, shared = attention_specs(heads, length)
    return pl.pallas_call(
        functools.partial(attention_backward, heads),
        grid=(heads,),
        in_specs=[head_column, column(heads), column(heads + 1), head_column, totals] + shared,
        out_specs=[head_column, whole((length, 2 * HEAD_SIZE)), whole((8, HEAD_SIZE))],
        out_shape=[
            jax.ShapeDtypeStruct((length, heads * HEAD_SIZE), BF),
            jax.ShapeDtypeStruct((length, 2 * HEAD_SIZE), BF),
            jax.ShapeDtypeStruct((8, HEAD_SIZE), F32),
        ],
        scratch_shapes=[
            pltpu.VMEM((length, HEAD_SIZE), BF),
            pltpu.VMEM((HEAD_SIZE, length), BF),
            pltpu.VMEM((length, HEAD_SIZE), BF),
            pltpu.VMEM((length, HEAD_SIZE), F32),
            pltpu.VMEM((length, HEAD_SIZE), F32),
        ],
        compiler_params=pltpu.CompilerParams(vmem_limit_bytes=48 * 2**20),
        cost_estimate=pl.CostEstimate(
            flops=10 * heads * length * length * HEAD_SIZE,
            bytes_accessed=10 * heads * length * HEAD_SIZE,
            transcendentals=heads * length * length,
        ),
    )(qkv, qkv, qkv, grad, totals_in, cosine, sine, gains, own, key_blocks)


def push(source, target, sends, recvs, device):
    copy = pltpu.make_async_remote_copy(
        src_ref=source,
        dst_ref=target,
        send_sem=sends,
        recv_sem=recvs,
        device_id=device,
        device_id_type=pl.DeviceIdType.MESH,
    )
    return copy


def greet(devices):
    barrier = pltpu.get_barrier_semaphore()
    for device in devices:
        pl.semaphore_signal(barrier, 1, device_id=device, device_id_type=pl.DeviceIdType.MESH)
    pl.semaphore_wait(barrier, len(devices))


class LineGather:
    def __init__(self, n_ctx, ctx, fsdp, own_ref, all_ref, up, down, arrived):
        self.n_ctx, self.ctx, self.fsdp = n_ctx, ctx, fsdp
        self.own_ref, self.all_ref = own_ref, all_ref
        self.up, self.down, self.arrived = up, down, arrived

    def copy(self, source, block, sems, step, to):
        return push(
            source, self.all_ref.at[block], sems.at[step], self.arrived.at[block], (to, self.fsdp)
        )

    def going_up(self, step):
        return (self.ctx - step >= 0) & (self.ctx < self.n_ctx - 1)

    def going_down(self, step):
        return (self.ctx + step < self.n_ctx) & (self.ctx > 0)

    def step(self, step):
        def hop(block, sems, to, more):
            if step > 0:
                self.copy(self.own_ref, block, sems, 0, to).wait_recv()

            @pl.when(more)
            def _():
                source = self.all_ref.at[block] if step > 0 else self.own_ref
                self.copy(source, block, sems, step, to).start()

        @pl.when(self.ctx - step >= 0)
        def _():
            hop(self.ctx - step, self.up, self.ctx + 1, self.ctx < self.n_ctx - 1)

        @pl.when(self.ctx + step < self.n_ctx)
        def _():
            hop(self.ctx + step, self.down, self.ctx - 1, self.ctx > 0)

    def finish(self):
        for step in range(self.n_ctx - 1):

            @pl.when(self.going_up(step))
            def _():
                self.copy(self.own_ref, 0, self.up, step, self.ctx).wait_send()

            @pl.when(self.going_down(step))
            def _():
                self.copy(self.own_ref, 0, self.down, step, self.ctx).wait_send()


class LineScatter:
    def __init__(self, n_ctx, ctx, fsdp, chunks, held, low, high, up, down, low_in, high_in):
        self.n_ctx, self.ctx, self.fsdp, self.chunks = n_ctx, ctx, fsdp, chunks
        self.held, self.low, self.high = held, low, high
        self.sems = {"up": (low, up, low_in), "down": (high, down, high_in)}
        self.size = held.shape[1] // chunks

    def copy(self, way, block, chunk, to):
        landing, sends, arrived = self.sems[way]
        rows = pl.ds(chunk * self.size, self.size)
        return push(
            self.held.at[block, rows],
            landing.at[block, rows],
            sends.at[block, chunk],
            arrived.at[block, chunk],
            (to, self.fsdp),
        )

    def scatter(self, chunk):
        rows = slice(chunk * self.size, (chunk + 1) * self.size)
        ctx, held = self.ctx, self.held

        def pass_on(way, block, to, first):
            @pl.when(jnp.logical_not(first))
            def _():
                self.copy(way, block, chunk, ctx).wait_recv()
                held[block, rows, :] = (
                    held[block, rows, :].astype(F32)
                    + self.sems[way][0][block, rows, :].astype(F32)
                ).astype(BF)

            self.copy(way, block, chunk, to).start()

        for step in range(self.n_ctx - 1):

            @pl.when(ctx < self.n_ctx - 1 - step)
            def _():
                pass_on("up", self.n_ctx - 1 - step, ctx + 1, ctx == 0)

            @pl.when(ctx > step)
            def _():
                pass_on("down", step, ctx - 1, ctx == self.n_ctx - 1)

    def settle(self, chunk, total_ref):
        rows = slice(chunk * self.size, (chunk + 1) * self.size)
        total_ref[rows, :] = self.held[self.ctx, rows, :].astype(F32)

        @pl.when(self.ctx > 0)
        def _():
            self.copy("up", self.ctx, chunk, self.ctx).wait_recv()
            total_ref[rows, :] += self.low[self.ctx, rows, :].astype(F32)

        @pl.when(self.ctx < self.n_ctx - 1)
        def _():
            self.copy("down", self.ctx, chunk, self.ctx).wait_recv()
            total_ref[rows, :] += self.high[self.ctx, rows, :].astype(F32)

    def finish(self):
        for chunk in range(self.chunks):
            for step in range(self.n_ctx - 1):

                @pl.when(self.ctx < self.n_ctx - 1 - step)
                def _():
                    self.copy("up", self.n_ctx - 1 - step, chunk, self.ctx).wait_send()

                @pl.when(self.ctx > step)
                def _():
                    self.copy("down", step, chunk, self.ctx).wait_send()


def first_gather(
    n_ctx,
    n_fsdp,
    x_ref,
    table_ref,
    packed_ref,
    x_all,
    table_all,
    packed_all,
    local,
    up,
    down,
    arrived,
    table_send,
    table_arrived,
    packed_send,
    passed_send,
    packed_arrived,
):
    ctx, fsdp = lax.axis_index("ctx"), lax.axis_index("fsdp")
    sibling = lax.rem(fsdp + 1, 2) + (fsdp // 2) * 2
    chips = n_fsdp // 2

    def same_core(offset):
        return lax.rem(fsdp + 2 * offset, n_fsdp)

    def along(offset):
        return lax.rem(ctx + offset, n_ctx)

    greet(
        [(along(i), fsdp) for i in range(1, n_ctx)]
        + [(ctx, same_core(i)) for i in range(1, chips)]
        + [(ctx, sibling)]
    )
    kept = [
        pltpu.make_async_copy(x_ref, x_all.at[ctx], local.at[0]),
        pltpu.make_async_copy(table_ref, table_all.at[ctx], local.at[1]),
        pltpu.make_async_copy(packed_ref, packed_all.at[fsdp], local.at[2]),
    ]
    for copy in kept:
        copy.start()

    def packed_copy(source, owner, sems, to):
        return push(source, packed_all.at[owner], sems, packed_arrived.at[owner], (ctx, to))

    for i in range(1, chips):
        packed_copy(packed_ref, fsdp, packed_send.at[i], same_core(i)).start()
    packed_copy(packed_ref, fsdp, packed_send.at[0], sibling).start()
    for i in range(1, n_ctx):
        push(
            table_ref, table_all.at[ctx], table_send.at[i], table_arrived.at[ctx], (along(i), fsdp)
        ).start()
    line = LineGather(n_ctx, ctx, fsdp, x_ref, x_all, up, down, arrived)
    for step in range(n_ctx):
        line.step(step)
    for i in range(1, chips):
        owner = same_core(chips - i)
        packed_copy(packed_ref, owner, packed_send.at[i], sibling).wait_recv()
        packed_copy(packed_all.at[owner], owner, passed_send.at[i], sibling).start()
    for i in range(chips):
        owner = lax.rem(sibling + 2 * i, n_fsdp)
        packed_copy(packed_ref, owner, packed_send.at[0], sibling).wait_recv()
    for i in range(1, n_ctx):
        owner = along(i)
        push(
            table_ref, table_all.at[owner], table_send.at[i], table_arrived.at[owner], (owner, fsdp)
        ).wait()
    line.finish()
    for i in range(chips):
        packed_copy(packed_ref, fsdp, packed_send.at[i], sibling).wait_send()
    for i in range(1, chips):
        packed_copy(packed_ref, fsdp, passed_send.at[i], sibling).wait_send()
    for copy in kept:
        copy.wait()


def run_first_gather(n_ctx, n_fsdp, x, table, packed):
    anywhere = pl.BlockSpec(memory_space=pl.ANY)
    dma = pltpu.SemaphoreType.DMA
    return pl.pallas_call(
        functools.partial(first_gather, n_ctx, n_fsdp),
        in_specs=[anywhere] * 3,
        out_specs=[anywhere] * 3,
        out_shape=[
            jax.ShapeDtypeStruct((n_ctx,) + x.shape, x.dtype),
            jax.ShapeDtypeStruct((n_ctx,) + table.shape, table.dtype),
            jax.ShapeDtypeStruct((n_fsdp,) + packed.shape, packed.dtype),
        ],
        scratch_shapes=[
            dma((3,)),
            dma((n_ctx,)),
            dma((n_ctx,)),
            dma((n_ctx,)),
            dma((n_ctx,)),
            dma((n_ctx,)),
            dma((n_fsdp // 2,)),
            dma((n_fsdp // 2,)),
            dma((n_fsdp,)),
        ],
        compiler_params=pltpu.CompilerParams(collective_id=1, has_side_effects=True),
        cost_estimate=pl.CostEstimate(
            flops=0, bytes_accessed=200 * 2**20, transcendentals=0
        ),
    )(x, table, packed)


TILE = 512
AUX = 128


def expert_exchange(
    n_ctx,
    n_fsdp,
    x_ref,
    sel_ref,
    selt_ref,
    gate_ref,
    up_ref,
    down_ref,
    grad_ref,
    dealt_ref,
    rows_ref,
    back_ref,
    part_ref,
    inner_ref,
    dg_ref,
    du_ref,
    y_ref,
    dealt_all,
    w_gate,
    w_up,
    w_down,
    held,
    staged,
    rows_in,
    grad_in,
    inner_out,
    dg_out,
    du_out,
    y_out,
    back_in,
    w_sems,
    local,
    held_send,
    held_arrived,
    rows_send,
    rows_arrived,
    back_send,
    back_arrived,
    part_send,
    part_arrived,
    dealt_send,
    dealt_arrived,
    out_sems,
):
    ctx, fsdp = lax.axis_index("ctx"), lax.axis_index("fsdp")
    experts = n_ctx * n_fsdp
    expert = ctx * n_fsdp + fsdp
    width, hidden = w_gate.shape
    wide = held.shape[2]
    capacity = staged.shape[2]
    half = n_fsdp // 2
    tiles = [(at, min(TILE, wide - at)) for at in range(0, wide, TILE)]

    def along(offset):
        return lax.rem(ctx + offset, n_ctx)

    def around(offset):
        return lax.rem(fsdp + offset, n_fsdp)

    greet(
        [(along(i), fsdp) for i in range(1, n_ctx)] + [(ctx, around(i)) for i in range(1, n_fsdp)]
    )
    weights = [
        pltpu.make_async_copy(gate_ref, w_gate, w_sems.at[0]),
        pltpu.make_async_copy(up_ref, w_up, w_sems.at[1]),
        pltpu.make_async_copy(down_ref, w_down, w_sems.at[2]),
    ]
    own = pltpu.make_async_copy(x_ref, held.at[ctx], local.at[0])
    own.start()
    for copy in weights:
        copy.start()

    def held_copy(step):
        to = lax.rem(ctx + n_ctx - step, n_ctx)
        return push(x_ref, held.at[ctx], held_send.at[step], held_arrived.at[ctx], (to, fsdp))

    def rows_copy(step, group, offset):
        to = around(offset)
        return push(
            staged.at[step, to],
            rows_ref.at[fsdp, group],
            rows_send.at[step, offset],
            rows_arrived.at[group, fsdp],
            (ctx, to),
        )

    def rows_kept(step, group):
        return pltpu.make_async_copy(
            staged.at[step, fsdp], rows_ref.at[fsdp, group], rows_arrived.at[group, fsdp]
        )

    def back_copy(step, group, offset):
        to = around(offset)
        return push(
            staged.at[step, to],
            back_ref.at[group, fsdp],
            back_send.at[step, offset],
            back_arrived.at[group, fsdp],
            (ctx, to),
        )

    def back_kept(step, group):
        return pltpu.make_async_copy(
            staged.at[step, fsdp], back_ref.at[group, fsdp], back_arrived.at[group, fsdp]
        )

    def outputs(group):
        return [
            pltpu.make_async_copy(inner_out, inner_ref.at[:, group], out_sems.at[0]),
            pltpu.make_async_copy(dg_out, dg_ref.at[:, group], out_sems.at[1]),
            pltpu.make_async_copy(du_out, du_ref.at[:, group], out_sems.at[2]),
            pltpu.make_async_copy(y_out, y_ref.at[:, group], out_sems.at[3]),
        ]

    def dispatch(step):
        group = along(step)

        @pl.when(step == 0)
        def _():
            own.wait()

        @pl.when(step > 0)
        def _():
            push(
                x_ref, held.at[group], held_send.at[step], held_arrived.at[group], (group, fsdp)
            ).wait_recv()

        @pl.when(step + 1 < n_ctx)
        def _():
            held_copy(step + 1).start()

        for at, size in tiles:
            picked = nn(sel_ref[group], held[group, :, at : at + size])
            staged[step, :, :, at : at + size] = picked.astype(BF).reshape(n_fsdp, capacity, size)
        rows_kept(step, group).start()
        for offset in range(1, n_fsdp):
            rows_copy(step, group, offset).start()

    def compute(step):
        group = along(step)
        rows_kept(step, group).wait()
        for offset in range(1, n_fsdp):
            source = around(offset)
            push(
                staged.at[step, source],
                rows_ref.at[source, group],
                rows_send.at[step, offset],
                rows_arrived.at[group, source],
                (ctx, source),
            ).wait_recv()
        load_rows = pltpu.make_async_copy(rows_ref.at[:, group], rows_in, local.at[1])
        load_inner = pltpu.make_async_copy(grad_ref.at[:, group], grad_in, local.at[2])
        load_rows.start()
        load_inner.start()

        @pl.when(step == 0)
        def _():
            for copy in weights:
                copy.wait()

        @pl.when(step > 0)
        def _():
            for copy in outputs(group):
                copy.wait()

        for offset in range(1, n_fsdp):
            rows_copy(step, group, offset).wait_send()
        load_rows.wait()
        load_inner.wait()
        count = half * capacity
        lane = lax.broadcasted_iota(jnp.int32, (count, AUX), 1)
        high, low = lane == expert, lane == experts + expert

        @pl.loop(0, 2)
        def _(part):
            sources = pl.ds(part * half, half)
            rows = rows_in[sources, :, :width].reshape(count, width)
            aux = rows_in[sources, :, width:].reshape(count, AUX).astype(F32)
            gate = jnp.sum(jnp.where(high | low, aux, 0.0), axis=1, keepdims=True)
            g = nn(rows, w_gate[...])
            u = nn(rows, w_up[...])
            s = jax.nn.sigmoid(g)
            inner = g * s * u
            d_inner = nt(grad_in[sources].reshape(count, width), w_down[...])
            d_gate = jnp.sum(inner * d_inner, axis=1, keepdims=True)
            d_inner = d_inner * gate
            dg = (d_inner * u * s * (1.0 + g * (1.0 - s))).astype(BF)
            du = (d_inner * g * s).astype(BF)
            inner_out[sources] = (inner * gate).astype(BF).reshape(half, capacity, hidden)
            dg_out[sources] = dg.reshape(half, capacity, hidden)
            du_out[sources] = du.reshape(half, capacity, hidden)
            rest = d_gate - d_gate.astype(BF).astype(F32)
            staged[step, sources, :, width:] = (
                jnp.where(high, d_gate, jnp.where(low, rest, 0.0))
                .astype(BF)
                .reshape(half, capacity, AUX)
            )
            for at in range(0, width, TILE):
                grad = nt(dg, w_gate[at : at + TILE, :]) + nt(du, w_up[at : at + TILE, :])
                staged[step, sources, :, at : at + TILE] = grad.astype(BF).reshape(
                    half, capacity, TILE
                )
            low_inner = inner.astype(BF)
            for at in range(0, width, TILE):
                y = nn(low_inner, w_down[:, at : at + TILE]) * gate
                y_out[sources, :, at : at + TILE] = y.astype(BF).reshape(half, capacity, TILE)

        def send_back(step, group):
            back_kept(step, group).start()
            for offset in range(1, n_fsdp):
                back_copy(step, group, offset).start()

        @pl.when(step > 0)
        def _():
            send_back(step, group)

        @pl.when(step == n_ctx - 1)
        def _():
            send_back(0, ctx)

        for copy in outputs(group):
            copy.start()

    def combine(step):
        group = along(step)
        back_kept(step, group).wait()
        for offset in range(1, n_fsdp):
            source = around(offset)
            push(
                staged.at[step, source],
                back_ref.at[group, source],
                back_send.at[step, offset],
                back_arrived.at[group, source],
                (ctx, source),
            ).wait_recv()
        load = pltpu.make_async_copy(back_ref.at[group], back_in, local.at[1])
        load.start()
        load.wait()
        for at, size in tiles:
            back = back_in[:, :, at : at + size].reshape(n_fsdp * capacity, size)
            held[group, :, at : at + size] = nn(selt_ref[group], back).astype(BF)

        @pl.when(step == 0)
        def _():
            pltpu.make_async_copy(
                held.at[group], part_ref.at[ctx], part_arrived.at[ctx]
            ).start()

        @pl.when(step > 0)
        def _():
            push(
                held.at[group],
                part_ref.at[ctx],
                part_send.at[step],
                part_arrived.at[ctx],
                (group, fsdp),
            ).start()

    def dealt_copy(offset):
        to = along(offset)
        return push(
            dealt_ref.at[to],
            dealt_all.at[ctx],
            dealt_send.at[offset],
            dealt_arrived.at[ctx],
            (to, fsdp),
        )

    dealt_kept = pltpu.make_async_copy(
        dealt_ref.at[ctx], dealt_all.at[ctx], dealt_arrived.at[ctx]
    )

    @pl.loop(0, n_ctx + 3)
    def _(tick):
        @pl.when(tick < n_ctx)
        def _():
            dispatch(tick)

        @pl.when(tick == n_ctx - 1)
        def _():
            dealt_kept.start()
            for offset in range(1, n_ctx):
                dealt_copy(offset).start()

        @pl.when((tick >= 1) & (tick <= n_ctx))
        def _():
            compute(tick - 1)

        @pl.when(tick >= 3)
        def _():
            combine(lax.rem(tick - 2, n_ctx))

    pltpu.make_async_copy(held.at[ctx], part_ref.at[ctx], part_arrived.at[ctx]).wait()
    for step in range(1, n_ctx):
        other = along(step)
        copy = push(
            held.at[other], part_ref.at[other], part_send.at[step], part_arrived.at[other], (other, fsdp)
        )
        copy.wait()
        held_copy(step).wait_send()
    dealt_kept.wait()
    for offset in range(1, n_ctx):
        other = along(offset)
        push(
            dealt_ref.at[other],
            dealt_all.at[other],
            dealt_send.at[offset],
            dealt_arrived.at[other],
            (other, fsdp),
        ).wait()
    for step in range(n_ctx):
        for offset in range(1, n_fsdp):
            back_copy(step, along(step), offset).wait_send()
    for copy in outputs(along(n_ctx - 1)):
        copy.wait()


def run_expert_exchange(n_ctx, n_fsdp, x, select, select_t, gate, up, down, grads, dealt):
    anywhere, inside = pl.BlockSpec(memory_space=pl.ANY), pl.BlockSpec(memory_space=pltpu.VMEM)
    span, wide = x.shape
    width, hidden = gate.shape
    capacity = grads.shape[2]
    slots = (n_fsdp, n_ctx, capacity)
    one = (n_fsdp, capacity)
    dma, vmem, shape = pltpu.SemaphoreType.DMA, pltpu.VMEM, jax.ShapeDtypeStruct
    return pl.pallas_call(
        functools.partial(expert_exchange, n_ctx, n_fsdp),
        in_specs=[anywhere, inside, inside] + [anywhere] * 5,
        out_specs=[anywhere] * 8,
        out_shape=[
            shape(slots + (wide,), BF),
            shape((n_ctx, n_fsdp, capacity, wide), BF),
            shape((n_ctx, span, wide), BF),
            shape(slots + (hidden,), BF),
            shape(slots + (hidden,), BF),
            shape(slots + (hidden,), BF),
            shape(slots + (width,), BF),
            shape(dealt.shape, BF),
        ],
        scratch_shapes=[
            vmem((width, hidden), BF),
            vmem((width, hidden), BF),
            vmem((hidden, width), BF),
            vmem((n_ctx, span, wide), BF),
            vmem((n_ctx,) + one + (wide,), BF),
            vmem(one + (wide,), BF),
            vmem(one + (width,), BF),
            vmem(one + (hidden,), BF),
            vmem(one + (hidden,), BF),
            vmem(one + (hidden,), BF),
            vmem(one + (width,), BF),
            vmem(one + (wide,), BF),
            dma((3,)),
            dma((3,)),
            dma((n_ctx,)),
            dma((n_ctx,)),
            dma((n_ctx, n_fsdp)),
            dma((n_ctx, n_fsdp)),
            dma((n_ctx, n_fsdp)),
            dma((n_ctx, n_fsdp)),
            dma((n_ctx,)),
            dma((n_ctx,)),
            dma((n_ctx,)),
            dma((n_ctx,)),
            dma((4,)),
        ],
        compiler_params=pltpu.CompilerParams(
            collective_id=2, has_side_effects=True, vmem_limit_bytes=60 * 2**20
        ),
        cost_estimate=pl.CostEstimate(
            flops=12 * n_fsdp * n_ctx * capacity * width * hidden,
            bytes_accessed=600 * 2**20,
            transcendentals=0,
        ),
    )(x, select, select_t, gate, up, down, grads, dealt)


def last_reduce(n_ctx, n_fsdp, *refs):
    ctx, fsdp = lax.axis_index("ctx"), lax.axis_index("fsdp")
    count = (len(refs) - 1) // 11
    ins, alls, local, refs = refs[:count], refs[count : 2 * count], refs[2 * count], refs[2 * count + 1 :]
    items = [refs[9 * i : 9 * i + 9] for i in range(count)]
    chips, chip, core = n_fsdp // 2, fsdp // 2, lax.rem(fsdp, 2)
    sibling = chip * 2 + 1 - core

    def along(offset):
        return lax.rem(ctx + offset, n_ctx)

    def other_chip(offset):
        return lax.rem(chip + offset, chips)

    greet(
        [(along(i), fsdp) for i in range(1, n_ctx)]
        + [(ctx, other_chip(i) * 2 + core) for i in range(1, chips)]
        + [(ctx, sibling)]
    )
    crossing, loads, lines = [], [], []
    for at, (in_ref, all_ref, item) in enumerate(zip(ins, alls, items)):
        mine, beside, landed, own, cross, sends, arrived, line_sems, line_arrived = item
        crossing.append(
            push(in_ref.at[:, 1 - core], beside, cross.at[0], cross.at[1], (ctx, sibling))
        )
        crossing[-1].start()
        loads.append(pltpu.make_async_copy(in_ref.at[:, core], mine, local.at[at]))
        loads[-1].start()
        lines.append(
            LineGather(
                n_ctx, ctx, fsdp, own, all_ref, line_sems.at[0], line_sems.at[1], line_arrived
            )
        )

    def chip_copy(item, offset):
        mine, beside, landed, own, cross, sends, arrived, line_sems, line_arrived = item
        to = other_chip(offset)
        return push(
            mine.at[to], landed.at[chip], sends.at[offset], arrived.at[chip], (ctx, to * 2 + core)
        )

    for crossed, loaded, item in zip(crossing, loads, items):
        mine, beside = item[:2]
        loaded.wait()
        crossed.wait_recv()
        for offset in range(1, chips + 1):
            to = other_chip(offset)
            mine[to] = (mine[to].astype(F32) + beside[to].astype(F32)).astype(BF)
            if offset < chips:
                chip_copy(item, offset).start()
    keeps = []
    for at, (item, line, all_ref) in enumerate(zip(items, lines, alls)):
        mine, beside, landed, own, cross, sends, arrived, line_sems, line_arrived = item
        total = mine[chip].astype(F32)
        for offset in range(1, chips):
            source = other_chip(offset)
            push(
                mine.at[source], landed.at[source], sends.at[offset], arrived.at[source], (ctx, sibling)
            ).wait_recv()
            total = total + landed[source].astype(F32)
        own[...] = total.astype(BF)
        line.step(0)
        keeps.append(pltpu.make_async_copy(own, all_ref.at[ctx], local.at[at]))
        keeps[-1].start()
    for step in range(1, n_ctx):
        for line in lines:
            line.step(step)
    for crossed, keep, line, item in zip(crossing, keeps, lines, items):
        crossed.wait_send()
        keep.wait()
        line.finish()
        for offset in range(1, chips):
            chip_copy(item, offset).wait_send()


def run_last_reduce(n_ctx, n_fsdp, grads):
    anywhere = pl.BlockSpec(memory_space=pl.ANY)
    dma, vmem, shape = pltpu.SemaphoreType.DMA, pltpu.VMEM, jax.ShapeDtypeStruct
    chips = n_fsdp // 2
    grads = [grad.reshape((chips, 2, -1) + grad.shape[-1:]) for grad in grads]
    blocks = [grad.shape[2:] for grad in grads]
    scratch = [dma((len(grads),))]
    for block in blocks:
        scratch += [
            vmem((chips,) + block, BF),
            vmem((chips,) + block, BF),
            vmem((chips,) + block, BF),
            vmem(block, BF),
            dma((2,)),
            dma((chips,)),
            dma((chips,)),
            dma((2, n_ctx)),
            dma((n_ctx,)),
        ]
    return pl.pallas_call(
        functools.partial(last_reduce, n_ctx, n_fsdp),
        in_specs=[anywhere] * len(grads),
        out_specs=[anywhere] * len(grads),
        out_shape=[shape((n_ctx,) + block, BF) for block in blocks],
        scratch_shapes=scratch,
        compiler_params=pltpu.CompilerParams(
            collective_id=3, has_side_effects=True, vmem_limit_bytes=60 * 2**20
        ),
        cost_estimate=pl.CostEstimate(flops=0, bytes_accessed=400 * 2**20, transcendentals=0),
    )(*grads)


def finish(
    n_ctx,
    share,
    experts,
    shared_ref,
    rest_ref,
    out_ref,
    dh_ref,
    x_ref,
    resid_grad_ref,
    resid_ref,
    moe_ref,
    gain_ref,
    query_ref,
    key_ref,
    value_ref,
    out_grad_ref,
    input_grad_ref,
    output_ref,
    router_ref,
    gains_ref,
):
    q_width = shared_ref.shape[2] - 2 * HEAD_SIZE
    for block in range(n_ctx):
        query_ref[:, block * q_width : (block + 1) * q_width] = shared_ref[
            block, :, :q_width
        ].astype(F32)
    for target, at in ((key_ref, q_width), (value_ref, q_width + HEAD_SIZE)):
        for kv in range(KEY_VALUE_HEADS):
            total = shared_ref[kv * share, :, at : at + HEAD_SIZE].astype(F32)
            for block in range(kv * share + 1, (kv + 1) * share):
                total = total + shared_ref[block, :, at : at + HEAD_SIZE].astype(F32)
            target[:, kv * HEAD_SIZE : (kv + 1) * HEAD_SIZE] = total
    out_grad_ref[...] = out_ref[0].astype(F32)
    x = x_ref[...].astype(F32)
    r = inverse_rms(x)
    n = dh_ref[...].astype(F32) * gain_ref[...]
    input_grad_ref[...] = (
        resid_grad_ref[...] + r * n - x * (r * r * r) * jnp.mean(n * x, axis=-1, keepdims=True)
    ).astype(BF)
    output_ref[...] = (resid_ref[...] + moe_ref[...].astype(F32)).astype(BF)

    @pl.when(pl.program_id(0) == n_ctx - 1)
    def _():
        rest = rest_ref[0].astype(F32)
        for block in range(1, n_ctx):
            rest = rest + rest_ref[block].astype(F32)
        router_ref[...] = rest[:, :experts]
        gains_ref[...] = rest.T[experts : experts + 8]


def run_finish(
    n_ctx, experts, shared, rest, out_grad, d_hidden, x, resid_grad, resid, moe, gain
):
    _, rows, wide = shared.shape
    span, width = x.shape
    _, piece, _ = out_grad.shape
    shape = jax.ShapeDtypeStruct
    part, tokens = rows // n_ctx, span // n_ctx
    whole = lambda dims: pl.BlockSpec(dims, lambda i: (0,) * len(dims))
    by_rows = lambda count, columns: pl.BlockSpec((count, columns), lambda i: (i, 0))
    q_columns, kv_columns = QUERY_HEADS * HEAD_SIZE, KEY_VALUE_HEADS * HEAD_SIZE
    return pl.pallas_call(
        functools.partial(finish, n_ctx, n_ctx // KEY_VALUE_HEADS, experts),
        grid=(n_ctx,),
        in_specs=[
            pl.BlockSpec((n_ctx, part, wide), lambda i: (0, i, 0)),
            whole(rest.shape),
            pl.BlockSpec((1, piece, width), lambda i: (i, 0, 0)),
        ]
        + [by_rows(tokens, width)] * 5
        + [whole((1, width))],
        out_specs=[
            by_rows(part, q_columns),
            by_rows(part, kv_columns),
            by_rows(part, kv_columns),
            by_rows(piece, width),
            by_rows(tokens, width),
            by_rows(tokens, width),
            whole((rows, experts)),
            whole((8, rows)),
        ],
        out_shape=[
            shape((rows, q_columns), F32),
            shape((rows, kv_columns), F32),
            shape((rows, kv_columns), F32),
            shape((n_ctx * piece, width), F32),
            shape((span, width), BF),
            shape((span, width), BF),
            shape((rows, experts), F32),
            shape((8, rows), F32),
        ],
        compiler_params=pltpu.CompilerParams(vmem_limit_bytes=48 * 2**20),
    )(shared, rest, out_grad, d_hidden, x, resid_grad, resid, moe, gain)


def attention_exchange(
    n_ctx,
    n_fsdp,
    heads,
    q_ref,
    k_ref,
    v_ref,
    cos_ref,
    sin_ref,
    gains_ref,
    own_ref,
    key_ref,
    sel_ref,
    grad_ref,
    out_ref,
    total_ref,
    dealt_ref,
    attn_ref,
    rows_ref,
    keys,
    values_t,
    mixed,
    w_out,
    held,
    low,
    high,
    grads,
    staged,
    local,
    grad_up,
    grad_down,
    grad_arrived,
    rows_send,
    rows_arrived,
    up_send,
    down_send,
    low_arrived,
    high_arrived,
):
    head = pl.program_id(0)
    ctx, fsdp = lax.axis_index("ctx"), lax.axis_index("fsdp")
    _, span, width = held.shape
    capacity = staged.shape[2]
    q_width = heads * HEAD_SIZE

    def along(offset):
        return lax.rem(ctx + offset, n_ctx)

    def around(offset):
        return lax.rem(fsdp + offset, n_fsdp)

    line = LineGather(n_ctx, ctx, fsdp, grad_ref, grads, grad_up, grad_down, grad_arrived)
    sums = LineScatter(
        n_ctx, ctx, fsdp, 4, held, low, high, up_send, down_send, low_arrived, high_arrived
    )
    own = pltpu.make_async_copy(grad_ref, grads.at[ctx], local.at[0])
    weights = pltpu.make_async_copy(
        out_ref.at[pl.ds(ctx * q_width, q_width)], w_out, local.at[1]
    )

    def rows_copy(group, offset):
        to = around(offset)
        return push(
            staged.at[group, to],
            rows_ref.at[fsdp, group],
            rows_send.at[group, offset],
            rows_arrived.at[group, fsdp],
            (ctx, to),
        )

    def rows_kept(group):
        return pltpu.make_async_copy(
            staged.at[group, fsdp], rows_ref.at[fsdp, group], rows_arrived.at[group, fsdp]
        )

    def pick(group):
        for at in range(0, width, TILE):
            picked = nn(sel_ref[group], grads[group, :, at : at + TILE])
            staged[group, :, :, at : at + TILE] = picked.astype(BF).reshape(n_fsdp, capacity, TILE)
        rows_kept(group).start()
        for offset in range(1, n_fsdp):
            rows_copy(group, offset).start()

    def pick_from(distance):
        @pl.when(ctx - distance >= 0)
        def _():
            pick(ctx - distance)

        @pl.when(ctx + distance < n_ctx)
        def _():
            pick(ctx + distance)

    @pl.when(head == 0)
    def _():
        own.start()
        weights.start()
        greet(
            [(along(i), fsdp) for i in range(1, n_ctx)]
            + [(ctx, around(i)) for i in range(1, n_fsdp)]
        )
        line.step(0)
        own.wait()
        pick(ctx)
        prepare_keys(k_ref, v_ref, cos_ref, sin_ref, gains_ref, keys, values_t)

    @pl.when(head < heads)
    def _():
        def store(start, count, out):
            columns = pl.ds(pl.multiple_of(head * HEAD_SIZE, HEAD_SIZE), HEAD_SIZE)
            mixed[start : start + count, columns] = out

        attend_head(
            q_ref,
            cos_ref,
            sin_ref,
            gains_ref,
            own_ref,
            key_ref,
            total_ref,
            dealt_ref,
            keys,
            values_t,
            store,
        )

    @pl.when(head == heads - 2)
    def _():
        line.step(1)
        pick_from(1)

    @pl.when(head == heads)
    def _():
        weights.wait()
        for block in range(n_ctx):
            for at in range(0, width, TILE):
                held[block, :, at : at + TILE] = nn(
                    mixed[block * span : (block + 1) * span, :], w_out[:, at : at + TILE]
                ).astype(BF)
        line.step(2)
        sums.scatter(0)
        pick_from(2)
        sums.scatter(1)
        for step in range(3, n_ctx):
            line.step(step)
            pick_from(step)
        sums.scatter(2)
        sums.scatter(3)
        for chunk in range(4):
            sums.settle(chunk, attn_ref)
        sums.finish()
        line.finish()
        for group in range(n_ctx):
            rows_kept(group).wait()
            for offset in range(1, n_fsdp):
                source = around(offset)
                push(
                    staged.at[group, source],
                    rows_ref.at[source, group],
                    rows_send.at[group, offset],
                    rows_arrived.at[group, source],
                    (ctx, source),
                ).wait()


def run_attention_exchange(
    qkv, heads, n_ctx, n_fsdp, cosine, sine, gains, own, key_blocks, select, grad, w_out
):
    length = qkv.shape[0]
    span, width = grad.shape
    capacity = select.shape[1] // n_fsdp
    anywhere = pl.BlockSpec(memory_space=pl.ANY)
    dma, vmem, shape = pltpu.SemaphoreType.DMA, pltpu.VMEM, jax.ShapeDtypeStruct
    last = heads - 1
    whole, column, _, _, shared = attention_specs(heads, length)
    clip = lambda h: jnp.minimum(h, last)
    return pl.pallas_call(
        functools.partial(attention_exchange, n_ctx, n_fsdp, heads),
        grid=(heads + 1,),
        in_specs=[
            pl.BlockSpec((length, HEAD_SIZE), lambda h: (0, clip(h))),
            column(heads),
            column(heads + 1),
        ]
        + shared
        + [whole(select.shape), anywhere, anywhere],
        out_specs=[
            pl.BlockSpec((1, 8, length), lambda h: (clip(h), 0, 0)),
            pl.BlockSpec(
                (1, length, HEAD_SIZE),
                lambda h: (lax.rem(clip(h), n_ctx), 0, lax.div(clip(h), n_ctx)),
            ),
            whole((span, width)),
            anywhere,
        ],
        out_shape=[
            shape((heads, 8, length), F32),
            shape((n_ctx, length, heads // n_ctx * HEAD_SIZE), BF),
            shape((span, width), F32),
            shape((n_fsdp, n_ctx, capacity, width), BF),
        ],
        scratch_shapes=[
            vmem((length, HEAD_SIZE), BF),
            vmem((HEAD_SIZE, length), BF),
            vmem((length, heads * HEAD_SIZE), BF),
            vmem((heads * HEAD_SIZE, width), BF),
            vmem((n_ctx, span, width), BF),
            vmem((n_ctx, span, width), BF),
            vmem((n_ctx, span, width), BF),
            vmem((n_ctx, span, width), BF),
            vmem((n_ctx, n_fsdp, capacity, width), BF),
            dma((2,)),
            dma((n_ctx,)),
            dma((n_ctx,)),
            dma((n_ctx,)),
            dma((n_ctx, n_fsdp)),
            dma((n_ctx, n_fsdp)),
            dma((n_ctx, 4)),
            dma((n_ctx, 4)),
            dma((n_ctx, 4)),
            dma((n_ctx, 4)),
        ],
        compiler_params=pltpu.CompilerParams(
            collective_id=4, has_side_effects=True, vmem_limit_bytes=60 * 2**20
        ),
        cost_estimate=pl.CostEstimate(
            flops=4 * heads * length * length * HEAD_SIZE,
            bytes_accessed=400 * 2**20,
            transcendentals=heads * length * length,
        ),
    )(qkv, qkv, qkv, cosine, sine, gains, own, key_blocks, select, grad, w_out)


def on_device(
    inputs,
    block_ids,
    expert_ids,
    drop_order,
    attn_gain,
    w_query,
    key_projection_weight,
    value_projection_weight,
    q_gain,
    key_norm_gain,
    w_out,
    ffn_gain,
    w_router,
    expert_gate,
    expert_up,
    expert_down,
    cotangent,
):
    n_ctx, n_fsdp = lax.axis_size("ctx"), lax.axis_size("fsdp")
    ctx = lax.axis_index("ctx")
    span, width = inputs.shape[1], inputs.shape[2]
    length = block_ids.shape[1]
    experts = n_ctx * n_fsdp
    capacity = 5 * span * TOP // (4 * experts)
    slots = experts * capacity
    heads = QUERY_HEADS // n_ctx
    share = n_ctx // KEY_VALUE_HEADS
    own_rows = w_query.shape[0]
    q_width = heads * HEAD_SIZE
    qkv_width = q_width + 2 * HEAD_SIZE
    extra_width = -(-(experts + 8) // 128) * 128

    def gather_ctx(array):
        return lax.all_gather(array, "ctx", axis=0, tiled=True)

    def scatter_ctx(array):
        return lax.psum_scatter(array.astype(BF), "ctx", scatter_dimension=0, tiled=True)

    def route(rows):
        return lax.all_to_all(rows, "fsdp", split_axis=0, concat_axis=0, tiled=True)

    def columns(weight, index, count):
        return lax.dynamic_slice_in_dim(weight, index * count, count, axis=1)

    def as_column(vector):
        return jnp.pad(vector, (0, own_rows - vector.shape[0]))[:, None]

    packed = jnp.concatenate(
        [
            columns(w_query, ctx, q_width),
            columns(key_projection_weight, ctx // share, HEAD_SIZE),
            columns(value_projection_weight, ctx // share, HEAD_SIZE),
            w_router,
            as_column(attn_gain),
            as_column(ffn_gain),
            as_column(q_gain),
            as_column(key_norm_gain),
            jnp.zeros((own_rows, extra_width - experts - 4), BF),
        ],
        axis=1,
    )
    table = jnp.concatenate(
        [expert_ids[0].T, drop_order[0], jnp.zeros((7, span), jnp.int32)], axis=0
    )
    inputs_all, tables, packed_all = run_first_gather(n_ctx, n_fsdp, inputs[0], table, packed)
    out_all = lax.all_gather(w_out, "fsdp", axis=0, tiled=True)
    out_here = lax.dynamic_slice_in_dim(out_all, ctx * q_width, q_width, axis=0)
    inputs_all = inputs_all.reshape(length, width)
    packed_all = packed_all.reshape(width, qkv_width + extra_width)
    w_qkv = packed_all[:, :qkv_width]
    extra = packed_all[:, qkv_width:].T
    router_t = extra[:experts]
    gain_attn = extra[experts : experts + 1].astype(F32)
    gain_ffn = extra[experts + 1 : experts + 2].astype(F32)

    def head_gain(at):
        return extra[at].reshape(n_fsdp, own_rows)[:, : HEAD_SIZE // n_fsdp].reshape(1, HEAD_SIZE)

    gains = jnp.concatenate(
        [head_gain(experts + 2), head_gain(experts + 3), jnp.zeros((6, HEAD_SIZE), BF)], axis=0
    ).astype(F32)

    named = tables[:, :TOP, :]
    ranks = tables[:, TOP, :]
    here = ctx * n_fsdp + jnp.arange(n_fsdp, dtype=jnp.int32)
    member = jnp.any(named[:, :, None, :] == here[None, None, :, None], axis=1)
    before = (ranks[:, :, None] < ranks[:, None, :]).astype(BF)
    place = jnp.einsum(
        "gjs,gst->gjt", member.astype(BF), before, preferred_element_type=F32
    ).astype(jnp.int32)
    place = jnp.where(member, place, capacity)
    select = (
        place[:, :, None, :] == jnp.arange(capacity, dtype=jnp.int32)[None, None, :, None]
    ).astype(BF)

    fused = capacity % 16 == 0 and 2 * experts <= AUX and experts == QUERY_HEADS
    select_rows = select.reshape(n_ctx, n_fsdp * capacity, span)

    def dispatch(rows):
        picked = jnp.einsum(
            "gjkt,gtd->jgkd", select, rows.reshape(n_ctx, span, width), preferred_element_type=F32
        ).astype(BF)
        return route(picked).reshape(slots, width)

    def combine(rows):
        return gather_slots(route(rows.reshape(n_fsdp, n_ctx, capacity, width)))

    def gather_slots(back):
        return jnp.einsum("gjkt,jgkd->gtd", select, back, preferred_element_type=F32).reshape(
            length, width
        )

    x_all = inputs_all.astype(F32)
    r_all = inverse_rms(x_all)
    hidden = (x_all * r_all * gain_attn).astype(BF)
    qkv = nn(hidden, w_qkv)
    exponent = np.arange(HALF, dtype=np.float32) * np.float32(2.0 / HEAD_SIZE)
    angles = np.arange(length, dtype=np.float32)[:, None] * (
        np.float32(ROPE_BASE) ** (-exponent)
    )
    cosine = jnp.asarray(np.tile(np.cos(angles), (1, 2)))
    sine = jnp.asarray(np.concatenate([-np.sin(angles), np.sin(angles)], axis=1))
    own_blocks = jnp.broadcast_to(block_ids, (8, length))
    key_blocks = block_ids.reshape(length, 1)
    piece = QUERY_HEADS * HEAD_SIZE // experts
    groups = n_fsdp // n_ctx
    if fused:
        totals, dealt, attn_out, grad_rows = run_attention_exchange(
            qkv,
            heads,
            n_ctx,
            n_fsdp,
            cosine,
            sine,
            gains,
            own_blocks,
            key_blocks,
            select_rows,
            cotangent[0],
            out_all,
        )
        grad_rows = grad_rows.reshape(slots, width)
    else:
        mixed, totals, _ = run_attention(
            qkv, heads, n_ctx, cosine, sine, gains, own_blocks, key_blocks
        )
        attn_out = scatter_ctx(nn(mixed, out_here))
        grad_rows = dispatch(gather_ctx(cotangent[0]))
        dealt = mixed.reshape(length, groups, n_ctx, piece).transpose(2, 0, 1, 3)
        dealt = dealt.reshape(n_ctx, length, groups * piece)

    x = inputs[0].astype(F32)
    resid = x + attn_out.astype(F32)
    r_ffn = inverse_rms(resid)
    normed = (resid * r_ffn * gain_ffn).astype(BF)
    if fused:
        chosen = jnp.any(
            expert_ids[0][:, :, None] == jnp.arange(experts, dtype=jnp.int32), axis=1
        )
        logits = nt(normed, router_t)
        gates = jax.nn.softmax(jnp.where(chosen, logits, -jnp.inf), axis=-1)
        high = lax.reduce_precision(gates, 8, 7)
        payload = jnp.concatenate(
            [
                normed,
                high.astype(BF),
                (gates - high).astype(BF),
                jnp.zeros((span, AUX - 2 * experts), BF),
            ],
            axis=1,
        )
        rows, _, parts, inner_low, dg, du, y, dealt = run_expert_exchange(
            n_ctx,
            n_fsdp,
            payload,
            select_rows,
            select_rows.swapaxes(1, 2),
            expert_gate[0],
            expert_up[0],
            expert_down[0],
            grad_rows.reshape(n_fsdp, n_ctx, capacity, width),
            dealt,
        )
        rows = rows.reshape(slots, width + AUX)[:, :width]
        inner_low, dg, du = (array.reshape(slots, -1) for array in (inner_low, dg, du))
        y = y.reshape(slots, width)
        parts = jnp.sum(parts.astype(F32), axis=0)
        d_gates = parts[:, width : width + experts] + parts[:, width + experts : width + 2 * experts]
        d_logits = gates * (d_gates - jnp.sum(gates * d_gates, axis=-1, keepdims=True))
        d_logits = d_logits.astype(BF)
        d_normed = parts[:, :width] + nn(d_logits, router_t)
    else:
        dealt = lax.all_to_all(dealt, "ctx", split_axis=0, concat_axis=0, tiled=True)
        chosen = jnp.any(
            named[:, :, :, None] == jnp.arange(experts, dtype=jnp.int32), axis=1
        ).reshape(length, experts)
        normed = gather_ctx(normed)
        normed, grad_rows = lax.optimization_barrier((normed, grad_rows))
        grad_inner = nt(grad_rows, expert_down[0])
        logits = nt(normed, router_t)
        gates = jax.nn.softmax(jnp.where(chosen, logits, -jnp.inf), axis=-1)
        gates_here = lax.dynamic_slice_in_dim(gates, ctx * n_fsdp, n_fsdp, axis=1)
        gates_here = gates_here.reshape(n_ctx, span, n_fsdp).transpose(0, 2, 1)
        slot_gates = jnp.sum(select.astype(F32) * gates_here[:, :, None, :], axis=-1)
        slot_gates = route(slot_gates.transpose(1, 0, 2)).reshape(slots, 1)
        rows = dispatch(normed)
        g = nn(rows, expert_gate[0])
        u = nn(rows, expert_up[0])
        s = jax.nn.sigmoid(g)
        inner = g * s * u
        slot_dgates = jnp.sum(inner * grad_inner, axis=-1).reshape(n_fsdp, n_ctx, capacity)
        d_inner = grad_inner * slot_gates
        dg = (d_inner * u * s * (1.0 + g * (1.0 - s))).astype(BF)
        du = (d_inner * g * s).astype(BF)
        d_rows = (nt(dg, expert_gate[0]) + nt(du, expert_up[0])).astype(BF)
        y = (nn(inner.astype(BF), expert_down[0]) * slot_gates).astype(BF)
        inner_low = (inner * slot_gates).astype(BF)
        d_gates = jnp.einsum(
            "gjkt,jgk->gjt", select.astype(F32), route(slot_dgates), precision=lax.Precision.HIGHEST
        )
        weighted = (d_gates * gates_here).transpose(0, 2, 1).reshape(length, n_fsdp)
        d_logits = lax.dynamic_update_slice_in_dim(
            jnp.zeros((length, experts), F32), weighted, ctx * n_fsdp, axis=1
        ) - gates * jnp.sum(weighted, axis=1, keepdims=True)
        d_logits = d_logits.astype(BF)
        d_normed = scatter_ctx(combine(d_rows) + nn(d_logits, router_t)).astype(F32)

    gate_grad = tn(rows, dg)
    up_grad = tn(rows, du)
    down_grad = tn(inner_low, grad_rows)
    router_grad = tn(normed, d_logits)

    grad = cotangent[0].astype(F32)
    n = d_normed * gain_ffn
    d_resid = grad + r_ffn * n - resid * r_ffn**3 * jnp.mean(n * resid, axis=-1, keepdims=True)
    ffn_gain_grad = jnp.sum(d_normed * resid * r_ffn, axis=0)
    d_attn = gather_ctx(d_resid.astype(BF))
    y_back = route(y.reshape(n_fsdp, n_ctx, capacity, width))
    y_back, gate_grad, up_grad, down_grad = lax.optimization_barrier(
        (y_back, gate_grad, up_grad, down_grad)
    )
    y_all = gather_slots(y_back).astype(BF)
    d_attn, y_all = lax.optimization_barrier((d_attn, y_all))

    d_mixed = nt(d_attn, out_here).astype(BF)
    moe = scatter_ctx(y_all)
    out_grad = jnp.einsum("ntk,td->nkd", dealt, d_attn, preferred_element_type=F32).astype(BF)

    dq, dkv, dgains = run_attention_back(
        qkv, d_mixed, totals, heads, cosine, sine, gains, own_blocks, key_blocks
    )
    d_qkv = jnp.concatenate([dq, dkv], axis=1)
    d_hidden = nt(d_qkv, w_qkv)
    attn_gain_grad = jnp.sum(d_hidden * x_all * r_all, axis=0)

    def spread(vector):
        parts = vector.reshape(n_fsdp, HEAD_SIZE // n_fsdp)
        return jnp.pad(parts, ((0, 0), (0, own_rows - parts.shape[1]))).reshape(width)

    small = jnp.stack(
        [attn_gain_grad, ffn_gain_grad, spread(dgains[0]), spread(dgains[1])], axis=1
    )
    extra_grad = jnp.concatenate(
        [
            router_grad.astype(BF),
            small.astype(BF),
            jnp.zeros((width, extra_width - experts - 4), BF),
        ],
        axis=1,
    )
    shared_grad = tn(hidden, d_qkv).astype(BF)
    d_hidden, moe, shared_grad, out_grad = lax.optimization_barrier(
        (d_hidden.astype(BF), moe, shared_grad, out_grad)
    )
    d_hidden = scatter_ctx(d_hidden)
    shared_grad, rest, out_grad = run_last_reduce(
        n_ctx, n_fsdp, [shared_grad, extra_grad, out_grad.reshape(n_fsdp * piece, width)]
    )
    query_grad, key_grad, value_grad, out_grad, input_grad, output, router_grad, gain_grads = (
        run_finish(
            n_ctx,
            experts,
            shared_grad,
            rest,
            out_grad,
            d_hidden,
            inputs[0],
            d_resid,
            resid,
            moe,
            gain_attn,
        )
    )
    head_rows = HEAD_SIZE // n_fsdp
    return (
        output[None],
        input_grad[None],
        gain_grads[0],
        query_grad,
        key_grad,
        value_grad,
        gain_grads[2, :head_rows],
        gain_grads[3, :head_rows],
        out_grad,
        gain_grads[1],
        router_grad,
        gate_grad[None],
        up_grad[None],
        down_grad[None],
    )


def solution(mesh):
    rows, tokens = P("fsdp", None), P("fsdp", "ctx", None)
    vector, expert = P("fsdp"), P(("ctx", "fsdp"), None, None)
    in_specs = (
        tokens,
        rows,
        tokens,
        tokens,
        vector,
        rows,
        rows,
        rows,
        vector,
        vector,
        rows,
        vector,
        rows,
        expert,
        expert,
        expert,
        tokens,
    )
    out_specs = (
        tokens,
        tokens,
        vector,
        rows,
        rows,
        rows,
        vector,
        vector,
        rows,
        vector,
        rows,
        expert,
        expert,
        expert,
    )
    return jax.shard_map(
        on_device, mesh=mesh, in_specs=in_specs, out_specs=out_specs, check_vma=False
    )
```

```python
import functools

import jax
import jax.numpy as jnp
import numpy as np
from jax import lax
from jax.experimental import pallas as pl
from jax.experimental.pallas import tpu as pltpu
from jax.sharding import PartitionSpec as P

QUERY_HEADS = 32
KEY_VALUE_HEADS = 4
HEAD_SIZE = 128
TOP = 8

EPSILON = 1e-06
ROPE_BASE = 1000000.0
MASKED = -1000000000.0
SCALE = HEAD_SIZE ** (-0.5)
HALF = HEAD_SIZE // 2
BF = jnp.bfloat16
F32 = jnp.float32


def nt(a, b):
    return lax.dot_general(a, b, (((1,), (1,)), ((), ())), preferred_element_type=F32)


def nn(a, b):
    return lax.dot_general(a, b, (((1,), (0,)), ((), ())), preferred_element_type=F32)


def tn(a, b):
    return lax.dot_general(a, b, (((0,), (0,)), ((), ())), preferred_element_type=F32)


def inverse_rms(values):
    return lax.rsqrt(jnp.mean(values * values, axis=-1, keepdims=True) + EPSILON)


def norm_rope(raw, gain, cosine, sine):
    z = raw * inverse_rms(raw) * gain
    return z * cosine + pltpu.roll(z, HALF, 1) * sine


def norm_rope_back(raw, gain, cosine, sine, grad):
    dz = grad * cosine - pltpu.roll(grad, HALF, 1) * sine
    r = inverse_rms(raw)
    n = dz * gain
    d_raw = r * n - raw * (r * r * r) * jnp.mean(n * raw, axis=-1, keepdims=True)
    return d_raw, jnp.sum(dz * raw * r, axis=0, keepdims=True)


def prepare_keys(k_ref, v_ref, cos_ref, sin_ref, gains_ref, keys, values_t):
    rotated = norm_rope(k_ref[...], gains_ref[1:2, :], cos_ref[...], sin_ref[...])
    keys[...] = rotated.astype(BF)
    values_t[...] = v_ref[...].T.astype(BF)


def attend_head(
    q_ref, cos_ref, sin_ref, gains_ref, own_ref, key_ref, total_ref, dealt_ref, keys, values_t, store
):
    queries = norm_rope(q_ref[...], gains_ref[0:1, :], cos_ref[...], sin_ref[...]).astype(BF)
    length = queries.shape[0]
    chunk = 256
    for start in range(0, length, chunk):
        scores = nt(keys[...], queries[start : start + chunk]) * SCALE
        seen = key_ref[...] <= own_ref[0:1, start : start + chunk]
        scores = jnp.where(seen, scores, MASKED)
        top = jnp.max(scores, axis=0, keepdims=True)
        weights = jnp.exp(scores - top)
        total = jnp.sum(weights, axis=0, keepdims=True)
        out = (nn(values_t[...], weights.astype(BF)) / total).T.astype(BF)
        store(start, chunk, out)
        dealt_ref[0, start : start + chunk, :] = out
        total_ref[0, :, start : start + chunk] = jnp.broadcast_to(top + jnp.log(total), (8, chunk))


def attention_forward(
    q_ref,
    k_ref,
    v_ref,
    cos_ref,
    sin_ref,
    gains_ref,
    own_ref,
    key_ref,
    mixed_ref,
    total_ref,
    dealt_ref,
    keys,
    values_t,
):
    @pl.when(pl.program_id(0) == 0)
    def _():
        prepare_keys(k_ref, v_ref, cos_ref, sin_ref, gains_ref, keys, values_t)

    def store(start, count, out):
        mixed_ref[start : start + count, :] = out

    attend_head(
        q_ref, cos_ref, sin_ref, gains_ref, own_ref, key_ref, total_ref, dealt_ref, keys, values_t, store
    )


def attention_backward(
    heads,
    q_ref,
    k_ref,
    v_ref,
    grad_ref,
    total_ref,
    cos_ref,
    sin_ref,
    gains_ref,
    own_ref,
    key_ref,
    dq_ref,
    dkv_ref,
    dgain_ref,
    keys,
    keys_t,
    values,
    dk,
    dv,
):
    cosine, sine = cos_ref[...], sin_ref[...]
    head = pl.program_id(0)

    @pl.when(head == 0)
    def _():
        rotated = norm_rope(k_ref[...], gains_ref[1:2, :], cosine, sine)
        keys[...] = rotated.astype(BF)
        keys_t[...] = rotated.T.astype(BF)
        values[...] = v_ref[...].astype(BF)
        dk[...] = jnp.zeros_like(dk)
        dv[...] = jnp.zeros_like(dv)
        dgain_ref[...] = jnp.zeros_like(dgain_ref)

    queries = norm_rope(q_ref[...], gains_ref[0:1, :], cosine, sine).astype(BF)
    length = queries.shape[0]
    chunk = 256
    for start in range(0, length, chunk):
        rows = slice(start, start + chunk)
        q_part = queries[rows]
        grad = grad_ref[rows, :]
        scores = nt(keys[...], q_part) * SCALE
        seen = key_ref[...] <= own_ref[0:1, rows]
        scores = jnp.where(seen, scores, MASKED)
        weights = jnp.exp(scores - total_ref[0, 0:1, rows])
        d_weights = nt(values[...], grad)
        row_dot = jnp.sum(weights * d_weights, axis=0, keepdims=True)
        d_scores = (weights * (d_weights - row_dot)).astype(BF)
        dv[...] += nn(weights.astype(BF), grad)
        dk[...] += nn(d_scores, q_part)
        d_queries = nn(keys_t[...], d_scores).T * SCALE
        d_raw, d_gain = norm_rope_back(
            q_ref[rows, :], gains_ref[0:1, :], cos_ref[rows, :], sin_ref[rows, :], d_queries
        )
        dq_ref[rows, :] = d_raw.astype(BF)
        dgain_ref[0:1, :] += d_gain

    @pl.when(head == heads - 1)
    def _():
        d_raw, d_gain = norm_rope_back(
            k_ref[...], gains_ref[1:2, :], cosine, sine, dk[...] * SCALE
        )
        dkv_ref[:, :HEAD_SIZE] = d_raw.astype(BF)
        dkv_ref[:, HEAD_SIZE:] = dv[...].astype(BF)
        dgain_ref[1:2, :] = d_gain


def attention_specs(heads, length):
    whole = lambda shape: pl.BlockSpec(shape, lambda h: (0,) * len(shape))
    column = lambda at: pl.BlockSpec((length, HEAD_SIZE), lambda h: (0, at))
    head_column = pl.BlockSpec((length, HEAD_SIZE), lambda h: (0, h))
    totals = pl.BlockSpec((1, 8, length), lambda h: (h, 0, 0))
    shared = [
        whole((length, HEAD_SIZE)),
        whole((length, HEAD_SIZE)),
        whole((8, HEAD_SIZE)),
        whole((8, length)),
        whole((length, 1)),
    ]
    return whole, column, head_column, totals, shared


def run_attention(qkv, heads, n_ctx, cosine, sine, gains, own, key_blocks):
    length = qkv.shape[0]
    whole, column, head_column, totals, shared = attention_specs(heads, length)
    deals = min(n_ctx, heads)
    return pl.pallas_call(
        attention_forward,
        grid=(heads,),
        in_specs=[head_column, column(heads), column(heads + 1)] + shared,
        out_specs=[
            head_column,
            totals,
            pl.BlockSpec((1, length, HEAD_SIZE), lambda h: (h % deals, 0, h // deals)),
        ],
        out_shape=[
            jax.ShapeDtypeStruct((length, heads * HEAD_SIZE), BF),
            jax.ShapeDtypeStruct((heads, 8, length), F32),
            jax.ShapeDtypeStruct((deals, length, heads // deals * HEAD_SIZE), BF),
        ],
        scratch_shapes=[
            pltpu.VMEM((length, HEAD_SIZE), BF),
            pltpu.VMEM((HEAD_SIZE, length), BF),
        ],
        compiler_params=pltpu.CompilerParams(vmem_limit_bytes=48 * 2**20),
        cost_estimate=pl.CostEstimate(
            flops=4 * heads * length * length * HEAD_SIZE,
            bytes_accessed=8 * heads * length * HEAD_SIZE,
            transcendentals=heads * length * length,
        ),
    )(qkv, qkv, qkv, cosine, sine, gains, own, key_blocks)


def run_attention_back(qkv, grad, totals_in, heads, cosine, sine, gains, own, key_blocks):
    length = qkv.shape[0]
    whole, column, head_column, totals, shared = attention_specs(heads, length)
    return pl.pallas_call(
        functools.partial(attention_backward, heads),
        grid=(heads,),
        in_specs=[head_column, column(heads), column(heads + 1), head_column, totals] + shared,
        out_specs=[head_column, whole((length, 2 * HEAD_SIZE)), whole((8, HEAD_SIZE))],
        out_shape=[
            jax.ShapeDtypeStruct((length, heads * HEAD_SIZE), BF),
            jax.ShapeDtypeStruct((length, 2 * HEAD_SIZE), BF),
            jax.ShapeDtypeStruct((8, HEAD_SIZE), F32),
        ],
        scratch_shapes=[
            pltpu.VMEM((length, HEAD_SIZE), BF),
            pltpu.VMEM((HEAD_SIZE, length), BF),
            pltpu.VMEM((length, HEAD_SIZE), BF),
            pltpu.VMEM((length, HEAD_SIZE), F32),
            pltpu.VMEM((length, HEAD_SIZE), F32),
        ],
        compiler_params=pltpu.CompilerParams(vmem_limit_bytes=48 * 2**20),
        cost_estimate=pl.CostEstimate(
            flops=10 * heads * length * length * HEAD_SIZE,
            bytes_accessed=10 * heads * length * HEAD_SIZE,
            transcendentals=heads * length * length,
        ),
    )(qkv, qkv, qkv, grad, totals_in, cosine, sine, gains, own, key_blocks)


def push(source, target, sends, recvs, device):
    copy = pltpu.make_async_remote_copy(
        src_ref=source,
        dst_ref=target,
        send_sem=sends,
        recv_sem=recvs,
        device_id=device,
        device_id_type=pl.DeviceIdType.MESH,
    )
    return copy


def greet(devices):
    barrier = pltpu.get_barrier_semaphore()
    for device in devices:
        pl.semaphore_signal(barrier, 1, device_id=device, device_id_type=pl.DeviceIdType.MESH)
    pl.semaphore_wait(barrier, len(devices))


class LineGather:
    def __init__(self, n_ctx, ctx, fsdp, own_ref, all_ref, up, down, arrived):
        self.n_ctx, self.ctx, self.fsdp = n_ctx, ctx, fsdp
        self.own_ref, self.all_ref = own_ref, all_ref
        self.up, self.down, self.arrived = up, down, arrived

    def copy(self, source, block, sems, step, to):
        return push(
            source, self.all_ref.at[block], sems.at[step], self.arrived.at[block], (to, self.fsdp)
        )

    def going_up(self, step):
        return (self.ctx - step >= 0) & (self.ctx < self.n_ctx - 1)

    def going_down(self, step):
        return (self.ctx + step < self.n_ctx) & (self.ctx > 0)

    def step(self, step):
        def hop(block, sems, to, more):
            if step > 0:
                self.copy(self.own_ref, block, sems, 0, to).wait_recv()

            @pl.when(more)
            def _():
                source = self.all_ref.at[block] if step > 0 else self.own_ref
                self.copy(source, block, sems, step, to).start()

        @pl.when(self.ctx - step >= 0)
        def _():
            hop(self.ctx - step, self.up, self.ctx + 1, self.ctx < self.n_ctx - 1)

        @pl.when(self.ctx + step < self.n_ctx)
        def _():
            hop(self.ctx + step, self.down, self.ctx - 1, self.ctx > 0)

    def finish(self):
        for step in range(self.n_ctx - 1):

            @pl.when(self.going_up(step))
            def _():
                self.copy(self.own_ref, 0, self.up, step, self.ctx).wait_send()

            @pl.when(self.going_down(step))
            def _():
                self.copy(self.own_ref, 0, self.down, step, self.ctx).wait_send()


class LineScatter:
    def __init__(self, n_ctx, ctx, fsdp, chunks, held, low, high, up, down, low_in, high_in):
        self.n_ctx, self.ctx, self.fsdp, self.chunks = n_ctx, ctx, fsdp, chunks
        self.held, self.low, self.high = held, low, high
        self.sems = {"up": (low, up, low_in), "down": (high, down, high_in)}
        self.size = held.shape[1] // chunks

    def copy(self, way, block, chunk, to):
        landing, sends, arrived = self.sems[way]
        rows = pl.ds(chunk * self.size, self.size)
        return push(
            self.held.at[block, rows],
            landing.at[block, rows],
            sends.at[block, chunk],
            arrived.at[block, chunk],
            (to, self.fsdp),
        )

    def scatter(self, chunk):
        rows = slice(chunk * self.size, (chunk + 1) * self.size)
        ctx, held = self.ctx, self.held

        def pass_on(way, block, to, first):
            @pl.when(jnp.logical_not(first))
            def _():
                self.copy(way, block, chunk, ctx).wait_recv()
                held[block, rows, :] = (
                    held[block, rows, :].astype(F32)
                    + self.sems[way][0][block, rows, :].astype(F32)
                ).astype(BF)

            self.copy(way, block, chunk, to).start()

        for step in range(self.n_ctx - 1):

            @pl.when(ctx < self.n_ctx - 1 - step)
            def _():
                pass_on("up", self.n_ctx - 1 - step, ctx + 1, ctx == 0)

            @pl.when(ctx > step)
            def _():
                pass_on("down", step, ctx - 1, ctx == self.n_ctx - 1)

    def settle(self, chunk, total_ref):
        rows = slice(chunk * self.size, (chunk + 1) * self.size)
        total_ref[rows, :] = self.held[self.ctx, rows, :].astype(F32)

        @pl.when(self.ctx > 0)
        def _():
            self.copy("up", self.ctx, chunk, self.ctx).wait_recv()
            total_ref[rows, :] += self.low[self.ctx, rows, :].astype(F32)

        @pl.when(self.ctx < self.n_ctx - 1)
        def _():
            self.copy("down", self.ctx, chunk, self.ctx).wait_recv()
            total_ref[rows, :] += self.high[self.ctx, rows, :].astype(F32)

    def finish(self):
        for chunk in range(self.chunks):
            for step in range(self.n_ctx - 1):

                @pl.when(self.ctx < self.n_ctx - 1 - step)
                def _():
                    self.copy("up", self.n_ctx - 1 - step, chunk, self.ctx).wait_send()

                @pl.when(self.ctx > step)
                def _():
                    self.copy("down", step, chunk, self.ctx).wait_send()


def first_gather(
    n_ctx,
    n_fsdp,
    x_ref,
    table_ref,
    packed_ref,
    x_all,
    table_all,
    packed_all,
    local,
    up,
    down,
    arrived,
    table_send,
    table_arrived,
    packed_send,
    passed_send,
    packed_arrived,
):
    ctx, fsdp = lax.axis_index("ctx"), lax.axis_index("fsdp")
    sibling = lax.rem(fsdp + 1, 2) + (fsdp // 2) * 2
    chips = n_fsdp // 2

    def same_core(offset):
        return lax.rem(fsdp + 2 * offset, n_fsdp)

    def along(offset):
        return lax.rem(ctx + offset, n_ctx)

    greet(
        [(along(i), fsdp) for i in range(1, n_ctx)]
        + [(ctx, same_core(i)) for i in range(1, chips)]
        + [(ctx, sibling)]
    )
    kept = [
        pltpu.make_async_copy(x_ref, x_all.at[ctx], local.at[0]),
        pltpu.make_async_copy(table_ref, table_all.at[ctx], local.at[1]),
        pltpu.make_async_copy(packed_ref, packed_all.at[fsdp], local.at[2]),
    ]
    for copy in kept:
        copy.start()

    def packed_copy(source, owner, sems, to):
        return push(source, packed_all.at[owner], sems, packed_arrived.at[owner], (ctx, to))

    for i in range(1, chips):
        packed_copy(packed_ref, fsdp, packed_send.at[i], same_core(i)).start()
    packed_copy(packed_ref, fsdp, packed_send.at[0], sibling).start()
    for i in range(1, n_ctx):
        push(
            table_ref, table_all.at[ctx], table_send.at[i], table_arrived.at[ctx], (along(i), fsdp)
        ).start()
    line = LineGather(n_ctx, ctx, fsdp, x_ref, x_all, up, down, arrived)
    for step in range(n_ctx):
        line.step(step)
    for i in range(1, chips):
        owner = same_core(chips - i)
        packed_copy(packed_ref, owner, packed_send.at[i], sibling).wait_recv()
        packed_copy(packed_all.at[owner], owner, passed_send.at[i], sibling).start()
    for i in range(chips):
        owner = lax.rem(sibling + 2 * i, n_fsdp)
        packed_copy(packed_ref, owner, packed_send.at[0], sibling).wait_recv()
    for i in range(1, n_ctx):
        owner = along(i)
        push(
            table_ref, table_all.at[owner], table_send.at[i], table_arrived.at[owner], (owner, fsdp)
        ).wait()
    line.finish()
    for i in range(chips):
        packed_copy(packed_ref, fsdp, packed_send.at[i], sibling).wait_send()
    for i in range(1, chips):
        packed_copy(packed_ref, fsdp, passed_send.at[i], sibling).wait_send()
    for copy in kept:
        copy.wait()


def run_first_gather(n_ctx, n_fsdp, x, table, packed):
    anywhere = pl.BlockSpec(memory_space=pl.ANY)
    dma = pltpu.SemaphoreType.DMA
    return pl.pallas_call(
        functools.partial(first_gather, n_ctx, n_fsdp),
        in_specs=[anywhere] * 3,
        out_specs=[anywhere] * 3,
        out_shape=[
            jax.ShapeDtypeStruct((n_ctx,) + x.shape, x.dtype),
            jax.ShapeDtypeStruct((n_ctx,) + table.shape, table.dtype),
            jax.ShapeDtypeStruct((n_fsdp,) + packed.shape, packed.dtype),
        ],
        scratch_shapes=[
            dma((3,)),
            dma((n_ctx,)),
            dma((n_ctx,)),
            dma((n_ctx,)),
            dma((n_ctx,)),
            dma((n_ctx,)),
            dma((n_fsdp // 2,)),
            dma((n_fsdp // 2,)),
            dma((n_fsdp,)),
        ],
        compiler_params=pltpu.CompilerParams(collective_id=1, has_side_effects=True),
        cost_estimate=pl.CostEstimate(
            flops=0, bytes_accessed=200 * 2**20, transcendentals=0
        ),
    )(x, table, packed)


TILE = 512
AUX = 128


def expert_exchange(
    n_ctx,
    n_fsdp,
    x_ref,
    sel_ref,
    selt_ref,
    gate_ref,
    up_ref,
    down_ref,
    grad_ref,
    dealt_ref,
    rows_ref,
    back_ref,
    part_ref,
    inner_ref,
    dg_ref,
    du_ref,
    y_low_ref,
    y_high_ref,
    dealt_all,
    w_gate,
    w_up,
    w_down,
    held,
    staged,
    rows_in,
    grad_in,
    inner_out,
    dg_out,
    du_out,
    y_out,
    back_in,
    w_sems,
    local,
    held_send,
    held_arrived,
    rows_send,
    rows_arrived,
    back_send,
    back_arrived,
    part_send,
    part_arrived,
    dealt_send,
    dealt_arrived,
    out_sems,
):
    ctx, fsdp = lax.axis_index("ctx"), lax.axis_index("fsdp")
    experts = n_ctx * n_fsdp
    expert = ctx * n_fsdp + fsdp
    width, hidden = w_gate.shape
    wide = held.shape[2]
    capacity = staged.shape[2]
    half = n_fsdp // 2
    tiles = [(at, min(TILE, wide - at)) for at in range(0, wide, TILE)]

    def along(offset):
        return lax.rem(ctx + offset, n_ctx)

    def around(offset):
        return lax.rem(fsdp + offset, n_fsdp)

    greet(
        [(along(i), fsdp) for i in range(1, n_ctx)] + [(ctx, around(i)) for i in range(1, n_fsdp)]
    )
    weights = [
        pltpu.make_async_copy(gate_ref, w_gate, w_sems.at[0]),
        pltpu.make_async_copy(up_ref, w_up, w_sems.at[1]),
        pltpu.make_async_copy(down_ref, w_down, w_sems.at[2]),
    ]
    own = pltpu.make_async_copy(x_ref, held.at[ctx], local.at[0])
    own.start()
    for copy in weights:
        copy.start()

    def held_copy(step):
        to = lax.rem(ctx + n_ctx - step, n_ctx)
        return push(x_ref, held.at[ctx], held_send.at[step], held_arrived.at[ctx], (to, fsdp))

    def rows_copy(step, group, offset):
        to = around(offset)
        return push(
            staged.at[step, to],
            rows_ref.at[fsdp, group],
            rows_send.at[step, offset],
            rows_arrived.at[group, fsdp],
            (ctx, to),
        )

    def rows_kept(step, group):
        return pltpu.make_async_copy(
            staged.at[step, fsdp], rows_ref.at[fsdp, group], rows_arrived.at[group, fsdp]
        )

    def back_copy(step, group, offset):
        to = around(offset)
        return push(
            staged.at[step, to],
            back_ref.at[group, fsdp],
            back_send.at[step, offset],
            back_arrived.at[group, fsdp],
            (ctx, to),
        )

    def back_kept(step, group):
        return pltpu.make_async_copy(
            staged.at[step, fsdp], back_ref.at[group, fsdp], back_arrived.at[group, fsdp]
        )

    def outputs(group):
        return [
            pltpu.make_async_copy(inner_out, inner_ref.at[:, group], out_sems.at[0]),
            pltpu.make_async_copy(dg_out, dg_ref.at[:, group], out_sems.at[1]),
            pltpu.make_async_copy(du_out, du_ref.at[:, group], out_sems.at[2]),
            pltpu.make_async_copy(
                y_out.at[:, :, : width // 2], y_low_ref.at[:, group], out_sems.at[3]
            ),
            pltpu.make_async_copy(
                y_out.at[:, :, width // 2 :], y_high_ref.at[:, group], out_sems.at[4]
            ),
        ]

    def dispatch(step):
        group = along(step)

        @pl.when(step == 0)
        def _():
            own.wait()

        @pl.when(step > 0)
        def _():
            push(
                x_ref, held.at[group], held_send.at[step], held_arrived.at[group], (group, fsdp)
            ).wait_recv()

        @pl.when(step + 1 < n_ctx)
        def _():
            held_copy(step + 1).start()

        for at, size in tiles:
            picked = nn(sel_ref[group], held[group, :, at : at + size])
            staged[step, :, :, at : at + size] = picked.astype(BF).reshape(n_fsdp, capacity, size)
        rows_kept(step, group).start()
        for offset in range(1, n_fsdp):
            rows_copy(step, group, offset).start()

    def compute(step):
        group = along(step)
        rows_kept(step, group).wait()
        for offset in range(1, n_fsdp):
            source = around(offset)
            push(
                staged.at[step, source],
                rows_ref.at[source, group],
                rows_send.at[step, offset],
                rows_arrived.at[group, source],
                (ctx, source),
            ).wait_recv()
        load_rows = pltpu.make_async_copy(rows_ref.at[:, group], rows_in, local.at[1])
        load_inner = pltpu.make_async_copy(grad_ref.at[:, group], grad_in, local.at[2])
        load_rows.start()
        load_inner.start()

        @pl.when(step == 0)
        def _():
            for copy in weights:
                copy.wait()

        @pl.when(step > 0)
        def _():
            for copy in outputs(group):
                copy.wait()

        for offset in range(1, n_fsdp):
            rows_copy(step, group, offset).wait_send()
        load_rows.wait()
        load_inner.wait()
        count = half * capacity
        lane = lax.broadcasted_iota(jnp.int32, (count, AUX), 1)
        high, low = lane == expert, lane == experts + expert

        @pl.loop(0, 2)
        def _(part):
            sources = pl.ds(part * half, half)
            rows = rows_in[sources, :, :width].reshape(count, width)
            aux = rows_in[sources, :, width:].reshape(count, AUX).astype(F32)
            gate = jnp.sum(jnp.where(high | low, aux, 0.0), axis=1, keepdims=True)
            g = nn(rows, w_gate[...])
            u = nn(rows, w_up[...])
            s = jax.nn.sigmoid(g)
            inner = g * s * u
            d_inner = nt(grad_in[sources].reshape(count, width), w_down[...])
            d_gate = jnp.sum(inner * d_inner, axis=1, keepdims=True)
            d_inner = d_inner * gate
            dg = (d_inner * u * s * (1.0 + g * (1.0 - s))).astype(BF)
            du = (d_inner * g * s).astype(BF)
            inner_out[sources] = (inner * gate).astype(BF).reshape(half, capacity, hidden)
            dg_out[sources] = dg.reshape(half, capacity, hidden)
            du_out[sources] = du.reshape(half, capacity, hidden)
            rest = d_gate - d_gate.astype(BF).astype(F32)
            staged[step, sources, :, width:] = (
                jnp.where(high, d_gate, jnp.where(low, rest, 0.0))
                .astype(BF)
                .reshape(half, capacity, AUX)
            )
            for at in range(0, width, TILE):
                grad = nt(dg, w_gate[at : at + TILE, :]) + nt(du, w_up[at : at + TILE, :])
                staged[step, sources, :, at : at + TILE] = grad.astype(BF).reshape(
                    half, capacity, TILE
                )
            low_inner = inner.astype(BF)
            for at in range(0, width, TILE):
                y = nn(low_inner, w_down[:, at : at + TILE]) * gate
                y_out[sources, :, at : at + TILE] = y.astype(BF).reshape(half, capacity, TILE)

        def send_back(step, group):
            back_kept(step, group).start()
            for offset in range(1, n_fsdp):
                back_copy(step, group, offset).start()

        @pl.when(step > 0)
        def _():
            send_back(step, group)

        @pl.when(step == n_ctx - 1)
        def _():
            send_back(0, ctx)

        for copy in outputs(group):
            copy.start()

    def combine(step):
        group = along(step)
        back_kept(step, group).wait()
        for offset in range(1, n_fsdp):
            source = around(offset)
            push(
                staged.at[step, source],
                back_ref.at[group, source],
                back_send.at[step, offset],
                back_arrived.at[group, source],
                (ctx, source),
            ).wait_recv()
        load = pltpu.make_async_copy(back_ref.at[group], back_in, local.at[1])
        load.start()
        load.wait()
        for at, size in tiles:
            back = back_in[:, :, at : at + size].reshape(n_fsdp * capacity, size)
            held[group, :, at : at + size] = nn(selt_ref[group], back).astype(BF)

        @pl.when(step == 0)
        def _():
            pltpu.make_async_copy(
                held.at[group], part_ref.at[ctx], part_arrived.at[ctx]
            ).start()

        @pl.when(step > 0)
        def _():
            push(
                held.at[group],
                part_ref.at[ctx],
                part_send.at[step],
                part_arrived.at[ctx],
                (group, fsdp),
            ).start()

    def dealt_copy(offset):
        to = along(offset)
        return push(
            dealt_ref.at[to],
            dealt_all.at[ctx],
            dealt_send.at[offset],
            dealt_arrived.at[ctx],
            (to, fsdp),
        )

    dealt_kept = pltpu.make_async_copy(
        dealt_ref.at[ctx], dealt_all.at[ctx], dealt_arrived.at[ctx]
    )

    @pl.loop(0, n_ctx + 3)
    def _(tick):
        @pl.when(tick < n_ctx)
        def _():
            dispatch(tick)

        @pl.when(tick == n_ctx - 1)
        def _():
            dealt_kept.start()
            for offset in range(1, n_ctx):
                dealt_copy(offset).start()

        @pl.when((tick >= 1) & (tick <= n_ctx))
        def _():
            compute(tick - 1)

        @pl.when(tick >= 3)
        def _():
            combine(lax.rem(tick - 2, n_ctx))

    pltpu.make_async_copy(held.at[ctx], part_ref.at[ctx], part_arrived.at[ctx]).wait()
    for step in range(1, n_ctx):
        other = along(step)
        copy = push(
            held.at[other], part_ref.at[other], part_send.at[step], part_arrived.at[other], (other, fsdp)
        )
        copy.wait()
        held_copy(step).wait_send()
    dealt_kept.wait()
    for offset in range(1, n_ctx):
        other = along(offset)
        push(
            dealt_ref.at[other],
            dealt_all.at[other],
            dealt_send.at[offset],
            dealt_arrived.at[other],
            (other, fsdp),
        ).wait()
    for step in range(n_ctx):
        for offset in range(1, n_fsdp):
            back_copy(step, along(step), offset).wait_send()
    for copy in outputs(along(n_ctx - 1)):
        copy.wait()


def run_expert_exchange(n_ctx, n_fsdp, x, select, select_t, gate, up, down, grads, dealt):
    anywhere, inside = pl.BlockSpec(memory_space=pl.ANY), pl.BlockSpec(memory_space=pltpu.VMEM)
    span, wide = x.shape
    width, hidden = gate.shape
    capacity = grads.shape[2]
    slots = (n_fsdp, n_ctx, capacity)
    one = (n_fsdp, capacity)
    dma, vmem, shape = pltpu.SemaphoreType.DMA, pltpu.VMEM, jax.ShapeDtypeStruct
    return pl.pallas_call(
        functools.partial(expert_exchange, n_ctx, n_fsdp),
        in_specs=[anywhere, inside, inside] + [anywhere] * 5,
        out_specs=[anywhere] * 9,
        out_shape=[
            shape(slots + (wide,), BF),
            shape((n_ctx, n_fsdp, capacity, wide), BF),
            shape((n_ctx, span, wide), BF),
            shape(slots + (hidden,), BF),
            shape(slots + (hidden,), BF),
            shape(slots + (hidden,), BF),
            shape(slots + (width // 2,), BF),
            shape(slots + (width // 2,), BF),
            shape(dealt.shape, BF),
        ],
        scratch_shapes=[
            vmem((width, hidden), BF),
            vmem((width, hidden), BF),
            vmem((hidden, width), BF),
            vmem((n_ctx, span, wide), BF),
            vmem((n_ctx,) + one + (wide,), BF),
            vmem(one + (wide,), BF),
            vmem(one + (width,), BF),
            vmem(one + (hidden,), BF),
            vmem(one + (hidden,), BF),
            vmem(one + (hidden,), BF),
            vmem(one + (width,), BF),
            vmem(one + (wide,), BF),
            dma((3,)),
            dma((3,)),
            dma((n_ctx,)),
            dma((n_ctx,)),
            dma((n_ctx, n_fsdp)),
            dma((n_ctx, n_fsdp)),
            dma((n_ctx, n_fsdp)),
            dma((n_ctx, n_fsdp)),
            dma((n_ctx,)),
            dma((n_ctx,)),
            dma((n_ctx,)),
            dma((n_ctx,)),
            dma((5,)),
        ],
        compiler_params=pltpu.CompilerParams(
            collective_id=2, has_side_effects=True, vmem_limit_bytes=60 * 2**20
        ),
        cost_estimate=pl.CostEstimate(
            flops=12 * n_fsdp * n_ctx * capacity * width * hidden,
            bytes_accessed=600 * 2**20,
            transcendentals=0,
        ),
    )(x, select, select_t, gate, up, down, grads, dealt)


def last_reduce(n_ctx, n_fsdp, *refs):
    ctx, fsdp = lax.axis_index("ctx"), lax.axis_index("fsdp")
    count = (len(refs) - 1) // 11
    ins, alls, local, refs = refs[:count], refs[count : 2 * count], refs[2 * count], refs[2 * count + 1 :]
    items = [refs[9 * i : 9 * i + 9] for i in range(count)]
    chips, chip, core = n_fsdp // 2, fsdp // 2, lax.rem(fsdp, 2)
    sibling = chip * 2 + 1 - core

    def along(offset):
        return lax.rem(ctx + offset, n_ctx)

    def other_chip(offset):
        return lax.rem(chip + offset, chips)

    greet(
        [(along(i), fsdp) for i in range(1, n_ctx)]
        + [(ctx, other_chip(i) * 2 + core) for i in range(1, chips)]
        + [(ctx, sibling)]
    )
    crossing, loads, lines = [], [], []
    for at, (in_ref, all_ref, item) in enumerate(zip(ins, alls, items)):
        mine, beside, landed, own, cross, sends, arrived, line_sems, line_arrived = item
        crossing.append(
            push(in_ref.at[:, 1 - core], beside, cross.at[0], cross.at[1], (ctx, sibling))
        )
        crossing[-1].start()
        loads.append(pltpu.make_async_copy(in_ref.at[:, core], mine, local.at[at]))
        loads[-1].start()
        lines.append(
            LineGather(
                n_ctx, ctx, fsdp, own, all_ref, line_sems.at[0], line_sems.at[1], line_arrived
            )
        )

    def chip_copy(item, offset):
        mine, beside, landed, own, cross, sends, arrived, line_sems, line_arrived = item
        to = other_chip(offset)
        return push(
            mine.at[to], landed.at[chip], sends.at[offset], arrived.at[chip], (ctx, to * 2 + core)
        )

    for crossed, loaded, item in zip(crossing, loads, items):
        mine, beside = item[:2]
        loaded.wait()
        crossed.wait_recv()
        for offset in range(1, chips + 1):
            to = other_chip(offset)
            mine[to] = (mine[to].astype(F32) + beside[to].astype(F32)).astype(BF)
            if offset < chips:
                chip_copy(item, offset).start()
    keeps = []
    for at, (item, line, all_ref) in enumerate(zip(items, lines, alls)):
        mine, beside, landed, own, cross, sends, arrived, line_sems, line_arrived = item
        total = mine[chip].astype(F32)
        for offset in range(1, chips):
            source = other_chip(offset)
            push(
                mine.at[source], landed.at[source], sends.at[offset], arrived.at[source], (ctx, sibling)
            ).wait_recv()
            total = total + landed[source].astype(F32)
        own[...] = total.astype(BF)
        line.step(0)
        keeps.append(pltpu.make_async_copy(own, all_ref.at[ctx], local.at[at]))
        keeps[-1].start()
    for step in range(1, n_ctx):
        for line in lines:
            line.step(step)
    for crossed, keep, line, item in zip(crossing, keeps, lines, items):
        crossed.wait_send()
        keep.wait()
        line.finish()
        for offset in range(1, chips):
            chip_copy(item, offset).wait_send()


def run_last_reduce(n_ctx, n_fsdp, grads):
    anywhere = pl.BlockSpec(memory_space=pl.ANY)
    dma, vmem, shape = pltpu.SemaphoreType.DMA, pltpu.VMEM, jax.ShapeDtypeStruct
    chips = n_fsdp // 2
    grads = [grad.reshape((chips, 2, -1) + grad.shape[-1:]) for grad in grads]
    blocks = [grad.shape[2:] for grad in grads]
    scratch = [dma((len(grads),))]
    for block in blocks:
        scratch += [
            vmem((chips,) + block, BF),
            vmem((chips,) + block, BF),
            vmem((chips,) + block, BF),
            vmem(block, BF),
            dma((2,)),
            dma((chips,)),
            dma((chips,)),
            dma((2, n_ctx)),
            dma((n_ctx,)),
        ]
    return pl.pallas_call(
        functools.partial(last_reduce, n_ctx, n_fsdp),
        in_specs=[anywhere] * len(grads),
        out_specs=[anywhere] * len(grads),
        out_shape=[shape((n_ctx,) + block, BF) for block in blocks],
        scratch_shapes=scratch,
        compiler_params=pltpu.CompilerParams(
            collective_id=3, has_side_effects=True, vmem_limit_bytes=60 * 2**20
        ),
        cost_estimate=pl.CostEstimate(flops=0, bytes_accessed=400 * 2**20, transcendentals=0),
    )(*grads)


def finish(
    n_ctx,
    share,
    experts,
    shared_ref,
    rest_ref,
    out_ref,
    dh_ref,
    x_ref,
    resid_grad_ref,
    resid_ref,
    moe_low_ref,
    moe_high_ref,
    gain_ref,
    query_ref,
    key_ref,
    value_ref,
    out_grad_ref,
    input_grad_ref,
    output_ref,
    router_ref,
    gains_ref,
):
    q_width = shared_ref.shape[2] - 2 * HEAD_SIZE
    for block in range(n_ctx):
        query_ref[:, block * q_width : (block + 1) * q_width] = shared_ref[
            block, :, :q_width
        ].astype(F32)
    for target, at in ((key_ref, q_width), (value_ref, q_width + HEAD_SIZE)):
        for kv in range(KEY_VALUE_HEADS):
            total = shared_ref[kv * share, :, at : at + HEAD_SIZE].astype(F32)
            for block in range(kv * share + 1, (kv + 1) * share):
                total = total + shared_ref[block, :, at : at + HEAD_SIZE].astype(F32)
            target[:, kv * HEAD_SIZE : (kv + 1) * HEAD_SIZE] = total
    out_grad_ref[...] = out_ref[0].astype(F32)
    x = x_ref[...].astype(F32)
    r = inverse_rms(x)
    n = dh_ref[...].astype(F32) * gain_ref[...]
    input_grad_ref[...] = (
        resid_grad_ref[...] + r * n - x * (r * r * r) * jnp.mean(n * x, axis=-1, keepdims=True)
    ).astype(BF)
    half = resid_ref.shape[1] // 2
    output_ref[:, :half] = (resid_ref[:, :half] + moe_low_ref[...].astype(F32)).astype(BF)
    output_ref[:, half:] = (resid_ref[:, half:] + moe_high_ref[...].astype(F32)).astype(BF)

    @pl.when(pl.program_id(0) == n_ctx - 1)
    def _():
        rest = rest_ref[0].astype(F32)
        for block in range(1, n_ctx):
            rest = rest + rest_ref[block].astype(F32)
        router_ref[...] = rest[:, :experts]
        gains_ref[...] = rest.T[experts : experts + 8]


def run_finish(
    n_ctx, experts, shared, rest, out_grad, d_hidden, x, resid_grad, resid, moe_low, moe_high, gain
):
    _, rows, wide = shared.shape
    span, width = x.shape
    _, piece, _ = out_grad.shape
    shape = jax.ShapeDtypeStruct
    part, tokens = rows // n_ctx, span // n_ctx
    whole = lambda dims: pl.BlockSpec(dims, lambda i: (0,) * len(dims))
    by_rows = lambda count, columns: pl.BlockSpec((count, columns), lambda i: (i, 0))
    q_columns, kv_columns = QUERY_HEADS * HEAD_SIZE, KEY_VALUE_HEADS * HEAD_SIZE
    return pl.pallas_call(
        functools.partial(finish, n_ctx, n_ctx // KEY_VALUE_HEADS, experts),
        grid=(n_ctx,),
        in_specs=[
            pl.BlockSpec((n_ctx, part, wide), lambda i: (0, i, 0)),
            whole(rest.shape),
            pl.BlockSpec((1, piece, width), lambda i: (i, 0, 0)),
        ]
        + [by_rows(tokens, width)] * 4
        + [by_rows(tokens, width // 2)] * 2
        + [whole((1, width))],
        out_specs=[
            by_rows(part, q_columns),
            by_rows(part, kv_columns),
            by_rows(part, kv_columns),
            by_rows(piece, width),
            by_rows(tokens, width),
            by_rows(tokens, width),
            whole((rows, experts)),
            whole((8, rows)),
        ],
        out_shape=[
            shape((rows, q_columns), F32),
            shape((rows, kv_columns), F32),
            shape((rows, kv_columns), F32),
            shape((n_ctx * piece, width), F32),
            shape((span, width), BF),
            shape((span, width), BF),
            shape((rows, experts), F32),
            shape((8, rows), F32),
        ],
        compiler_params=pltpu.CompilerParams(vmem_limit_bytes=48 * 2**20),
    )(shared, rest, out_grad, d_hidden, x, resid_grad, resid, moe_low, moe_high, gain)


def attention_exchange(
    n_ctx,
    n_fsdp,
    heads,
    q_ref,
    k_ref,
    v_ref,
    cos_ref,
    sin_ref,
    gains_ref,
    own_ref,
    key_ref,
    sel_ref,
    grad_ref,
    out_ref,
    total_ref,
    dealt_ref,
    attn_ref,
    rows_ref,
    keys,
    values_t,
    mixed,
    w_out,
    held,
    low,
    high,
    grads,
    staged,
    local,
    grad_up,
    grad_down,
    grad_arrived,
    rows_send,
    rows_arrived,
    up_send,
    down_send,
    low_arrived,
    high_arrived,
):
    head = pl.program_id(0)
    ctx, fsdp = lax.axis_index("ctx"), lax.axis_index("fsdp")
    _, span, width = held.shape
    capacity = staged.shape[2]
    q_width = heads * HEAD_SIZE

    def along(offset):
        return lax.rem(ctx + offset, n_ctx)

    def around(offset):
        return lax.rem(fsdp + offset, n_fsdp)

    line = LineGather(n_ctx, ctx, fsdp, grad_ref, grads, grad_up, grad_down, grad_arrived)
    sums = LineScatter(
        n_ctx, ctx, fsdp, 4, held, low, high, up_send, down_send, low_arrived, high_arrived
    )
    own = pltpu.make_async_copy(grad_ref, grads.at[ctx], local.at[0])
    weights = pltpu.make_async_copy(
        out_ref.at[pl.ds(ctx * q_width, q_width)], w_out, local.at[1]
    )

    def rows_copy(group, offset):
        to = around(offset)
        return push(
            staged.at[group, to],
            rows_ref.at[fsdp, group],
            rows_send.at[group, offset],
            rows_arrived.at[group, fsdp],
            (ctx, to),
        )

    def rows_kept(group):
        return pltpu.make_async_copy(
            staged.at[group, fsdp], rows_ref.at[fsdp, group], rows_arrived.at[group, fsdp]
        )

    def pick(group):
        for at in range(0, width, TILE):
            picked = nn(sel_ref[group], grads[group, :, at : at + TILE])
            staged[group, :, :, at : at + TILE] = picked.astype(BF).reshape(n_fsdp, capacity, TILE)
        rows_kept(group).start()
        for offset in range(1, n_fsdp):
            rows_copy(group, offset).start()

    def pick_from(distance):
        @pl.when(ctx - distance >= 0)
        def _():
            pick(ctx - distance)

        @pl.when(ctx + distance < n_ctx)
        def _():
            pick(ctx + distance)

    @pl.when(head == 0)
    def _():
        own.start()
        weights.start()
        greet(
            [(along(i), fsdp) for i in range(1, n_ctx)]
            + [(ctx, around(i)) for i in range(1, n_fsdp)]
        )
        line.step(0)
        own.wait()
        pick(ctx)
        prepare_keys(k_ref, v_ref, cos_ref, sin_ref, gains_ref, keys, values_t)

    @pl.when(head < heads)
    def _():
        def store(start, count, out):
            columns = pl.ds(pl.multiple_of(head * HEAD_SIZE, HEAD_SIZE), HEAD_SIZE)
            mixed[start : start + count, columns] = out

        attend_head(
            q_ref,
            cos_ref,
            sin_ref,
            gains_ref,
            own_ref,
            key_ref,
            total_ref,
            dealt_ref,
            keys,
            values_t,
            store,
        )

    @pl.when(head == heads - 2)
    def _():
        line.step(1)
        pick_from(1)

    @pl.when(head == heads)
    def _():
        weights.wait()
        for block in range(n_ctx):
            for at in range(0, width, TILE):
                held[block, :, at : at + TILE] = nn(
                    mixed[block * span : (block + 1) * span, :], w_out[:, at : at + TILE]
                ).astype(BF)
        line.step(2)
        sums.scatter(0)
        pick_from(2)
        sums.scatter(1)
        for step in range(3, n_ctx):
            line.step(step)
            pick_from(step)
        sums.scatter(2)
        sums.scatter(3)
        for chunk in range(4):
            sums.settle(chunk, attn_ref)
        sums.finish()
        line.finish()
        for group in range(n_ctx):
            rows_kept(group).wait()
            for offset in range(1, n_fsdp):
                source = around(offset)
                push(
                    staged.at[group, source],
                    rows_ref.at[source, group],
                    rows_send.at[group, offset],
                    rows_arrived.at[group, source],
                    (ctx, source),
                ).wait()


def run_attention_exchange(
    qkv, heads, n_ctx, n_fsdp, cosine, sine, gains, own, key_blocks, select, grad, w_out
):
    length = qkv.shape[0]
    span, width = grad.shape
    capacity = select.shape[1] // n_fsdp
    anywhere = pl.BlockSpec(memory_space=pl.ANY)
    dma, vmem, shape = pltpu.SemaphoreType.DMA, pltpu.VMEM, jax.ShapeDtypeStruct
    last = heads - 1
    whole, column, _, _, shared = attention_specs(heads, length)
    clip = lambda h: jnp.minimum(h, last)
    return pl.pallas_call(
        functools.partial(attention_exchange, n_ctx, n_fsdp, heads),
        grid=(heads + 1,),
        in_specs=[
            pl.BlockSpec((length, HEAD_SIZE), lambda h: (0, clip(h))),
            column(heads),
            column(heads + 1),
        ]
        + shared
        + [whole(select.shape), anywhere, anywhere],
        out_specs=[
            pl.BlockSpec((1, 8, length), lambda h: (clip(h), 0, 0)),
            pl.BlockSpec(
                (1, length, HEAD_SIZE),
                lambda h: (lax.rem(clip(h), n_ctx), 0, lax.div(clip(h), n_ctx)),
            ),
            whole((span, width)),
            anywhere,
        ],
        out_shape=[
            shape((heads, 8, length), F32),
            shape((n_ctx, length, heads // n_ctx * HEAD_SIZE), BF),
            shape((span, width), F32),
            shape((n_fsdp, n_ctx, capacity, width), BF),
        ],
        scratch_shapes=[
            vmem((length, HEAD_SIZE), BF),
            vmem((HEAD_SIZE, length), BF),
            vmem((length, heads * HEAD_SIZE), BF),
            vmem((heads * HEAD_SIZE, width), BF),
            vmem((n_ctx, span, width), BF),
            vmem((n_ctx, span, width), BF),
            vmem((n_ctx, span, width), BF),
            vmem((n_ctx, span, width), BF),
            vmem((n_ctx, n_fsdp, capacity, width), BF),
            dma((2,)),
            dma((n_ctx,)),
            dma((n_ctx,)),
            dma((n_ctx,)),
            dma((n_ctx, n_fsdp)),
            dma((n_ctx, n_fsdp)),
            dma((n_ctx, 4)),
            dma((n_ctx, 4)),
            dma((n_ctx, 4)),
            dma((n_ctx, 4)),
        ],
        compiler_params=pltpu.CompilerParams(
            collective_id=4, has_side_effects=True, vmem_limit_bytes=60 * 2**20
        ),
        cost_estimate=pl.CostEstimate(
            flops=4 * heads * length * length * HEAD_SIZE,
            bytes_accessed=400 * 2**20,
            transcendentals=heads * length * length,
        ),
    )(qkv, qkv, qkv, cosine, sine, gains, own, key_blocks, select, grad, w_out)


def on_device(
    inputs,
    block_ids,
    expert_ids,
    drop_order,
    attn_gain,
    w_query,
    key_projection_weight,
    value_projection_weight,
    q_gain,
    key_norm_gain,
    w_out,
    ffn_gain,
    w_router,
    expert_gate,
    expert_up,
    expert_down,
    cotangent,
):
    n_ctx, n_fsdp = lax.axis_size("ctx"), lax.axis_size("fsdp")
    ctx = lax.axis_index("ctx")
    span, width = inputs.shape[1], inputs.shape[2]
    length = block_ids.shape[1]
    experts = n_ctx * n_fsdp
    capacity = 5 * span * TOP // (4 * experts)
    slots = experts * capacity
    heads = QUERY_HEADS // n_ctx
    share = n_ctx // KEY_VALUE_HEADS
    own_rows = w_query.shape[0]
    q_width = heads * HEAD_SIZE
    qkv_width = q_width + 2 * HEAD_SIZE
    extra_width = -(-(experts + 8) // 128) * 128

    def gather_ctx(array):
        return lax.all_gather(array, "ctx", axis=0, tiled=True)

    def scatter_ctx(array):
        return lax.psum_scatter(array.astype(BF), "ctx", scatter_dimension=0, tiled=True)

    def route(rows):
        return lax.all_to_all(rows, "fsdp", split_axis=0, concat_axis=0, tiled=True)

    def columns(weight, index, count):
        return lax.dynamic_slice_in_dim(weight, index * count, count, axis=1)

    def as_column(vector):
        return jnp.pad(vector, (0, own_rows - vector.shape[0]))[:, None]

    packed = jnp.concatenate(
        [
            columns(w_query, ctx, q_width),
            columns(key_projection_weight, ctx // share, HEAD_SIZE),
            columns(value_projection_weight, ctx // share, HEAD_SIZE),
            w_router,
            as_column(attn_gain),
            as_column(ffn_gain),
            as_column(q_gain),
            as_column(key_norm_gain),
            jnp.zeros((own_rows, extra_width - experts - 4), BF),
        ],
        axis=1,
    )
    table = jnp.concatenate(
        [expert_ids[0].T, drop_order[0], jnp.zeros((7, span), jnp.int32)], axis=0
    )
    inputs_all, tables, packed_all = run_first_gather(n_ctx, n_fsdp, inputs[0], table, packed)
    out_all = lax.all_gather(w_out, "fsdp", axis=0, tiled=True)
    out_here = lax.dynamic_slice_in_dim(out_all, ctx * q_width, q_width, axis=0)
    inputs_all = inputs_all.reshape(length, width)
    packed_all = packed_all.reshape(width, qkv_width + extra_width)
    w_qkv = packed_all[:, :qkv_width]
    extra = packed_all[:, qkv_width:].T
    router_t = extra[:experts]
    gain_attn = extra[experts : experts + 1].astype(F32)
    gain_ffn = extra[experts + 1 : experts + 2].astype(F32)

    def head_gain(at):
        return extra[at].reshape(n_fsdp, own_rows)[:, : HEAD_SIZE // n_fsdp].reshape(1, HEAD_SIZE)

    gains = jnp.concatenate(
        [head_gain(experts + 2), head_gain(experts + 3), jnp.zeros((6, HEAD_SIZE), BF)], axis=0
    ).astype(F32)

    named = tables[:, :TOP, :]
    ranks = tables[:, TOP, :]
    here = ctx * n_fsdp + jnp.arange(n_fsdp, dtype=jnp.int32)
    member = jnp.any(named[:, :, None, :] == here[None, None, :, None], axis=1)
    before = (ranks[:, :, None] < ranks[:, None, :]).astype(BF)
    place = jnp.einsum(
        "gjs,gst->gjt", member.astype(BF), before, preferred_element_type=F32
    ).astype(jnp.int32)
    place = jnp.where(member, place, capacity)
    select = (
        place[:, :, None, :] == jnp.arange(capacity, dtype=jnp.int32)[None, None, :, None]
    ).astype(BF)

    fused = capacity % 16 == 0 and 2 * experts <= AUX and experts == QUERY_HEADS
    select_rows = select.reshape(n_ctx, n_fsdp * capacity, span)

    def dispatch(rows):
        picked = jnp.einsum(
            "gjkt,gtd->jgkd", select, rows.reshape(n_ctx, span, width), preferred_element_type=F32
        ).astype(BF)
        return route(picked).reshape(slots, width)

    def combine(rows):
        return gather_slots(route(rows.reshape(n_fsdp, n_ctx, capacity, width)))

    def gather_slots(back):
        return jnp.einsum("gjkt,jgkd->gtd", select, back, preferred_element_type=F32).reshape(
            length, -1
        )

    x_all = inputs_all.astype(F32)
    r_all = inverse_rms(x_all)
    hidden = (x_all * r_all * gain_attn).astype(BF)
    qkv = nn(hidden, w_qkv)
    exponent = np.arange(HALF, dtype=np.float32) * np.float32(2.0 / HEAD_SIZE)
    angles = np.arange(length, dtype=np.float32)[:, None] * (
        np.float32(ROPE_BASE) ** (-exponent)
    )
    cosine = jnp.asarray(np.tile(np.cos(angles), (1, 2)))
    sine = jnp.asarray(np.concatenate([-np.sin(angles), np.sin(angles)], axis=1))
    own_blocks = jnp.broadcast_to(block_ids, (8, length))
    key_blocks = block_ids.reshape(length, 1)
    piece = QUERY_HEADS * HEAD_SIZE // experts
    groups = n_fsdp // n_ctx
    if fused:
        totals, dealt, attn_out, grad_rows = run_attention_exchange(
            qkv,
            heads,
            n_ctx,
            n_fsdp,
            cosine,
            sine,
            gains,
            own_blocks,
            key_blocks,
            select_rows,
            cotangent[0],
            out_all,
        )
        grad_rows = grad_rows.reshape(slots, width)
    else:
        mixed, totals, _ = run_attention(
            qkv, heads, n_ctx, cosine, sine, gains, own_blocks, key_blocks
        )
        attn_out = scatter_ctx(nn(mixed, out_here))
        grad_rows = dispatch(gather_ctx(cotangent[0]))
        dealt = mixed.reshape(length, groups, n_ctx, piece).transpose(2, 0, 1, 3)
        dealt = dealt.reshape(n_ctx, length, groups * piece)

    x = inputs[0].astype(F32)
    resid = x + attn_out.astype(F32)
    r_ffn = inverse_rms(resid)
    normed = (resid * r_ffn * gain_ffn).astype(BF)
    if fused:
        chosen = jnp.any(
            expert_ids[0][:, :, None] == jnp.arange(experts, dtype=jnp.int32), axis=1
        )
        logits = nt(normed, router_t)
        gates = jax.nn.softmax(jnp.where(chosen, logits, -jnp.inf), axis=-1)
        high = lax.reduce_precision(gates, 8, 7)
        payload = jnp.concatenate(
            [
                normed,
                high.astype(BF),
                (gates - high).astype(BF),
                jnp.zeros((span, AUX - 2 * experts), BF),
            ],
            axis=1,
        )
        rows, _, parts, inner_low, dg, du, y_low, y_high, dealt = run_expert_exchange(
            n_ctx,
            n_fsdp,
            payload,
            select_rows,
            select_rows.swapaxes(1, 2),
            expert_gate[0],
            expert_up[0],
            expert_down[0],
            grad_rows.reshape(n_fsdp, n_ctx, capacity, width),
            dealt,
        )
        rows = rows.reshape(slots, width + AUX)[:, :width]
        inner_low, dg, du = (array.reshape(slots, -1) for array in (inner_low, dg, du))
        parts = jnp.sum(parts.astype(F32), axis=0)
        d_gates = parts[:, width : width + experts] + parts[:, width + experts : width + 2 * experts]
        d_logits = gates * (d_gates - jnp.sum(gates * d_gates, axis=-1, keepdims=True))
        d_logits = d_logits.astype(BF)
        d_normed = parts[:, :width] + nn(d_logits, router_t)
    else:
        dealt = lax.all_to_all(dealt, "ctx", split_axis=0, concat_axis=0, tiled=True)
        chosen = jnp.any(
            named[:, :, :, None] == jnp.arange(experts, dtype=jnp.int32), axis=1
        ).reshape(length, experts)
        normed = gather_ctx(normed)
        normed, grad_rows = lax.optimization_barrier((normed, grad_rows))
        grad_inner = nt(grad_rows, expert_down[0])
        logits = nt(normed, router_t)
        gates = jax.nn.softmax(jnp.where(chosen, logits, -jnp.inf), axis=-1)
        gates_here = lax.dynamic_slice_in_dim(gates, ctx * n_fsdp, n_fsdp, axis=1)
        gates_here = gates_here.reshape(n_ctx, span, n_fsdp).transpose(0, 2, 1)
        slot_gates = jnp.sum(select.astype(F32) * gates_here[:, :, None, :], axis=-1)
        slot_gates = route(slot_gates.transpose(1, 0, 2)).reshape(slots, 1)
        rows = dispatch(normed)
        g = nn(rows, expert_gate[0])
        u = nn(rows, expert_up[0])
        s = jax.nn.sigmoid(g)
        inner = g * s * u
        slot_dgates = jnp.sum(inner * grad_inner, axis=-1).reshape(n_fsdp, n_ctx, capacity)
        d_inner = grad_inner * slot_gates
        dg = (d_inner * u * s * (1.0 + g * (1.0 - s))).astype(BF)
        du = (d_inner * g * s).astype(BF)
        d_rows = (nt(dg, expert_gate[0]) + nt(du, expert_up[0])).astype(BF)
        y = (nn(inner.astype(BF), expert_down[0]) * slot_gates).astype(BF)
        y = y.reshape(n_fsdp, n_ctx, capacity, width)
        y_low, y_high = y[..., : width // 2], y[..., width // 2 :]
        inner_low = (inner * slot_gates).astype(BF)
        d_gates = jnp.einsum(
            "gjkt,jgk->gjt", select.astype(F32), route(slot_dgates), precision=lax.Precision.HIGHEST
        )
        weighted = (d_gates * gates_here).transpose(0, 2, 1).reshape(length, n_fsdp)
        d_logits = lax.dynamic_update_slice_in_dim(
            jnp.zeros((length, experts), F32), weighted, ctx * n_fsdp, axis=1
        ) - gates * jnp.sum(weighted, axis=1, keepdims=True)
        d_logits = d_logits.astype(BF)
        d_normed = scatter_ctx(combine(d_rows) + nn(d_logits, router_t)).astype(F32)

    gate_grad = tn(rows, dg)
    up_grad = tn(rows, du)
    down_grad = tn(inner_low, grad_rows)
    router_grad = tn(normed, d_logits)

    grad = cotangent[0].astype(F32)
    n = d_normed * gain_ffn
    d_resid = grad + r_ffn * n - resid * r_ffn**3 * jnp.mean(n * resid, axis=-1, keepdims=True)
    ffn_gain_grad = jnp.sum(d_normed * resid * r_ffn, axis=0)
    d_attn = gather_ctx(d_resid.astype(BF))
    y_low, y_high = route(y_low), route(y_high)
    y_low, d_attn = lax.optimization_barrier((gather_slots(y_low).astype(BF), d_attn))
    moe_low = scatter_ctx(y_low)
    d_mixed = nt(d_attn, out_here).astype(BF)
    out_grad = jnp.einsum("ntk,td->nkd", dealt, d_attn, preferred_element_type=F32).astype(BF)
    y_high, d_mixed, out_grad, gate_grad, up_grad, down_grad = lax.optimization_barrier(
        (y_high, d_mixed, out_grad, gate_grad, up_grad, down_grad)
    )
    y_high = gather_slots(y_high).astype(BF)
    y_high, d_mixed, moe_low = lax.optimization_barrier((y_high, d_mixed, moe_low))
    moe_high = scatter_ctx(y_high)

    dq, dkv, dgains = run_attention_back(
        qkv, d_mixed, totals, heads, cosine, sine, gains, own_blocks, key_blocks
    )
    d_qkv = jnp.concatenate([dq, dkv], axis=1)
    d_hidden = nt(d_qkv, w_qkv)
    attn_gain_grad = jnp.sum(d_hidden * x_all * r_all, axis=0)

    def spread(vector):
        parts = vector.reshape(n_fsdp, HEAD_SIZE // n_fsdp)
        return jnp.pad(parts, ((0, 0), (0, own_rows - parts.shape[1]))).reshape(width)

    small = jnp.stack(
        [attn_gain_grad, ffn_gain_grad, spread(dgains[0]), spread(dgains[1])], axis=1
    )
    extra_grad = jnp.concatenate(
        [
            router_grad.astype(BF),
            small.astype(BF),
            jnp.zeros((width, extra_width - experts - 4), BF),
        ],
        axis=1,
    )
    shared_grad = tn(hidden, d_qkv).astype(BF)
    d_hidden, moe_high, shared_grad, out_grad = lax.optimization_barrier(
        (d_hidden.astype(BF), moe_high, shared_grad, out_grad)
    )
    d_hidden = scatter_ctx(d_hidden)
    shared_grad, rest, out_grad = run_last_reduce(
        n_ctx, n_fsdp, [shared_grad, extra_grad, out_grad.reshape(n_fsdp * piece, width)]
    )
    query_grad, key_grad, value_grad, out_grad, input_grad, output, router_grad, gain_grads = (
        run_finish(
            n_ctx,
            experts,
            shared_grad,
            rest,
            out_grad,
            d_hidden,
            inputs[0],
            d_resid,
            resid,
            moe_low,
            moe_high,
            gain_attn,
        )
    )
    head_rows = HEAD_SIZE // n_fsdp
    return (
        output[None],
        input_grad[None],
        gain_grads[0],
        query_grad,
        key_grad,
        value_grad,
        gain_grads[2, :head_rows],
        gain_grads[3, :head_rows],
        out_grad,
        gain_grads[1],
        router_grad,
        gate_grad[None],
        up_grad[None],
        down_grad[None],
    )


def solution(mesh):
    rows, tokens = P("fsdp", None), P("fsdp", "ctx", None)
    vector, expert = P("fsdp"), P(("ctx", "fsdp"), None, None)
    in_specs = (
        tokens,
        rows,
        tokens,
        tokens,
        vector,
        rows,
        rows,
        rows,
        vector,
        vector,
        rows,
        vector,
        rows,
        expert,
        expert,
        expert,
        tokens,
    )
    out_specs = (
        tokens,
        tokens,
        vector,
        rows,
        rows,
        rows,
        vector,
        vector,
        rows,
        vector,
        rows,
        expert,
        expert,
        expert,
    )
    return jax.shard_map(
        on_device, mesh=mesh, in_specs=in_specs, out_specs=out_specs, check_vma=False
    )
```

```python
import functools

import jax
import jax.numpy as jnp
import numpy as np
from jax import lax
from jax.experimental import pallas as pl
from jax.experimental.pallas import tpu as pltpu
from jax.sharding import PartitionSpec as P

QUERY_HEADS = 32
KEY_VALUE_HEADS = 4
HEAD_SIZE = 128
TOP = 8

EPSILON = 1e-06
ROPE_BASE = 1000000.0
MASKED = -1000000000.0
SCALE = HEAD_SIZE ** (-0.5)
HALF = HEAD_SIZE // 2
BF = jnp.bfloat16
F32 = jnp.float32


def nt(a, b):
    return lax.dot_general(a, b, (((1,), (1,)), ((), ())), preferred_element_type=F32)


def nn(a, b):
    return lax.dot_general(a, b, (((1,), (0,)), ((), ())), preferred_element_type=F32)


def tn(a, b):
    return lax.dot_general(a, b, (((0,), (0,)), ((), ())), preferred_element_type=F32)


def inverse_rms(values):
    return lax.rsqrt(jnp.mean(values * values, axis=-1, keepdims=True) + EPSILON)


def norm_rope(raw, gain, cosine, sine):
    z = raw * inverse_rms(raw) * gain
    return z * cosine + pltpu.roll(z, HALF, 1) * sine


def norm_rope_back(raw, gain, cosine, sine, grad):
    dz = grad * cosine - pltpu.roll(grad, HALF, 1) * sine
    r = inverse_rms(raw)
    n = dz * gain
    d_raw = r * n - raw * (r * r * r) * jnp.mean(n * raw, axis=-1, keepdims=True)
    return d_raw, jnp.sum(dz * raw * r, axis=0, keepdims=True)


def prepare_keys(k_ref, v_ref, cos_ref, sin_ref, gains_ref, keys, values_t):
    rotated = norm_rope(k_ref[...], gains_ref[1:2, :], cos_ref[...], sin_ref[...])
    keys[...] = rotated.astype(BF)
    values_t[...] = v_ref[...].T.astype(BF)


def attend_head(
    q_ref, cos_ref, sin_ref, gains_ref, own_ref, key_ref, total_ref, dealt_ref, keys, values_t, store
):
    queries = norm_rope(q_ref[...], gains_ref[0:1, :], cos_ref[...], sin_ref[...]).astype(BF)
    length = queries.shape[0]
    chunk = 256
    for start in range(0, length, chunk):
        scores = nt(keys[...], queries[start : start + chunk]) * SCALE
        seen = key_ref[...] <= own_ref[0:1, start : start + chunk]
        scores = jnp.where(seen, scores, MASKED)
        top = jnp.max(scores, axis=0, keepdims=True)
        weights = jnp.exp(scores - top)
        total = jnp.sum(weights, axis=0, keepdims=True)
        out = (nn(values_t[...], weights.astype(BF)) / total).T.astype(BF)
        store(start, chunk, out)
        dealt_ref[0, start : start + chunk, :] = out
        total_ref[0, :, start : start + chunk] = jnp.broadcast_to(top + jnp.log(total), (8, chunk))


def attention_forward(
    q_ref,
    k_ref,
    v_ref,
    cos_ref,
    sin_ref,
    gains_ref,
    own_ref,
    key_ref,
    mixed_ref,
    total_ref,
    dealt_ref,
    keys,
    values_t,
):
    @pl.when(pl.program_id(0) == 0)
    def _():
        prepare_keys(k_ref, v_ref, cos_ref, sin_ref, gains_ref, keys, values_t)

    def store(start, count, out):
        mixed_ref[start : start + count, :] = out

    attend_head(
        q_ref, cos_ref, sin_ref, gains_ref, own_ref, key_ref, total_ref, dealt_ref, keys, values_t, store
    )


def attention_backward(
    heads,
    q_ref,
    k_ref,
    v_ref,
    grad_ref,
    total_ref,
    cos_ref,
    sin_ref,
    gains_ref,
    own_ref,
    key_ref,
    dq_ref,
    dkv_ref,
    dgain_ref,
    keys,
    keys_t,
    values,
    dk,
    dv,
):
    cosine, sine = cos_ref[...], sin_ref[...]
    head = pl.program_id(0)

    @pl.when(head == 0)
    def _():
        rotated = norm_rope(k_ref[...], gains_ref[1:2, :], cosine, sine)
        keys[...] = rotated.astype(BF)
        keys_t[...] = rotated.T.astype(BF)
        values[...] = v_ref[...].astype(BF)
        dk[...] = jnp.zeros_like(dk)
        dv[...] = jnp.zeros_like(dv)
        dgain_ref[...] = jnp.zeros_like(dgain_ref)

    queries = norm_rope(q_ref[...], gains_ref[0:1, :], cosine, sine).astype(BF)
    length = queries.shape[0]
    chunk = 256
    for start in range(0, length, chunk):
        rows = slice(start, start + chunk)
        q_part = queries[rows]
        grad = grad_ref[rows, :]
        scores = nt(keys[...], q_part) * SCALE
        seen = key_ref[...] <= own_ref[0:1, rows]
        scores = jnp.where(seen, scores, MASKED)
        weights = jnp.exp(scores - total_ref[0, 0:1, rows])
        d_weights = nt(values[...], grad)
        row_dot = jnp.sum(weights * d_weights, axis=0, keepdims=True)
        d_scores = (weights * (d_weights - row_dot)).astype(BF)
        dv[...] += nn(weights.astype(BF), grad)
        dk[...] += nn(d_scores, q_part)
        d_queries = nn(keys_t[...], d_scores).T * SCALE
        d_raw, d_gain = norm_rope_back(
            q_ref[rows, :], gains_ref[0:1, :], cos_ref[rows, :], sin_ref[rows, :], d_queries
        )
        dq_ref[rows, :] = d_raw.astype(BF)
        dgain_ref[0:1, :] += d_gain

    @pl.when(head == heads - 1)
    def _():
        d_raw, d_gain = norm_rope_back(
            k_ref[...], gains_ref[1:2, :], cosine, sine, dk[...] * SCALE
        )
        dkv_ref[:, :HEAD_SIZE] = d_raw.astype(BF)
        dkv_ref[:, HEAD_SIZE:] = dv[...].astype(BF)
        dgain_ref[1:2, :] = d_gain


def attention_specs(heads, length):
    whole = lambda shape: pl.BlockSpec(shape, lambda h: (0,) * len(shape))
    column = lambda at: pl.BlockSpec((length, HEAD_SIZE), lambda h: (0, at))
    head_column = pl.BlockSpec((length, HEAD_SIZE), lambda h: (0, h))
    totals = pl.BlockSpec((1, 8, length), lambda h: (h, 0, 0))
    shared = [
        whole((length, HEAD_SIZE)),
        whole((length, HEAD_SIZE)),
        whole((8, HEAD_SIZE)),
        whole((8, length)),
        whole((length, 1)),
    ]
    return whole, column, head_column, totals, shared


def run_attention(qkv, heads, n_ctx, cosine, sine, gains, own, key_blocks):
    length = qkv.shape[0]
    whole, column, head_column, totals, shared = attention_specs(heads, length)
    deals = min(n_ctx, heads)
    return pl.pallas_call(
        attention_forward,
        grid=(heads,),
        in_specs=[head_column, column(heads), column(heads + 1)] + shared,
        out_specs=[
            head_column,
            totals,
            pl.BlockSpec((1, length, HEAD_SIZE), lambda h: (h % deals, 0, h // deals)),
        ],
        out_shape=[
            jax.ShapeDtypeStruct((length, heads * HEAD_SIZE), BF),
            jax.ShapeDtypeStruct((heads, 8, length), F32),
            jax.ShapeDtypeStruct((deals, length, heads // deals * HEAD_SIZE), BF),
        ],
        scratch_shapes=[
            pltpu.VMEM((length, HEAD_SIZE), BF),
            pltpu.VMEM((HEAD_SIZE, length), BF),
        ],
        compiler_params=pltpu.CompilerParams(vmem_limit_bytes=48 * 2**20),
        cost_estimate=pl.CostEstimate(
            flops=4 * heads * length * length * HEAD_SIZE,
            bytes_accessed=8 * heads * length * HEAD_SIZE,
            transcendentals=heads * length * length,
        ),
    )(qkv, qkv, qkv, cosine, sine, gains, own, key_blocks)


def run_attention_back(qkv, grad, totals_in, heads, cosine, sine, gains, own, key_blocks):
    length = qkv.shape[0]
    whole, column, head_column, totals, shared = attention_specs(heads, length)
    return pl.pallas_call(
        functools.partial(attention_backward, heads),
        grid=(heads,),
        in_specs=[head_column, column(heads), column(heads + 1), head_column, totals] + shared,
        out_specs=[head_column, whole((length, 2 * HEAD_SIZE)), whole((8, HEAD_SIZE))],
        out_shape=[
            jax.ShapeDtypeStruct((length, heads * HEAD_SIZE), BF),
            jax.ShapeDtypeStruct((length, 2 * HEAD_SIZE), BF),
            jax.ShapeDtypeStruct((8, HEAD_SIZE), F32),
        ],
        scratch_shapes=[
            pltpu.VMEM((length, HEAD_SIZE), BF),
            pltpu.VMEM((HEAD_SIZE, length), BF),
            pltpu.VMEM((length, HEAD_SIZE), BF),
            pltpu.VMEM((length, HEAD_SIZE), F32),
            pltpu.VMEM((length, HEAD_SIZE), F32),
        ],
        compiler_params=pltpu.CompilerParams(vmem_limit_bytes=48 * 2**20),
        cost_estimate=pl.CostEstimate(
            flops=10 * heads * length * length * HEAD_SIZE,
            bytes_accessed=10 * heads * length * HEAD_SIZE,
            transcendentals=heads * length * length,
        ),
    )(qkv, qkv, qkv, grad, totals_in, cosine, sine, gains, own, key_blocks)


def push(source, target, sends, recvs, device):
    copy = pltpu.make_async_remote_copy(
        src_ref=source,
        dst_ref=target,
        send_sem=sends,
        recv_sem=recvs,
        device_id=device,
        device_id_type=pl.DeviceIdType.MESH,
    )
    return copy


def greet(devices):
    barrier = pltpu.get_barrier_semaphore()
    for device in devices:
        pl.semaphore_signal(barrier, 1, device_id=device, device_id_type=pl.DeviceIdType.MESH)
    pl.semaphore_wait(barrier, len(devices))


class LineGather:
    def __init__(self, n_ctx, ctx, fsdp, own_ref, all_ref, up, down, arrived):
        self.n_ctx, self.ctx, self.fsdp = n_ctx, ctx, fsdp
        self.own_ref, self.all_ref = own_ref, all_ref
        self.up, self.down, self.arrived = up, down, arrived

    def copy(self, source, block, sems, step, to):
        return push(
            source, self.all_ref.at[block], sems.at[step], self.arrived.at[block], (to, self.fsdp)
        )

    def going_up(self, step):
        return (self.ctx - step >= 0) & (self.ctx < self.n_ctx - 1)

    def going_down(self, step):
        return (self.ctx + step < self.n_ctx) & (self.ctx > 0)

    def step(self, step):
        def hop(block, sems, to, more):
            if step > 0:
                self.copy(self.own_ref, block, sems, 0, to).wait_recv()

            @pl.when(more)
            def _():
                source = self.all_ref.at[block] if step > 0 else self.own_ref
                self.copy(source, block, sems, step, to).start()

        @pl.when(self.ctx - step >= 0)
        def _():
            hop(self.ctx - step, self.up, self.ctx + 1, self.ctx < self.n_ctx - 1)

        @pl.when(self.ctx + step < self.n_ctx)
        def _():
            hop(self.ctx + step, self.down, self.ctx - 1, self.ctx > 0)

    def finish(self):
        for step in range(self.n_ctx - 1):

            @pl.when(self.going_up(step))
            def _():
                self.copy(self.own_ref, 0, self.up, step, self.ctx).wait_send()

            @pl.when(self.going_down(step))
            def _():
                self.copy(self.own_ref, 0, self.down, step, self.ctx).wait_send()


class LineScatter:
    def __init__(self, n_ctx, ctx, fsdp, chunks, held, low, high, up, down, low_in, high_in):
        self.n_ctx, self.ctx, self.fsdp, self.chunks = n_ctx, ctx, fsdp, chunks
        self.held, self.low, self.high = held, low, high
        self.sems = {"up": (low, up, low_in), "down": (high, down, high_in)}
        self.size = held.shape[1] // chunks

    def copy(self, way, block, chunk, to):
        landing, sends, arrived = self.sems[way]
        rows = pl.ds(chunk * self.size, self.size)
        return push(
            self.held.at[block, rows],
            landing.at[block, rows],
            sends.at[block, chunk],
            arrived.at[block, chunk],
            (to, self.fsdp),
        )

    def scatter(self, chunk):
        rows = slice(chunk * self.size, (chunk + 1) * self.size)
        ctx, held = self.ctx, self.held

        def pass_on(way, block, to, first):
            @pl.when(jnp.logical_not(first))
            def _():
                self.copy(way, block, chunk, ctx).wait_recv()
                held[block, rows, :] = (
                    held[block, rows, :].astype(F32)
                    + self.sems[way][0][block, rows, :].astype(F32)
                ).astype(BF)

            self.copy(way, block, chunk, to).start()

        for step in range(self.n_ctx - 1):

            @pl.when(ctx < self.n_ctx - 1 - step)
            def _():
                pass_on("up", self.n_ctx - 1 - step, ctx + 1, ctx == 0)

            @pl.when(ctx > step)
            def _():
                pass_on("down", step, ctx - 1, ctx == self.n_ctx - 1)

    def settle(self, chunk, total_ref):
        rows = slice(chunk * self.size, (chunk + 1) * self.size)
        total_ref[rows, :] = self.held[self.ctx, rows, :].astype(F32)

        @pl.when(self.ctx > 0)
        def _():
            self.copy("up", self.ctx, chunk, self.ctx).wait_recv()
            total_ref[rows, :] += self.low[self.ctx, rows, :].astype(F32)

        @pl.when(self.ctx < self.n_ctx - 1)
        def _():
            self.copy("down", self.ctx, chunk, self.ctx).wait_recv()
            total_ref[rows, :] += self.high[self.ctx, rows, :].astype(F32)

    def finish(self):
        for chunk in range(self.chunks):
            for step in range(self.n_ctx - 1):

                @pl.when(self.ctx < self.n_ctx - 1 - step)
                def _():
                    self.copy("up", self.n_ctx - 1 - step, chunk, self.ctx).wait_send()

                @pl.when(self.ctx > step)
                def _():
                    self.copy("down", step, chunk, self.ctx).wait_send()


def first_gather(
    n_ctx,
    n_fsdp,
    x_ref,
    table_ref,
    packed_ref,
    x_all,
    table_all,
    packed_all,
    local,
    up,
    down,
    arrived,
    table_send,
    table_arrived,
    packed_send,
    passed_send,
    packed_arrived,
):
    ctx, fsdp = lax.axis_index("ctx"), lax.axis_index("fsdp")
    sibling = lax.rem(fsdp + 1, 2) + (fsdp // 2) * 2
    chips = n_fsdp // 2

    def same_core(offset):
        return lax.rem(fsdp + 2 * offset, n_fsdp)

    def along(offset):
        return lax.rem(ctx + offset, n_ctx)

    greet(
        [(along(i), fsdp) for i in range(1, n_ctx)]
        + [(ctx, same_core(i)) for i in range(1, chips)]
        + [(ctx, sibling)]
    )
    kept = [
        pltpu.make_async_copy(x_ref, x_all.at[ctx], local.at[0]),
        pltpu.make_async_copy(table_ref, table_all.at[ctx], local.at[1]),
        pltpu.make_async_copy(packed_ref, packed_all.at[fsdp], local.at[2]),
    ]
    for copy in kept:
        copy.start()

    def packed_copy(source, owner, sems, to):
        return push(source, packed_all.at[owner], sems, packed_arrived.at[owner], (ctx, to))

    for i in range(1, chips):
        packed_copy(packed_ref, fsdp, packed_send.at[i], same_core(i)).start()
    packed_copy(packed_ref, fsdp, packed_send.at[0], sibling).start()
    for i in range(1, n_ctx):
        push(
            table_ref, table_all.at[ctx], table_send.at[i], table_arrived.at[ctx], (along(i), fsdp)
        ).start()
    line = LineGather(n_ctx, ctx, fsdp, x_ref, x_all, up, down, arrived)
    for step in range(n_ctx):
        line.step(step)
    for i in range(1, chips):
        owner = same_core(chips - i)
        packed_copy(packed_ref, owner, packed_send.at[i], sibling).wait_recv()
        packed_copy(packed_all.at[owner], owner, passed_send.at[i], sibling).start()
    for i in range(chips):
        owner = lax.rem(sibling + 2 * i, n_fsdp)
        packed_copy(packed_ref, owner, packed_send.at[0], sibling).wait_recv()
    for i in range(1, n_ctx):
        owner = along(i)
        push(
            table_ref, table_all.at[owner], table_send.at[i], table_arrived.at[owner], (owner, fsdp)
        ).wait()
    line.finish()
    for i in range(chips):
        packed_copy(packed_ref, fsdp, packed_send.at[i], sibling).wait_send()
    for i in range(1, chips):
        packed_copy(packed_ref, fsdp, passed_send.at[i], sibling).wait_send()
    for copy in kept:
        copy.wait()


def run_first_gather(n_ctx, n_fsdp, x, table, packed):
    anywhere = pl.BlockSpec(memory_space=pl.ANY)
    dma = pltpu.SemaphoreType.DMA
    return pl.pallas_call(
        functools.partial(first_gather, n_ctx, n_fsdp),
        in_specs=[anywhere] * 3,
        out_specs=[anywhere] * 3,
        out_shape=[
            jax.ShapeDtypeStruct((n_ctx,) + x.shape, x.dtype),
            jax.ShapeDtypeStruct((n_ctx,) + table.shape, table.dtype),
            jax.ShapeDtypeStruct((n_fsdp,) + packed.shape, packed.dtype),
        ],
        scratch_shapes=[
            dma((3,)),
            dma((n_ctx,)),
            dma((n_ctx,)),
            dma((n_ctx,)),
            dma((n_ctx,)),
            dma((n_ctx,)),
            dma((n_fsdp // 2,)),
            dma((n_fsdp // 2,)),
            dma((n_fsdp,)),
        ],
        compiler_params=pltpu.CompilerParams(collective_id=1, has_side_effects=True),
        cost_estimate=pl.CostEstimate(
            flops=0, bytes_accessed=200 * 2**20, transcendentals=0
        ),
    )(x, table, packed)


TILE = 512
AUX = 128


def expert_exchange(
    n_ctx,
    n_fsdp,
    x_ref,
    sel_ref,
    selt_ref,
    gate_ref,
    up_ref,
    down_ref,
    grad_ref,
    dealt_ref,
    rows_ref,
    back_ref,
    part_ref,
    inner_ref,
    dg_ref,
    du_ref,
    y_low_ref,
    y_high_ref,
    dealt_all,
    w_gate,
    w_up,
    w_down,
    held,
    staged,
    rows_in,
    grad_in,
    inner_out,
    dg_out,
    du_out,
    y_out,
    back_in,
    w_sems,
    local,
    held_send,
    held_arrived,
    rows_send,
    rows_arrived,
    back_send,
    back_arrived,
    part_send,
    part_arrived,
    dealt_send,
    dealt_arrived,
    out_sems,
):
    ctx, fsdp = lax.axis_index("ctx"), lax.axis_index("fsdp")
    experts = n_ctx * n_fsdp
    expert = ctx * n_fsdp + fsdp
    width, hidden = w_gate.shape
    wide = held.shape[2]
    capacity = staged.shape[2]
    half = n_fsdp // 2
    tiles = [(at, min(TILE, wide - at)) for at in range(0, wide, TILE)]

    def along(offset):
        return lax.rem(ctx + offset, n_ctx)

    def around(offset):
        return lax.rem(fsdp + offset, n_fsdp)

    greet(
        [(along(i), fsdp) for i in range(1, n_ctx)] + [(ctx, around(i)) for i in range(1, n_fsdp)]
    )
    weights = [
        pltpu.make_async_copy(gate_ref, w_gate, w_sems.at[0]),
        pltpu.make_async_copy(up_ref, w_up, w_sems.at[1]),
        pltpu.make_async_copy(down_ref, w_down, w_sems.at[2]),
    ]
    own = pltpu.make_async_copy(x_ref, held.at[ctx], local.at[0])
    own.start()
    for copy in weights:
        copy.start()

    def held_copy(step):
        to = lax.rem(ctx + n_ctx - step, n_ctx)
        return push(x_ref, held.at[ctx], held_send.at[step], held_arrived.at[ctx], (to, fsdp))

    def rows_copy(step, group, offset):
        to = around(offset)
        return push(
            staged.at[step, to],
            rows_ref.at[fsdp, group],
            rows_send.at[step, offset],
            rows_arrived.at[group, fsdp],
            (ctx, to),
        )

    def rows_kept(step, group):
        return pltpu.make_async_copy(
            staged.at[step, fsdp], rows_ref.at[fsdp, group], rows_arrived.at[group, fsdp]
        )

    def back_copy(step, group, offset):
        to = around(offset)
        return push(
            staged.at[step, to],
            back_ref.at[group, fsdp],
            back_send.at[step, offset],
            back_arrived.at[group, fsdp],
            (ctx, to),
        )

    def back_kept(step, group):
        return pltpu.make_async_copy(
            staged.at[step, fsdp], back_ref.at[group, fsdp], back_arrived.at[group, fsdp]
        )

    def outputs(group):
        return [
            pltpu.make_async_copy(inner_out, inner_ref.at[:, group], out_sems.at[0]),
            pltpu.make_async_copy(dg_out, dg_ref.at[:, group], out_sems.at[1]),
            pltpu.make_async_copy(du_out, du_ref.at[:, group], out_sems.at[2]),
            pltpu.make_async_copy(
                y_out.at[:, :, : width // 2], y_low_ref.at[:, group], out_sems.at[3]
            ),
            pltpu.make_async_copy(
                y_out.at[:, :, width // 2 :], y_high_ref.at[:, group], out_sems.at[4]
            ),
        ]

    def dispatch(step):
        group = along(step)

        @pl.when(step == 0)
        def _():
            own.wait()

        @pl.when(step > 0)
        def _():
            push(
                x_ref, held.at[group], held_send.at[step], held_arrived.at[group], (group, fsdp)
            ).wait_recv()

        @pl.when(step + 1 < n_ctx)
        def _():
            held_copy(step + 1).start()

        for at, size in tiles:
            picked = nn(sel_ref[group], held[group, :, at : at + size])
            staged[step, :, :, at : at + size] = picked.astype(BF).reshape(n_fsdp, capacity, size)
        rows_kept(step, group).start()
        for offset in range(1, n_fsdp):
            rows_copy(step, group, offset).start()

    def compute(step):
        group = along(step)
        rows_kept(step, group).wait()
        for offset in range(1, n_fsdp):
            source = around(offset)
            push(
                staged.at[step, source],
                rows_ref.at[source, group],
                rows_send.at[step, offset],
                rows_arrived.at[group, source],
                (ctx, source),
            ).wait_recv()
        load_rows = pltpu.make_async_copy(rows_ref.at[:, group], rows_in, local.at[1])
        load_inner = pltpu.make_async_copy(grad_ref.at[:, group], grad_in, local.at[2])
        load_rows.start()
        load_inner.start()

        @pl.when(step == 0)
        def _():
            for copy in weights:
                copy.wait()

        @pl.when(step > 0)
        def _():
            for copy in outputs(group):
                copy.wait()

        for offset in range(1, n_fsdp):
            rows_copy(step, group, offset).wait_send()
        load_rows.wait()
        load_inner.wait()
        count = half * capacity
        lane = lax.broadcasted_iota(jnp.int32, (count, AUX), 1)
        high, low = lane == expert, lane == experts + expert

        @pl.loop(0, 2)
        def _(part):
            sources = pl.ds(part * half, half)
            rows = rows_in[sources, :, :width].reshape(count, width)
            aux = rows_in[sources, :, width:].reshape(count, AUX).astype(F32)
            gate = jnp.sum(jnp.where(high | low, aux, 0.0), axis=1, keepdims=True)
            g = nn(rows, w_gate[...])
            u = nn(rows, w_up[...])
            s = jax.nn.sigmoid(g)
            inner = g * s * u
            d_inner = nt(grad_in[sources].reshape(count, width), w_down[...])
            d_gate = jnp.sum(inner * d_inner, axis=1, keepdims=True)
            d_inner = d_inner * gate
            dg = (d_inner * u * s * (1.0 + g * (1.0 - s))).astype(BF)
            du = (d_inner * g * s).astype(BF)
            inner_out[sources] = (inner * gate).astype(BF).reshape(half, capacity, hidden)
            dg_out[sources] = dg.reshape(half, capacity, hidden)
            du_out[sources] = du.reshape(half, capacity, hidden)
            rest = d_gate - d_gate.astype(BF).astype(F32)
            staged[step, sources, :, width:] = (
                jnp.where(high, d_gate, jnp.where(low, rest, 0.0))
                .astype(BF)
                .reshape(half, capacity, AUX)
            )
            for at in range(0, width, TILE):
                grad = nt(dg, w_gate[at : at + TILE, :]) + nt(du, w_up[at : at + TILE, :])
                staged[step, sources, :, at : at + TILE] = grad.astype(BF).reshape(
                    half, capacity, TILE
                )
            low_inner = inner.astype(BF)
            for at in range(0, width, TILE):
                y = nn(low_inner, w_down[:, at : at + TILE]) * gate
                y_out[sources, :, at : at + TILE] = y.astype(BF).reshape(half, capacity, TILE)

        def send_back(step, group):
            back_kept(step, group).start()
            for offset in range(1, n_fsdp):
                back_copy(step, group, offset).start()

        @pl.when(step > 0)
        def _():
            send_back(step, group)

        @pl.when(step == n_ctx - 1)
        def _():
            send_back(0, ctx)

        for copy in outputs(group):
            copy.start()

    def combine(step):
        group = along(step)
        back_kept(step, group).wait()
        for offset in range(1, n_fsdp):
            source = around(offset)
            push(
                staged.at[step, source],
                back_ref.at[group, source],
                back_send.at[step, offset],
                back_arrived.at[group, source],
                (ctx, source),
            ).wait_recv()
        load = pltpu.make_async_copy(back_ref.at[group], back_in, local.at[1])
        load.start()
        load.wait()
        for at, size in tiles:
            back = back_in[:, :, at : at + size].reshape(n_fsdp * capacity, size)
            held[group, :, at : at + size] = nn(selt_ref[group], back).astype(BF)

        @pl.when(step == 0)
        def _():
            pltpu.make_async_copy(
                held.at[group], part_ref.at[ctx], part_arrived.at[ctx]
            ).start()

        @pl.when(step > 0)
        def _():
            push(
                held.at[group],
                part_ref.at[ctx],
                part_send.at[step],
                part_arrived.at[ctx],
                (group, fsdp),
            ).start()

    def dealt_copy(offset):
        to = along(offset)
        return push(
            dealt_ref.at[to],
            dealt_all.at[ctx],
            dealt_send.at[offset],
            dealt_arrived.at[ctx],
            (to, fsdp),
        )

    dealt_kept = pltpu.make_async_copy(
        dealt_ref.at[ctx], dealt_all.at[ctx], dealt_arrived.at[ctx]
    )

    @pl.loop(0, n_ctx + 3)
    def _(tick):
        @pl.when(tick < n_ctx)
        def _():
            dispatch(tick)

        @pl.when(tick == n_ctx - 1)
        def _():
            dealt_kept.start()
            for offset in range(1, n_ctx):
                dealt_copy(offset).start()

        @pl.when((tick >= 1) & (tick <= n_ctx))
        def _():
            compute(tick - 1)

        @pl.when(tick >= 3)
        def _():
            combine(lax.rem(tick - 2, n_ctx))

    pltpu.make_async_copy(held.at[ctx], part_ref.at[ctx], part_arrived.at[ctx]).wait()
    for step in range(1, n_ctx):
        other = along(step)
        copy = push(
            held.at[other], part_ref.at[other], part_send.at[step], part_arrived.at[other], (other, fsdp)
        )
        copy.wait()
        held_copy(step).wait_send()
    dealt_kept.wait()
    for offset in range(1, n_ctx):
        other = along(offset)
        push(
            dealt_ref.at[other],
            dealt_all.at[other],
            dealt_send.at[offset],
            dealt_arrived.at[other],
            (other, fsdp),
        ).wait()
    for step in range(n_ctx):
        for offset in range(1, n_fsdp):
            back_copy(step, along(step), offset).wait_send()
    for copy in outputs(along(n_ctx - 1)):
        copy.wait()


def run_expert_exchange(n_ctx, n_fsdp, x, select, select_t, gate, up, down, grads, dealt):
    anywhere, inside = pl.BlockSpec(memory_space=pl.ANY), pl.BlockSpec(memory_space=pltpu.VMEM)
    span, wide = x.shape
    width, hidden = gate.shape
    capacity = grads.shape[2]
    slots = (n_fsdp, n_ctx, capacity)
    one = (n_fsdp, capacity)
    dma, vmem, shape = pltpu.SemaphoreType.DMA, pltpu.VMEM, jax.ShapeDtypeStruct
    return pl.pallas_call(
        functools.partial(expert_exchange, n_ctx, n_fsdp),
        in_specs=[anywhere, inside, inside] + [anywhere] * 5,
        out_specs=[anywhere] * 9,
        out_shape=[
            shape(slots + (wide,), BF),
            shape((n_ctx, n_fsdp, capacity, wide), BF),
            shape((n_ctx, span, wide), BF),
            shape(slots + (hidden,), BF),
            shape(slots + (hidden,), BF),
            shape(slots + (hidden,), BF),
            shape(slots + (width // 2,), BF),
            shape(slots + (width // 2,), BF),
            shape(dealt.shape, BF),
        ],
        scratch_shapes=[
            vmem((width, hidden), BF),
            vmem((width, hidden), BF),
            vmem((hidden, width), BF),
            vmem((n_ctx, span, wide), BF),
            vmem((n_ctx,) + one + (wide,), BF),
            vmem(one + (wide,), BF),
            vmem(one + (width,), BF),
            vmem(one + (hidden,), BF),
            vmem(one + (hidden,), BF),
            vmem(one + (hidden,), BF),
            vmem(one + (width,), BF),
            vmem(one + (wide,), BF),
            dma((3,)),
            dma((3,)),
            dma((n_ctx,)),
            dma((n_ctx,)),
            dma((n_ctx, n_fsdp)),
            dma((n_ctx, n_fsdp)),
            dma((n_ctx, n_fsdp)),
            dma((n_ctx, n_fsdp)),
            dma((n_ctx,)),
            dma((n_ctx,)),
            dma((n_ctx,)),
            dma((n_ctx,)),
            dma((5,)),
        ],
        compiler_params=pltpu.CompilerParams(
            collective_id=2, has_side_effects=True, vmem_limit_bytes=60 * 2**20
        ),
        cost_estimate=pl.CostEstimate(
            flops=12 * n_fsdp * n_ctx * capacity * width * hidden,
            bytes_accessed=600 * 2**20,
            transcendentals=0,
        ),
    )(x, select, select_t, gate, up, down, grads, dealt)


def last_reduce(n_ctx, n_fsdp, *refs):
    ctx, fsdp = lax.axis_index("ctx"), lax.axis_index("fsdp")
    count = (len(refs) - 1) // 11
    ins, alls, local, refs = refs[:count], refs[count : 2 * count], refs[2 * count], refs[2 * count + 1 :]
    items = [refs[9 * i : 9 * i + 9] for i in range(count)]
    chips, chip, core = n_fsdp // 2, fsdp // 2, lax.rem(fsdp, 2)
    sibling = chip * 2 + 1 - core

    def along(offset):
        return lax.rem(ctx + offset, n_ctx)

    def other_chip(offset):
        return lax.rem(chip + offset, chips)

    greet(
        [(along(i), fsdp) for i in range(1, n_ctx)]
        + [(ctx, other_chip(i) * 2 + core) for i in range(1, chips)]
        + [(ctx, sibling)]
    )
    crossing, loads, lines = [], [], []
    for at, (in_ref, all_ref, item) in enumerate(zip(ins, alls, items)):
        mine, beside, landed, own, cross, sends, arrived, line_sems, line_arrived = item
        crossing.append(
            push(in_ref.at[:, 1 - core], beside, cross.at[0], cross.at[1], (ctx, sibling))
        )
        crossing[-1].start()
        loads.append(pltpu.make_async_copy(in_ref.at[:, core], mine, local.at[at]))
        loads[-1].start()
        lines.append(
            LineGather(
                n_ctx, ctx, fsdp, own, all_ref, line_sems.at[0], line_sems.at[1], line_arrived
            )
        )

    def chip_copy(item, offset):
        mine, beside, landed, own, cross, sends, arrived, line_sems, line_arrived = item
        to = other_chip(offset)
        return push(
            mine.at[to], landed.at[chip], sends.at[offset], arrived.at[chip], (ctx, to * 2 + core)
        )

    for crossed, loaded, item in zip(crossing, loads, items):
        mine, beside = item[:2]
        loaded.wait()
        crossed.wait_recv()
        for offset in range(1, chips + 1):
            to = other_chip(offset)
            mine[to] = (mine[to].astype(F32) + beside[to].astype(F32)).astype(BF)
            if offset < chips:
                chip_copy(item, offset).start()
    keeps = []
    for at, (item, line, all_ref) in enumerate(zip(items, lines, alls)):
        mine, beside, landed, own, cross, sends, arrived, line_sems, line_arrived = item
        total = mine[chip].astype(F32)
        for offset in range(1, chips):
            source = other_chip(offset)
            push(
                mine.at[source], landed.at[source], sends.at[offset], arrived.at[source], (ctx, sibling)
            ).wait_recv()
            total = total + landed[source].astype(F32)
        own[...] = total.astype(BF)
        line.step(0)
        keeps.append(pltpu.make_async_copy(own, all_ref.at[ctx], local.at[at]))
        keeps[-1].start()
    for step in range(1, n_ctx):
        for line in lines:
            line.step(step)
    for crossed, keep, line, item in zip(crossing, keeps, lines, items):
        crossed.wait_send()
        keep.wait()
        line.finish()
        for offset in range(1, chips):
            chip_copy(item, offset).wait_send()


def run_last_reduce(n_ctx, n_fsdp, grads):
    anywhere = pl.BlockSpec(memory_space=pl.ANY)
    dma, vmem, shape = pltpu.SemaphoreType.DMA, pltpu.VMEM, jax.ShapeDtypeStruct
    chips = n_fsdp // 2
    grads = [grad.reshape((chips, 2, -1) + grad.shape[-1:]) for grad in grads]
    blocks = [grad.shape[2:] for grad in grads]
    scratch = [dma((len(grads),))]
    for block in blocks:
        scratch += [
            vmem((chips,) + block, BF),
            vmem((chips,) + block, BF),
            vmem((chips,) + block, BF),
            vmem(block, BF),
            dma((2,)),
            dma((chips,)),
            dma((chips,)),
            dma((2, n_ctx)),
            dma((n_ctx,)),
        ]
    return pl.pallas_call(
        functools.partial(last_reduce, n_ctx, n_fsdp),
        in_specs=[anywhere] * len(grads),
        out_specs=[anywhere] * len(grads),
        out_shape=[shape((n_ctx,) + block, BF) for block in blocks],
        scratch_shapes=scratch,
        compiler_params=pltpu.CompilerParams(
            collective_id=3, has_side_effects=True, vmem_limit_bytes=60 * 2**20
        ),
        cost_estimate=pl.CostEstimate(flops=0, bytes_accessed=400 * 2**20, transcendentals=0),
    )(*grads)


def finish(
    n_ctx,
    share,
    experts,
    shared_ref,
    rest_ref,
    out_ref,
    dh_ref,
    x_ref,
    resid_grad_ref,
    resid_ref,
    moe_low_ref,
    moe_high_ref,
    gain_ref,
    query_ref,
    key_ref,
    value_ref,
    out_grad_ref,
    input_grad_ref,
    output_ref,
    router_ref,
    gains_ref,
):
    q_width = shared_ref.shape[2] - 2 * HEAD_SIZE
    for block in range(n_ctx):
        query_ref[:, block * q_width : (block + 1) * q_width] = shared_ref[
            block, :, :q_width
        ].astype(F32)
    for target, at in ((key_ref, q_width), (value_ref, q_width + HEAD_SIZE)):
        for kv in range(KEY_VALUE_HEADS):
            total = shared_ref[kv * share, :, at : at + HEAD_SIZE].astype(F32)
            for block in range(kv * share + 1, (kv + 1) * share):
                total = total + shared_ref[block, :, at : at + HEAD_SIZE].astype(F32)
            target[:, kv * HEAD_SIZE : (kv + 1) * HEAD_SIZE] = total
    out_grad_ref[...] = out_ref[0].astype(F32)
    x = x_ref[...].astype(F32)
    r = inverse_rms(x)
    n = dh_ref[...].astype(F32) * gain_ref[...]
    input_grad_ref[...] = (
        resid_grad_ref[...] + r * n - x * (r * r * r) * jnp.mean(n * x, axis=-1, keepdims=True)
    ).astype(BF)
    half = resid_ref.shape[1] // 2
    output_ref[:, :half] = (resid_ref[:, :half] + moe_low_ref[...].astype(F32)).astype(BF)
    output_ref[:, half:] = (resid_ref[:, half:] + moe_high_ref[...].astype(F32)).astype(BF)

    @pl.when(pl.program_id(0) == n_ctx - 1)
    def _():
        rest = rest_ref[0].astype(F32)
        for block in range(1, n_ctx):
            rest = rest + rest_ref[block].astype(F32)
        router_ref[...] = rest[:, :experts]
        gains_ref[...] = rest.T[experts : experts + 8]


def run_finish(
    n_ctx, experts, shared, rest, out_grad, d_hidden, x, resid_grad, resid, moe_low, moe_high, gain
):
    _, rows, wide = shared.shape
    span, width = x.shape
    _, piece, _ = out_grad.shape
    shape = jax.ShapeDtypeStruct
    part, tokens = rows // n_ctx, span // n_ctx
    whole = lambda dims: pl.BlockSpec(dims, lambda i: (0,) * len(dims))
    by_rows = lambda count, columns: pl.BlockSpec((count, columns), lambda i: (i, 0))
    q_columns, kv_columns = QUERY_HEADS * HEAD_SIZE, KEY_VALUE_HEADS * HEAD_SIZE
    return pl.pallas_call(
        functools.partial(finish, n_ctx, n_ctx // KEY_VALUE_HEADS, experts),
        grid=(n_ctx,),
        in_specs=[
            pl.BlockSpec((n_ctx, part, wide), lambda i: (0, i, 0)),
            whole(rest.shape),
            pl.BlockSpec((1, piece, width), lambda i: (i, 0, 0)),
        ]
        + [by_rows(tokens, width)] * 4
        + [by_rows(tokens, width // 2)] * 2
        + [whole((1, width))],
        out_specs=[
            by_rows(part, q_columns),
            by_rows(part, kv_columns),
            by_rows(part, kv_columns),
            by_rows(piece, width),
            by_rows(tokens, width),
            by_rows(tokens, width),
            whole((rows, experts)),
            whole((8, rows)),
        ],
        out_shape=[
            shape((rows, q_columns), F32),
            shape((rows, kv_columns), F32),
            shape((rows, kv_columns), F32),
            shape((n_ctx * piece, width), F32),
            shape((span, width), BF),
            shape((span, width), BF),
            shape((rows, experts), F32),
            shape((8, rows), F32),
        ],
        compiler_params=pltpu.CompilerParams(vmem_limit_bytes=48 * 2**20),
    )(shared, rest, out_grad, d_hidden, x, resid_grad, resid, moe_low, moe_high, gain)


def attention_exchange(
    n_ctx,
    n_fsdp,
    heads,
    q_ref,
    k_ref,
    v_ref,
    cos_ref,
    sin_ref,
    gains_ref,
    own_ref,
    key_ref,
    sel_ref,
    grad_ref,
    out_ref,
    total_ref,
    dealt_ref,
    attn_ref,
    rows_ref,
    keys,
    values_t,
    mixed,
    w_out,
    held,
    low,
    high,
    grads,
    staged,
    local,
    grad_up,
    grad_down,
    grad_arrived,
    rows_send,
    rows_arrived,
    up_send,
    down_send,
    low_arrived,
    high_arrived,
):
    head = pl.program_id(0)
    ctx, fsdp = lax.axis_index("ctx"), lax.axis_index("fsdp")
    _, span, width = held.shape
    capacity = staged.shape[2]
    q_width = heads * HEAD_SIZE

    def along(offset):
        return lax.rem(ctx + offset, n_ctx)

    def around(offset):
        return lax.rem(fsdp + offset, n_fsdp)

    line = LineGather(n_ctx, ctx, fsdp, grad_ref, grads, grad_up, grad_down, grad_arrived)
    sums = LineScatter(
        n_ctx, ctx, fsdp, 4, held, low, high, up_send, down_send, low_arrived, high_arrived
    )
    own = pltpu.make_async_copy(grad_ref, grads.at[ctx], local.at[0])
    weights = pltpu.make_async_copy(
        out_ref.at[pl.ds(ctx * q_width, q_width)], w_out, local.at[1]
    )

    def rows_copy(group, offset):
        to = around(offset)
        return push(
            staged.at[group, to],
            rows_ref.at[fsdp, group],
            rows_send.at[group, offset],
            rows_arrived.at[group, fsdp],
            (ctx, to),
        )

    def rows_kept(group):
        return pltpu.make_async_copy(
            staged.at[group, fsdp], rows_ref.at[fsdp, group], rows_arrived.at[group, fsdp]
        )

    def pick(group):
        for at in range(0, width, TILE):
            picked = nn(sel_ref[group], grads[group, :, at : at + TILE])
            staged[group, :, :, at : at + TILE] = picked.astype(BF).reshape(n_fsdp, capacity, TILE)
        rows_kept(group).start()
        for offset in range(1, n_fsdp):
            rows_copy(group, offset).start()

    def pick_from(distance):
        @pl.when(ctx - distance >= 0)
        def _():
            pick(ctx - distance)

        @pl.when(ctx + distance < n_ctx)
        def _():
            pick(ctx + distance)

    @pl.when(head == 0)
    def _():
        own.start()
        weights.start()
        greet(
            [(along(i), fsdp) for i in range(1, n_ctx)]
            + [(ctx, around(i)) for i in range(1, n_fsdp)]
        )
        line.step(0)
        own.wait()
        pick(ctx)
        prepare_keys(k_ref, v_ref, cos_ref, sin_ref, gains_ref, keys, values_t)

    @pl.when(head < heads)
    def _():
        def store(start, count, out):
            columns = pl.ds(pl.multiple_of(head * HEAD_SIZE, HEAD_SIZE), HEAD_SIZE)
            mixed[start : start + count, columns] = out

        attend_head(
            q_ref,
            cos_ref,
            sin_ref,
            gains_ref,
            own_ref,
            key_ref,
            total_ref,
            dealt_ref,
            keys,
            values_t,
            store,
        )

    @pl.when(head == heads - 2)
    def _():
        line.step(1)
        pick_from(1)

    @pl.when(head == heads)
    def _():
        weights.wait()
        for block in range(n_ctx):
            for at in range(0, width, TILE):
                held[block, :, at : at + TILE] = nn(
                    mixed[block * span : (block + 1) * span, :], w_out[:, at : at + TILE]
                ).astype(BF)
        line.step(2)
        sums.scatter(0)
        pick_from(2)
        sums.scatter(1)
        for step in range(3, n_ctx):
            line.step(step)
            pick_from(step)
        sums.scatter(2)
        sums.scatter(3)
        for chunk in range(4):
            sums.settle(chunk, attn_ref)
        sums.finish()
        line.finish()
        for group in range(n_ctx):
            rows_kept(group).wait()
            for offset in range(1, n_fsdp):
                source = around(offset)
                push(
                    staged.at[group, source],
                    rows_ref.at[source, group],
                    rows_send.at[group, offset],
                    rows_arrived.at[group, source],
                    (ctx, source),
                ).wait()


def run_attention_exchange(
    qkv, heads, n_ctx, n_fsdp, cosine, sine, gains, own, key_blocks, select, grad, w_out
):
    length = qkv.shape[0]
    span, width = grad.shape
    capacity = select.shape[1] // n_fsdp
    anywhere = pl.BlockSpec(memory_space=pl.ANY)
    dma, vmem, shape = pltpu.SemaphoreType.DMA, pltpu.VMEM, jax.ShapeDtypeStruct
    last = heads - 1
    whole, column, _, _, shared = attention_specs(heads, length)
    clip = lambda h: jnp.minimum(h, last)
    return pl.pallas_call(
        functools.partial(attention_exchange, n_ctx, n_fsdp, heads),
        grid=(heads + 1,),
        in_specs=[
            pl.BlockSpec((length, HEAD_SIZE), lambda h: (0, clip(h))),
            column(heads),
            column(heads + 1),
        ]
        + shared
        + [whole(select.shape), anywhere, anywhere],
        out_specs=[
            pl.BlockSpec((1, 8, length), lambda h: (clip(h), 0, 0)),
            pl.BlockSpec(
                (1, length, HEAD_SIZE),
                lambda h: (lax.rem(clip(h), n_ctx), 0, lax.div(clip(h), n_ctx)),
            ),
            whole((span, width)),
            anywhere,
        ],
        out_shape=[
            shape((heads, 8, length), F32),
            shape((n_ctx, length, heads // n_ctx * HEAD_SIZE), BF),
            shape((span, width), F32),
            shape((n_fsdp, n_ctx, capacity, width), BF),
        ],
        scratch_shapes=[
            vmem((length, HEAD_SIZE), BF),
            vmem((HEAD_SIZE, length), BF),
            vmem((length, heads * HEAD_SIZE), BF),
            vmem((heads * HEAD_SIZE, width), BF),
            vmem((n_ctx, span, width), BF),
            vmem((n_ctx, span, width), BF),
            vmem((n_ctx, span, width), BF),
            vmem((n_ctx, span, width), BF),
            vmem((n_ctx, n_fsdp, capacity, width), BF),
            dma((2,)),
            dma((n_ctx,)),
            dma((n_ctx,)),
            dma((n_ctx,)),
            dma((n_ctx, n_fsdp)),
            dma((n_ctx, n_fsdp)),
            dma((n_ctx, 4)),
            dma((n_ctx, 4)),
            dma((n_ctx, 4)),
            dma((n_ctx, 4)),
        ],
        compiler_params=pltpu.CompilerParams(
            collective_id=4, has_side_effects=True, vmem_limit_bytes=60 * 2**20
        ),
        cost_estimate=pl.CostEstimate(
            flops=4 * heads * length * length * HEAD_SIZE,
            bytes_accessed=400 * 2**20,
            transcendentals=heads * length * length,
        ),
    )(qkv, qkv, qkv, cosine, sine, gains, own, key_blocks, select, grad, w_out)


def on_device(
    inputs,
    block_ids,
    expert_ids,
    drop_order,
    attn_gain,
    w_query,
    key_projection_weight,
    value_projection_weight,
    q_gain,
    key_norm_gain,
    w_out,
    ffn_gain,
    w_router,
    expert_gate,
    expert_up,
    expert_down,
    cotangent,
):
    n_ctx, n_fsdp = lax.axis_size("ctx"), lax.axis_size("fsdp")
    ctx = lax.axis_index("ctx")
    span, width = inputs.shape[1], inputs.shape[2]
    length = block_ids.shape[1]
    experts = n_ctx * n_fsdp
    capacity = 5 * span * TOP // (4 * experts)
    slots = experts * capacity
    heads = QUERY_HEADS // n_ctx
    share = n_ctx // KEY_VALUE_HEADS
    own_rows = w_query.shape[0]
    q_width = heads * HEAD_SIZE
    qkv_width = q_width + 2 * HEAD_SIZE
    extra_width = -(-(experts + 8) // 128) * 128

    def gather_ctx(array):
        return lax.all_gather(array, "ctx", axis=0, tiled=True)

    def scatter_ctx(array):
        return lax.psum_scatter(array.astype(BF), "ctx", scatter_dimension=0, tiled=True)

    def route(rows):
        return lax.all_to_all(rows, "fsdp", split_axis=0, concat_axis=0, tiled=True)

    def columns(weight, index, count):
        return lax.dynamic_slice_in_dim(weight, index * count, count, axis=1)

    def as_column(vector):
        return jnp.pad(vector, (0, own_rows - vector.shape[0]))[:, None]

    packed = jnp.concatenate(
        [
            columns(w_query, ctx, q_width),
            columns(key_projection_weight, ctx // share, HEAD_SIZE),
            columns(value_projection_weight, ctx // share, HEAD_SIZE),
            w_router,
            as_column(attn_gain),
            as_column(ffn_gain),
            as_column(q_gain),
            as_column(key_norm_gain),
            jnp.zeros((own_rows, extra_width - experts - 4), BF),
        ],
        axis=1,
    )
    table = jnp.concatenate(
        [expert_ids[0].T, drop_order[0], jnp.zeros((7, span), jnp.int32)], axis=0
    )
    inputs_all, tables, packed_all = run_first_gather(n_ctx, n_fsdp, inputs[0], table, packed)
    out_all = lax.all_gather(w_out, "fsdp", axis=0, tiled=True)
    out_here = lax.dynamic_slice_in_dim(out_all, ctx * q_width, q_width, axis=0)
    inputs_all = inputs_all.reshape(length, width)
    packed_all = packed_all.reshape(width, qkv_width + extra_width)
    w_qkv = packed_all[:, :qkv_width]
    extra = packed_all[:, qkv_width:].T
    router_t = extra[:experts]
    gain_attn = extra[experts : experts + 1].astype(F32)
    gain_ffn = extra[experts + 1 : experts + 2].astype(F32)

    def head_gain(at):
        return extra[at].reshape(n_fsdp, own_rows)[:, : HEAD_SIZE // n_fsdp].reshape(1, HEAD_SIZE)

    gains = jnp.concatenate(
        [head_gain(experts + 2), head_gain(experts + 3), jnp.zeros((6, HEAD_SIZE), BF)], axis=0
    ).astype(F32)

    named = tables[:, :TOP, :]
    ranks = tables[:, TOP, :]
    here = ctx * n_fsdp + jnp.arange(n_fsdp, dtype=jnp.int32)
    member = jnp.any(named[:, :, None, :] == here[None, None, :, None], axis=1)
    before = (ranks[:, :, None] < ranks[:, None, :]).astype(BF)
    place = jnp.einsum(
        "gjs,gst->gjt", member.astype(BF), before, preferred_element_type=F32
    ).astype(jnp.int32)
    place = jnp.where(member, place, capacity)
    select = (
        place[:, :, None, :] == jnp.arange(capacity, dtype=jnp.int32)[None, None, :, None]
    ).astype(BF)

    fused = capacity % 16 == 0 and 2 * experts <= AUX and experts == QUERY_HEADS
    select_rows = select.reshape(n_ctx, n_fsdp * capacity, span)

    def dispatch(rows):
        picked = jnp.einsum(
            "gjkt,gtd->jgkd", select, rows.reshape(n_ctx, span, width), preferred_element_type=F32
        ).astype(BF)
        return route(picked).reshape(slots, width)

    def combine(rows):
        return gather_slots(route(rows.reshape(n_fsdp, n_ctx, capacity, width)))

    def gather_slots(back):
        return jnp.einsum("gjkt,jgkd->gtd", select, back, preferred_element_type=F32).reshape(
            length, -1
        )

    x_all = inputs_all.astype(F32)
    r_all = inverse_rms(x_all)
    hidden = (x_all * r_all * gain_attn).astype(BF)
    qkv = nn(hidden, w_qkv)
    exponent = np.arange(HALF, dtype=np.float32) * np.float32(2.0 / HEAD_SIZE)
    angles = np.arange(length, dtype=np.float32)[:, None] * (
        np.float32(ROPE_BASE) ** (-exponent)
    )
    cosine = jnp.asarray(np.tile(np.cos(angles), (1, 2)))
    sine = jnp.asarray(np.concatenate([-np.sin(angles), np.sin(angles)], axis=1))
    own_blocks = jnp.broadcast_to(block_ids, (8, length))
    key_blocks = block_ids.reshape(length, 1)
    piece = QUERY_HEADS * HEAD_SIZE // experts
    groups = n_fsdp // n_ctx
    if fused:
        totals, dealt, attn_out, grad_rows = run_attention_exchange(
            qkv,
            heads,
            n_ctx,
            n_fsdp,
            cosine,
            sine,
            gains,
            own_blocks,
            key_blocks,
            select_rows,
            cotangent[0],
            out_all,
        )
        grad_rows = grad_rows.reshape(slots, width)
    else:
        mixed, totals, _ = run_attention(
            qkv, heads, n_ctx, cosine, sine, gains, own_blocks, key_blocks
        )
        attn_out = scatter_ctx(nn(mixed, out_here))
        grad_rows = dispatch(gather_ctx(cotangent[0]))
        dealt = mixed.reshape(length, groups, n_ctx, piece).transpose(2, 0, 1, 3)
        dealt = dealt.reshape(n_ctx, length, groups * piece)

    x = inputs[0].astype(F32)
    resid = x + attn_out.astype(F32)
    r_ffn = inverse_rms(resid)
    normed = (resid * r_ffn * gain_ffn).astype(BF)
    if fused:
        chosen = jnp.any(
            expert_ids[0][:, :, None] == jnp.arange(experts, dtype=jnp.int32), axis=1
        )
        logits = nt(normed, router_t)
        gates = jax.nn.softmax(jnp.where(chosen, logits, -jnp.inf), axis=-1)
        high = lax.reduce_precision(gates, 8, 7)
        payload = jnp.concatenate(
            [
                normed,
                high.astype(BF),
                (gates - high).astype(BF),
                jnp.zeros((span, AUX - 2 * experts), BF),
            ],
            axis=1,
        )
        rows, _, parts, inner_low, dg, du, y_low, y_high, dealt = run_expert_exchange(
            n_ctx,
            n_fsdp,
            payload,
            select_rows,
            select_rows.swapaxes(1, 2),
            expert_gate[0],
            expert_up[0],
            expert_down[0],
            grad_rows.reshape(n_fsdp, n_ctx, capacity, width),
            dealt,
        )
        rows = rows.reshape(slots, width + AUX)[:, :width]
        inner_low, dg, du = (array.reshape(slots, -1) for array in (inner_low, dg, du))
        parts = jnp.sum(parts.astype(F32), axis=0)
        d_gates = parts[:, width : width + experts] + parts[:, width + experts : width + 2 * experts]
        d_logits = gates * (d_gates - jnp.sum(gates * d_gates, axis=-1, keepdims=True))
        d_logits = d_logits.astype(BF)
        d_normed = parts[:, :width] + nn(d_logits, router_t)
    else:
        dealt = lax.all_to_all(dealt, "ctx", split_axis=0, concat_axis=0, tiled=True)
        chosen = jnp.any(
            named[:, :, :, None] == jnp.arange(experts, dtype=jnp.int32), axis=1
        ).reshape(length, experts)
        normed = gather_ctx(normed)
        normed, grad_rows = lax.optimization_barrier((normed, grad_rows))
        grad_inner = nt(grad_rows, expert_down[0])
        logits = nt(normed, router_t)
        gates = jax.nn.softmax(jnp.where(chosen, logits, -jnp.inf), axis=-1)
        gates_here = lax.dynamic_slice_in_dim(gates, ctx * n_fsdp, n_fsdp, axis=1)
        gates_here = gates_here.reshape(n_ctx, span, n_fsdp).transpose(0, 2, 1)
        slot_gates = jnp.sum(select.astype(F32) * gates_here[:, :, None, :], axis=-1)
        slot_gates = route(slot_gates.transpose(1, 0, 2)).reshape(slots, 1)
        rows = dispatch(normed)
        g = nn(rows, expert_gate[0])
        u = nn(rows, expert_up[0])
        s = jax.nn.sigmoid(g)
        inner = g * s * u
        slot_dgates = jnp.sum(inner * grad_inner, axis=-1).reshape(n_fsdp, n_ctx, capacity)
        d_inner = grad_inner * slot_gates
        dg = (d_inner * u * s * (1.0 + g * (1.0 - s))).astype(BF)
        du = (d_inner * g * s).astype(BF)
        d_rows = (nt(dg, expert_gate[0]) + nt(du, expert_up[0])).astype(BF)
        y = (nn(inner.astype(BF), expert_down[0]) * slot_gates).astype(BF)
        y = y.reshape(n_fsdp, n_ctx, capacity, width)
        y_low, y_high = y[..., : width // 2], y[..., width // 2 :]
        inner_low = (inner * slot_gates).astype(BF)
        d_gates = jnp.einsum(
            "gjkt,jgk->gjt", select.astype(F32), route(slot_dgates), precision=lax.Precision.HIGHEST
        )
        weighted = (d_gates * gates_here).transpose(0, 2, 1).reshape(length, n_fsdp)
        d_logits = lax.dynamic_update_slice_in_dim(
            jnp.zeros((length, experts), F32), weighted, ctx * n_fsdp, axis=1
        ) - gates * jnp.sum(weighted, axis=1, keepdims=True)
        d_logits = d_logits.astype(BF)
        d_normed = scatter_ctx(combine(d_rows) + nn(d_logits, router_t)).astype(F32)

    gate_grad = tn(rows, dg)
    up_grad = tn(rows, du)
    down_grad = tn(inner_low, grad_rows)
    router_grad = tn(normed, d_logits)

    grad = cotangent[0].astype(F32)
    n = d_normed * gain_ffn
    d_resid = grad + r_ffn * n - resid * r_ffn**3 * jnp.mean(n * resid, axis=-1, keepdims=True)
    ffn_gain_grad = jnp.sum(d_normed * resid * r_ffn, axis=0)
    d_attn = gather_ctx(d_resid.astype(BF))
    y_low, y_high = route(y_low), route(y_high)
    y_low, d_attn = lax.optimization_barrier((gather_slots(y_low).astype(BF), d_attn))
    moe_low = scatter_ctx(y_low)
    d_mixed = nt(d_attn, out_here).astype(BF)
    out_grad = jnp.einsum("ntk,td->nkd", dealt, d_attn, preferred_element_type=F32).astype(BF)
    y_high, d_mixed, out_grad, gate_grad, up_grad, down_grad, router_grad = (
        lax.optimization_barrier(
            (y_high, d_mixed, out_grad, gate_grad, up_grad, down_grad, router_grad)
        )
    )
    y_high = gather_slots(y_high).astype(BF)
    y_high, d_mixed, moe_low = lax.optimization_barrier((y_high, d_mixed, moe_low))
    moe_high = scatter_ctx(y_high)

    dq, dkv, dgains = run_attention_back(
        qkv, d_mixed, totals, heads, cosine, sine, gains, own_blocks, key_blocks
    )
    d_qkv = jnp.concatenate([dq, dkv], axis=1)
    d_hidden = nt(d_qkv, w_qkv)
    attn_gain_grad = jnp.sum(d_hidden * x_all * r_all, axis=0)

    def spread(vector):
        parts = vector.reshape(n_fsdp, HEAD_SIZE // n_fsdp)
        return jnp.pad(parts, ((0, 0), (0, own_rows - parts.shape[1]))).reshape(width)

    small = jnp.stack(
        [attn_gain_grad, ffn_gain_grad, spread(dgains[0]), spread(dgains[1])], axis=1
    )
    extra_grad = jnp.concatenate(
        [
            router_grad.astype(BF),
            small.astype(BF),
            jnp.zeros((width, extra_width - experts - 4), BF),
        ],
        axis=1,
    )
    shared_grad = tn(hidden, d_qkv).astype(BF)
    d_hidden, moe_high = lax.optimization_barrier((d_hidden.astype(BF), moe_high))
    d_hidden = scatter_ctx(d_hidden)
    shared_grad, rest, out_grad = run_last_reduce(
        n_ctx, n_fsdp, [shared_grad, extra_grad, out_grad.reshape(n_fsdp * piece, width)]
    )
    query_grad, key_grad, value_grad, out_grad, input_grad, output, router_grad, gain_grads = (
        run_finish(
            n_ctx,
            experts,
            shared_grad,
            rest,
            out_grad,
            d_hidden,
            inputs[0],
            d_resid,
            resid,
            moe_low,
            moe_high,
            gain_attn,
        )
    )
    head_rows = HEAD_SIZE // n_fsdp
    return (
        output[None],
        input_grad[None],
        gain_grads[0],
        query_grad,
        key_grad,
        value_grad,
        gain_grads[2, :head_rows],
        gain_grads[3, :head_rows],
        out_grad,
        gain_grads[1],
        router_grad,
        gate_grad[None],
        up_grad[None],
        down_grad[None],
    )


def solution(mesh):
    rows, tokens = P("fsdp", None), P("fsdp", "ctx", None)
    vector, expert = P("fsdp"), P(("ctx", "fsdp"), None, None)
    in_specs = (
        tokens,
        rows,
        tokens,
        tokens,
        vector,
        rows,
        rows,
        rows,
        vector,
        vector,
        rows,
        vector,
        rows,
        expert,
        expert,
        expert,
        tokens,
    )
    out_specs = (
        tokens,
        tokens,
        vector,
        rows,
        rows,
        rows,
        vector,
        vector,
        rows,
        vector,
        rows,
        expert,
        expert,
        expert,
    )
    return jax.shard_map(
        on_device, mesh=mesh, in_specs=in_specs, out_specs=out_specs, check_vma=False
    )
```

```python
import functools

import jax
import jax.numpy as jnp
import numpy as np
from jax import lax
from jax.experimental import pallas as pl
from jax.experimental.pallas import tpu as pltpu
from jax.sharding import PartitionSpec as P

QUERY_HEADS = 32
KEY_VALUE_HEADS = 4
HEAD_SIZE = 128
TOP = 8

EPSILON = 1e-06
ROPE_BASE = 1000000.0
MASKED = -1000000000.0
SCALE = HEAD_SIZE ** (-0.5)
HALF = HEAD_SIZE // 2
BF = jnp.bfloat16
F32 = jnp.float32


def nt(a, b):
    return lax.dot_general(a, b, (((1,), (1,)), ((), ())), preferred_element_type=F32)


def nn(a, b):
    return lax.dot_general(a, b, (((1,), (0,)), ((), ())), preferred_element_type=F32)


def tn(a, b):
    return lax.dot_general(a, b, (((0,), (0,)), ((), ())), preferred_element_type=F32)


def inverse_rms(values):
    return lax.rsqrt(jnp.mean(values * values, axis=-1, keepdims=True) + EPSILON)


def norm_rope(raw, gain, cosine, sine):
    z = raw * inverse_rms(raw) * gain
    return z * cosine + pltpu.roll(z, HALF, 1) * sine


def norm_rope_back(raw, gain, cosine, sine, grad):
    dz = grad * cosine - pltpu.roll(grad, HALF, 1) * sine
    r = inverse_rms(raw)
    n = dz * gain
    d_raw = r * n - raw * (r * r * r) * jnp.mean(n * raw, axis=-1, keepdims=True)
    return d_raw, jnp.sum(dz * raw * r, axis=0, keepdims=True)


def prepare_keys(k_ref, v_ref, cos_ref, sin_ref, gains_ref, keys, values_t):
    rotated = norm_rope(k_ref[...], gains_ref[1:2, :], cos_ref[...], sin_ref[...])
    keys[...] = rotated.astype(BF)
    values_t[...] = v_ref[...].T.astype(BF)


def attend_head(
    q_ref, cos_ref, sin_ref, gains_ref, own_ref, key_ref, total_ref, dealt_ref, keys, values_t, store
):
    queries = norm_rope(q_ref[...], gains_ref[0:1, :], cos_ref[...], sin_ref[...]).astype(BF)
    length = queries.shape[0]
    chunk = 256
    for start in range(0, length, chunk):
        scores = nt(keys[...], queries[start : start + chunk]) * SCALE
        seen = key_ref[...] <= own_ref[0:1, start : start + chunk]
        scores = jnp.where(seen, scores, MASKED)
        top = jnp.max(scores, axis=0, keepdims=True)
        weights = jnp.exp(scores - top)
        total = jnp.sum(weights, axis=0, keepdims=True)
        out = (nn(values_t[...], weights.astype(BF)) / total).T.astype(BF)
        store(start, chunk, out)
        dealt_ref[0, start : start + chunk, :] = out
        total_ref[0, :, start : start + chunk] = jnp.broadcast_to(top + jnp.log(total), (8, chunk))


def attention_forward(
    q_ref,
    k_ref,
    v_ref,
    cos_ref,
    sin_ref,
    gains_ref,
    own_ref,
    key_ref,
    mixed_ref,
    total_ref,
    dealt_ref,
    keys,
    values_t,
):
    @pl.when(pl.program_id(0) == 0)
    def _():
        prepare_keys(k_ref, v_ref, cos_ref, sin_ref, gains_ref, keys, values_t)

    def store(start, count, out):
        mixed_ref[start : start + count, :] = out

    attend_head(
        q_ref, cos_ref, sin_ref, gains_ref, own_ref, key_ref, total_ref, dealt_ref, keys, values_t, store
    )


def attention_backward(
    heads,
    q_ref,
    k_ref,
    v_ref,
    grad_ref,
    total_ref,
    cos_ref,
    sin_ref,
    gains_ref,
    own_ref,
    key_ref,
    dq_ref,
    dkv_ref,
    dgain_ref,
    keys,
    keys_t,
    values,
    dk,
    dv,
):
    cosine, sine = cos_ref[...], sin_ref[...]
    head = pl.program_id(0)

    @pl.when(head == 0)
    def _():
        rotated = norm_rope(k_ref[...], gains_ref[1:2, :], cosine, sine)
        keys[...] = rotated.astype(BF)
        keys_t[...] = rotated.T.astype(BF)
        values[...] = v_ref[...].astype(BF)
        dk[...] = jnp.zeros_like(dk)
        dv[...] = jnp.zeros_like(dv)
        dgain_ref[...] = jnp.zeros_like(dgain_ref)

    queries = norm_rope(q_ref[...], gains_ref[0:1, :], cosine, sine).astype(BF)
    length = queries.shape[0]
    chunk = 512
    for start in range(0, length, chunk):
        rows = slice(start, start + chunk)
        q_part = queries[rows]
        grad = grad_ref[rows, :]
        scores = nt(keys[...], q_part) * SCALE
        seen = key_ref[...] <= own_ref[0:1, rows]
        scores = jnp.where(seen, scores, MASKED)
        weights = jnp.exp(scores - total_ref[0, 0:1, rows])
        d_weights = nt(values[...], grad)
        row_dot = jnp.sum(weights * d_weights, axis=0, keepdims=True)
        d_scores = (weights * (d_weights - row_dot)).astype(BF)
        dv[...] += nn(weights.astype(BF), grad)
        dk[...] += nn(d_scores, q_part)
        d_queries = nn(keys_t[...], d_scores).T * SCALE
        d_raw, d_gain = norm_rope_back(
            q_ref[rows, :], gains_ref[0:1, :], cos_ref[rows, :], sin_ref[rows, :], d_queries
        )
        dq_ref[rows, :] = d_raw.astype(BF)
        dgain_ref[0:1, :] += d_gain

    @pl.when(head == heads - 1)
    def _():
        d_raw, d_gain = norm_rope_back(
            k_ref[...], gains_ref[1:2, :], cosine, sine, dk[...] * SCALE
        )
        dkv_ref[:, :HEAD_SIZE] = d_raw.astype(BF)
        dkv_ref[:, HEAD_SIZE:] = dv[...].astype(BF)
        dgain_ref[1:2, :] = d_gain


def attention_specs(heads, length):
    whole = lambda shape: pl.BlockSpec(shape, lambda h: (0,) * len(shape))
    column = lambda at: pl.BlockSpec((length, HEAD_SIZE), lambda h: (0, at))
    head_column = pl.BlockSpec((length, HEAD_SIZE), lambda h: (0, h))
    totals = pl.BlockSpec((1, 8, length), lambda h: (h, 0, 0))
    shared = [
        whole((length, HEAD_SIZE)),
        whole((length, HEAD_SIZE)),
        whole((8, HEAD_SIZE)),
        whole((8, length)),
        whole((length, 1)),
    ]
    return whole, column, head_column, totals, shared


def run_attention(qkv, heads, n_ctx, cosine, sine, gains, own, key_blocks):
    length = qkv.shape[0]
    whole, column, head_column, totals, shared = attention_specs(heads, length)
    deals = min(n_ctx, heads)
    return pl.pallas_call(
        attention_forward,
        grid=(heads,),
        in_specs=[head_column, column(heads), column(heads + 1)] + shared,
        out_specs=[
            head_column,
            totals,
            pl.BlockSpec((1, length, HEAD_SIZE), lambda h: (h % deals, 0, h // deals)),
        ],
        out_shape=[
            jax.ShapeDtypeStruct((length, heads * HEAD_SIZE), BF),
            jax.ShapeDtypeStruct((heads, 8, length), F32),
            jax.ShapeDtypeStruct((deals, length, heads // deals * HEAD_SIZE), BF),
        ],
        scratch_shapes=[
            pltpu.VMEM((length, HEAD_SIZE), BF),
            pltpu.VMEM((HEAD_SIZE, length), BF),
        ],
        compiler_params=pltpu.CompilerParams(vmem_limit_bytes=48 * 2**20),
        cost_estimate=pl.CostEstimate(
            flops=4 * heads * length * length * HEAD_SIZE,
            bytes_accessed=8 * heads * length * HEAD_SIZE,
            transcendentals=heads * length * length,
        ),
    )(qkv, qkv, qkv, cosine, sine, gains, own, key_blocks)


def run_attention_back(qkv, grad, totals_in, heads, cosine, sine, gains, own, key_blocks):
    length = qkv.shape[0]
    whole, column, head_column, totals, shared = attention_specs(heads, length)
    return pl.pallas_call(
        functools.partial(attention_backward, heads),
        grid=(heads,),
        in_specs=[head_column, column(heads), column(heads + 1), head_column, totals] + shared,
        out_specs=[head_column, whole((length, 2 * HEAD_SIZE)), whole((8, HEAD_SIZE))],
        out_shape=[
            jax.ShapeDtypeStruct((length, heads * HEAD_SIZE), BF),
            jax.ShapeDtypeStruct((length, 2 * HEAD_SIZE), BF),
            jax.ShapeDtypeStruct((8, HEAD_SIZE), F32),
        ],
        scratch_shapes=[
            pltpu.VMEM((length, HEAD_SIZE), BF),
            pltpu.VMEM((HEAD_SIZE, length), BF),
            pltpu.VMEM((length, HEAD_SIZE), BF),
            pltpu.VMEM((length, HEAD_SIZE), F32),
            pltpu.VMEM((length, HEAD_SIZE), F32),
        ],
        compiler_params=pltpu.CompilerParams(vmem_limit_bytes=48 * 2**20),
        cost_estimate=pl.CostEstimate(
            flops=10 * heads * length * length * HEAD_SIZE,
            bytes_accessed=10 * heads * length * HEAD_SIZE,
            transcendentals=heads * length * length,
        ),
    )(qkv, qkv, qkv, grad, totals_in, cosine, sine, gains, own, key_blocks)


def push(source, target, sends, recvs, device):
    copy = pltpu.make_async_remote_copy(
        src_ref=source,
        dst_ref=target,
        send_sem=sends,
        recv_sem=recvs,
        device_id=device,
        device_id_type=pl.DeviceIdType.MESH,
    )
    return copy


def greet(devices):
    barrier = pltpu.get_barrier_semaphore()
    for device in devices:
        pl.semaphore_signal(barrier, 1, device_id=device, device_id_type=pl.DeviceIdType.MESH)
    pl.semaphore_wait(barrier, len(devices))


class LineGather:
    def __init__(self, n_ctx, ctx, fsdp, own_ref, all_ref, up, down, arrived):
        self.n_ctx, self.ctx, self.fsdp = n_ctx, ctx, fsdp
        self.own_ref, self.all_ref = own_ref, all_ref
        self.up, self.down, self.arrived = up, down, arrived

    def copy(self, source, block, sems, step, to):
        return push(
            source, self.all_ref.at[block], sems.at[step], self.arrived.at[block], (to, self.fsdp)
        )

    def going_up(self, step):
        return (self.ctx - step >= 0) & (self.ctx < self.n_ctx - 1)

    def going_down(self, step):
        return (self.ctx + step < self.n_ctx) & (self.ctx > 0)

    def step(self, step):
        def hop(block, sems, to, more):
            if step > 0:
                self.copy(self.own_ref, block, sems, 0, to).wait_recv()

            @pl.when(more)
            def _():
                source = self.all_ref.at[block] if step > 0 else self.own_ref
                self.copy(source, block, sems, step, to).start()

        @pl.when(self.ctx - step >= 0)
        def _():
            hop(self.ctx - step, self.up, self.ctx + 1, self.ctx < self.n_ctx - 1)

        @pl.when(self.ctx + step < self.n_ctx)
        def _():
            hop(self.ctx + step, self.down, self.ctx - 1, self.ctx > 0)

    def finish(self):
        for step in range(self.n_ctx - 1):

            @pl.when(self.going_up(step))
            def _():
                self.copy(self.own_ref, 0, self.up, step, self.ctx).wait_send()

            @pl.when(self.going_down(step))
            def _():
                self.copy(self.own_ref, 0, self.down, step, self.ctx).wait_send()


class LineScatter:
    def __init__(self, n_ctx, ctx, fsdp, chunks, held, low, high, up, down, low_in, high_in):
        self.n_ctx, self.ctx, self.fsdp, self.chunks = n_ctx, ctx, fsdp, chunks
        self.held, self.low, self.high = held, low, high
        self.sems = {"up": (low, up, low_in), "down": (high, down, high_in)}
        self.size = held.shape[1] // chunks

    def copy(self, way, block, chunk, to):
        landing, sends, arrived = self.sems[way]
        rows = pl.ds(chunk * self.size, self.size)
        return push(
            self.held.at[block, rows],
            landing.at[block, rows],
            sends.at[block, chunk],
            arrived.at[block, chunk],
            (to, self.fsdp),
        )

    def scatter(self, chunk):
        rows = slice(chunk * self.size, (chunk + 1) * self.size)
        ctx, held = self.ctx, self.held

        def pass_on(way, block, to, first):
            @pl.when(jnp.logical_not(first))
            def _():
                self.copy(way, block, chunk, ctx).wait_recv()
                held[block, rows, :] = (
                    held[block, rows, :].astype(F32)
                    + self.sems[way][0][block, rows, :].astype(F32)
                ).astype(BF)

            self.copy(way, block, chunk, to).start()

        for step in range(self.n_ctx - 1):

            @pl.when(ctx < self.n_ctx - 1 - step)
            def _():
                pass_on("up", self.n_ctx - 1 - step, ctx + 1, ctx == 0)

            @pl.when(ctx > step)
            def _():
                pass_on("down", step, ctx - 1, ctx == self.n_ctx - 1)

    def settle(self, chunk, total_ref):
        rows = slice(chunk * self.size, (chunk + 1) * self.size)
        total_ref[rows, :] = self.held[self.ctx, rows, :].astype(F32)

        @pl.when(self.ctx > 0)
        def _():
            self.copy("up", self.ctx, chunk, self.ctx).wait_recv()
            total_ref[rows, :] += self.low[self.ctx, rows, :].astype(F32)

        @pl.when(self.ctx < self.n_ctx - 1)
        def _():
            self.copy("down", self.ctx, chunk, self.ctx).wait_recv()
            total_ref[rows, :] += self.high[self.ctx, rows, :].astype(F32)

    def finish(self):
        for chunk in range(self.chunks):
            for step in range(self.n_ctx - 1):

                @pl.when(self.ctx < self.n_ctx - 1 - step)
                def _():
                    self.copy("up", self.n_ctx - 1 - step, chunk, self.ctx).wait_send()

                @pl.when(self.ctx > step)
                def _():
                    self.copy("down", step, chunk, self.ctx).wait_send()


def first_gather(
    n_ctx,
    n_fsdp,
    x_ref,
    table_ref,
    packed_ref,
    x_all,
    table_all,
    packed_all,
    local,
    up,
    down,
    arrived,
    table_send,
    table_arrived,
    packed_send,
    passed_send,
    packed_arrived,
):
    ctx, fsdp = lax.axis_index("ctx"), lax.axis_index("fsdp")
    sibling = lax.rem(fsdp + 1, 2) + (fsdp // 2) * 2
    chips = n_fsdp // 2

    def same_core(offset):
        return lax.rem(fsdp + 2 * offset, n_fsdp)

    def along(offset):
        return lax.rem(ctx + offset, n_ctx)

    greet(
        [(along(i), fsdp) for i in range(1, n_ctx)]
        + [(ctx, same_core(i)) for i in range(1, chips)]
        + [(ctx, sibling)]
    )
    kept = [
        pltpu.make_async_copy(x_ref, x_all.at[ctx], local.at[0]),
        pltpu.make_async_copy(table_ref, table_all.at[ctx], local.at[1]),
        pltpu.make_async_copy(packed_ref, packed_all.at[fsdp], local.at[2]),
    ]
    for copy in kept:
        copy.start()

    def packed_copy(source, owner, sems, to):
        return push(source, packed_all.at[owner], sems, packed_arrived.at[owner], (ctx, to))

    for i in range(1, chips):
        packed_copy(packed_ref, fsdp, packed_send.at[i], same_core(i)).start()
    packed_copy(packed_ref, fsdp, packed_send.at[0], sibling).start()
    for i in range(1, n_ctx):
        push(
            table_ref, table_all.at[ctx], table_send.at[i], table_arrived.at[ctx], (along(i), fsdp)
        ).start()
    line = LineGather(n_ctx, ctx, fsdp, x_ref, x_all, up, down, arrived)
    for step in range(n_ctx):
        line.step(step)
    for i in range(1, chips):
        owner = same_core(chips - i)
        packed_copy(packed_ref, owner, packed_send.at[i], sibling).wait_recv()
        packed_copy(packed_all.at[owner], owner, passed_send.at[i], sibling).start()
    for i in range(chips):
        owner = lax.rem(sibling + 2 * i, n_fsdp)
        packed_copy(packed_ref, owner, packed_send.at[0], sibling).wait_recv()
    for i in range(1, n_ctx):
        owner = along(i)
        push(
            table_ref, table_all.at[owner], table_send.at[i], table_arrived.at[owner], (owner, fsdp)
        ).wait()
    line.finish()
    for i in range(chips):
        packed_copy(packed_ref, fsdp, packed_send.at[i], sibling).wait_send()
    for i in range(1, chips):
        packed_copy(packed_ref, fsdp, passed_send.at[i], sibling).wait_send()
    for copy in kept:
        copy.wait()


def run_first_gather(n_ctx, n_fsdp, x, table, packed):
    anywhere = pl.BlockSpec(memory_space=pl.ANY)
    dma = pltpu.SemaphoreType.DMA
    return pl.pallas_call(
        functools.partial(first_gather, n_ctx, n_fsdp),
        in_specs=[anywhere] * 3,
        out_specs=[anywhere] * 3,
        out_shape=[
            jax.ShapeDtypeStruct((n_ctx,) + x.shape, x.dtype),
            jax.ShapeDtypeStruct((n_ctx,) + table.shape, table.dtype),
            jax.ShapeDtypeStruct((n_fsdp,) + packed.shape, packed.dtype),
        ],
        scratch_shapes=[
            dma((3,)),
            dma((n_ctx,)),
            dma((n_ctx,)),
            dma((n_ctx,)),
            dma((n_ctx,)),
            dma((n_ctx,)),
            dma((n_fsdp // 2,)),
            dma((n_fsdp // 2,)),
            dma((n_fsdp,)),
        ],
        compiler_params=pltpu.CompilerParams(collective_id=1, has_side_effects=True),
        cost_estimate=pl.CostEstimate(
            flops=0, bytes_accessed=200 * 2**20, transcendentals=0
        ),
    )(x, table, packed)


TILE = 512
AUX = 128


def expert_exchange(
    n_ctx,
    n_fsdp,
    x_ref,
    sel_ref,
    selt_ref,
    gate_ref,
    up_ref,
    down_ref,
    grad_ref,
    dealt_ref,
    rows_ref,
    back_ref,
    part_ref,
    inner_ref,
    dg_ref,
    du_ref,
    y_low_ref,
    y_high_ref,
    dealt_all,
    w_gate,
    w_up,
    w_down,
    held,
    staged,
    rows_in,
    grad_in,
    inner_out,
    dg_out,
    du_out,
    y_out,
    back_in,
    w_sems,
    local,
    held_send,
    held_arrived,
    rows_send,
    rows_arrived,
    back_send,
    back_arrived,
    part_send,
    part_arrived,
    dealt_send,
    dealt_arrived,
    out_sems,
):
    ctx, fsdp = lax.axis_index("ctx"), lax.axis_index("fsdp")
    experts = n_ctx * n_fsdp
    expert = ctx * n_fsdp + fsdp
    width, hidden = w_gate.shape
    wide = held.shape[2]
    capacity = staged.shape[2]
    half = n_fsdp // 2
    tiles = [(at, min(TILE, wide - at)) for at in range(0, wide, TILE)]

    def along(offset):
        return lax.rem(ctx + offset, n_ctx)

    def around(offset):
        return lax.rem(fsdp + offset, n_fsdp)

    greet(
        [(along(i), fsdp) for i in range(1, n_ctx)] + [(ctx, around(i)) for i in range(1, n_fsdp)]
    )
    weights = [
        pltpu.make_async_copy(gate_ref, w_gate, w_sems.at[0]),
        pltpu.make_async_copy(up_ref, w_up, w_sems.at[1]),
        pltpu.make_async_copy(down_ref, w_down, w_sems.at[2]),
    ]
    own = pltpu.make_async_copy(x_ref, held.at[ctx], local.at[0])
    own.start()
    for copy in weights:
        copy.start()

    def held_copy(step):
        to = lax.rem(ctx + n_ctx - step, n_ctx)
        return push(x_ref, held.at[ctx], held_send.at[step], held_arrived.at[ctx], (to, fsdp))

    def rows_copy(step, group, offset):
        to = around(offset)
        return push(
            staged.at[step, to],
            rows_ref.at[fsdp, group],
            rows_send.at[step, offset],
            rows_arrived.at[group, fsdp],
            (ctx, to),
        )

    def rows_kept(step, group):
        return pltpu.make_async_copy(
            staged.at[step, fsdp], rows_ref.at[fsdp, group], rows_arrived.at[group, fsdp]
        )

    def back_copy(step, group, offset):
        to = around(offset)
        return push(
            staged.at[step, to],
            back_ref.at[group, fsdp],
            back_send.at[step, offset],
            back_arrived.at[group, fsdp],
            (ctx, to),
        )

    def back_kept(step, group):
        return pltpu.make_async_copy(
            staged.at[step, fsdp], back_ref.at[group, fsdp], back_arrived.at[group, fsdp]
        )

    def outputs(group):
        return [
            pltpu.make_async_copy(inner_out, inner_ref.at[:, group], out_sems.at[0]),
            pltpu.make_async_copy(dg_out, dg_ref.at[:, group], out_sems.at[1]),
            pltpu.make_async_copy(du_out, du_ref.at[:, group], out_sems.at[2]),
            pltpu.make_async_copy(
                y_out.at[:, :, : width // 2], y_low_ref.at[:, group], out_sems.at[3]
            ),
            pltpu.make_async_copy(
                y_out.at[:, :, width // 2 :], y_high_ref.at[:, group], out_sems.at[4]
            ),
        ]

    def dispatch(step):
        group = along(step)

        @pl.when(step == 0)
        def _():
            own.wait()

        @pl.when(step > 0)
        def _():
            push(
                x_ref, held.at[group], held_send.at[step], held_arrived.at[group], (group, fsdp)
            ).wait_recv()

        @pl.when(step + 1 < n_ctx)
        def _():
            held_copy(step + 1).start()

        for at, size in tiles:
            picked = nn(sel_ref[group], held[group, :, at : at + size])
            staged[step, :, :, at : at + size] = picked.astype(BF).reshape(n_fsdp, capacity, size)
        rows_kept(step, group).start()
        for offset in range(1, n_fsdp):
            rows_copy(step, group, offset).start()

    def compute(step):
        group = along(step)
        rows_kept(step, group).wait()
        for offset in range(1, n_fsdp):
            source = around(offset)
            push(
                staged.at[step, source],
                rows_ref.at[source, group],
                rows_send.at[step, offset],
                rows_arrived.at[group, source],
                (ctx, source),
            ).wait_recv()
        load_rows = pltpu.make_async_copy(rows_ref.at[:, group], rows_in, local.at[1])
        load_inner = pltpu.make_async_copy(grad_ref.at[:, group], grad_in, local.at[2])
        load_rows.start()
        load_inner.start()

        @pl.when(step == 0)
        def _():
            for copy in weights:
                copy.wait()

        @pl.when(step > 0)
        def _():
            for copy in outputs(group):
                copy.wait()

        for offset in range(1, n_fsdp):
            rows_copy(step, group, offset).wait_send()
        load_rows.wait()
        load_inner.wait()
        count = half * capacity
        lane = lax.broadcasted_iota(jnp.int32, (count, AUX), 1)
        high, low = lane == expert, lane == experts + expert

        @pl.loop(0, 2)
        def _(part):
            sources = pl.ds(part * half, half)
            rows = rows_in[sources, :, :width].reshape(count, width)
            aux = rows_in[sources, :, width:].reshape(count, AUX).astype(F32)
            gate = jnp.sum(jnp.where(high | low, aux, 0.0), axis=1, keepdims=True)
            g = nn(rows, w_gate[...])
            u = nn(rows, w_up[...])
            s = jax.nn.sigmoid(g)
            inner = g * s * u
            d_inner = nt(grad_in[sources].reshape(count, width), w_down[...])
            d_gate = jnp.sum(inner * d_inner, axis=1, keepdims=True)
            d_inner = d_inner * gate
            dg = (d_inner * u * s * (1.0 + g * (1.0 - s))).astype(BF)
            du = (d_inner * g * s).astype(BF)
            inner_out[sources] = (inner * gate).astype(BF).reshape(half, capacity, hidden)
            dg_out[sources] = dg.reshape(half, capacity, hidden)
            du_out[sources] = du.reshape(half, capacity, hidden)
            rest = d_gate - d_gate.astype(BF).astype(F32)
            staged[step, sources, :, width:] = (
                jnp.where(high, d_gate, jnp.where(low, rest, 0.0))
                .astype(BF)
                .reshape(half, capacity, AUX)
            )
            for at in range(0, width, TILE):
                grad = nt(dg, w_gate[at : at + TILE, :]) + nt(du, w_up[at : at + TILE, :])
                staged[step, sources, :, at : at + TILE] = grad.astype(BF).reshape(
                    half, capacity, TILE
                )
            low_inner = inner.astype(BF)
            for at in range(0, width, TILE):
                y = nn(low_inner, w_down[:, at : at + TILE]) * gate
                y_out[sources, :, at : at + TILE] = y.astype(BF).reshape(half, capacity, TILE)

        def send_back(step, group):
            back_kept(step, group).start()
            for offset in range(1, n_fsdp):
                back_copy(step, group, offset).start()

        @pl.when(step > 0)
        def _():
            send_back(step, group)

        @pl.when(step == n_ctx - 1)
        def _():
            send_back(0, ctx)

        for copy in outputs(group):
            copy.start()

    def combine(step):
        group = along(step)
        back_kept(step, group).wait()
        for offset in range(1, n_fsdp):
            source = around(offset)
            push(
                staged.at[step, source],
                back_ref.at[group, source],
                back_send.at[step, offset],
                back_arrived.at[group, source],
                (ctx, source),
            ).wait_recv()
        load = pltpu.make_async_copy(back_ref.at[group], back_in, local.at[1])
        load.start()
        load.wait()
        for at, size in tiles:
            back = back_in[:, :, at : at + size].reshape(n_fsdp * capacity, size)
            held[group, :, at : at + size] = nn(selt_ref[group], back).astype(BF)

        @pl.when(step == 0)
        def _():
            pltpu.make_async_copy(
                held.at[group], part_ref.at[ctx], part_arrived.at[ctx]
            ).start()

        @pl.when(step > 0)
        def _():
            push(
                held.at[group],
                part_ref.at[ctx],
                part_send.at[step],
                part_arrived.at[ctx],
                (group, fsdp),
            ).start()

    def dealt_copy(offset):
        to = along(offset)
        return push(
            dealt_ref.at[to],
            dealt_all.at[ctx],
            dealt_send.at[offset],
            dealt_arrived.at[ctx],
            (to, fsdp),
        )

    dealt_kept = pltpu.make_async_copy(
        dealt_ref.at[ctx], dealt_all.at[ctx], dealt_arrived.at[ctx]
    )

    @pl.loop(0, n_ctx + 3)
    def _(tick):
        @pl.when(tick < n_ctx)
        def _():
            dispatch(tick)

        @pl.when(tick == n_ctx - 1)
        def _():
            dealt_kept.start()
            for offset in range(1, n_ctx):
                dealt_copy(offset).start()

        @pl.when((tick >= 1) & (tick <= n_ctx))
        def _():
            compute(tick - 1)

        @pl.when(tick >= 3)
        def _():
            combine(lax.rem(tick - 2, n_ctx))

    pltpu.make_async_copy(held.at[ctx], part_ref.at[ctx], part_arrived.at[ctx]).wait()
    for step in range(1, n_ctx):
        other = along(step)
        copy = push(
            held.at[other], part_ref.at[other], part_send.at[step], part_arrived.at[other], (other, fsdp)
        )
        copy.wait()
        held_copy(step).wait_send()
    dealt_kept.wait()
    for offset in range(1, n_ctx):
        other = along(offset)
        push(
            dealt_ref.at[other],
            dealt_all.at[other],
            dealt_send.at[offset],
            dealt_arrived.at[other],
            (other, fsdp),
        ).wait()
    for step in range(n_ctx):
        for offset in range(1, n_fsdp):
            back_copy(step, along(step), offset).wait_send()
    for copy in outputs(along(n_ctx - 1)):
        copy.wait()


def run_expert_exchange(n_ctx, n_fsdp, x, select, select_t, gate, up, down, grads, dealt):
    anywhere, inside = pl.BlockSpec(memory_space=pl.ANY), pl.BlockSpec(memory_space=pltpu.VMEM)
    span, wide = x.shape
    width, hidden = gate.shape
    capacity = grads.shape[2]
    slots = (n_fsdp, n_ctx, capacity)
    one = (n_fsdp, capacity)
    dma, vmem, shape = pltpu.SemaphoreType.DMA, pltpu.VMEM, jax.ShapeDtypeStruct
    return pl.pallas_call(
        functools.partial(expert_exchange, n_ctx, n_fsdp),
        in_specs=[anywhere, inside, inside] + [anywhere] * 5,
        out_specs=[anywhere] * 9,
        out_shape=[
            shape(slots + (wide,), BF),
            shape((n_ctx, n_fsdp, capacity, wide), BF),
            shape((n_ctx, span, wide), BF),
            shape(slots + (hidden,), BF),
            shape(slots + (hidden,), BF),
            shape(slots + (hidden,), BF),
            shape(slots + (width // 2,), BF),
            shape(slots + (width // 2,), BF),
            shape(dealt.shape, BF),
        ],
        scratch_shapes=[
            vmem((width, hidden), BF),
            vmem((width, hidden), BF),
            vmem((hidden, width), BF),
            vmem((n_ctx, span, wide), BF),
            vmem((n_ctx,) + one + (wide,), BF),
            vmem(one + (wide,), BF),
            vmem(one + (width,), BF),
            vmem(one + (hidden,), BF),
            vmem(one + (hidden,), BF),
            vmem(one + (hidden,), BF),
            vmem(one + (width,), BF),
            vmem(one + (wide,), BF),
            dma((3,)),
            dma((3,)),
            dma((n_ctx,)),
            dma((n_ctx,)),
            dma((n_ctx, n_fsdp)),
            dma((n_ctx, n_fsdp)),
            dma((n_ctx, n_fsdp)),
            dma((n_ctx, n_fsdp)),
            dma((n_ctx,)),
            dma((n_ctx,)),
            dma((n_ctx,)),
            dma((n_ctx,)),
            dma((5,)),
        ],
        compiler_params=pltpu.CompilerParams(
            collective_id=2, has_side_effects=True, vmem_limit_bytes=60 * 2**20
        ),
        cost_estimate=pl.CostEstimate(
            flops=12 * n_fsdp * n_ctx * capacity * width * hidden,
            bytes_accessed=600 * 2**20,
            transcendentals=0,
        ),
    )(x, select, select_t, gate, up, down, grads, dealt)


def last_reduce(n_ctx, n_fsdp, *refs):
    ctx, fsdp = lax.axis_index("ctx"), lax.axis_index("fsdp")
    count = (len(refs) - 1) // 11
    ins, alls, local, refs = refs[:count], refs[count : 2 * count], refs[2 * count], refs[2 * count + 1 :]
    items = [refs[9 * i : 9 * i + 9] for i in range(count)]
    chips, chip, core = n_fsdp // 2, fsdp // 2, lax.rem(fsdp, 2)
    sibling = chip * 2 + 1 - core

    def along(offset):
        return lax.rem(ctx + offset, n_ctx)

    def other_chip(offset):
        return lax.rem(chip + offset, chips)

    greet(
        [(along(i), fsdp) for i in range(1, n_ctx)]
        + [(ctx, other_chip(i) * 2 + core) for i in range(1, chips)]
        + [(ctx, sibling)]
    )
    crossing, loads, lines = [], [], []
    for at, (in_ref, all_ref, item) in enumerate(zip(ins, alls, items)):
        mine, beside, landed, own, cross, sends, arrived, line_sems, line_arrived = item
        crossing.append(
            push(in_ref.at[:, 1 - core], beside, cross.at[0], cross.at[1], (ctx, sibling))
        )
        crossing[-1].start()
        loads.append(pltpu.make_async_copy(in_ref.at[:, core], mine, local.at[at]))
        loads[-1].start()
        lines.append(
            LineGather(
                n_ctx, ctx, fsdp, own, all_ref, line_sems.at[0], line_sems.at[1], line_arrived
            )
        )

    def chip_copy(item, offset):
        mine, beside, landed, own, cross, sends, arrived, line_sems, line_arrived = item
        to = other_chip(offset)
        return push(
            mine.at[to], landed.at[chip], sends.at[offset], arrived.at[chip], (ctx, to * 2 + core)
        )

    for crossed, loaded, item in zip(crossing, loads, items):
        mine, beside = item[:2]
        loaded.wait()
        crossed.wait_recv()
        for offset in range(1, chips + 1):
            to = other_chip(offset)
            mine[to] = (mine[to].astype(F32) + beside[to].astype(F32)).astype(BF)
            if offset < chips:
                chip_copy(item, offset).start()
    keeps = []
    for at, (item, line, all_ref) in enumerate(zip(items, lines, alls)):
        mine, beside, landed, own, cross, sends, arrived, line_sems, line_arrived = item
        total = mine[chip].astype(F32)
        for offset in range(1, chips):
            source = other_chip(offset)
            push(
                mine.at[source], landed.at[source], sends.at[offset], arrived.at[source], (ctx, sibling)
            ).wait_recv()
            total = total + landed[source].astype(F32)
        own[...] = total.astype(BF)
        line.step(0)
        keeps.append(pltpu.make_async_copy(own, all_ref.at[ctx], local.at[at]))
        keeps[-1].start()
    for step in range(1, n_ctx):
        for line in lines:
            line.step(step)
    for crossed, keep, line, item in zip(crossing, keeps, lines, items):
        crossed.wait_send()
        keep.wait()
        line.finish()
        for offset in range(1, chips):
            chip_copy(item, offset).wait_send()


def run_last_reduce(n_ctx, n_fsdp, grads):
    anywhere = pl.BlockSpec(memory_space=pl.ANY)
    dma, vmem, shape = pltpu.SemaphoreType.DMA, pltpu.VMEM, jax.ShapeDtypeStruct
    chips = n_fsdp // 2
    grads = [grad.reshape((chips, 2, -1) + grad.shape[-1:]) for grad in grads]
    blocks = [grad.shape[2:] for grad in grads]
    scratch = [dma((len(grads),))]
    for block in blocks:
        scratch += [
            vmem((chips,) + block, BF),
            vmem((chips,) + block, BF),
            vmem((chips,) + block, BF),
            vmem(block, BF),
            dma((2,)),
            dma((chips,)),
            dma((chips,)),
            dma((2, n_ctx)),
            dma((n_ctx,)),
        ]
    return pl.pallas_call(
        functools.partial(last_reduce, n_ctx, n_fsdp),
        in_specs=[anywhere] * len(grads),
        out_specs=[anywhere] * len(grads),
        out_shape=[shape((n_ctx,) + block, BF) for block in blocks],
        scratch_shapes=scratch,
        compiler_params=pltpu.CompilerParams(
            collective_id=3, has_side_effects=True, vmem_limit_bytes=60 * 2**20
        ),
        cost_estimate=pl.CostEstimate(flops=0, bytes_accessed=400 * 2**20, transcendentals=0),
    )(*grads)


def finish(
    n_ctx,
    share,
    experts,
    shared_ref,
    rest_ref,
    out_ref,
    dh_ref,
    x_ref,
    resid_grad_ref,
    resid_ref,
    moe_low_ref,
    moe_high_ref,
    gain_ref,
    query_ref,
    key_ref,
    value_ref,
    out_grad_ref,
    input_grad_ref,
    output_ref,
    router_ref,
    gains_ref,
):
    q_width = shared_ref.shape[2] - 2 * HEAD_SIZE
    for block in range(n_ctx):
        query_ref[:, block * q_width : (block + 1) * q_width] = shared_ref[
            block, :, :q_width
        ].astype(F32)
    for target, at in ((key_ref, q_width), (value_ref, q_width + HEAD_SIZE)):
        for kv in range(KEY_VALUE_HEADS):
            total = shared_ref[kv * share, :, at : at + HEAD_SIZE].astype(F32)
            for block in range(kv * share + 1, (kv + 1) * share):
                total = total + shared_ref[block, :, at : at + HEAD_SIZE].astype(F32)
            target[:, kv * HEAD_SIZE : (kv + 1) * HEAD_SIZE] = total
    out_grad_ref[...] = out_ref[0].astype(F32)
    x = x_ref[...].astype(F32)
    r = inverse_rms(x)
    n = dh_ref[...].astype(F32) * gain_ref[...]
    input_grad_ref[...] = (
        resid_grad_ref[...] + r * n - x * (r * r * r) * jnp.mean(n * x, axis=-1, keepdims=True)
    ).astype(BF)
    half = resid_ref.shape[1] // 2
    output_ref[:, :half] = (resid_ref[:, :half] + moe_low_ref[...].astype(F32)).astype(BF)
    output_ref[:, half:] = (resid_ref[:, half:] + moe_high_ref[...].astype(F32)).astype(BF)

    @pl.when(pl.program_id(0) == n_ctx - 1)
    def _():
        rest = rest_ref[0].astype(F32)
        for block in range(1, n_ctx):
            rest = rest + rest_ref[block].astype(F32)
        router_ref[...] = rest[:, :experts]
        gains_ref[...] = rest.T[experts : experts + 8]


def run_finish(
    n_ctx, experts, shared, rest, out_grad, d_hidden, x, resid_grad, resid, moe_low, moe_high, gain
):
    _, rows, wide = shared.shape
    span, width = x.shape
    _, piece, _ = out_grad.shape
    shape = jax.ShapeDtypeStruct
    part, tokens = rows // n_ctx, span // n_ctx
    whole = lambda dims: pl.BlockSpec(dims, lambda i: (0,) * len(dims))
    by_rows = lambda count, columns: pl.BlockSpec((count, columns), lambda i: (i, 0))
    q_columns, kv_columns = QUERY_HEADS * HEAD_SIZE, KEY_VALUE_HEADS * HEAD_SIZE
    return pl.pallas_call(
        functools.partial(finish, n_ctx, n_ctx // KEY_VALUE_HEADS, experts),
        grid=(n_ctx,),
        in_specs=[
            pl.BlockSpec((n_ctx, part, wide), lambda i: (0, i, 0)),
            whole(rest.shape),
            pl.BlockSpec((1, piece, width), lambda i: (i, 0, 0)),
        ]
        + [by_rows(tokens, width)] * 4
        + [by_rows(tokens, width // 2)] * 2
        + [whole((1, width))],
        out_specs=[
            by_rows(part, q_columns),
            by_rows(part, kv_columns),
            by_rows(part, kv_columns),
            by_rows(piece, width),
            by_rows(tokens, width),
            by_rows(tokens, width),
            whole((rows, experts)),
            whole((8, rows)),
        ],
        out_shape=[
            shape((rows, q_columns), F32),
            shape((rows, kv_columns), F32),
            shape((rows, kv_columns), F32),
            shape((n_ctx * piece, width), F32),
            shape((span, width), BF),
            shape((span, width), BF),
            shape((rows, experts), F32),
            shape((8, rows), F32),
        ],
        compiler_params=pltpu.CompilerParams(vmem_limit_bytes=48 * 2**20),
    )(shared, rest, out_grad, d_hidden, x, resid_grad, resid, moe_low, moe_high, gain)


def attention_exchange(
    n_ctx,
    n_fsdp,
    heads,
    q_ref,
    k_ref,
    v_ref,
    cos_ref,
    sin_ref,
    gains_ref,
    own_ref,
    key_ref,
    sel_ref,
    grad_ref,
    out_ref,
    total_ref,
    dealt_ref,
    attn_ref,
    rows_ref,
    keys,
    values_t,
    mixed,
    w_out,
    held,
    low,
    high,
    grads,
    staged,
    local,
    grad_up,
    grad_down,
    grad_arrived,
    rows_send,
    rows_arrived,
    up_send,
    down_send,
    low_arrived,
    high_arrived,
):
    head = pl.program_id(0)
    ctx, fsdp = lax.axis_index("ctx"), lax.axis_index("fsdp")
    _, span, width = held.shape
    capacity = staged.shape[2]
    q_width = heads * HEAD_SIZE

    def along(offset):
        return lax.rem(ctx + offset, n_ctx)

    def around(offset):
        return lax.rem(fsdp + offset, n_fsdp)

    line = LineGather(n_ctx, ctx, fsdp, grad_ref, grads, grad_up, grad_down, grad_arrived)
    sums = LineScatter(
        n_ctx, ctx, fsdp, 4, held, low, high, up_send, down_send, low_arrived, high_arrived
    )
    own = pltpu.make_async_copy(grad_ref, grads.at[ctx], local.at[0])
    weights = pltpu.make_async_copy(
        out_ref.at[pl.ds(ctx * q_width, q_width)], w_out, local.at[1]
    )

    def rows_copy(group, offset):
        to = around(offset)
        return push(
            staged.at[group, to],
            rows_ref.at[fsdp, group],
            rows_send.at[group, offset],
            rows_arrived.at[group, fsdp],
            (ctx, to),
        )

    def rows_kept(group):
        return pltpu.make_async_copy(
            staged.at[group, fsdp], rows_ref.at[fsdp, group], rows_arrived.at[group, fsdp]
        )

    def pick(group):
        for at in range(0, width, TILE):
            picked = nn(sel_ref[group], grads[group, :, at : at + TILE])
            staged[group, :, :, at : at + TILE] = picked.astype(BF).reshape(n_fsdp, capacity, TILE)
        rows_kept(group).start()
        for offset in range(1, n_fsdp):
            rows_copy(group, offset).start()

    def pick_from(distance):
        @pl.when(ctx - distance >= 0)
        def _():
            pick(ctx - distance)

        @pl.when(ctx + distance < n_ctx)
        def _():
            pick(ctx + distance)

    @pl.when(head == 0)
    def _():
        own.start()
        weights.start()
        greet(
            [(along(i), fsdp) for i in range(1, n_ctx)]
            + [(ctx, around(i)) for i in range(1, n_fsdp)]
        )
        line.step(0)
        own.wait()
        pick(ctx)
        prepare_keys(k_ref, v_ref, cos_ref, sin_ref, gains_ref, keys, values_t)

    @pl.when(head < heads)
    def _():
        def store(start, count, out):
            columns = pl.ds(pl.multiple_of(head * HEAD_SIZE, HEAD_SIZE), HEAD_SIZE)
            mixed[start : start + count, columns] = out

        attend_head(
            q_ref,
            cos_ref,
            sin_ref,
            gains_ref,
            own_ref,
            key_ref,
            total_ref,
            dealt_ref,
            keys,
            values_t,
            store,
        )

    @pl.when(head == heads - 2)
    def _():
        line.step(1)
        pick_from(1)

    @pl.when(head == heads)
    def _():
        weights.wait()
        for block in range(n_ctx):
            for at in range(0, width, TILE):
                held[block, :, at : at + TILE] = nn(
                    mixed[block * span : (block + 1) * span, :], w_out[:, at : at + TILE]
                ).astype(BF)
        line.step(2)
        sums.scatter(0)
        pick_from(2)
        sums.scatter(1)
        for step in range(3, n_ctx):
            line.step(step)
            pick_from(step)
        sums.scatter(2)
        sums.scatter(3)
        for chunk in range(4):
            sums.settle(chunk, attn_ref)
        sums.finish()
        line.finish()
        for group in range(n_ctx):
            rows_kept(group).wait()
            for offset in range(1, n_fsdp):
                source = around(offset)
                push(
                    staged.at[group, source],
                    rows_ref.at[source, group],
                    rows_send.at[group, offset],
                    rows_arrived.at[group, source],
                    (ctx, source),
                ).wait()


def run_attention_exchange(
    qkv, heads, n_ctx, n_fsdp, cosine, sine, gains, own, key_blocks, select, grad, w_out
):
    length = qkv.shape[0]
    span, width = grad.shape
    capacity = select.shape[1] // n_fsdp
    anywhere = pl.BlockSpec(memory_space=pl.ANY)
    dma, vmem, shape = pltpu.SemaphoreType.DMA, pltpu.VMEM, jax.ShapeDtypeStruct
    last = heads - 1
    whole, column, _, _, shared = attention_specs(heads, length)
    clip = lambda h: jnp.minimum(h, last)
    return pl.pallas_call(
        functools.partial(attention_exchange, n_ctx, n_fsdp, heads),
        grid=(heads + 1,),
        in_specs=[
            pl.BlockSpec((length, HEAD_SIZE), lambda h: (0, clip(h))),
            column(heads),
            column(heads + 1),
        ]
        + shared
        + [whole(select.shape), anywhere, anywhere],
        out_specs=[
            pl.BlockSpec((1, 8, length), lambda h: (clip(h), 0, 0)),
            pl.BlockSpec(
                (1, length, HEAD_SIZE),
                lambda h: (lax.rem(clip(h), n_ctx), 0, lax.div(clip(h), n_ctx)),
            ),
            whole((span, width)),
            anywhere,
        ],
        out_shape=[
            shape((heads, 8, length), F32),
            shape((n_ctx, length, heads // n_ctx * HEAD_SIZE), BF),
            shape((span, width), F32),
            shape((n_fsdp, n_ctx, capacity, width), BF),
        ],
        scratch_shapes=[
            vmem((length, HEAD_SIZE), BF),
            vmem((HEAD_SIZE, length), BF),
            vmem((length, heads * HEAD_SIZE), BF),
            vmem((heads * HEAD_SIZE, width), BF),
            vmem((n_ctx, span, width), BF),
            vmem((n_ctx, span, width), BF),
            vmem((n_ctx, span, width), BF),
            vmem((n_ctx, span, width), BF),
            vmem((n_ctx, n_fsdp, capacity, width), BF),
            dma((2,)),
            dma((n_ctx,)),
            dma((n_ctx,)),
            dma((n_ctx,)),
            dma((n_ctx, n_fsdp)),
            dma((n_ctx, n_fsdp)),
            dma((n_ctx, 4)),
            dma((n_ctx, 4)),
            dma((n_ctx, 4)),
            dma((n_ctx, 4)),
        ],
        compiler_params=pltpu.CompilerParams(
            collective_id=4, has_side_effects=True, vmem_limit_bytes=60 * 2**20
        ),
        cost_estimate=pl.CostEstimate(
            flops=4 * heads * length * length * HEAD_SIZE,
            bytes_accessed=400 * 2**20,
            transcendentals=heads * length * length,
        ),
    )(qkv, qkv, qkv, cosine, sine, gains, own, key_blocks, select, grad, w_out)


def on_device(
    inputs,
    block_ids,
    expert_ids,
    drop_order,
    attn_gain,
    w_query,
    key_projection_weight,
    value_projection_weight,
    q_gain,
    key_norm_gain,
    w_out,
    ffn_gain,
    w_router,
    expert_gate,
    expert_up,
    expert_down,
    cotangent,
):
    n_ctx, n_fsdp = lax.axis_size("ctx"), lax.axis_size("fsdp")
    ctx = lax.axis_index("ctx")
    span, width = inputs.shape[1], inputs.shape[2]
    length = block_ids.shape[1]
    experts = n_ctx * n_fsdp
    capacity = 5 * span * TOP // (4 * experts)
    slots = experts * capacity
    heads = QUERY_HEADS // n_ctx
    share = n_ctx // KEY_VALUE_HEADS
    own_rows = w_query.shape[0]
    q_width = heads * HEAD_SIZE
    qkv_width = q_width + 2 * HEAD_SIZE
    extra_width = -(-(experts + 8) // 128) * 128

    def gather_ctx(array):
        return lax.all_gather(array, "ctx", axis=0, tiled=True)

    def scatter_ctx(array):
        return lax.psum_scatter(array.astype(BF), "ctx", scatter_dimension=0, tiled=True)

    def route(rows):
        return lax.all_to_all(rows, "fsdp", split_axis=0, concat_axis=0, tiled=True)

    def columns(weight, index, count):
        return lax.dynamic_slice_in_dim(weight, index * count, count, axis=1)

    def as_column(vector):
        return jnp.pad(vector, (0, own_rows - vector.shape[0]))[:, None]

    packed = jnp.concatenate(
        [
            columns(w_query, ctx, q_width),
            columns(key_projection_weight, ctx // share, HEAD_SIZE),
            columns(value_projection_weight, ctx // share, HEAD_SIZE),
            w_router,
            as_column(attn_gain),
            as_column(ffn_gain),
            as_column(q_gain),
            as_column(key_norm_gain),
            jnp.zeros((own_rows, extra_width - experts - 4), BF),
        ],
        axis=1,
    )
    table = jnp.concatenate(
        [expert_ids[0].T, drop_order[0], jnp.zeros((7, span), jnp.int32)], axis=0
    )
    inputs_all, tables, packed_all = run_first_gather(n_ctx, n_fsdp, inputs[0], table, packed)
    out_all = lax.all_gather(w_out, "fsdp", axis=0, tiled=True)
    out_here = lax.dynamic_slice_in_dim(out_all, ctx * q_width, q_width, axis=0)
    inputs_all = inputs_all.reshape(length, width)
    packed_all = packed_all.reshape(width, qkv_width + extra_width)
    w_qkv = packed_all[:, :qkv_width]
    extra = packed_all[:, qkv_width:].T
    router_t = extra[:experts]
    gain_attn = extra[experts : experts + 1].astype(F32)
    gain_ffn = extra[experts + 1 : experts + 2].astype(F32)

    def head_gain(at):
        return extra[at].reshape(n_fsdp, own_rows)[:, : HEAD_SIZE // n_fsdp].reshape(1, HEAD_SIZE)

    gains = jnp.concatenate(
        [head_gain(experts + 2), head_gain(experts + 3), jnp.zeros((6, HEAD_SIZE), BF)], axis=0
    ).astype(F32)

    named = tables[:, :TOP, :]
    ranks = tables[:, TOP, :]
    here = ctx * n_fsdp + jnp.arange(n_fsdp, dtype=jnp.int32)
    member = jnp.any(named[:, :, None, :] == here[None, None, :, None], axis=1)
    before = (ranks[:, :, None] < ranks[:, None, :]).astype(BF)
    place = jnp.einsum(
        "gjs,gst->gjt", member.astype(BF), before, preferred_element_type=F32
    ).astype(jnp.int32)
    place = jnp.where(member, place, capacity)
    select = (
        place[:, :, None, :] == jnp.arange(capacity, dtype=jnp.int32)[None, None, :, None]
    ).astype(BF)

    fused = capacity % 16 == 0 and 2 * experts <= AUX and experts == QUERY_HEADS
    select_rows = select.reshape(n_ctx, n_fsdp * capacity, span)

    def dispatch(rows):
        picked = jnp.einsum(
            "gjkt,gtd->jgkd", select, rows.reshape(n_ctx, span, width), preferred_element_type=F32
        ).astype(BF)
        return route(picked).reshape(slots, width)

    def combine(rows):
        return gather_slots(route(rows.reshape(n_fsdp, n_ctx, capacity, width)))

    def gather_slots(back):
        return jnp.einsum("gjkt,jgkd->gtd", select, back, preferred_element_type=F32).reshape(
            length, -1
        )

    x_all = inputs_all.astype(F32)
    r_all = inverse_rms(x_all)
    hidden = (x_all * r_all * gain_attn).astype(BF)
    qkv = nn(hidden, w_qkv)
    exponent = np.arange(HALF, dtype=np.float32) * np.float32(2.0 / HEAD_SIZE)
    angles = np.arange(length, dtype=np.float32)[:, None] * (
        np.float32(ROPE_BASE) ** (-exponent)
    )
    cosine = jnp.asarray(np.tile(np.cos(angles), (1, 2)))
    sine = jnp.asarray(np.concatenate([-np.sin(angles), np.sin(angles)], axis=1))
    own_blocks = jnp.broadcast_to(block_ids, (8, length))
    key_blocks = block_ids.reshape(length, 1)
    piece = QUERY_HEADS * HEAD_SIZE // experts
    groups = n_fsdp // n_ctx
    if fused:
        totals, dealt, attn_out, grad_rows = run_attention_exchange(
            qkv,
            heads,
            n_ctx,
            n_fsdp,
            cosine,
            sine,
            gains,
            own_blocks,
            key_blocks,
            select_rows,
            cotangent[0],
            out_all,
        )
        grad_rows = grad_rows.reshape(slots, width)
    else:
        mixed, totals, _ = run_attention(
            qkv, heads, n_ctx, cosine, sine, gains, own_blocks, key_blocks
        )
        attn_out = scatter_ctx(nn(mixed, out_here))
        grad_rows = dispatch(gather_ctx(cotangent[0]))
        dealt = mixed.reshape(length, groups, n_ctx, piece).transpose(2, 0, 1, 3)
        dealt = dealt.reshape(n_ctx, length, groups * piece)

    x = inputs[0].astype(F32)
    resid = x + attn_out.astype(F32)
    r_ffn = inverse_rms(resid)
    normed = (resid * r_ffn * gain_ffn).astype(BF)
    if fused:
        chosen = jnp.any(
            expert_ids[0][:, :, None] == jnp.arange(experts, dtype=jnp.int32), axis=1
        )
        logits = nt(normed, router_t)
        gates = jax.nn.softmax(jnp.where(chosen, logits, -jnp.inf), axis=-1)
        high = lax.reduce_precision(gates, 8, 7)
        payload = jnp.concatenate(
            [
                normed,
                high.astype(BF),
                (gates - high).astype(BF),
                jnp.zeros((span, AUX - 2 * experts), BF),
            ],
            axis=1,
        )
        rows, _, parts, inner_low, dg, du, y_low, y_high, dealt = run_expert_exchange(
            n_ctx,
            n_fsdp,
            payload,
            select_rows,
            select_rows.swapaxes(1, 2),
            expert_gate[0],
            expert_up[0],
            expert_down[0],
            grad_rows.reshape(n_fsdp, n_ctx, capacity, width),
            dealt,
        )
        rows = rows.reshape(slots, width + AUX)[:, :width]
        inner_low, dg, du = (array.reshape(slots, -1) for array in (inner_low, dg, du))
        parts = jnp.sum(parts.astype(F32), axis=0)
        d_gates = parts[:, width : width + experts] + parts[:, width + experts : width + 2 * experts]
        d_logits = gates * (d_gates - jnp.sum(gates * d_gates, axis=-1, keepdims=True))
        d_logits = d_logits.astype(BF)
        d_normed = parts[:, :width] + nn(d_logits, router_t)
    else:
        dealt = lax.all_to_all(dealt, "ctx", split_axis=0, concat_axis=0, tiled=True)
        chosen = jnp.any(
            named[:, :, :, None] == jnp.arange(experts, dtype=jnp.int32), axis=1
        ).reshape(length, experts)
        normed = gather_ctx(normed)
        normed, grad_rows = lax.optimization_barrier((normed, grad_rows))
        grad_inner = nt(grad_rows, expert_down[0])
        logits = nt(normed, router_t)
        gates = jax.nn.softmax(jnp.where(chosen, logits, -jnp.inf), axis=-1)
        gates_here = lax.dynamic_slice_in_dim(gates, ctx * n_fsdp, n_fsdp, axis=1)
        gates_here = gates_here.reshape(n_ctx, span, n_fsdp).transpose(0, 2, 1)
        slot_gates = jnp.sum(select.astype(F32) * gates_here[:, :, None, :], axis=-1)
        slot_gates = route(slot_gates.transpose(1, 0, 2)).reshape(slots, 1)
        rows = dispatch(normed)
        g = nn(rows, expert_gate[0])
        u = nn(rows, expert_up[0])
        s = jax.nn.sigmoid(g)
        inner = g * s * u
        slot_dgates = jnp.sum(inner * grad_inner, axis=-1).reshape(n_fsdp, n_ctx, capacity)
        d_inner = grad_inner * slot_gates
        dg = (d_inner * u * s * (1.0 + g * (1.0 - s))).astype(BF)
        du = (d_inner * g * s).astype(BF)
        d_rows = (nt(dg, expert_gate[0]) + nt(du, expert_up[0])).astype(BF)
        y = (nn(inner.astype(BF), expert_down[0]) * slot_gates).astype(BF)
        y = y.reshape(n_fsdp, n_ctx, capacity, width)
        y_low, y_high = y[..., : width // 2], y[..., width // 2 :]
        inner_low = (inner * slot_gates).astype(BF)
        d_gates = jnp.einsum(
            "gjkt,jgk->gjt", select.astype(F32), route(slot_dgates), precision=lax.Precision.HIGHEST
        )
        weighted = (d_gates * gates_here).transpose(0, 2, 1).reshape(length, n_fsdp)
        d_logits = lax.dynamic_update_slice_in_dim(
            jnp.zeros((length, experts), F32), weighted, ctx * n_fsdp, axis=1
        ) - gates * jnp.sum(weighted, axis=1, keepdims=True)
        d_logits = d_logits.astype(BF)
        d_normed = scatter_ctx(combine(d_rows) + nn(d_logits, router_t)).astype(F32)

    gate_grad = tn(rows, dg)
    up_grad = tn(rows, du)
    down_grad = tn(inner_low, grad_rows)
    router_grad = tn(normed, d_logits)

    grad = cotangent[0].astype(F32)
    n = d_normed * gain_ffn
    d_resid = grad + r_ffn * n - resid * r_ffn**3 * jnp.mean(n * resid, axis=-1, keepdims=True)
    ffn_gain_grad = jnp.sum(d_normed * resid * r_ffn, axis=0)
    d_attn = gather_ctx(d_resid.astype(BF))
    y_low, y_high = route(y_low), route(y_high)
    y_low, d_attn = lax.optimization_barrier((gather_slots(y_low).astype(BF), d_attn))
    moe_low = scatter_ctx(y_low)
    d_mixed = nt(d_attn, out_here).astype(BF)
    out_grad = jnp.einsum("ntk,td->nkd", dealt, d_attn, preferred_element_type=F32).astype(BF)
    y_high, d_mixed, out_grad, gate_grad, up_grad, down_grad, router_grad = (
        lax.optimization_barrier(
            (y_high, d_mixed, out_grad, gate_grad, up_grad, down_grad, router_grad)
        )
    )
    y_high = gather_slots(y_high).astype(BF)
    y_high, d_mixed, moe_low = lax.optimization_barrier((y_high, d_mixed, moe_low))
    moe_high = scatter_ctx(y_high)

    dq, dkv, dgains = run_attention_back(
        qkv, d_mixed, totals, heads, cosine, sine, gains, own_blocks, key_blocks
    )
    d_qkv = jnp.concatenate([dq, dkv], axis=1)
    d_hidden = nt(d_qkv, w_qkv)
    attn_gain_grad = jnp.sum(d_hidden * x_all * r_all, axis=0)

    def spread(vector):
        parts = vector.reshape(n_fsdp, HEAD_SIZE // n_fsdp)
        return jnp.pad(parts, ((0, 0), (0, own_rows - parts.shape[1]))).reshape(width)

    small = jnp.stack(
        [attn_gain_grad, ffn_gain_grad, spread(dgains[0]), spread(dgains[1])], axis=1
    )
    extra_grad = jnp.concatenate(
        [
            router_grad.astype(BF),
            small.astype(BF),
            jnp.zeros((width, extra_width - experts - 4), BF),
        ],
        axis=1,
    )
    shared_grad = tn(hidden, d_qkv).astype(BF)
    d_hidden, moe_high = lax.optimization_barrier((d_hidden.astype(BF), moe_high))
    d_hidden = scatter_ctx(d_hidden)
    shared_grad, rest, out_grad = run_last_reduce(
        n_ctx, n_fsdp, [shared_grad, extra_grad, out_grad.reshape(n_fsdp * piece, width)]
    )
    query_grad, key_grad, value_grad, out_grad, input_grad, output, router_grad, gain_grads = (
        run_finish(
            n_ctx,
            experts,
            shared_grad,
            rest,
            out_grad,
            d_hidden,
            inputs[0],
            d_resid,
            resid,
            moe_low,
            moe_high,
            gain_attn,
        )
    )
    head_rows = HEAD_SIZE // n_fsdp
    return (
        output[None],
        input_grad[None],
        gain_grads[0],
        query_grad,
        key_grad,
        value_grad,
        gain_grads[2, :head_rows],
        gain_grads[3, :head_rows],
        out_grad,
        gain_grads[1],
        router_grad,
        gate_grad[None],
        up_grad[None],
        down_grad[None],
    )


def solution(mesh):
    rows, tokens = P("fsdp", None), P("fsdp", "ctx", None)
    vector, expert = P("fsdp"), P(("ctx", "fsdp"), None, None)
    in_specs = (
        tokens,
        rows,
        tokens,
        tokens,
        vector,
        rows,
        rows,
        rows,
        vector,
        vector,
        rows,
        vector,
        rows,
        expert,
        expert,
        expert,
        tokens,
    )
    out_specs = (
        tokens,
        tokens,
        vector,
        rows,
        rows,
        rows,
        vector,
        vector,
        rows,
        vector,
        rows,
        expert,
        expert,
        expert,
    )
    return jax.shard_map(
        on_device, mesh=mesh, in_specs=in_specs, out_specs=out_specs, check_vma=False
    )
```
